256 devices in a mesh: row: 32 (over x, z_lo, core), col: 8 (over y, z_hi).
Axes of the slice: x: 4, y: 4, z: 8 (z_hi: 2, z_lo: 4; z = z_hi * 4 + z_lo), core: 2. Of those that a mesh axis runs over, the one named last changes fastest.
Arguments:
- embed: bfloat16 [2048, 512], P(('row', 'col')), may hold values from -6 to 6
- left_proj: bfloat16 [512, 32], replicated, may hold values from -0.25 to 0.25
- right_proj: bfloat16 [512, 32], replicated, may hold values from -0.25 to 0.25
- conv_w: bfloat16 [9, 32, 32], replicated, may hold values from -0.375 to 0.375
- cotangent: bfloat16 [32, 2048, 2048], P(None, 'row', 'col'), may hold values from -0.1796875 to 0.1796875
Outputs:
- pair_out: bfloat16 [32, 2048, 2048], P(None, 'row', 'col')
- conv_grad: float32 [9, 32, 32], replicated
- left_grad: float32 [512, 32], replicated
- right_grad: float32 [512, 32], replicated
- embed_grad: float32 [2048, 512], P(('row', 'col'))
The draws below stay inside these ranges and needn't reach their ends.
All inputs are finite; a program needn't handle non-finite values.
Results may differ from the reference program's by a relative error of at most 0.0057.
Values may be sent and summed in bfloat16 or wider, within the bound.
A program may use at most 128 MiB of HBM per device.

```python
import jax
import jax.numpy as jnp
from jax import lax

D = 512
C = 32
DILATION_STEP = 4
NB = 2048


def raised(entries, stream_key, source, target, blocks, factor):
    owner, partner = [(jnp.arange(entries.shape[dim]) // (entries.shape[dim] // blocks)).reshape([-1 if axis == dim else 1 for axis in range(entries.ndim)]) for dim in (source, target)]
    chosen = jax.random.permutation(stream_key, blocks)[partner]
    strong = (owner == chosen) | (owner == (partner + blocks // 2) % blocks)
    return jnp.where(strong, factor * entries, entries)


def level_of(stream_key, shape, shards, least, top_value):
    loudness = 1.0
    for axis_at, blocks in shards:
        draws = jax.random.uniform(jax.random.fold_in(jax.random.fold_in(stream_key, 6), axis_at), (blocks,), jnp.float32, least / len(shards), top_value / len(shards))
        loudness = loudness * jnp.repeat(jnp.exp(draws), shape[axis_at] // blocks).reshape((-1,) + (1,) * (len(shape) - 1 - axis_at))
    return loudness


def bell_draw(key, shape, scale, limit, shards=(), kind=jnp.bfloat16):
    entries = jax.random.normal(key, shape, jnp.float32) * scale
    if len(shards) > 0:
        entries = level_of(key, shape, shards, -0.22, 0.18) * entries
    return jnp.clip(entries, min=-limit, max=limit).astype(kind)


def gaussian_with(rng, extent, scale, limit, shards, heavy, kind=jnp.bfloat16):
    result = scale * jax.random.normal(rng, extent, jnp.float32)
    if shards:
        result = result * level_of(rng, extent, shards, -0.22, 0.18)
    return jnp.clip(raised(result, jax.random.fold_in(rng, 3), *heavy), -limit, limit).astype(kind)


def setup_inputs(seed: int = 0) -> dict:
    key_list = jax.random.split(jax.random.key(seed), 6)
    return {
        "embed": bell_draw(key_list[0], (NB, D), 1.0, 6.0, ((0, 256),)),
        "left_proj": bell_draw(key_list[1], (D, C), D ** -0.5, 0.25),
        "right_proj": bell_draw(key_list[2], (D, C), D ** -0.5, 0.25),
        "conv_w": bell_draw(key_list[3], (9, C, C), (9 * C) ** -0.5, 0.375),
        "cotangent": gaussian_with(key_list[4], (C, NB, NB), 0.03, 0.1796875, ((1, 32), (2, 8)), (1, 2, 32, 2.75)),
    }


def reference(embed, left_proj, right_proj, conv_w, cotangent):
    total_bins = embed.shape[0]
    channels = conv_w.shape[1]
    block_rows = min(128, total_bins)
    dilation_rate = DILATION_STEP
    left_feat = jnp.dot(embed, left_proj, preferred_element_type=jnp.float32).astype(jnp.bfloat16)
    right_feat = jnp.dot(embed, right_proj, preferred_element_type=jnp.float32).astype(jnp.bfloat16)
    left_table = jnp.pad(left_feat.astype(jnp.float32).T, ((0, 0), (dilation_rate, dilation_rate)))
    right_table = right_feat.astype(jnp.float32).T
    weights = conv_w.astype(jnp.float32)
    padded_gradient = jnp.pad(cotangent, ((0, 0), (dilation_rate, dilation_rate), (dilation_rate, dilation_rate)))
    cols_all = jnp.arange(total_bins, dtype=jnp.int32)
    cols_pad = jnp.arange(total_bins + 2 * dilation_rate, dtype=jnp.int32) - dilation_rate

    def row_block(carried, first_row):
        conv_acc, col_acc = carried
        rows_win = first_row - dilation_rate + jnp.arange(block_rows + 2 * dilation_rate, dtype=jnp.int32)
        range_inside = (rows_win >= 0) & (rows_win < total_bins)
        left_win = lax.dynamic_slice(left_table, (jnp.int32(0), first_row), (channels, block_rows + 2 * dilation_rate))
        summed = left_win[:, :, None] + right_table[:, None, :]
        active_taps = jnp.where(range_inside[None, :, None], jax.nn.softplus(summed), 0.0).astype(jnp.bfloat16)
        slope = jax.nn.sigmoid(summed[:, dilation_rate:dilation_rate + block_rows, :])
        padded_input = jnp.pad(active_taps, ((0, 0), (0, 0), (dilation_rate, dilation_rate))).astype(jnp.float32)
        grad_win = lax.dynamic_slice(padded_gradient, (jnp.int32(0), first_row, jnp.int32(0)), (channels, block_rows + 2 * dilation_rate, total_bins + 2 * dilation_rate))
        mask_win = cols_pad[None, :] >= rows_win[:, None]
        grad_win = jnp.where(mask_win[None], grad_win, jnp.zeros((), jnp.bfloat16)).astype(jnp.float32)
        rows_mid = first_row + jnp.arange(block_rows, dtype=jnp.int32)
        upper_mask = cols_all[None, :] >= rows_mid[:, None]
        center_grad = grad_win[:, dilation_rate:dilation_rate + block_rows, dilation_rate:dilation_rate + total_bins]
        conv_out = jnp.zeros((channels, block_rows, total_bins), jnp.float32)
        input_grad = jnp.zeros((channels, block_rows, total_bins), jnp.float32)
        tap_grads = []
        for tap_row in range(3):
            for tap_col in range(3):
                tap = 3 * tap_row + tap_col
                window = padded_input[:, dilation_rate * tap_row:dilation_rate * tap_row + block_rows, dilation_rate * tap_col:dilation_rate * tap_col + total_bins]
                conv_out = conv_out + jnp.einsum('oc,cij->oij', weights[tap], window)
                shifted = grad_win[:, dilation_rate * (2 - tap_row):dilation_rate * (2 - tap_row) + block_rows, dilation_rate * (2 - tap_col):dilation_rate * (2 - tap_col) + total_bins]
                input_grad = input_grad + jnp.einsum('oc,oij->cij', weights[tap], shifted)
                tap_grads.append(jnp.einsum('oij,cij->oc', center_grad, window))
        pair_block = jnp.where(upper_mask[None], conv_out, 0.0).astype(jnp.bfloat16)
        pre_grad = input_grad * slope
        return (conv_acc + jnp.stack(tap_grads), col_acc + pre_grad.sum(1)), (pair_block, pre_grad.sum(2))

    starts = jnp.arange(0, total_bins, block_rows, dtype=jnp.int32)
    init = (jnp.zeros((9, channels, channels), jnp.float32), jnp.zeros((channels, total_bins), jnp.float32))
    (conv_sum, col_sum), (pair_blocks, row_sums) = lax.scan(row_block, init, starts)
    pair_out = jnp.moveaxis(pair_blocks, 0, 1).reshape(channels, total_bins, total_bins)
    row_grad = jnp.moveaxis(row_sums, 0, 1).reshape(channels, total_bins).T
    col_grad = col_sum.T
    highest = lax.Precision.HIGHEST
    embed_grad = jnp.dot(row_grad, left_proj.astype(jnp.float32).T, precision=highest) + jnp.dot(col_grad, right_proj.astype(jnp.float32).T, precision=highest)
    grad_scale = 32.0 / total_bins
    embed_full = embed.astype(jnp.float32)
    left_grad = jnp.dot(embed_full.T, row_grad, precision=highest) * grad_scale
    right_grad = jnp.dot(embed_full.T, col_grad, precision=highest) * grad_scale
    return pair_out, conv_sum * grad_scale, left_grad, right_grad, embed_grad
```

```python
import functools

import jax
import jax.numpy as jnp
from jax import lax
from jax.experimental import pallas as pl
from jax.experimental.pallas import tpu as pltpu
from jax.sharding import PartitionSpec as P

MESH = pl.DeviceIdType.MESH
STEP = 4
OUTSIDE = -1e30
F32 = jnp.float32
BF16 = jnp.bfloat16
VMEM = pl.BlockSpec(memory_space=pltpu.VMEM)


def iota(shape, dim):
    return lax.broadcasted_iota(jnp.int32, shape, dim)


def one_hot(cond):
    return jnp.where(cond, 1.0, 0.0).astype(BF16)


def dot(a, b):
    return jnp.dot(a, b, preferred_element_type=F32)


def dot_nt(a, b):
    return lax.dot_general(a, b, (((1,), (1,)), ((), ())), preferred_element_type=F32)


def dot_tn(a, b):
    return lax.dot_general(a, b, (((0,), (0,)), ((), ())), preferred_element_type=F32)


def halves(x):
    high = x.astype(BF16)
    return high, (x - high.astype(F32)).astype(BF16)


def loop(n, f):
    def body(k, _):
        f(k)
        return 0

    lax.fori_loop(0, n, body, 0)


def wait_bytes(ref, sem):
    pltpu.make_async_copy(ref, ref, sem).wait()


def gather_kernel(nr, nc, e_ref, lp_ref, rp_ref, lf_ref, rf_ref, proj, src, fill, rl, rr, sem_l, sem_r, send):
    r, c = lax.axis_index("row"), lax.axis_index("col")
    per = nr // nc
    me_b = r * nc + c
    ct, q = r // per, me_b % (per * nc)
    n_right = per * nc
    last = rr.shape[0] - 1
    barrier = pltpu.get_barrier_semaphore()

    def greet(dst_r, dst_c):
        pl.semaphore_signal(barrier, inc=1, device_id=(dst_r, dst_c), device_id_type=MESH)

    loop(nc, lambda k: pl.when(k != c)(lambda: greet(r, k)))
    pl.when(r > 0)(lambda: greet(r - 1, nc - 1))
    pl.when(r < nr - 1)(lambda: greet(r + 1, 0))

    def greet_other(a, b):
        pl.when((a != r) | (b != c))(lambda: greet(a, b))

    loop(n_right, lambda k: greet_other(per * c + k // nc, k % nc))

    low_self = (per * c - 1 == r) & (c == nc - 1)
    high_self = (per * c + per == r) & (c == 0)
    pl.when((c > 0) & jnp.logical_not(low_self))(lambda: greet(per * c - 1, nc - 1))
    pl.when((c < nc - 1) & jnp.logical_not(high_self))(lambda: greet(per * c + per, 0))

    proj[...] = jnp.zeros_like(proj)
    proj[:, 0:32] = lp_ref[...]
    proj[:, 32:64] = rp_ref[...]
    src[...] = dot(e_ref[...], proj[...]).astype(BF16).astype(F32)
    fill[...] = jnp.full_like(fill, OUTSIDE)
    rr[n_right + 1 : last] = jnp.zeros_like(rr[n_right + 1 : last])

    own = (c == ct).astype(jnp.int32)
    up_l = (c == nc - 1) & (r < nr - 1)
    down_l = (c == 0) & (r > 0)
    up_r = (q == n_right - 1) & (ct < nc - 1)
    down_r = (q == 0) & (ct > 0)
    own_up = (c == ct + 1).astype(jnp.int32)
    own_down = (c == ct - 1).astype(jnp.int32)
    n_sends = nc - 1 + n_right - own
    n_sends += jnp.where(up_l, nc, 0) + jnp.where(down_l, nc, 0)
    n_sends += jnp.where(up_r, n_right - own_up, 0) + jnp.where(down_r, n_right - own_down, 0)
    pl.semaphore_wait(barrier, n_sends)

    def put(dst_r, dst_c, dst, sem, cls):
        mine = (dst_r == r) & (dst_c == c)

        @pl.when(mine)
        def _():
            pltpu.make_async_copy(src, dst, sem).start()

        @pl.when(jnp.logical_not(mine))
        def _():
            pltpu.make_async_remote_copy(
                src, dst, send.at[cls], sem, device_id=(dst_r, dst_c), device_id_type=MESH
            ).start()

    loop(nc, lambda k: put(r, k, rl.at[c + 1], sem_l, 0))
    loop(n_right, lambda k: put(k, ct, rr.at[q], sem_r, 1))
    pl.when(up_l)(lambda: loop(nc, lambda k: put(r + 1, k, rl.at[0], sem_l, 2)))
    pl.when(down_l)(lambda: loop(nc, lambda k: put(r - 1, k, rl.at[nc + 1], sem_l, 3)))
    pl.when(up_r)(lambda: loop(n_right, lambda k: put(k, ct + 1, rr.at[last], sem_r, 4)))
    pl.when(down_r)(lambda: loop(n_right, lambda k: put(k, ct - 1, rr.at[n_right], sem_r, 5)))

    def outside(cond, dst, sem):
        pl.when(cond)(lambda: pltpu.make_async_copy(fill, dst, sem).start())

    outside(r == 0, rl.at[0], sem_l)
    outside(r == nr - 1, rl.at[nc + 1], sem_l)
    outside(c == 0, rr.at[last], sem_r)
    outside(c == nc - 1, rr.at[n_right], sem_r)

    wait_bytes(rl, sem_l)
    lf_ref[...] = rl[...].reshape(rl.shape[0] * 8, 128)[STEP : STEP + lf_ref.shape[0]]
    wait_bytes(rr.at[0 : n_right + 2], sem_r)
    rf_ref[...] = rr[...].reshape(rr.shape[0] * 8, 128).T[32:64]

    wait_bytes(rr.at[0 : nc - 1], send.at[0])
    pl.when(own == 1)(lambda: wait_bytes(rr.at[0 : n_right - 1], send.at[1]))
    pl.when(own == 0)(lambda: wait_bytes(rr.at[0:n_right], send.at[1]))
    pl.when(up_l)(lambda: wait_bytes(rr.at[0:nc], send.at[2]))
    pl.when(down_l)(lambda: wait_bytes(rr.at[0:nc], send.at[3]))
    for cond, mine, sem in ((up_r, own_up, send.at[4]), (down_r, own_down, send.at[5])):
        pl.when(cond & (mine == 1))(lambda s=sem: wait_bytes(rr.at[0 : n_right - 1], s))
        pl.when(cond & (mine == 0))(lambda s=sem: wait_bytes(rr.at[0:n_right], s))


def build_taps(w_ref, tf, tb):
    spread = one_hot(iota((256, 32), 0) // 8 == iota((256, 32), 1))
    widen = one_hot(iota((32, 256), 1) // 8 == iota((32, 256), 0))
    s0, s1 = iota((256, 256), 0) % 8, iota((256, 256), 1) % 8
    same, above, below = s1 == s0, s1 == s0 + 4, s1 == s0 - 4

    def expand(x):
        return dot(spread, x.astype(BF16))

    for b in range(3):
        x = [expand(dot(w_ref[3 * a + b], widen)) for a in range(3)]
        tf[:, 256 * b : 256 * b + 256] = jnp.where(same, x[0], jnp.where(above, x[1], 0.0)).astype(BF16)
        tf[:, 768 + 256 * b : 1024 + 256 * b] = jnp.where(same, x[2], jnp.where(below, x[1], 0.0)).astype(BF16)
        y = [expand(dot_tn(w_ref[3 * a + b], widen)) for a in range(3)]
        rows = slice(256 * b, 256 * b + 256)
        tb[rows, 0:256] = jnp.where(same, y[2], jnp.where(above, y[1], 0.0)).astype(BF16)
        tb[rows, 256:512] = jnp.where(same, y[0], jnp.where(below, y[1], 0.0)).astype(BF16)


def mask_cotangent(r, c, cot_ref, m2):
    zero = jnp.zeros((256, 256), BF16)
    m2[:, 0:256] = zero
    m2[:, 2304:2560] = zero
    for k in range(4):
        x = cot_ref[:, 16 * k : 16 * k + 16, :].astype(F32)
        row = r * 64 + 16 * k + iota((16, 256), 0)
        col = c * 256 + iota((16, 256), 1)
        x = jnp.where((col >= row)[None], x, 0.0)
        m2[:, 256 * (2 * k + 1) : 256 * (2 * k + 2)] = x[:, 0:8].reshape(256, 256).astype(BF16)
        m2[:, 256 * (2 * k + 2) : 256 * (2 * k + 3)] = x[:, 8:16].reshape(256, 256).astype(BF16)


def lanes(h):
    return pl.ds(pl.multiple_of(h * 256, 256), 256)


def input_gradient(m2, tb, z):
    def body(h, _):
        pair = jnp.concatenate([m2[:, lanes(h)], m2[:, lanes(h + 1)]], axis=0)
        z[h] = dot(tb[...], pair)
        return 0

    lax.fori_loop(0, 9, body, 0)


def elementwise(lf, rf, z, a2, cacc, rowp):
    cacc[...] = jnp.zeros_like(cacc)
    rowp[...] = jnp.zeros_like(rowp)
    lane = iota((8, 128), 1)

    def body(h, _):
        base = pl.multiple_of(h * 8, 8)
        left = lf[pl.ds(base, 8), :]
        row = jnp.zeros((8, 128), F32)
        for pair in range(16):
            acts = []
            for c in (2 * pair, 2 * pair + 1):
                s = left[:, c : c + 1] + rf[c : c + 1, :]
                t = jnp.exp(-jnp.abs(s))
                act = jnp.maximum(s, 0.0) + jnp.log1p(t)
                slope = jnp.where(s >= 0, 1.0, t) / (1.0 + t)
                acts.append(act)
                total = jnp.zeros((8, 128), F32)
                for b, shift in enumerate((4, 0, 380)):
                    moved = pltpu.roll(slope, shift, 1) if shift else slope
                    p = z[h, pl.ds(256 * b + 8 * c, 8), :] * moved[:, 0:256]
                    cacc[b, 8 * c : 8 * c + 8, :] += p
                    total += p[:, 0:128] + p[:, 128:256]
                row = jnp.where(lane == c, jnp.sum(total, axis=1, keepdims=True), row)
            for b, shift in enumerate((4, 0, 380)):
                both = [(pltpu.roll(x, shift, 1) if shift else x)[:, 0:256] for x in acts]
                a2[b, 16 * pair : 16 * pair + 16, lanes(h)] = jnp.concatenate(both, axis=0).astype(BF16)
        rowp[pl.ds(base + 4, 8), :] = row
        return 0

    lax.fori_loop(0, 9, body, 0)


def column_sums(cacc, colp):
    pick = one_hot(iota((256, 128), 0) // 8 + 32 == iota((256, 128), 1))
    colp[...] = jnp.zeros_like(colp)
    for b in range(3):
        high, low = halves(cacc[b])
        colp[4 + 4 * b : 260 + 4 * b, :] += dot_tn(high, pick) + dot_tn(low, pick)


def convolve(r, c, a2, tf, out_ref):
    def body(k, _):
        parts = []
        for g in (2 * k, 2 * k + 1):
            stack = [a2[b, :, lanes(g + u)] for u in range(2) for b in range(3)]
            y = dot(tf[...], jnp.concatenate(stack, axis=0))
            parts.append(y.reshape(32, 8, 256))
        y = jnp.concatenate(parts, axis=1)
        row = r * 64 + 16 * k + iota((16, 256), 0)
        col = c * 256 + iota((16, 256), 1)
        y = jnp.where((col >= row)[None], y, 0.0).astype(BF16)
        out_ref[:, pl.ds(pl.multiple_of(16 * k, 16), 16), :] = y
        return 0

    lax.fori_loop(0, 4, body, 0)


def tap_gradient(m2, a2, taps):
    s0, s1 = iota((256, 256), 0) % 8, iota((256, 256), 1) % 8
    same, above, below = s1 == s0, s1 == s0 + 4, s1 == s0 - 4
    gather_rows = one_hot(iota((32, 256), 1) // 8 == iota((32, 256), 0))
    taps[...] = jnp.zeros_like(taps)
    for b in range(3):
        g0 = dot_nt(m2[:, 256:2304], a2[b, :, 0:2048])
        g1 = dot_nt(m2[:, 256:2304], a2[b, :, 256:2304])
        ys = (
            jnp.where(same, g0, 0.0),
            jnp.where(above, g0, jnp.where(below, g1, 0.0)),
            jnp.where(same, g1, 0.0),
        )
        for a in range(3):
            q, k = divmod(3 * a + b, 4)
            pick = one_hot(iota((256, 128), 0) // 8 + 32 * k == iota((256, 128), 1))
            high, low = halves(ys[a])
            rows = dot(gather_rows, high) + dot(gather_rows, low)
            high, low = halves(rows)
            taps[32 * q : 32 * q + 32, :] += dot(high, pick) + dot(low, pick)


def compute_kernel(lf, rf, cot_ref, w_ref, out_ref, taps, rowp, colp, m2, a2, z, tf, tb, cacc):
    r, c = lax.axis_index("row"), lax.axis_index("col")
    build_taps(w_ref, tf, tb)
    mask_cotangent(r, c, cot_ref, m2)
    input_gradient(m2, tb, z)
    elementwise(lf, rf, z, a2, cacc, rowp)
    column_sums(cacc, colp)
    convolve(r, c, a2, tf, out_ref)
    tap_gradient(m2, a2, taps)


def reduce_kernel(
    nr, nc, e_ref, lp_ref, rp_ref, rowp, colp, taps,
    sums_ref, eg_ref,
    proj, rrow, rrow2, rcol, rcol2, buf, r1, r2, r3, mid, fin, recv, send,
):
    r, c = lax.axis_index("row"), lax.axis_index("col")
    per = nr // nc
    n_right = per * nc
    me_b = r * nc + c
    ct, q = r // per, me_b % n_right
    k1 = (r % 8) * 2 + c % 2
    k2 = (r // 8) * 4 + c // 2

    def member1(k):
        return r // 8 * 8 + k // 2, c // 2 * 2 + k % 2

    def member2(k):
        return k // 4 * 8 + r % 8, k % 4 * 2 + c % 2

    barrier = pltpu.get_barrier_semaphore()

    def greet(dst_r, dst_c):
        pl.semaphore_signal(barrier, inc=1, device_id=(dst_r, dst_c), device_id_type=MESH)

    up_l = (c == nc - 1) & (r < nr - 1)
    down_l = (c == 0) & (r > 0)
    up_r = (q == n_right - 1) & (ct < nc - 1)
    down_r = (q == 0) & (ct > 0)

    def greet_other(a, b):
        pl.when((a != r) | (b != c))(lambda: greet(a, b))

    loop(nc, lambda k: greet_other(r, k))
    loop(nr, lambda k: greet_other(k, ct))
    pl.when(up_l)(lambda: loop(nc, lambda k: greet(r + 1, k)))
    pl.when(down_l)(lambda: loop(nc, lambda k: greet(r - 1, k)))
    pl.when(up_r)(lambda: loop(nr, lambda k: greet_other(k, ct + 1)))
    pl.when(down_r)(lambda: loop(nr, lambda k: greet_other(k, ct - 1)))
    loop(16, lambda k: greet_other(*member1(k)))
    loop(16, lambda k: greet_other(*member2(k)))

    own = (c == ct).astype(jnp.int32)
    low_self = (per * c - 1 == r) & (c == nc - 1)
    high_self = (per * c + per == r) & (c == 0)
    n_sends = nc - 1 + n_right - own + 30
    n_sends += jnp.where(r > 0, 1, 0) + jnp.where(r < nr - 1, 1, 0)
    n_sends += jnp.where((c > 0) & jnp.logical_not(low_self), 1, 0)
    n_sends += jnp.where((c < nc - 1) & jnp.logical_not(high_self), 1, 0)
    pl.semaphore_wait(barrier, n_sends)

    def put(src, dst_r, dst_c, dst, sem, cls):
        mine = (dst_r == r) & (dst_c == c)

        @pl.when(mine)
        def _():
            pltpu.make_async_copy(src, dst, recv.at[sem]).start()

        @pl.when(jnp.logical_not(mine))
        def _():
            pltpu.make_async_remote_copy(
                src, dst, send.at[cls], recv.at[sem], device_id=(dst_r, dst_c), device_id_type=MESH
            ).start()

    loop(n_right, lambda k: put(colp.at[k + 1], per * c + k // nc, k % nc, rcol.at[r], 0, 0))
    loop(nc, lambda k: put(rowp.at[k + 1], r, k, rrow.at[c], 1, 1))
    pl.when(c > 0)(lambda: put(colp.at[0], per * c - 1, nc - 1, rcol2.at[r], 2, 2))
    pl.when(c < nc - 1)(lambda: put(colp.at[n_right + 1], per * c + per, 0, rcol2.at[r], 2, 3))
    pl.when(r > 0)(lambda: put(rowp.at[0], r - 1, nc - 1, rrow2.at[c], 3, 4))
    pl.when(r < nr - 1)(lambda: put(rowp.at[nc + 1], r + 1, 0, rrow2.at[c], 3, 5))

    proj[...] = jnp.zeros_like(proj)
    proj[:, 0:32] = lp_ref[...]
    proj[:, 32:64] = rp_ref[...]
    buf[...] = jnp.zeros_like(buf)
    for k in range(taps.shape[0] // 8):
        buf[k, :, 256:384] = taps[8 * k : 8 * k + 8, :]

    rrow2_wanted = up_l | down_l
    rcol2_wanted = up_r | down_r
    pl.when(jnp.logical_not(rrow2_wanted))(lambda: rrow2.__setitem__(..., jnp.zeros(rrow2.shape, F32)))
    pl.when(jnp.logical_not(rcol2_wanted))(lambda: rcol2.__setitem__(..., jnp.zeros(rcol2.shape, F32)))
    wait_bytes(rrow, recv.at[1])
    wait_bytes(rcol, recv.at[0])
    pl.when(rcol2_wanted)(lambda: wait_bytes(rcol2, recv.at[2]))
    pl.when(rrow2_wanted)(lambda: wait_bytes(rrow2, recv.at[3]))
    grads = jnp.sum(rrow[...], axis=0) + jnp.sum(rcol[...], axis=0)
    grads += jnp.sum(rrow2[...], axis=0) + jnp.sum(rcol2[...], axis=0)
    high, low = halves(grads)
    lr = dot_tn(high, e_ref[...]) + dot_tn(low, e_ref[...])
    for k in range(16):
        buf[k, :, 0:256] = lr[8 * (k // 2) : 8 * (k // 2) + 8, 256 * (k % 2) : 256 * (k % 2) + 256]

    loop(16, lambda k: put(buf.at[k], *member1(k), r1.at[k1], 4, 6))
    eg_ref[...] = dot_nt(high, proj[...]) + dot_nt(low, proj[...])
    wait_bytes(r1, recv.at[4])
    mid[...] = jnp.sum(r1[...], axis=0)
    loop(16, lambda k: put(mid, *member2(k), r2.at[k2], 5, 7))
    wait_bytes(r2, recv.at[5])
    fin[...] = jnp.sum(r2[...], axis=0)
    loop(16, lambda k: put(fin, *member1(k), r3.at[k1], 6, 8))
    wait_bytes(r3, recv.at[6])
    sums_ref[...] = r3[...]

    pl.when(own == 1)(lambda: wait_bytes(rcol.at[0 : n_right - 1], send.at[0]))
    pl.when(own == 0)(lambda: wait_bytes(rcol.at[0:n_right], send.at[0]))
    wait_bytes(rrow.at[0 : nc - 1], send.at[1])
    pl.when((c > 0) & jnp.logical_not(low_self))(lambda: wait_bytes(colp.at[0], send.at[2]))
    pl.when((c < nc - 1) & jnp.logical_not(high_self))(lambda: wait_bytes(colp.at[0], send.at[3]))
    pl.when(r > 0)(lambda: wait_bytes(rowp.at[0], send.at[4]))
    pl.when(r < nr - 1)(lambda: wait_bytes(rowp.at[0], send.at[5]))
    for cls in (6, 7, 8):
        wait_bytes(r1.at[0:15], send.at[cls])


def finish_kernel(scale, sums, conv_ref, left_ref, right_ref):
    for k in range(9):
        q, at = divmod(k, 4)
        for part in range(4):
            piece = sums[4 * q + part, :, 256 + 32 * at : 288 + 32 * at]
            conv_ref[k, 8 * part : 8 * part + 8, :] = piece * scale
    for ref, first in ((left_ref, 0), (right_ref, 8)):
        for half in range(2):
            block = jnp.concatenate([sums[first + 2 * part + half, :, 0:256] for part in range(4)], axis=0)
            ref[256 * half : 256 * half + 256, :] = block.T * scale


def run_compute(lf, rf, cot, w):
    return pl.pallas_call(
        compute_kernel,
        out_shape=(
            jax.ShapeDtypeStruct((32, 64, 256), BF16),
            jax.ShapeDtypeStruct((96, 128), F32),
            jax.ShapeDtypeStruct((80, 128), F32),
            jax.ShapeDtypeStruct((272, 128), F32),
        ),
        in_specs=[VMEM] * 4,
        out_specs=(VMEM,) * 4,
        scratch_shapes=[
            pltpu.VMEM((256, 2560), BF16),
            pltpu.VMEM((3, 256, 2304), BF16),
            pltpu.VMEM((9, 768, 256), F32),
            pltpu.VMEM((256, 1536), BF16),
            pltpu.VMEM((768, 512), BF16),
            pltpu.VMEM((3, 256, 256), F32),
        ],
        compiler_params=pltpu.CompilerParams(vmem_limit_bytes=56 * 1024 * 1024),
        name="pair_compute",
    )(lf, rf, cot, w)


def shards(nr, nc, embed, left_proj, right_proj, conv_w, cotangent):
    lf, rf = pl.pallas_call(
        functools.partial(gather_kernel, nr, nc),
        out_shape=(jax.ShapeDtypeStruct((72, 128), F32), jax.ShapeDtypeStruct((32, 384), F32)),
        in_specs=[VMEM] * 3,
        out_specs=(VMEM,) * 2,
        scratch_shapes=[
            pltpu.VMEM((512, 128), BF16),
            pltpu.VMEM((8, 128), F32),
            pltpu.VMEM((8, 128), F32),
            pltpu.VMEM((nc + 2, 8, 128), F32),
            pltpu.VMEM((48, 8, 128), F32),
            pltpu.SemaphoreType.DMA,
            pltpu.SemaphoreType.DMA,
            pltpu.SemaphoreType.DMA((6,)),
        ],
        compiler_params=pltpu.CompilerParams(
            collective_id=0, has_side_effects=True, vmem_limit_bytes=32 * 1024 * 1024
        ),
        name="feature_gather",
    )(embed, left_proj, right_proj)
    pair_out, taps, rowp, colp = run_compute(lf, rf, cotangent, conv_w)
    sums, embed_grad = pl.pallas_call(
        functools.partial(reduce_kernel, nr, nc),
        out_shape=(jax.ShapeDtypeStruct((16, 8, 384), F32), jax.ShapeDtypeStruct((8, 512), F32)),
        in_specs=[VMEM] * 6,
        out_specs=(VMEM,) * 2,
        scratch_shapes=[
            pltpu.VMEM((512, 128), BF16),
            pltpu.VMEM((nc, 8, 128), F32),
            pltpu.VMEM((nc, 8, 128), F32),
            pltpu.VMEM((nr, 8, 128), F32),
            pltpu.VMEM((nr, 8, 128), F32),
            pltpu.VMEM((16, 8, 384), F32),
            pltpu.VMEM((16, 8, 384), F32),
            pltpu.VMEM((16, 8, 384), F32),
            pltpu.VMEM((16, 8, 384), F32),
            pltpu.VMEM((8, 384), F32),
            pltpu.VMEM((8, 384), F32),
            pltpu.SemaphoreType.DMA((7,)),
            pltpu.SemaphoreType.DMA((9,)),
        ],
        compiler_params=pltpu.CompilerParams(
            collective_id=1, has_side_effects=True, vmem_limit_bytes=32 * 1024 * 1024
        ),
        name="reduce_sums",
    )(embed, left_proj, right_proj, rowp.reshape(10, 8, 128), colp.reshape(34, 8, 128), taps)
    conv_grad, left_grad, right_grad = pl.pallas_call(
        functools.partial(finish_kernel, 32.0 / (8 * nr * nc)),
        out_shape=(
            jax.ShapeDtypeStruct((9, 32, 32), F32),
            jax.ShapeDtypeStruct((512, 32), F32),
            jax.ShapeDtypeStruct((512, 32), F32),
        ),
        in_specs=[VMEM],
        out_specs=(VMEM,) * 3,
        name="finish",
    )(sums)
    return pair_out, conv_grad, left_grad, right_grad, embed_grad


def solution(mesh):
    body = functools.partial(shards, mesh.shape["row"], mesh.shape["col"])
    in_specs = (P(("row", "col"), None), P(), P(), P(), P(None, "row", "col"))
    out_specs = (P(None, "row", "col"), P(), P(), P(), P(("row", "col"), None))
    return jax.shard_map(body, mesh=mesh, in_specs=in_specs, out_specs=out_specs, check_vma=False)
```

```python
import functools

import jax
import jax.numpy as jnp
from jax import lax
from jax.experimental import pallas as pl
from jax.experimental.pallas import tpu as pltpu
from jax.sharding import PartitionSpec as P

MESH = pl.DeviceIdType.MESH
OUTSIDE = -1e30
LOG2E = 1.4426950408889634
LN2 = 0.6931471805599453
F32 = jnp.float32
BF16 = jnp.bfloat16
VMEM = pl.BlockSpec(memory_space=pltpu.VMEM)
HBM = pl.BlockSpec(memory_space=pltpu.HBM)


def iota(shape, dim):
    return lax.broadcasted_iota(jnp.int32, shape, dim)


def one_hot(cond):
    return jnp.where(cond, 1.0, 0.0).astype(BF16)


def dot(a, b):
    return jnp.dot(a, b, preferred_element_type=F32)


def dot_nt(a, b):
    return lax.dot_general(a, b, (((1,), (1,)), ((), ())), preferred_element_type=F32)


def dot_tn(a, b):
    return lax.dot_general(a, b, (((0,), (0,)), ((), ())), preferred_element_type=F32)


def halves(x):
    high = x.astype(BF16)
    return high, (x - high.astype(F32)).astype(BF16)


def loop(n, f):
    def body(k, _):
        f(k)
        return 0

    lax.fori_loop(0, n, body, 0)


def lanes(h):
    return pl.ds(pl.multiple_of(h * 256, 256), 256)


def wait_bytes(ref, sem):
    pltpu.make_async_copy(ref, ref, sem).wait()


def softplus_and_slope(s):
    t = jnp.exp2(-jnp.abs(s * LOG2E))
    u = 1.0 + t
    inv = pl.reciprocal(u, approx=True)
    inv = inv * (2.0 - u * inv)
    log = jnp.where(t < 1 / 256, t - 0.5 * t * t, LN2 * jnp.log2(u))
    return jnp.maximum(s, 0.0) + log, jnp.where(s >= 0, inv, t * inv)


def build_taps(w_ref, tf, tb):
    spread = one_hot((iota((256, 32), 0) >> 3) == iota((256, 32), 1))
    widen = one_hot((iota((32, 256), 1) >> 3) == iota((32, 256), 0))
    s0, s1 = (iota((256, 256), 0) & 7), (iota((256, 256), 1) & 7)
    same, above, below = s1 == s0, s1 == s0 + 4, s1 == s0 - 4

    def expand(x):
        return dot(spread, x.astype(BF16))

    for b in range(3):
        x = [expand(dot(w_ref[3 * a + b], widen)) for a in range(3)]
        tf[:, 256 * b : 256 * b + 256] = jnp.where(same, x[0], jnp.where(above, x[1], 0.0)).astype(BF16)
        tf[:, 768 + 256 * b : 1024 + 256 * b] = jnp.where(same, x[2], jnp.where(below, x[1], 0.0)).astype(BF16)
        y = [expand(dot_tn(w_ref[3 * a + b], widen)) for a in range(3)]
        tb[:, 512 * b : 512 * b + 256] = jnp.where(same, y[2], jnp.where(above, y[1], 0.0)).astype(BF16)
        tb[:, 512 * b + 256 : 512 * b + 512] = jnp.where(same, y[0], jnp.where(below, y[1], 0.0)).astype(BF16)


def build_shift(shift):
    k, n = iota((256, 512), 0), iota((256, 512), 1)
    shift[...] = one_hot(k == jnp.where(n < 256, n - 4, n - 252))


def mask_cotangent(r, c, cot_ref, shift, m3):
    for b in range(3):
        m3[b, :, 0:256] = jnp.zeros((256, 256), BF16)
        m3[b, :, 2304:2560] = jnp.zeros((256, 256), BF16)
    for k in range(4):
        x = cot_ref[:, 16 * k : 16 * k + 16, :].astype(F32)
        row = r * 64 + 16 * k + iota((16, 256), 0)
        x = jnp.where((c * 256 + iota((16, 256), 1) >= row)[None], x, 0.0)
        for half in range(2):
            m3[1, :, lanes(2 * k + half + 1)] = x[:, 8 * half : 8 * half + 8].reshape(256, 256).astype(BF16)

    def body(g):
        moved = dot(m3[1, :, lanes(g + 1)], shift[...]).astype(BF16)
        m3[2, :, lanes(g + 1)] = moved[:, 0:256]
        m3[0, :, lanes(g + 1)] = moved[:, 256:512]

    loop(8, body)


def input_gradient(m3, tb, z):
    def body(h):
        stack = [m3[b, :, lanes(h + u)] for b in range(3) for u in range(2)]
        z[h] = dot(tb[...], jnp.concatenate(stack, axis=0))

    loop(9, body)


def input_gradient_edge(m3, tb, z_edge):
    lane = iota((256, 128), 1)
    edges = jnp.zeros((256, 128), BF16)
    for g in range(8):
        at = 256 * (g + 1)
        ends = jnp.where(lane < 64, m3[1, :, at : at + 128], m3[1, :, at + 128 : at + 256])
        edges = jnp.where((lane >> 3) == g + 1, pltpu.roll(ends, (8 * g + 12) % 128, 1), edges)
    pair = jnp.concatenate([edges, pltpu.roll(edges, 120, 1)], axis=0)
    z_edge[...] = jnp.where((lane & 7) < 4, dot(tb[:, 1024:1536], pair), dot(tb[:, 0:512], pair))


def edge_part(lf, around, z_edge, act_edge, p_edge, left_m):
    spread = one_hot((iota((256, 128), 0) >> 3) == iota((256, 128), 1))
    spread_right = one_hot((iota((256, 128), 0) >> 3) + 32 == iota((256, 128), 1))
    row, lane = iota((256, 128), 0), iota((256, 128), 1)
    rows = jnp.concatenate([lf[...], jnp.zeros((56, 128), F32)], axis=0).astype(BF16)
    left = jnp.where((lane & 7) == (row & 7), dot_nt(spread, rows), 0.0).astype(BF16)
    left_m[...] = left
    block = one_hot((iota((128, 128), 0) >> 3) == (iota((128, 128), 1) >> 3))
    right = jnp.concatenate([around] * 16, axis=0).astype(BF16)
    act, slope = softplus_and_slope(dot(left, block) + dot_nt(spread_right, right))
    act_edge[...] = act.astype(BF16)
    p_edge[...] = slope * z_edge[...]


def elementwise(rf, z, act_edge, p_edge, left_m, shift, lb, a2, cacc, rhi, rlo):
    cacc[...] = jnp.zeros_like(cacc)

    def body(h):
        lb[...] = dot(left_m[...], one_hot((iota((128, 128), 0) >> 3) == h))
        here = (iota((8, 128), 1) >> 3) == h
        at = pl.ds(pl.multiple_of(h * 128, 128), 128)
        for pair in range(16):
            acts, totals = [], []
            for c in (2 * pair, 2 * pair + 1):
                rows = slice(8 * c, 8 * c + 8)
                total = jnp.where(here, p_edge[rows, :], 0.0)
                parts = []
                for tile in (slice(0, 128), slice(128, 256)):
                    act, slope = softplus_and_slope(lb[rows, :] + rf[c : c + 1, tile])
                    p = z[h, rows, tile] * slope
                    cacc[rows, tile] += p
                    total += p
                    parts.append(act)
                acts.append(jnp.concatenate(parts, axis=1))
                totals.append(total)
            rows = slice(16 * pair, 16 * pair + 16)
            a2[1, rows, lanes(h)] = jnp.concatenate(acts, axis=0).astype(BF16)
            high, low = halves(jnp.concatenate(totals, axis=0))
            rhi[rows, at] = high
            rlo[rows, at] = low
        k, n = iota((128, 512), 0), iota((128, 512), 1)
        source = jnp.where(n < 4, n + 4, jnp.where(n >= 508, n - 508, -1024)) + 8 * h
        pick = jnp.concatenate([shift[...], one_hot(k == source)], axis=0)
        moved = dot(jnp.concatenate([a2[1, :, lanes(h)], act_edge[...]], axis=1), pick).astype(BF16)
        a2[0, :, lanes(h)] = moved[:, 0:256]
        a2[2, :, lanes(h)] = moved[:, 256:512]

    loop(9, body)


def sums(cacc, p_edge, rhi, rlo, cols, col_ends, row_main, row_ends):
    by_channel = one_hot((iota((32, 256), 1) >> 3) == iota((32, 256), 0))
    lane = iota((16, 128), 1)

    def total(x):
        high, low = halves(x)
        return dot(by_channel, high) + dot(by_channel, low)

    def packed(first, second):
        return jnp.where(lane < 64, first, second)

    x = total(cacc[...])
    for q in range(4):
        tile = x[:, 128 * (q // 2) : 128 * (q // 2) + 128]
        turned = pltpu.roll(tile, 64, 1)
        cols[q] = packed(turned[0:16], tile[16:32]) if q % 2 else packed(tile[0:16], turned[16:32])
    high, low = halves(total(p_edge[...]))
    fold = one_hot((iota((128, 128), 0) & 7) == (iota((128, 128), 1) & 7))
    x = dot(high, fold) + dot(low, fold)
    x = packed(x[0:16], x[16:32])
    col_ends[0] = jnp.where((lane & 63) >= 60, x, 0.0)
    col_ends[1] = jnp.where((lane & 63) < 4, x, 0.0)
    by_group = one_hot((iota((1152, 128), 0) >> 7) == (iota((1152, 128), 1) >> 3))
    x = dot(rhi[...], by_group) + dot(rlo[...], by_group)
    x = total(jnp.where((iota((256, 128), 0) & 7) == (iota((256, 128), 1) & 7), x, 0.0))
    row_main[...] = packed(pltpu.roll(x[0:16], 124, 1), pltpu.roll(x[16:32], 60, 1))
    x = packed(pltpu.roll(x[0:16], 60, 1), pltpu.roll(x[16:32], 124, 1))
    row_ends[0] = jnp.where((lane & 63) >= 60, x, 0.0)
    row_ends[1] = jnp.where((lane & 63) < 4, x, 0.0)


def convolve(r, c, k, a2, tf, out_ref):
    parts = []
    for g in (2 * k, 2 * k + 1):
        stack = [a2[b, :, lanes(g + u)] for u in range(2) for b in range(3)]
        y = dot(tf[...], jnp.concatenate(stack, axis=0))
        parts.append(y.reshape(32, 8, 256))
    y = jnp.concatenate(parts, axis=1)
    row = r * 64 + 16 * k + iota((16, 256), 0)
    col = c * 256 + iota((16, 256), 1)
    y = jnp.where((col >= row)[None], y, 0.0).astype(BF16)
    out_ref[:, pl.ds(pl.multiple_of(16 * k, 16), 16), :] = y


def tap_gradient(m3, a2, taps):
    s0, s1 = iota((256, 256), 0) & 7, iota((256, 256), 1) & 7
    same, above, below = s1 == s0, s1 == s0 + 4, s1 == s0 - 4
    by_channel = one_hot(((iota((32, 512), 1) & 255) >> 3) == iota((32, 512), 0))
    rows = [None] * 9
    for b in range(3):
        g0 = dot_nt(m3[1, :, 256:2304], a2[b, :, 0:2048])
        g1 = dot_nt(m3[1, :, 256:2304], a2[b, :, 256:2304])
        ys = (
            jnp.where(same, g0, 0.0),
            jnp.where(above, g0, jnp.where(below, g1, 0.0)),
            jnp.where(same, g1, 0.0),
        )
        for a in range(3):
            rows[3 * a + b] = dot(by_channel, jnp.concatenate(halves(ys[a]), axis=0))
    for q in range(3):
        group = rows[4 * q : 4 * q + 4]
        pick = jnp.concatenate(
            [one_hot((iota((256, 128), 0) >> 3) + 32 * k == iota((256, 128), 1)) for k in range(len(group))], axis=0
        )
        high, low = halves(jnp.concatenate(group, axis=1))
        taps[32 * q : 32 * q + 32, :] = dot(high, pick) + dot(low, pick)


LOCAL_SCRATCH = [
    pltpu.VMEM((72, 128), F32),
    pltpu.VMEM((32, 256), F32),
    pltpu.VMEM((96, 128), F32),
    pltpu.VMEM((3, 256, 2560), BF16),
    pltpu.VMEM((3, 256, 2304), BF16),
    pltpu.VMEM((9, 256, 256), F32),
    pltpu.VMEM((256, 128), F32),
    pltpu.VMEM((256, 128), BF16),
    pltpu.VMEM((256, 128), F32),
    pltpu.VMEM((256, 1536), BF16),
    pltpu.VMEM((256, 1536), BF16),
    pltpu.VMEM((256, 256), F32),
    pltpu.VMEM((256, 512), BF16),
    pltpu.VMEM((256, 128), BF16),
    pltpu.VMEM((256, 128), F32),
    pltpu.VMEM((256, 1152), BF16),
    pltpu.VMEM((256, 1152), BF16),
    pltpu.VMEM((4, 16, 128), F32),
    pltpu.VMEM((2, 16, 128), F32),
    pltpu.VMEM((16, 128), F32),
    pltpu.VMEM((2, 16, 128), F32),
]


class Place:
    def __init__(self, nr, nc):
        r, c = lax.axis_index("row"), lax.axis_index("col")
        self.r, self.c, self.nr, self.nc = r, c, nr, nc
        self.per = nr // nc
        self.rb, self.rm = r // self.per, r % self.per
        self.k1 = r % 2 + 2 * (r // 2 % 2) + 4 * (r // 8 % 2) + 8 * (c // 2 % 2)
        self.k2 = r // 4 % 2 + 2 * (r // 16) + 4 * (c % 2) + 8 * (c // 4)
        self.has_up, self.has_down = r > 0, r < nr - 1
        self.has_left, self.has_right = c > 0, c < nc - 1
        self.ends_block = (self.rm == self.per - 1) & (self.rb < nc - 1)
        self.starts_block = (self.rm == 0) & (self.rb > 0)
        self.in_others = self.rb == c

    def member1(self, k):
        row = self.r // 16 * 16 + self.r // 4 % 2 * 4 + k % 2 + 2 * (k // 2 % 2) + 8 * (k // 4 % 2)
        return row, self.c // 4 * 4 + self.c % 2 + 2 * (k // 8)

    def member2(self, k):
        row = self.r // 8 % 2 * 8 + self.r % 4 + 4 * (k % 2) + 16 * (k // 2 % 2)
        return row, self.c // 2 % 2 * 2 + k // 4 % 2 + 4 * (k // 8)

    def other(self, k):
        return self.per * self.c + k, self.rb

    def greet(self):
        r, c, nc, per = self.r, self.c, self.nc, self.per
        barrier = pltpu.get_barrier_semaphore()

        def signal(a, b):
            pl.semaphore_signal(barrier, inc=1, device_id=(a, b), device_id_type=MESH)

        def signal_other(a, b):
            pl.when((a != r) | (b != c))(lambda: signal(a, b))

        def signal_all(col):
            for k in range(per):
                signal(per * c + k, col)

        for k in range(1, nc):
            signal(r, lax.rem(c + k, nc))
        for k in range(per):
            signal_other(*self.other(k))
        for k in range(1, 16):
            signal(*self.member1(lax.rem(self.k1 + k, 16)))
        for k in range(1, 16):
            signal(*self.member2(lax.rem(self.k2 + k, 16)))
        pl.when(self.has_up)(lambda: signal(r - 1, c))
        pl.when(self.has_down)(lambda: signal(r + 1, c))
        pl.when(self.has_left)(lambda: signal(per * c - 1, self.rb))
        pl.when(self.has_right)(lambda: signal(per * c + per, self.rb))
        pl.when(self.ends_block)(lambda: signal_all(self.rb + 1))
        pl.when(self.starts_block)(lambda: signal_all(self.rb - 1))
        n = nc - 1 + per + 30
        for cond, m in (
            (self.in_others, -1), (self.has_up, 1), (self.has_down, 1), (self.has_left, 1),
            (self.has_right, 1), (self.ends_block, per), (self.starts_block, per),
        ):
            n = n + jnp.where(cond, m, 0)
        return n

    def senders(self, send, recv):
        def put(src, dst_r, dst_c, dst, sem):
            pltpu.make_async_remote_copy(
                src, dst, send.at[sem], recv.at[sem], device_id=(dst_r, dst_c), device_id_type=MESH
            ).start()

        def put_other(src, k, dst, sem):
            a, b = self.other(k)
            mine = (a == self.r) & (b == self.c)
            pl.when(mine)(lambda: pltpu.make_async_copy(src, dst, recv.at[sem]).start())
            pl.when(jnp.logical_not(mine))(lambda: put(src, a, b, dst, sem))

        return put, put_other


def pair_kernel(
    nr, nc, e_hbm, lpt_hbm, rpt_hbm, w_hbm, cot_hbm,
    out_ref, sums_ref, eg_ref,
    lf, rf, taps, m3, a2, z, z_edge, act_edge, p_edge, tf, tb, cacc, shift, left_m, lb, rhi, rlo,
    cols, col_ends, row_main, row_ends,
    e_ref, w_ref, cot_ref, proj, es, eb, el, eh, fb, blocks, row_feats, col_feats,
    cparts, cends, rends, turned, gparts, buf, r1, r2, r3, mid, fin, recv, send, loads,
):
    ins = ((e_hbm, e_ref), (w_hbm, w_ref), (lpt_hbm, proj.at[0:32]), (rpt_hbm, proj.at[32:64]), (cot_hbm, cot_ref))
    ins = [pltpu.make_async_copy(src, dst, loads.at[k]) for k, (src, dst) in enumerate(ins)]
    for copy in ins:
        copy.start()
    p = Place(nr, nc)
    r, c, per, rb, rm, k1, k2 = p.r, p.c, p.per, p.rb, p.rm, p.k1, p.k2
    greeted = p.greet()
    put, put_other = p.senders(send, recv)

    proj[64:128, :] = jnp.zeros((64, 512), BF16)
    el[...] = jnp.zeros_like(el)
    eh[...] = jnp.zeros_like(eh)
    build_shift(shift)
    ins[0].wait()
    e = e_ref[...].astype(F32)
    es[...] = jnp.concatenate([e[:, 0:256], e[:, 256:512]], axis=0).astype(BF16)
    ins[1].wait()
    build_taps(w_ref, tf, tb)
    ins[4].wait()
    mask_cotangent(r, c, cot_ref, shift, m3)
    pl.semaphore_wait(pltpu.get_barrier_semaphore(), greeted)

    for k in range(1, nc):
        put(es, r, lax.rem(c + k, nc), eb.at[c], 0)
    pltpu.make_async_copy(es, eb.at[c], recv.at[0]).start()
    input_gradient(m3, tb, z)
    ins[2].wait()
    ins[3].wait()
    wait_bytes(eb, recv.at[0])
    e = eb[...].astype(F32)
    el[0:64, :] = e[:, 0:8].reshape(64, 256).astype(BF16)
    eh[0:64, :] = e[:, 8:16].reshape(64, 256).astype(BF16)
    feats = dot_nt(el[0:64, :], proj[:, 0:256]) + dot_nt(eh[0:64, :], proj[:, 256:512])
    fb[...] = feats.astype(BF16)

    for k in range(per):
        put_other(fb, k, blocks.at[rm], 1)
    bottom, top = fb.at[48:64], fb.at[0:16]

    def put_all(src, col, dst, sem):
        for k in range(per):
            put(src, per * c + k, col, dst, sem)

    pl.when(p.has_down)(lambda: put(bottom, r + 1, c, row_feats.at[0], 2))
    pl.when(p.has_up)(lambda: put(top, r - 1, c, row_feats.at[1], 3))
    pl.when(p.ends_block)(lambda: put_all(bottom, rb + 1, col_feats.at[0], 4))
    pl.when(p.starts_block)(lambda: put_all(top, rb - 1, col_feats.at[1], 5))
    input_gradient_edge(m3, tb, z_edge)

    def arrive(cond, ref, sem):
        pl.when(cond)(lambda: wait_bytes(ref, sem))
        pl.when(jnp.logical_not(cond))(lambda: ref.__setitem__(..., jnp.full(ref.shape, OUTSIDE, BF16)))

    arrive(p.has_up, row_feats.at[0], recv.at[2])
    arrive(p.has_down, row_feats.at[1], recv.at[3])
    arrive(p.has_left, col_feats.at[0], recv.at[4])
    arrive(p.has_right, col_feats.at[1], recv.at[5])
    wait_bytes(blocks, recv.at[1])
    lf[0:4, :] = row_feats[0].astype(F32)[12:16]
    lf[4:68, :] = fb[...].astype(F32)
    lf[68:72, :] = row_feats[1].astype(F32)[0:4]
    pick_right = one_hot(iota((32, 128), 0) + 32 == iota((32, 128), 1))
    rf[...] = dot_nt(pick_right, blocks[...].reshape(64 * per, 128))
    around = jnp.concatenate([col_feats[1].astype(F32)[0:4], col_feats[0].astype(F32)[12:16]], axis=0)
    edge_part(lf, around, z_edge, act_edge, p_edge, left_m)
    elementwise(rf, z, act_edge, p_edge, left_m, shift, lb, a2, cacc, rhi, rlo)
    sums(cacc, p_edge, rhi, rlo, cols, col_ends, row_main, row_ends)

    for k in range(per):
        put_other(cols.at[k], k, cparts.at[rm], 6)
    pl.when(p.has_up)(lambda: put(row_ends.at[0], r - 1, c, rends.at[0], 7))
    pl.when(p.has_down)(lambda: put(row_ends.at[1], r + 1, c, rends.at[1], 8))
    pl.when(p.has_left)(lambda: put(col_ends.at[0], per * c - 1, rb, cends.at[0, rm], 9))
    pl.when(p.has_right)(lambda: put(col_ends.at[1], per * c + per, rb, cends.at[1, rm], 10))

    tap_gradient(m3, a2, taps)
    for k in range(12):
        buf[k, :, 256:384] = taps[8 * k : 8 * k + 8, :]
    buf[12:16, :, 256:384] = jnp.zeros((4, 8, 128), F32)

    def gather_sum(cond, ref, sem):
        pl.when(cond)(lambda: wait_bytes(ref, sem))
        pl.when(jnp.logical_not(cond))(lambda: ref.__setitem__(..., jnp.zeros(ref.shape, F32)))

    gather_sum(p.has_down, rends.at[0], recv.at[7])
    gather_sum(p.has_up, rends.at[1], recv.at[8])
    gather_sum(p.ends_block, cends.at[0], recv.at[9])
    gather_sum(p.starts_block, cends.at[1], recv.at[10])
    wait_bytes(cparts, recv.at[6])
    grads = (
        row_main[...] + rends[0] + rends[1],
        jnp.sum(cparts[...], axis=0) + jnp.sum(cends[0], axis=0) + jnp.sum(cends[1], axis=0),
    )
    lower = iota((16, 128), 1) < 64
    grads = [jnp.where(lower, y, 0.0) for x in grads for y in (x, pltpu.roll(x, 64, 1))]
    grads = jnp.concatenate(grads, axis=0)

    high, low = halves(grads)
    for half, ref in enumerate((el, eh)):
        part = dot(high, ref[...]) + dot(low, ref[...])
        for k in range(8):
            buf[2 * k + half, :, 0:256] = part[8 * k : 8 * k + 8]

    for k in range(1, 16):
        at = lax.rem(k1 + k, 16)
        put(buf.at[at], *p.member1(at), r1.at[k1], 11)
    pltpu.make_async_copy(buf.at[k1], r1.at[k1], recv.at[11]).start()

    turned[...] = jnp.concatenate([grads, jnp.zeros((64, 128), F32)], axis=0).T
    for k in range(1, nc):
        at = lax.rem(c + k, nc)
        put(turned.at[pl.ds(pl.multiple_of(8 * at, 8), 8)], r, at, gparts.at[c], 14)
    pltpu.make_async_copy(turned.at[pl.ds(pl.multiple_of(8 * c, 8), 8)], gparts.at[c], recv.at[14]).start()

    convolve(r, c, 0, a2, tf, out_ref)
    convolve(r, c, 1, a2, tf, out_ref)
    wait_bytes(r1, recv.at[11])
    mid[...] = jnp.sum(r1[...], axis=0)
    for k in range(1, 16):
        put(mid, *p.member2(lax.rem(k2 + k, 16)), r2.at[k2], 12)
    pltpu.make_async_copy(mid, r2.at[k2], recv.at[12]).start()

    convolve(r, c, 2, a2, tf, out_ref)
    convolve(r, c, 3, a2, tf, out_ref)
    wait_bytes(r2, recv.at[12])
    fin[...] = jnp.sum(r2[...], axis=0)
    for k in range(1, 16):
        put(fin, *p.member1(lax.rem(k1 + k, 16)), r3.at[k1], 13)
    pltpu.make_async_copy(fin, r3.at[k1], recv.at[13]).start()

    wait_bytes(gparts, recv.at[14])
    high, low = halves(jnp.sum(gparts[...], axis=0))
    eg_ref[...] = dot(high, proj[...]) + dot(low, proj[...])

    wait_bytes(eb.at[0 : nc - 1], send.at[0])
    pl.when(p.in_others)(lambda: wait_bytes(blocks.at[0 : per - 1], send.at[1]))
    pl.when(jnp.logical_not(p.in_others))(lambda: wait_bytes(blocks, send.at[1]))
    pl.when(p.has_down)(lambda: wait_bytes(bottom, send.at[2]))
    pl.when(p.has_up)(lambda: wait_bytes(top, send.at[3]))
    pl.when(p.ends_block)(lambda: wait_bytes(fb, send.at[4]))
    pl.when(p.starts_block)(lambda: wait_bytes(fb, send.at[5]))
    pl.when(p.in_others)(lambda: wait_bytes(cparts.at[0 : per - 1], send.at[6]))
    pl.when(jnp.logical_not(p.in_others))(lambda: wait_bytes(cparts, send.at[6]))
    pl.when(p.has_up)(lambda: wait_bytes(row_ends.at[0], send.at[7]))
    pl.when(p.has_down)(lambda: wait_bytes(row_ends.at[1], send.at[8]))
    pl.when(p.has_left)(lambda: wait_bytes(col_ends.at[0], send.at[9]))
    pl.when(p.has_right)(lambda: wait_bytes(col_ends.at[1], send.at[10]))
    wait_bytes(r1.at[0:15], send.at[11])
    wait_bytes(r2.at[0:15], send.at[12])
    wait_bytes(gparts.at[0 : nc - 1], send.at[14])

    wait_bytes(r3, recv.at[13])
    sums_ref[...] = r3[...]
    wait_bytes(r3.at[0:15], send.at[13])


def finish_kernel(scale, sums_in, eg_in, conv_ref, left_ref, right_ref, eg_ref):
    for k in range(9):
        q, at = divmod(k, 4)
        for part in range(4):
            piece = sums_in[4 * q + part, :, 256 + 32 * at : 288 + 32 * at]
            conv_ref[k, 8 * part : 8 * part + 8, :] = piece * scale
    for ref, first in ((left_ref, 0), (right_ref, 8)):
        for half in range(2):
            for part in range(4):
                piece = sums_in[first + 2 * part + half, :, 0:256]
                ref[8 * part : 8 * part + 8, 256 * half : 256 * half + 256] = piece * scale
    eg_ref[...] = eg_in[...]


def shards(nr, nc, embed, left_proj, right_proj, conv_w, cotangent):
    per = nr // nc
    pair_out, totals, embed_grad = pl.pallas_call(
        functools.partial(pair_kernel, nr, nc),
        out_shape=(
            jax.ShapeDtypeStruct((32, 64, 256), BF16),
            jax.ShapeDtypeStruct((16, 8, 384), F32),
            jax.ShapeDtypeStruct((8, 512), F32),
        ),
        in_specs=[HBM] * 5,
        out_specs=(VMEM,) * 3,
        scratch_shapes=LOCAL_SCRATCH
        + [
            pltpu.VMEM((8, 512), BF16),
            pltpu.VMEM((9, 32, 32), BF16),
            pltpu.VMEM((32, 64, 256), BF16),
            pltpu.VMEM((128, 512), BF16),
            pltpu.VMEM((16, 256), BF16),
            pltpu.VMEM((nc, 16, 256), BF16),
            pltpu.VMEM((128, 256), BF16),
            pltpu.VMEM((128, 256), BF16),
            pltpu.VMEM((64, 128), BF16),
            pltpu.VMEM((per, 64, 128), BF16),
            pltpu.VMEM((2, 16, 128), BF16),
            pltpu.VMEM((2, 16, 128), BF16),
            pltpu.VMEM((per, 16, 128), F32),
            pltpu.VMEM((2, per, 16, 128), F32),
            pltpu.VMEM((2, 16, 128), F32),
            pltpu.VMEM((128, 128), F32),
            pltpu.VMEM((nc, 8, 128), F32),
            pltpu.VMEM((16, 8, 384), F32),
            pltpu.VMEM((16, 8, 384), F32),
            pltpu.VMEM((16, 8, 384), F32),
            pltpu.VMEM((16, 8, 384), F32),
            pltpu.VMEM((8, 384), F32),
            pltpu.VMEM((8, 384), F32),
            pltpu.SemaphoreType.DMA((15,)),
            pltpu.SemaphoreType.DMA((15,)),
            pltpu.SemaphoreType.DMA((5,)),
        ],
        compiler_params=pltpu.CompilerParams(
            collective_id=0, has_side_effects=True, vmem_limit_bytes=60 * 1024 * 1024
        ),
        name="pair_kernel",
    )(embed, left_proj.T, right_proj.T, conv_w, cotangent)
    conv_grad, left_t, right_t, embed_grad = pl.pallas_call(
        functools.partial(finish_kernel, 32.0 / (8 * nr * nc)),
        out_shape=(
            jax.ShapeDtypeStruct((9, 32, 32), F32),
            jax.ShapeDtypeStruct((32, 512), F32),
            jax.ShapeDtypeStruct((32, 512), F32),
            jax.ShapeDtypeStruct((8, 512), F32),
        ),
        in_specs=[VMEM] * 2,
        out_specs=(VMEM,) * 4,
        compiler_params=pltpu.CompilerParams(vmem_limit_bytes=60 * 1024 * 1024),
        name="finish",
    )(totals, embed_grad)
    return pair_out, conv_grad, left_t.T, right_t.T, embed_grad


def solution(mesh):
    body = functools.partial(shards, mesh.shape["row"], mesh.shape["col"])
    in_specs = (P(("row", "col"), None), P(), P(), P(), P(None, "row", "col"))
    out_specs = (P(None, "row", "col"), P(), P(), P(), P(("row", "col"), None))
    return jax.shard_map(body, mesh=mesh, in_specs=in_specs, out_specs=out_specs, check_vma=False)
```

```python
import functools

import jax
import jax.numpy as jnp
from jax import lax
from jax.experimental import pallas as pl
from jax.experimental.pallas import tpu as pltpu
from jax.sharding import PartitionSpec as P

MESH = pl.DeviceIdType.MESH
OUTSIDE = -1e30
LOG2E = 1.4426950408889634
LN2 = 0.6931471805599453
F32 = jnp.float32
BF16 = jnp.bfloat16
VMEM = pl.BlockSpec(memory_space=pltpu.VMEM)
HBM = pl.BlockSpec(memory_space=pltpu.HBM)


def iota(shape, dim):
    return lax.broadcasted_iota(jnp.int32, shape, dim)


def one_hot(cond):
    return jnp.where(cond, 1.0, 0.0).astype(BF16)


def dot(a, b):
    return jnp.dot(a, b, preferred_element_type=F32)


def dot_nt(a, b):
    return lax.dot_general(a, b, (((1,), (1,)), ((), ())), preferred_element_type=F32)


def dot_tn(a, b):
    return lax.dot_general(a, b, (((0,), (0,)), ((), ())), preferred_element_type=F32)


def halves(x):
    high = x.astype(BF16)
    return high, (x - high.astype(F32)).astype(BF16)


def loop(n, f):
    def body(k, _):
        f(k)
        return 0

    lax.fori_loop(0, n, body, 0)


def lanes(h):
    return pl.ds(pl.multiple_of(h * 256, 256), 256)


def wait_bytes(ref, sem):
    pltpu.make_async_copy(ref, ref, sem).wait()


def softplus_and_slope(y):
    t = jnp.exp2(-jnp.abs(y))
    u = 1.0 + t
    inv = pltpu.reciprocal(u, approx=True, full_range=False)
    inv = inv * (2.0 - u * inv)
    log = jnp.where(t < 1 / 256, t * (LOG2E - (0.5 * LOG2E) * t), jnp.log2(u))
    return LN2 * (jnp.maximum(y, 0.0) + log), jnp.where(y >= 0, inv, t * inv)


def build_taps(w_ref, tf):
    spread = one_hot((iota((256, 32), 0) >> 3) == iota((256, 32), 1))
    widen = one_hot((iota((32, 256), 1) >> 3) == iota((32, 256), 0))
    s0, s1 = iota((256, 256), 0) & 7, iota((256, 256), 1) & 7
    same, above, below = s1 == s0, s1 == s0 + 4, s1 == s0 - 4
    for b in range(3):
        x = [dot(spread, dot(w_ref[3 * a + b], widen).astype(BF16)) for a in range(3)]
        tf[:, 256 * b : 256 * b + 256] = jnp.where(same, x[0], jnp.where(above, x[1], 0.0)).astype(BF16)
        tf[:, 768 + 256 * b : 1024 + 256 * b] = jnp.where(same, x[2], jnp.where(below, x[1], 0.0)).astype(BF16)


def mask_cotangent(r, c, cot_ref, mall, mt):
    for k in range(4):
        x = cot_ref[:, 16 * k : 16 * k + 16, :].astype(F32)
        row = r * 64 + 16 * k + iota((16, 256), 0)
        x = jnp.where((c * 256 + iota((16, 256), 1) >= row)[None], x, 0.0)
        for half in range(2):
            mall[:, lanes(2 * k + half)] = x[:, 8 * half : 8 * half + 8].reshape(256, 256).astype(BF16)
    for b in range(3):
        mt[0, :, 256 * b : 256 * b + 256] = jnp.zeros((272, 256), BF16)
        mt[9, :, 256 * b : 256 * b + 256] = jnp.zeros((272, 256), BF16)

    def body(g):
        for b in range(3):
            move = one_hot(iota((272, 256), 0) - 4 * b == iota((272, 256), 1))
            mt[g + 1, :, 256 * b : 256 * b + 256] = dot_nt(move, mall[:, lanes(g)]).astype(BF16)

    loop(8, body)


def input_gradient(mt, tf, z):
    def body(h):
        z[h] = dot_nt_blocks(mt, tf, h)

    loop(9, body)


def dot_nt_blocks(mt, tf, h):
    left = jnp.concatenate([mt[h], mt[h + 1]], axis=1)
    right = jnp.concatenate(
        [tf[:, 768 * (1 - u) + 256 * b : 768 * (1 - u) + 256 * b + 256] for u in range(2) for b in range(3)], axis=0
    )
    return dot(left, right)


def features(rows, cols, rowf, colf):
    k, n = iota((128, 256), 0), iota((128, 256), 1) >> 3
    colf[...] = dot(cols, one_hot(k == n + 32)) * LOG2E
    x = dot(rows, one_hot(k == n))
    x = jnp.where((iota((128, 256), 0) & 7) == (iota((128, 256), 1) & 7), x, 0.0).astype(BF16)
    rowf[...] = dot(one_hot((iota((16, 128), 1) >> 3) == iota((16, 128), 0)), x) * LOG2E


def elementwise(rowf, colf, z, act, cacc, rsum):
    rsum[...] = jnp.zeros_like(rsum)

    def body(step):
        for part in range(3):
            rows = pl.ds(pl.multiple_of(24 * step + 8 * part, 8), 8)
            right = colf[rows, :]
            total = jnp.zeros((8, 256), F32)
            for h in range(9):
                value, slope = softplus_and_slope(right + rowf[h : h + 1, :])
                act[h, rows, :] = value
                p = z[h, rows, :] * slope
                total += p
                rsum[8 * h : 8 * h + 8, :] += p
            cacc[rows, :] = total

    loop(11, body)


def sums(cacc, rsum, cols, col_ends, row_main, row_ends):
    k, n = iota((256, 128), 0) >> 3, iota((256, 128), 1)
    picks = [one_hot(k + 32 * g == n) for g in range(4)]
    pick = jnp.concatenate(picks, axis=0)
    x = [
        jnp.concatenate([cacc[4 + 64 * q + 16 * g : 20 + 64 * q + 16 * g, :] for g in range(4)], axis=1) for q in range(4)
    ]
    high, low = halves(jnp.concatenate(x, axis=0))
    x = dot(high, pick) + dot(low, pick)
    for q in range(4):
        cols[q] = x[16 * q : 16 * q + 16]
    sub, lane = iota((16, 128), 0), iota((16, 128), 1)
    ends = jnp.concatenate([cacc[0:8, :], cacc[256:264, :]], axis=0)
    high, low = halves(ends)
    first = dot(high, picks[3]) + dot(low, picks[3])
    second = dot(high, picks[0]) + dot(low, picks[0])
    col_ends[0] = jnp.where(sub >= 12, pltpu.roll(first, 12, 0), 0.0)
    col_ends[1] = jnp.where(sub < 4, pltpu.roll(second, 4, 0), 0.0)
    x = jnp.concatenate([rsum[...], jnp.zeros((56, 256), F32)], axis=0)
    by_group = one_hot((iota((80, 128), 0) >> 3) == (iota((80, 128), 1) >> 3))
    high, low = halves(x)
    x = dot(by_group, high) + dot(by_group, low)
    x = jnp.where((iota((80, 256), 0) & 7) == (iota((80, 256), 1) & 7), x, 0.0)
    high, low = halves(jnp.concatenate([x[4 + 16 * g : 20 + 16 * g] for g in range(4)], axis=1))
    row_main[...] = dot(high, pick) + dot(low, pick)
    ends = jnp.concatenate([x[0:8], x[64:72]], axis=0)
    high, low = halves(ends)
    first = dot(high, picks[3]) + dot(low, picks[3])
    second = dot(high, picks[0]) + dot(low, picks[0])
    row_ends[0] = jnp.where(sub >= 12, pltpu.roll(first, 12, 0), 0.0)
    row_ends[1] = jnp.where(sub < 4, pltpu.roll(second, 4, 0), 0.0)


def build_windows(act, a3):
    def body(h):
        at = pl.ds(pl.multiple_of(256 * h, 256), 256)
        for b in range(3):
            a3[at, 256 * b : 256 * b + 256] = act[h, 4 * b : 4 * b + 256, :].astype(BF16)

    loop(9, body)


def convolve(r, c, k, a3, tf, out_ref):
    parts = []
    for g in (2 * k, 2 * k + 1):
        both = jnp.concatenate([a3[256 * (g + u) : 256 * (g + u) + 256, :] for u in range(2)], axis=1)
        parts.append(dot_nt(tf[...], both).reshape(32, 8, 256))
    y = jnp.concatenate(parts, axis=1)
    row = r * 64 + 16 * k + iota((16, 256), 0)
    col = c * 256 + iota((16, 256), 1)
    out_ref[:, 16 * k : 16 * k + 16, :] = jnp.where((col >= row)[None], y, 0.0).astype(BF16)


def tap_gradient(mall, a3, taps):
    s0, s1 = iota((256, 256), 0) & 7, iota((256, 256), 1) & 7
    same, above, below = s1 == s0, s1 == s0 + 4, s1 == s0 - 4
    by_channel = one_hot(((iota((32, 512), 1) & 255) >> 3) == iota((32, 512), 0))
    rows = [None] * 9
    for b in range(3):
        g0 = dot(mall[...], a3[0:2048, 256 * b : 256 * b + 256])
        g1 = dot(mall[...], a3[256:2304, 256 * b : 256 * b + 256])
        ys = (
            jnp.where(same, g0, 0.0),
            jnp.where(above, g0, jnp.where(below, g1, 0.0)),
            jnp.where(same, g1, 0.0),
        )
        for a in range(3):
            rows[3 * a + b] = dot(by_channel, jnp.concatenate(halves(ys[a]), axis=0))
    for q in range(3):
        group = rows[4 * q : 4 * q + 4]
        pick = jnp.concatenate(
            [one_hot((iota((256, 128), 0) >> 3) + 32 * k == iota((256, 128), 1)) for k in range(len(group))], axis=0
        )
        high, low = halves(jnp.concatenate(group, axis=1))
        taps[32 * q : 32 * q + 32, :] = dot(high, pick) + dot(low, pick)


LOCAL_SCRATCH = [
    pltpu.VMEM((16, 256), F32),
    pltpu.VMEM((272, 256), F32),
    pltpu.VMEM((96, 128), F32),
    pltpu.VMEM((256, 2048), BF16),
    pltpu.VMEM((10, 272, 768), BF16),
    pltpu.VMEM((9, 272, 256), F32),
    pltpu.VMEM((2304, 768), BF16),
    pltpu.VMEM((9, 272, 256), F32),
    pltpu.VMEM((256, 1536), BF16),
    pltpu.VMEM((272, 256), F32),
    pltpu.VMEM((72, 256), F32),
    pltpu.VMEM((4, 16, 128), F32),
    pltpu.VMEM((2, 16, 128), F32),
    pltpu.VMEM((16, 128), F32),
    pltpu.VMEM((2, 16, 128), F32),
]


class Place:
    def __init__(self, nr, nc):
        r, c = lax.axis_index("row"), lax.axis_index("col")
        self.r, self.c, self.nr, self.nc = r, c, nr, nc
        self.per = nr // nc
        self.rb, self.rm = lax.div(r, self.per), lax.rem(r, self.per)
        bits1 = ((r, 1, 0), (r, 2, 0), (r, 8, 0), (c, 2, 1))
        bits2 = ((r, 4, 0), (r, 16, 0), (c, 1, 1), (c, 4, 1))
        self.k1, self.group1 = self.group(bits1)
        self.k2, self.group2 = self.group(bits2)
        _, self.group0 = self.group(((c, 1, 1), (c, 2, 1), (c, 4, 1)))
        self.has_up, self.has_down = r > 0, r < nr - 1
        self.has_left, self.has_right = c > 0, c < nc - 1
        self.ends_block = (self.rm == self.per - 1) & (self.rb < nc - 1)
        self.starts_block = (self.rm == 0) & (self.rb > 0)
        self.in_others = self.rb == c

    def group(self, bits):
        number, turns = 0, []
        for k, (x, weight, is_col) in enumerate(bits):
            bit = lax.rem(lax.div(x, weight), 2)
            number = number + bit * (1 << k)
            sign = 1 - 2 * bit
            turns.append((sign * weight, is_col, sign * (1 << k)))
        members = [(self.r, self.c, number)]
        for move, is_col, step in turns:
            members += [
                (a, b + move, n + step) if is_col else (a + move, b, n + step) for a, b, n in members
            ]
        return number, members[:0:-1]

    def other(self, k):
        return self.per * self.c + k, self.rb

    def greet(self):
        r, c, nc, per = self.r, self.c, self.nc, self.per
        barrier = pltpu.get_barrier_semaphore()

        def signal(a, b):
            pl.semaphore_signal(barrier, inc=1, device_id=(a, b), device_id_type=MESH)

        def signal_other(a, b):
            pl.when((a != r) | (b != c))(lambda: signal(a, b))

        def signal_all(col):
            for k in range(per):
                signal(per * c + k, col)

        for a, b, _ in self.group0 + self.group1 + self.group2:
            signal(a, b)
        for k in range(per):
            signal_other(*self.other(k))
        pl.when(self.has_up)(lambda: signal(r - 1, c))
        pl.when(self.has_down)(lambda: signal(r + 1, c))
        pl.when(self.has_left)(lambda: signal(per * c - 1, self.rb))
        pl.when(self.has_right)(lambda: signal(per * c + per, self.rb))
        pl.when(self.ends_block)(lambda: signal_all(self.rb + 1))
        pl.when(self.starts_block)(lambda: signal_all(self.rb - 1))
        n = nc - 1 + per + 30
        for cond, m in (
            (self.in_others, -1), (self.has_up, 1), (self.has_down, 1), (self.has_left, 1),
            (self.has_right, 1), (self.ends_block, per), (self.starts_block, per),
        ):
            n = n + jnp.where(cond, m, 0)
        return n

    def senders(self, send, recv):
        def put(src, dst_r, dst_c, dst, sem):
            pltpu.make_async_remote_copy(
                src, dst, send.at[sem], recv.at[sem], device_id=(dst_r, dst_c), device_id_type=MESH
            ).start()

        def put_other(src, k, dst, sem):
            a, b = self.other(k)
            mine = (a == self.r) & (b == self.c)
            pl.when(mine)(lambda: pltpu.make_async_copy(src, dst, recv.at[sem]).start())
            pl.when(jnp.logical_not(mine))(lambda: put(src, a, b, dst, sem))

        return put, put_other


def pair_kernel(
    nr, nc, e_hbm, lpt_hbm, rpt_hbm, w_hbm, cot_hbm,
    out_hbm, sums_ref, eg_ref,
    rowf, colf, taps, mall, mt, act, a3, z, tf, cacc, rsum, cols, col_ends, row_main, row_ends,
    out_ref, feats, e_ref, w_ref, cot_ref, proj, es, eb, el, eh, fb, blocks, row_feats, col_feats,
    cparts, cends, rends, turned, gparts, buf, r1, r2, r3, mid, fin, recv, send, loads, stores,
):
    ins = ((e_hbm, e_ref), (w_hbm, w_ref), (lpt_hbm, proj.at[0:32]), (rpt_hbm, proj.at[32:64]), (cot_hbm, cot_ref))
    ins = [pltpu.make_async_copy(src, dst, loads.at[k]) for k, (src, dst) in enumerate(ins)]
    for copy in ins:
        copy.start()
    p = Place(nr, nc)
    r, c, per, rb, rm, k1, k2 = p.r, p.c, p.per, p.rb, p.rm, p.k1, p.k2
    greeted = p.greet()
    put, put_other = p.senders(send, recv)

    ins[0].wait()
    e = e_ref[...].astype(F32)
    es[...] = jnp.concatenate([e[:, 0:256], e[:, 256:512]], axis=0).astype(BF16)
    pl.semaphore_wait(pltpu.get_barrier_semaphore(), greeted)

    for a, b, _ in p.group0:
        put(es, a, b, eb.at[c], 0)
    pltpu.make_async_copy(es, eb.at[c], recv.at[0]).start()
    proj[64:128, :] = jnp.zeros((64, 512), BF16)
    ins[1].wait()
    build_taps(w_ref, tf)
    ins[4].wait()
    mask_cotangent(r, c, cot_ref, mall, mt)
    ins[2].wait()
    ins[3].wait()
    wait_bytes(eb, recv.at[0])
    e = eb[...].astype(F32)
    el[...] = e[:, 0:8].reshape(64, 256).astype(BF16)
    eh[...] = e[:, 8:16].reshape(64, 256).astype(BF16)
    fb[...] = (dot_nt(el[...], proj[:, 0:256]) + dot_nt(eh[...], proj[:, 256:512])).astype(BF16)

    for k in range(per):
        put_other(fb, k, blocks.at[rm], 1)
    bottom, top = fb.at[48:64], fb.at[0:16]

    def put_all(src, col, dst, sem):
        for k in range(per):
            put(src, per * c + k, col, dst, sem)

    pl.when(p.has_down)(lambda: put(bottom, r + 1, c, row_feats.at[0], 2))
    pl.when(p.has_up)(lambda: put(top, r - 1, c, row_feats.at[1], 3))
    pl.when(p.ends_block)(lambda: put_all(bottom, rb + 1, col_feats.at[0], 4))
    pl.when(p.starts_block)(lambda: put_all(top, rb - 1, col_feats.at[1], 5))
    input_gradient(mt, tf, z)

    def arrive(cond, ref, sem):
        pl.when(cond)(lambda: wait_bytes(ref, sem))
        pl.when(jnp.logical_not(cond))(lambda: ref.__setitem__(..., jnp.full(ref.shape, OUTSIDE, BF16)))

    arrive(p.has_up, row_feats.at[0], recv.at[2])
    arrive(p.has_down, row_feats.at[1], recv.at[3])
    arrive(p.has_left, col_feats.at[0], recv.at[4])
    arrive(p.has_right, col_feats.at[1], recv.at[5])
    wait_bytes(blocks, recv.at[1])
    feats[0:4, :] = row_feats[0].astype(F32)[12:16]
    feats[4:68, :] = fb[...].astype(F32)
    feats[68:72, :] = row_feats[1].astype(F32)[0:4]
    feats[72:128, :] = jnp.zeros((56, 128), F32)
    rows = feats[0:128, :].astype(BF16)
    feats[128:132, :] = col_feats[0].astype(F32)[12:16]
    feats[132 : 132 + 64 * per, :] = blocks[...].reshape(64 * per, 128).astype(F32)
    feats[388:392, :] = col_feats[1].astype(F32)[0:4]
    feats[392:400, :] = jnp.zeros((8, 128), F32)
    features(rows, feats[128:400, :].astype(BF16), rowf, colf)
    elementwise(rowf, colf, z, act, cacc, rsum)
    sums(cacc, rsum, cols, col_ends, row_main, row_ends)

    for k in range(per):
        put_other(cols.at[k], k, cparts.at[rm], 6)
    pl.when(p.has_up)(lambda: put(row_ends.at[0], r - 1, c, rends.at[0], 7))
    pl.when(p.has_down)(lambda: put(row_ends.at[1], r + 1, c, rends.at[1], 8))
    pl.when(p.has_left)(lambda: put(col_ends.at[0], per * c - 1, rb, cends.at[0, rm], 9))
    pl.when(p.has_right)(lambda: put(col_ends.at[1], per * c + per, rb, cends.at[1, rm], 10))

    build_windows(act, a3)
    tap_gradient(mall, a3, taps)
    for k in range(12):
        buf[k, :, 256:384] = taps[8 * k : 8 * k + 8, :]
    buf[12:16, :, 256:384] = jnp.zeros((4, 8, 128), F32)

    def gather_sum(cond, ref, sem):
        pl.when(cond)(lambda: wait_bytes(ref, sem))
        pl.when(jnp.logical_not(cond))(lambda: ref.__setitem__(..., jnp.zeros(ref.shape, F32)))

    gather_sum(p.has_down, rends.at[0], recv.at[7])
    gather_sum(p.has_up, rends.at[1], recv.at[8])
    gather_sum(p.ends_block, cends.at[0], recv.at[9])
    gather_sum(p.starts_block, cends.at[1], recv.at[10])
    wait_bytes(cparts, recv.at[6])
    grads = (
        row_main[...] + rends[0] + rends[1],
        jnp.sum(cparts[...], axis=0) + jnp.sum(cends[0], axis=0) + jnp.sum(cends[1], axis=0),
    )
    lane = iota((16, 128), 1)
    spread = []
    for g in range(4):
        parts = [x if turn % 128 == 0 else pltpu.roll(x, turn % 128, 1) for x, turn in zip(grads, (-32 * g, 32 - 32 * g))]
        spread.append(jnp.where(lane < 32, parts[0], jnp.where(lane < 64, parts[1], 0.0)))
    turned[...] = jnp.concatenate(spread, axis=0)

    high, low = halves(turned[...])
    for half, ref in enumerate((el, eh)):
        part = dot_tn(high, ref[...]) + dot_tn(low, ref[...])
        for k in range(8):
            buf[2 * k + half, :, 0:256] = part[8 * k : 8 * k + 8]

    for a, b, at in p.group1:
        put(buf.at[at], a, b, r1.at[k1], 11)
    pltpu.make_async_copy(buf.at[k1], r1.at[k1], recv.at[11]).start()

    for a, b, _ in p.group0:
        put(turned.at[pl.ds(pl.multiple_of(8 * b, 8), 8)], a, b, gparts.at[c], 14)
    pltpu.make_async_copy(turned.at[pl.ds(pl.multiple_of(8 * c, 8), 8)], gparts.at[c], recv.at[14]).start()

    outs = [
        pltpu.make_async_copy(out_ref.at[:, 16 * q : 16 * q + 16, :], out_hbm.at[:, 16 * q : 16 * q + 16, :], stores.at[q])
        for q in range(4)
    ]
    convolve(r, c, 0, a3, tf, out_ref)
    outs[0].start()
    convolve(r, c, 1, a3, tf, out_ref)
    outs[1].start()
    wait_bytes(r1, recv.at[11])
    mid[...] = jnp.sum(r1[...], axis=0)
    for a, b, _ in p.group2:
        put(mid, a, b, r2.at[k2], 12)
    pltpu.make_async_copy(mid, r2.at[k2], recv.at[12]).start()

    convolve(r, c, 2, a3, tf, out_ref)
    outs[2].start()
    convolve(r, c, 3, a3, tf, out_ref)
    outs[3].start()
    wait_bytes(r2, recv.at[12])
    fin[...] = jnp.sum(r2[...], axis=0)
    for a, b, _ in p.group1:
        put(fin, a, b, r3.at[k1], 13)
    pltpu.make_async_copy(fin, r3.at[k1], recv.at[13]).start()

    wait_bytes(gparts, recv.at[14])
    high, low = halves(jnp.sum(gparts[...], axis=0))
    eg_ref[...] = dot(high, proj[...]) + dot(low, proj[...])

    for copy in outs:
        copy.wait()
    wait_bytes(eb.at[0 : nc - 1], send.at[0])
    pl.when(p.in_others)(lambda: wait_bytes(blocks.at[0 : per - 1], send.at[1]))
    pl.when(jnp.logical_not(p.in_others))(lambda: wait_bytes(blocks, send.at[1]))
    pl.when(p.has_down)(lambda: wait_bytes(bottom, send.at[2]))
    pl.when(p.has_up)(lambda: wait_bytes(top, send.at[3]))
    pl.when(p.ends_block)(lambda: wait_bytes(fb, send.at[4]))
    pl.when(p.starts_block)(lambda: wait_bytes(fb, send.at[5]))
    pl.when(p.in_others)(lambda: wait_bytes(cparts.at[0 : per - 1], send.at[6]))
    pl.when(jnp.logical_not(p.in_others))(lambda: wait_bytes(cparts, send.at[6]))
    pl.when(p.has_up)(lambda: wait_bytes(row_ends.at[0], send.at[7]))
    pl.when(p.has_down)(lambda: wait_bytes(row_ends.at[1], send.at[8]))
    pl.when(p.has_left)(lambda: wait_bytes(col_ends.at[0], send.at[9]))
    pl.when(p.has_right)(lambda: wait_bytes(col_ends.at[1], send.at[10]))
    wait_bytes(r1.at[0:15], send.at[11])
    wait_bytes(r2.at[0:15], send.at[12])
    wait_bytes(gparts.at[0 : nc - 1], send.at[14])

    wait_bytes(r3, recv.at[13])
    sums_ref[...] = r3[...]
    wait_bytes(r3.at[0:15], send.at[13])


def finish_kernel(
    scale, sums_in, eg_in, pair_in, conv_ref, left_ref, right_ref, eg_ref, pair_ref, held, loads, stores
):
    def piece(k):
        return slice(8 * k, 8 * k + 8)

    ins = [pltpu.make_async_copy(pair_in.at[piece(k)], held.at[piece(k)], loads.at[k]) for k in range(4)]
    outs = [pltpu.make_async_copy(held.at[piece(k)], pair_ref.at[piece(k)], stores.at[k]) for k in range(4)]
    for copy in ins:
        copy.start()
    for k in range(9):
        q, at = divmod(k, 4)
        for part in range(4):
            x = sums_in[4 * q + part, :, 256 + 32 * at : 288 + 32 * at]
            conv_ref[k, 8 * part : 8 * part + 8, :] = x * scale
    for ref, first in ((left_ref, 0), (right_ref, 8)):
        for half in range(2):
            for part in range(4):
                x = sums_in[first + 2 * part + half, :, 0:256]
                ref[8 * part : 8 * part + 8, 256 * half : 256 * half + 256] = x * scale
    eg_ref[...] = eg_in[...]
    for k in range(4):
        ins[k].wait()
        outs[k].start()
    for copy in outs:
        copy.wait()


def shards(nr, nc, embed, left_proj, right_proj, conv_w, cotangent):
    per = nr // nc
    pair_out, totals, embed_grad = pl.pallas_call(
        functools.partial(pair_kernel, nr, nc),
        out_shape=(
            jax.ShapeDtypeStruct((32, 64, 256), BF16),
            jax.ShapeDtypeStruct((16, 8, 384), F32),
            jax.ShapeDtypeStruct((8, 512), F32),
        ),
        in_specs=[HBM] * 5,
        out_specs=(HBM, VMEM, VMEM),
        scratch_shapes=LOCAL_SCRATCH
        + [
            pltpu.VMEM((32, 64, 256), BF16),
            pltpu.VMEM((400, 128), F32),
            pltpu.VMEM((8, 512), BF16),
            pltpu.VMEM((9, 32, 32), BF16),
            pltpu.VMEM((32, 64, 256), BF16),
            pltpu.VMEM((128, 512), BF16),
            pltpu.VMEM((16, 256), BF16),
            pltpu.VMEM((nc, 16, 256), BF16),
            pltpu.VMEM((64, 256), BF16),
            pltpu.VMEM((64, 256), BF16),
            pltpu.VMEM((64, 128), BF16),
            pltpu.VMEM((per, 64, 128), BF16),
            pltpu.VMEM((2, 16, 128), BF16),
            pltpu.VMEM((2, 16, 128), BF16),
            pltpu.VMEM((per, 16, 128), F32),
            pltpu.VMEM((2, per, 16, 128), F32),
            pltpu.VMEM((2, 16, 128), F32),
            pltpu.VMEM((64, 128), F32),
            pltpu.VMEM((nc, 8, 128), F32),
            pltpu.VMEM((16, 8, 384), F32),
            pltpu.VMEM((16, 8, 384), F32),
            pltpu.VMEM((16, 8, 384), F32),
            pltpu.VMEM((16, 8, 384), F32),
            pltpu.VMEM((8, 384), F32),
            pltpu.VMEM((8, 384), F32),
            pltpu.SemaphoreType.DMA((15,)),
            pltpu.SemaphoreType.DMA((15,)),
            pltpu.SemaphoreType.DMA((5,)),
            pltpu.SemaphoreType.DMA((4,)),
        ],
        compiler_params=pltpu.CompilerParams(
            collective_id=0, has_side_effects=True, vmem_limit_bytes=60 * 1024 * 1024
        ),
        name="pair_kernel",
    )(embed, left_proj.T, right_proj.T, conv_w, cotangent)
    conv_grad, left_t, right_t, embed_grad, pair_out = pl.pallas_call(
        functools.partial(finish_kernel, 32.0 / (8 * nr * nc)),
        out_shape=(
            jax.ShapeDtypeStruct((9, 32, 32), F32),
            jax.ShapeDtypeStruct((32, 512), F32),
            jax.ShapeDtypeStruct((32, 512), F32),
            jax.ShapeDtypeStruct((8, 512), F32),
            jax.ShapeDtypeStruct((32, 64, 256), BF16),
        ),
        in_specs=[VMEM, VMEM, HBM],
        out_specs=(VMEM,) * 4 + (HBM,),
        scratch_shapes=[
            pltpu.VMEM((32, 64, 256), BF16),
            pltpu.SemaphoreType.DMA((4,)),
            pltpu.SemaphoreType.DMA((4,)),
        ],
        compiler_params=pltpu.CompilerParams(vmem_limit_bytes=60 * 1024 * 1024),
        name="finish",
    )(totals, embed_grad, pair_out)
    return pair_out, conv_grad, left_t.T, right_t.T, embed_grad


def solution(mesh):
    body = functools.partial(shards, mesh.shape["row"], mesh.shape["col"])
    in_specs = (P(("row", "col"), None), P(), P(), P(), P(None, "row", "col"))
    out_specs = (P(None, "row", "col"), P(), P(), P(), P(("row", "col"), None))
    return jax.shard_map(body, mesh=mesh, in_specs=in_specs, out_specs=out_specs, check_vma=False)
```

```python
import functools

import jax
import jax.numpy as jnp
from jax import lax
from jax.experimental import pallas as pl
from jax.experimental.pallas import tpu as pltpu
from jax.sharding import PartitionSpec as P

MESH = pl.DeviceIdType.MESH
OUTSIDE = -1e30
LOG2E = 1.4426950408889634
LN2 = 0.6931471805599453
F32 = jnp.float32
BF16 = jnp.bfloat16
VMEM = pl.BlockSpec(memory_space=pltpu.VMEM)
HBM = pl.BlockSpec(memory_space=pltpu.HBM)


def iota(shape, dim):
    return lax.broadcasted_iota(jnp.int32, shape, dim)


def one_hot(cond):
    return jnp.where(cond, 1.0, 0.0).astype(BF16)


def dot(a, b):
    return jnp.dot(a, b, preferred_element_type=F32)


def dot_nt(a, b):
    return lax.dot_general(a, b, (((1,), (1,)), ((), ())), preferred_element_type=F32)


def dot_tn(a, b):
    return lax.dot_general(a, b, (((0,), (0,)), ((), ())), preferred_element_type=F32)


def halves(x):
    high = x.astype(BF16)
    return high, (x - high.astype(F32)).astype(BF16)


def loop(n, f):
    def body(k, _):
        f(k)
        return 0

    lax.fori_loop(0, n, body, 0)


def lanes(h):
    return pl.ds(pl.multiple_of(h * 256, 256), 256)


def wait_bytes(ref, sem):
    pltpu.make_async_copy(ref, ref, sem).wait()


def softplus_and_slope(y):
    t = jnp.exp2(-jnp.abs(y))
    u = 1.0 + t
    inv = pltpu.reciprocal(u, approx=True, full_range=False)
    inv = inv * (2.0 - u * inv)
    log = jnp.where(t < 1 / 256, t * (LOG2E - (0.5 * LOG2E) * t), jnp.log2(u))
    return LN2 * (jnp.maximum(y, 0.0) + log), jnp.where(y >= 0, inv, t * inv)


def build_taps(w_ref, tf):
    spread = one_hot((iota((256, 32), 0) >> 3) == iota((256, 32), 1))
    widen = one_hot((iota((32, 256), 1) >> 3) == iota((32, 256), 0))
    s0, s1 = iota((256, 256), 0) & 7, iota((256, 256), 1) & 7
    same, above, below = s1 == s0, s1 == s0 + 4, s1 == s0 - 4
    for b in range(3):
        x = [dot(spread, dot(w_ref[3 * a + b], widen).astype(BF16)) for a in range(3)]
        tf[:, 256 * b : 256 * b + 256] = jnp.where(same, x[0], jnp.where(above, x[1], 0.0)).astype(BF16)
        tf[:, 768 + 256 * b : 1024 + 256 * b] = jnp.where(same, x[2], jnp.where(below, x[1], 0.0)).astype(BF16)


def mask_cotangent(r, c, cot_ref, mall, mt):
    for k in range(4):
        x = cot_ref[:, 16 * k : 16 * k + 16, :].astype(F32)
        row = r * 64 + 16 * k + iota((16, 256), 0)
        x = jnp.where((c * 256 + iota((16, 256), 1) >= row)[None], x, 0.0)
        for half in range(2):
            mall[:, lanes(2 * k + half)] = x[:, 8 * half : 8 * half + 8].reshape(256, 256).astype(BF16)
    for b in range(3):
        mt[0, :, 256 * b : 256 * b + 256] = jnp.zeros((272, 256), BF16)
        mt[9, :, 256 * b : 256 * b + 256] = jnp.zeros((272, 256), BF16)

    def body(g):
        for b in range(3):
            move = one_hot(iota((272, 256), 0) - 4 * b == iota((272, 256), 1))
            mt[g + 1, :, 256 * b : 256 * b + 256] = dot_nt(move, mall[:, lanes(g)]).astype(BF16)

    loop(8, body)


def input_gradient(mt, tf, z):
    def body(h):
        z[h] = dot_nt_blocks(mt, tf, h)

    loop(9, body)


def dot_nt_blocks(mt, tf, h):
    left = jnp.concatenate([mt[h], mt[h + 1]], axis=1)
    right = jnp.concatenate(
        [tf[:, 768 * (1 - u) + 256 * b : 768 * (1 - u) + 256 * b + 256] for u in range(2) for b in range(3)], axis=0
    )
    return dot(left, right)


def features(rows, cols, rowf, colf):
    k, n = iota((128, 256), 0), iota((128, 256), 1) >> 3
    colf[...] = dot(cols, one_hot(k == n + 32)) * LOG2E
    x = dot(rows, one_hot(k == n))
    x = jnp.where((iota((128, 256), 0) & 7) == (iota((128, 256), 1) & 7), x, 0.0).astype(BF16)
    rowf[...] = dot(one_hot((iota((16, 128), 1) >> 3) == iota((16, 128), 0)), x) * LOG2E


def elementwise(rowf, colf, z, act, cacc, rsum):
    rsum[...] = jnp.zeros_like(rsum)

    def body(step):
        for part in range(3):
            rows = pl.ds(pl.multiple_of(24 * step + 8 * part, 8), 8)
            right = colf[rows, :]
            total = jnp.zeros((8, 256), F32)
            for h in range(9):
                value, slope = softplus_and_slope(right + rowf[h : h + 1, :])
                act[h, rows, :] = value
                p = z[h, rows, :] * slope
                total += p
                rsum[8 * h : 8 * h + 8, :] += p
            cacc[rows, :] = total

    loop(11, body)


def sums(cacc, rsum, cols, col_ends, row_main, row_ends):
    k, n = iota((256, 128), 0) >> 3, iota((256, 128), 1)
    picks = [one_hot(k + 32 * g == n) for g in range(4)]
    pick = jnp.concatenate(picks, axis=0)
    x = [
        jnp.concatenate([cacc[4 + 64 * q + 16 * g : 20 + 64 * q + 16 * g, :] for g in range(4)], axis=1) for q in range(4)
    ]
    high, low = halves(jnp.concatenate(x, axis=0))
    x = dot(high, pick) + dot(low, pick)
    for q in range(4):
        cols[q] = x[16 * q : 16 * q + 16]
    sub, lane = iota((16, 128), 0), iota((16, 128), 1)
    ends = jnp.concatenate([cacc[0:8, :], cacc[256:264, :]], axis=0)
    high, low = halves(ends)
    first = dot(high, picks[3]) + dot(low, picks[3])
    second = dot(high, picks[0]) + dot(low, picks[0])
    col_ends[0] = jnp.where(sub >= 12, pltpu.roll(first, 12, 0), 0.0)
    col_ends[1] = jnp.where(sub < 4, pltpu.roll(second, 4, 0), 0.0)
    x = jnp.concatenate([rsum[...], jnp.zeros((56, 256), F32)], axis=0)
    by_group = one_hot((iota((80, 128), 0) >> 3) == (iota((80, 128), 1) >> 3))
    high, low = halves(x)
    x = dot(by_group, high) + dot(by_group, low)
    x = jnp.where((iota((80, 256), 0) & 7) == (iota((80, 256), 1) & 7), x, 0.0)
    high, low = halves(jnp.concatenate([x[4 + 16 * g : 20 + 16 * g] for g in range(4)], axis=1))
    row_main[...] = dot(high, pick) + dot(low, pick)
    ends = jnp.concatenate([x[0:8], x[64:72]], axis=0)
    high, low = halves(ends)
    first = dot(high, picks[3]) + dot(low, picks[3])
    second = dot(high, picks[0]) + dot(low, picks[0])
    row_ends[0] = jnp.where(sub >= 12, pltpu.roll(first, 12, 0), 0.0)
    row_ends[1] = jnp.where(sub < 4, pltpu.roll(second, 4, 0), 0.0)


def build_windows(act, a3):
    def body(h):
        at = pl.ds(pl.multiple_of(256 * h, 256), 256)
        for b in range(3):
            a3[at, 256 * b : 256 * b + 256] = act[h, 4 * b : 4 * b + 256, :].astype(BF16)

    loop(9, body)


def convolve(r, c, k, a3, tf, out_ref):
    parts = []
    for g in (2 * k, 2 * k + 1):
        both = jnp.concatenate([a3[256 * (g + u) : 256 * (g + u) + 256, :] for u in range(2)], axis=1)
        parts.append(dot_nt(tf[...], both).reshape(32, 8, 256))
    y = jnp.concatenate(parts, axis=1)
    row = r * 64 + 16 * k + iota((16, 256), 0)
    col = c * 256 + iota((16, 256), 1)
    out_ref[:, 16 * k : 16 * k + 16, :] = jnp.where((col >= row)[None], y, 0.0).astype(BF16)


def tap_gradient(mall, a3, taps):
    s0, s1 = iota((256, 256), 0) & 7, iota((256, 256), 1) & 7
    same, above, below = s1 == s0, s1 == s0 + 4, s1 == s0 - 4
    by_channel = one_hot(((iota((32, 512), 1) & 255) >> 3) == iota((32, 512), 0))
    rows = [None] * 9
    for b in range(3):
        g0 = dot(mall[...], a3[0:2048, 256 * b : 256 * b + 256])
        g1 = dot(mall[...], a3[256:2304, 256 * b : 256 * b + 256])
        ys = (
            jnp.where(same, g0, 0.0),
            jnp.where(above, g0, jnp.where(below, g1, 0.0)),
            jnp.where(same, g1, 0.0),
        )
        for a in range(3):
            rows[3 * a + b] = dot(by_channel, jnp.concatenate(halves(ys[a]), axis=0))
    for q in range(3):
        group = rows[4 * q : 4 * q + 4]
        pick = jnp.concatenate(
            [one_hot((iota((256, 128), 0) >> 3) + 32 * k == iota((256, 128), 1)) for k in range(len(group))], axis=0
        )
        high, low = halves(jnp.concatenate(group, axis=1))
        taps[32 * q : 32 * q + 32, :] = dot(high, pick) + dot(low, pick)


LOCAL_SCRATCH = [
    pltpu.VMEM((16, 256), F32),
    pltpu.VMEM((272, 256), F32),
    pltpu.VMEM((96, 128), F32),
    pltpu.VMEM((256, 2048), BF16),
    pltpu.VMEM((10, 272, 768), BF16),
    pltpu.VMEM((9, 272, 256), F32),
    pltpu.VMEM((2304, 768), BF16),
    pltpu.VMEM((9, 272, 256), F32),
    pltpu.VMEM((256, 1536), BF16),
    pltpu.VMEM((272, 256), F32),
    pltpu.VMEM((72, 256), F32),
    pltpu.VMEM((4, 16, 128), F32),
    pltpu.VMEM((2, 16, 128), F32),
    pltpu.VMEM((16, 128), F32),
    pltpu.VMEM((2, 16, 128), F32),
]


class Place:
    def __init__(self, nr, nc):
        r, c = lax.axis_index("row"), lax.axis_index("col")
        self.r, self.c, self.nr, self.nc = r, c, nr, nc
        self.per = nr // nc
        self.rb, self.rm = lax.div(r, self.per), lax.rem(r, self.per)
        bits1 = ((r, 8, 0), (r, 16, 0), (c, 2, 1), (c, 4, 1))
        bits2 = ((r, 1, 0), (r, 2, 0), (r, 4, 0), (c, 1, 1))
        self.k1, self.group1 = self.group(bits1)
        self.k2, self.group2 = self.group(bits2)
        _, self.group0 = self.group(((c, 1, 1), (c, 2, 1), (c, 4, 1)))
        self.has_up, self.has_down = r > 0, r < nr - 1
        self.has_left, self.has_right = c > 0, c < nc - 1
        self.ends_block = (self.rm == self.per - 1) & (self.rb < nc - 1)
        self.starts_block = (self.rm == 0) & (self.rb > 0)
        self.in_others = self.rb == c

    def group(self, bits):
        number, turns = 0, []
        for k, (x, weight, is_col) in enumerate(bits):
            bit = lax.rem(lax.div(x, weight), 2)
            number = number + bit * (1 << k)
            sign = 1 - 2 * bit
            turns.append((sign * weight, is_col, sign * (1 << k)))
        members = [(self.r, self.c, number)]
        for move, is_col, step in turns:
            members += [
                (a, b + move, n + step) if is_col else (a + move, b, n + step) for a, b, n in members
            ]
        return number, members[:0:-1]

    def other(self, k):
        return self.per * self.c + k, self.rb

    def greet(self):
        r, c, nc, per = self.r, self.c, self.nc, self.per
        barrier = pltpu.get_barrier_semaphore()

        def signal(a, b):
            pl.semaphore_signal(barrier, inc=1, device_id=(a, b), device_id_type=MESH)

        def signal_other(a, b):
            pl.when((a != r) | (b != c))(lambda: signal(a, b))

        def signal_all(col):
            for k in range(per):
                signal(per * c + k, col)

        for a, b, _ in self.group0 + self.group1 + self.group2:
            signal(a, b)
        for k in range(per):
            signal_other(*self.other(k))
        pl.when(self.has_up)(lambda: signal(r - 1, c))
        pl.when(self.has_down)(lambda: signal(r + 1, c))
        pl.when(self.has_left)(lambda: signal(per * c - 1, self.rb))
        pl.when(self.has_right)(lambda: signal(per * c + per, self.rb))
        pl.when(self.ends_block)(lambda: signal_all(self.rb + 1))
        pl.when(self.starts_block)(lambda: signal_all(self.rb - 1))
        n = nc - 1 + per + 30
        for cond, m in (
            (self.in_others, -1), (self.has_up, 1), (self.has_down, 1), (self.has_left, 1),
            (self.has_right, 1), (self.ends_block, per), (self.starts_block, per),
        ):
            n = n + jnp.where(cond, m, 0)
        return n

    def senders(self, send, recv):
        def put(src, dst_r, dst_c, dst, sem):
            pltpu.make_async_remote_copy(
                src, dst, send.at[sem], recv.at[sem], device_id=(dst_r, dst_c), device_id_type=MESH
            ).start()

        def put_other(src, k, dst, sem):
            a, b = self.other(k)
            mine = (a == self.r) & (b == self.c)
            pl.when(mine)(lambda: pltpu.make_async_copy(src, dst, recv.at[sem]).start())
            pl.when(jnp.logical_not(mine))(lambda: put(src, a, b, dst, sem))

        return put, put_other


def pair_kernel(
    nr, nc, e_hbm, lpt_hbm, rpt_hbm, w_hbm, cot_hbm,
    out_hbm, sums_hbm, eg_hbm,
    rowf, colf, taps, mall, mt, act, a3, z, tf, cacc, rsum, cols, col_ends, row_main, row_ends,
    out_ref, eg_ref, feats, e_ref, w_ref, cot_ref, proj, es, eb, el, eh, fb, blocks, row_feats, col_feats,
    cparts, cends, rends, turned, gparts, buf, r1, r2, r3, mid, fin, recv, send, loads, stores,
):
    ins = ((e_hbm, e_ref), (w_hbm, w_ref), (lpt_hbm, proj.at[0:32]), (rpt_hbm, proj.at[32:64]), (cot_hbm, cot_ref))
    ins = [pltpu.make_async_copy(src, dst, loads.at[k]) for k, (src, dst) in enumerate(ins)]
    for copy in ins:
        copy.start()
    p = Place(nr, nc)
    r, c, per, rb, rm, k1, k2 = p.r, p.c, p.per, p.rb, p.rm, p.k1, p.k2
    greeted = p.greet()
    put, put_other = p.senders(send, recv)

    ins[0].wait()
    e = e_ref[...].astype(F32)
    es[...] = jnp.concatenate([e[:, 0:256], e[:, 256:512]], axis=0).astype(BF16)
    pl.semaphore_wait(pltpu.get_barrier_semaphore(), greeted)

    for a, b, _ in p.group0:
        put(es, a, b, eb.at[c], 0)
    pltpu.make_async_copy(es, eb.at[c], recv.at[0]).start()
    proj[64:128, :] = jnp.zeros((64, 512), BF16)
    ins[1].wait()
    build_taps(w_ref, tf)
    ins[4].wait()
    mask_cotangent(r, c, cot_ref, mall, mt)
    ins[2].wait()
    ins[3].wait()
    wait_bytes(eb, recv.at[0])
    e = eb[...].astype(F32)
    el[...] = e[:, 0:8].reshape(64, 256).astype(BF16)
    eh[...] = e[:, 8:16].reshape(64, 256).astype(BF16)
    fb[...] = (dot_nt(el[...], proj[:, 0:256]) + dot_nt(eh[...], proj[:, 256:512])).astype(BF16)

    for k in range(per):
        put_other(fb, k, blocks.at[rm], 1)
    bottom, top = fb.at[48:64], fb.at[0:16]

    def put_all(src, col, dst, sem):
        for k in range(per):
            put(src, per * c + k, col, dst, sem)

    pl.when(p.has_down)(lambda: put(bottom, r + 1, c, row_feats.at[0], 2))
    pl.when(p.has_up)(lambda: put(top, r - 1, c, row_feats.at[1], 3))
    pl.when(p.ends_block)(lambda: put_all(bottom, rb + 1, col_feats.at[0], 4))
    pl.when(p.starts_block)(lambda: put_all(top, rb - 1, col_feats.at[1], 5))
    input_gradient(mt, tf, z)

    def arrive(cond, ref, sem):
        pl.when(cond)(lambda: wait_bytes(ref, sem))
        pl.when(jnp.logical_not(cond))(lambda: ref.__setitem__(..., jnp.full(ref.shape, OUTSIDE, BF16)))

    arrive(p.has_up, row_feats.at[0], recv.at[2])
    arrive(p.has_down, row_feats.at[1], recv.at[3])
    arrive(p.has_left, col_feats.at[0], recv.at[4])
    arrive(p.has_right, col_feats.at[1], recv.at[5])
    wait_bytes(blocks, recv.at[1])
    feats[0:4, :] = row_feats[0].astype(F32)[12:16]
    feats[4:68, :] = fb[...].astype(F32)
    feats[68:72, :] = row_feats[1].astype(F32)[0:4]
    feats[72:128, :] = jnp.zeros((56, 128), F32)
    rows = feats[0:128, :].astype(BF16)
    feats[128:132, :] = col_feats[0].astype(F32)[12:16]
    feats[132 : 132 + 64 * per, :] = blocks[...].reshape(64 * per, 128).astype(F32)
    feats[388:392, :] = col_feats[1].astype(F32)[0:4]
    feats[392:400, :] = jnp.zeros((8, 128), F32)
    features(rows, feats[128:400, :].astype(BF16), rowf, colf)
    elementwise(rowf, colf, z, act, cacc, rsum)
    sums(cacc, rsum, cols, col_ends, row_main, row_ends)

    for k in range(per):
        put_other(cols.at[k], k, cparts.at[rm], 6)
    pl.when(p.has_up)(lambda: put(row_ends.at[0], r - 1, c, rends.at[0], 7))
    pl.when(p.has_down)(lambda: put(row_ends.at[1], r + 1, c, rends.at[1], 8))
    pl.when(p.has_left)(lambda: put(col_ends.at[0], per * c - 1, rb, cends.at[0, rm], 9))
    pl.when(p.has_right)(lambda: put(col_ends.at[1], per * c + per, rb, cends.at[1, rm], 10))

    build_windows(act, a3)
    tap_gradient(mall, a3, taps)
    for k in range(16):
        piece = taps[8 * k : 8 * k + 8, :] if k < 12 else jnp.zeros((8, 128), F32)
        buf[k, 16:32, :] = jnp.concatenate([piece, jnp.zeros((8, 128), F32)], axis=0).astype(BF16)

    def gather_sum(cond, ref, sem):
        pl.when(cond)(lambda: wait_bytes(ref, sem))
        pl.when(jnp.logical_not(cond))(lambda: ref.__setitem__(..., jnp.zeros(ref.shape, F32)))

    gather_sum(p.has_down, rends.at[0], recv.at[7])
    gather_sum(p.has_up, rends.at[1], recv.at[8])
    gather_sum(p.ends_block, cends.at[0], recv.at[9])
    gather_sum(p.starts_block, cends.at[1], recv.at[10])
    wait_bytes(cparts, recv.at[6])
    grads = (
        row_main[...] + rends[0] + rends[1],
        jnp.sum(cparts[...], axis=0) + jnp.sum(cends[0], axis=0) + jnp.sum(cends[1], axis=0),
    )
    lane = iota((16, 128), 1)
    spread = []
    for g in range(4):
        parts = [x if turn % 128 == 0 else pltpu.roll(x, turn % 128, 1) for x, turn in zip(grads, (-32 * g, 32 - 32 * g))]
        spread.append(jnp.where(lane < 32, parts[0], jnp.where(lane < 64, parts[1], 0.0)))
    turned[...] = jnp.concatenate(spread, axis=0)

    high, low = halves(turned[...])
    for half, ref in enumerate((el, eh)):
        part = dot_tn(high, ref[...]) + dot_tn(low, ref[...])
        for k in range(8):
            at = slice(16 * (k // 2), 16 * (k // 2) + 16), slice(128 * (k % 2), 128 * (k % 2) + 128)
            buf[4 * (k // 2) + 2 * half + k % 2, 0:16, :] = part[at].astype(BF16)

    for a, b, at in p.group1:
        put(buf.at[at], a, b, r1.at[k1], 11)
    pltpu.make_async_copy(buf.at[k1], r1.at[k1], recv.at[11]).start()

    for a, b, _ in p.group0:
        put(turned.at[pl.ds(pl.multiple_of(8 * b, 8), 8)], a, b, gparts.at[c], 14)
    pltpu.make_async_copy(turned.at[pl.ds(pl.multiple_of(8 * c, 8), 8)], gparts.at[c], recv.at[14]).start()

    outs = [
        pltpu.make_async_copy(out_ref.at[:, 16 * q : 16 * q + 16, :], out_hbm.at[:, 16 * q : 16 * q + 16, :], stores.at[q])
        for q in range(4)
    ]
    convolve(r, c, 0, a3, tf, out_ref)
    outs[0].start()
    convolve(r, c, 1, a3, tf, out_ref)
    outs[1].start()
    wait_bytes(r1, recv.at[11])
    mid[...] = jnp.sum(r1[...].astype(F32), axis=0).astype(BF16)
    for a, b, _ in p.group2:
        put(mid, a, b, r2.at[k2], 12)
    pltpu.make_async_copy(mid, r2.at[k2], recv.at[12]).start()

    convolve(r, c, 2, a3, tf, out_ref)
    outs[2].start()
    convolve(r, c, 3, a3, tf, out_ref)
    outs[3].start()
    wait_bytes(r2, recv.at[12])
    fin[...] = jnp.sum(r2[...].astype(F32), axis=0).astype(BF16)
    for a, b, _ in p.group1:
        put(fin, a, b, r3.at[k1], 13)
    pltpu.make_async_copy(fin, r3.at[k1], recv.at[13]).start()

    wait_bytes(gparts, recv.at[14])
    high, low = halves(jnp.sum(gparts[...], axis=0))
    eg_ref[...] = dot(high, proj[...]) + dot(low, proj[...])
    outs.append(pltpu.make_async_copy(eg_ref, eg_hbm, stores.at[4]))
    outs[4].start()

    for copy in outs:
        copy.wait()
    wait_bytes(eb.at[0 : nc - 1], send.at[0])
    pl.when(p.in_others)(lambda: wait_bytes(blocks.at[0 : per - 1], send.at[1]))
    pl.when(jnp.logical_not(p.in_others))(lambda: wait_bytes(blocks, send.at[1]))
    pl.when(p.has_down)(lambda: wait_bytes(bottom, send.at[2]))
    pl.when(p.has_up)(lambda: wait_bytes(top, send.at[3]))
    pl.when(p.ends_block)(lambda: wait_bytes(fb, send.at[4]))
    pl.when(p.starts_block)(lambda: wait_bytes(fb, send.at[5]))
    pl.when(p.in_others)(lambda: wait_bytes(cparts.at[0 : per - 1], send.at[6]))
    pl.when(jnp.logical_not(p.in_others))(lambda: wait_bytes(cparts, send.at[6]))
    pl.when(p.has_up)(lambda: wait_bytes(row_ends.at[0], send.at[7]))
    pl.when(p.has_down)(lambda: wait_bytes(row_ends.at[1], send.at[8]))
    pl.when(p.has_left)(lambda: wait_bytes(col_ends.at[0], send.at[9]))
    pl.when(p.has_right)(lambda: wait_bytes(col_ends.at[1], send.at[10]))
    wait_bytes(r1.at[0:15], send.at[11])
    wait_bytes(r2.at[0:15], send.at[12])
    wait_bytes(gparts.at[0 : nc - 1], send.at[14])

    wait_bytes(r3, recv.at[13])
    last = pltpu.make_async_copy(r3, sums_hbm, stores.at[5])
    last.start()
    wait_bytes(r3.at[0:15], send.at[13])
    last.wait()


def finish_kernel(
    scale, sums_in, eg_in, pair_in, conv_out, left_out, right_out, eg_out, pair_out,
    sums_ref, eg_ref, held, conv_ref, left_ref, right_ref, loads, stores,
):
    def piece(k):
        return slice(8 * k, 8 * k + 8)

    ins = [pltpu.make_async_copy(sums_in, sums_ref, loads.at[0]), pltpu.make_async_copy(eg_in, eg_ref, loads.at[1])]
    ins += [pltpu.make_async_copy(pair_in.at[piece(k)], held.at[piece(k)], loads.at[2 + k]) for k in range(4)]
    outs = [
        pltpu.make_async_copy(conv_ref, conv_out, stores.at[0]),
        pltpu.make_async_copy(left_ref, left_out, stores.at[1]),
        pltpu.make_async_copy(right_ref, right_out, stores.at[2]),
        pltpu.make_async_copy(eg_ref, eg_out, stores.at[3]),
    ]
    outs += [pltpu.make_async_copy(held.at[piece(k)], pair_out.at[piece(k)], stores.at[4 + k]) for k in range(4)]
    for copy in ins:
        copy.start()
    ins[0].wait()
    for ref, first, at in ((left_ref, 0, 1), (right_ref, 8, 2)):
        for k in range(8):
            x = sums_ref[first + k, 0:16, :].astype(F32)
            ref[16 * (k // 4) : 16 * (k // 4) + 16, 128 * (k % 4) : 128 * (k % 4) + 128] = x * scale
        outs[at].start()
    ins[1].wait()
    outs[3].start()
    for k in range(4):
        ins[2 + k].wait()
        outs[4 + k].start()
    for k in range(9):
        q, at = divmod(k, 4)
        for part in range(4):
            x = sums_ref[4 * q + part, 16:32, :].astype(F32)
            conv_ref[k, 8 * part : 8 * part + 8, :] = x[0:8, 32 * at : 32 * at + 32] * scale
    outs[0].start()
    for copy in outs:
        copy.wait()


def shards(nr, nc, embed, left_proj, right_proj, conv_w, cotangent):
    per = nr // nc
    pair_out, totals, embed_grad = pl.pallas_call(
        functools.partial(pair_kernel, nr, nc),
        out_shape=(
            jax.ShapeDtypeStruct((32, 64, 256), BF16),
            jax.ShapeDtypeStruct((16, 32, 128), BF16),
            jax.ShapeDtypeStruct((8, 512), F32),
        ),
        in_specs=[HBM] * 5,
        out_specs=(HBM,) * 3,
        scratch_shapes=LOCAL_SCRATCH
        + [
            pltpu.VMEM((32, 64, 256), BF16),
            pltpu.VMEM((8, 512), F32),
            pltpu.VMEM((400, 128), F32),
            pltpu.VMEM((8, 512), BF16),
            pltpu.VMEM((9, 32, 32), BF16),
            pltpu.VMEM((32, 64, 256), BF16),
            pltpu.VMEM((128, 512), BF16),
            pltpu.VMEM((16, 256), BF16),
            pltpu.VMEM((nc, 16, 256), BF16),
            pltpu.VMEM((64, 256), BF16),
            pltpu.VMEM((64, 256), BF16),
            pltpu.VMEM((64, 128), BF16),
            pltpu.VMEM((per, 64, 128), BF16),
            pltpu.VMEM((2, 16, 128), BF16),
            pltpu.VMEM((2, 16, 128), BF16),
            pltpu.VMEM((per, 16, 128), F32),
            pltpu.VMEM((2, per, 16, 128), F32),
            pltpu.VMEM((2, 16, 128), F32),
            pltpu.VMEM((64, 128), F32),
            pltpu.VMEM((nc, 8, 128), F32),
            pltpu.VMEM((16, 32, 128), BF16),
            pltpu.VMEM((16, 32, 128), BF16),
            pltpu.VMEM((16, 32, 128), BF16),
            pltpu.VMEM((16, 32, 128), BF16),
            pltpu.VMEM((32, 128), BF16),
            pltpu.VMEM((32, 128), BF16),
            pltpu.SemaphoreType.DMA((15,)),
            pltpu.SemaphoreType.DMA((15,)),
            pltpu.SemaphoreType.DMA((5,)),
            pltpu.SemaphoreType.DMA((6,)),
        ],
        compiler_params=pltpu.CompilerParams(
            collective_id=0, has_side_effects=True, vmem_limit_bytes=60 * 1024 * 1024
        ),
        name="pair_kernel",
    )(embed, left_proj.T, right_proj.T, conv_w, cotangent)
    conv_grad, left_t, right_t, embed_grad, pair_out = pl.pallas_call(
        functools.partial(finish_kernel, 32.0 / (8 * nr * nc)),
        out_shape=(
            jax.ShapeDtypeStruct((9, 32, 32), F32),
            jax.ShapeDtypeStruct((32, 512), F32),
            jax.ShapeDtypeStruct((32, 512), F32),
            jax.ShapeDtypeStruct((8, 512), F32),
            jax.ShapeDtypeStruct((32, 64, 256), BF16),
        ),
        in_specs=[HBM] * 3,
        out_specs=(HBM,) * 5,
        scratch_shapes=[
            pltpu.VMEM((16, 32, 128), BF16),
            pltpu.VMEM((8, 512), F32),
            pltpu.VMEM((32, 64, 256), BF16),
            pltpu.VMEM((9, 32, 32), F32),
            pltpu.VMEM((32, 512), F32),
            pltpu.VMEM((32, 512), F32),
            pltpu.SemaphoreType.DMA((6,)),
            pltpu.SemaphoreType.DMA((8,)),
        ],
        compiler_params=pltpu.CompilerParams(vmem_limit_bytes=60 * 1024 * 1024),
        name="finish",
    )(totals, embed_grad, pair_out)
    return pair_out, conv_grad, left_t.T, right_t.T, embed_grad


def solution(mesh):
    body = functools.partial(shards, mesh.shape["row"], mesh.shape["col"])
    in_specs = (P(("row", "col"), None), P(), P(), P(), P(None, "row", "col"))
    out_specs = (P(None, "row", "col"), P(), P(), P(), P(("row", "col"), None))
    return jax.shard_map(body, mesh=mesh, in_specs=in_specs, out_specs=out_specs, check_vma=False)
```

```python
import functools

import jax
import jax.numpy as jnp
from jax import lax
from jax.experimental import pallas as pl
from jax.experimental.pallas import tpu as pltpu
from jax.sharding import PartitionSpec as P

MESH = pl.DeviceIdType.MESH
OUTSIDE = -1e30
LOG2E = 1.4426950408889634
LN2 = 0.6931471805599453
F32 = jnp.float32
BF16 = jnp.bfloat16
VMEM = pl.BlockSpec(memory_space=pltpu.VMEM)
HBM = pl.BlockSpec(memory_space=pltpu.HBM)


def iota(shape, dim):
    return lax.broadcasted_iota(jnp.int32, shape, dim)


def one_hot(cond):
    return jnp.where(cond, 1.0, 0.0).astype(BF16)


def dot(a, b):
    return jnp.dot(a, b, preferred_element_type=F32)


def dot_nt(a, b):
    return lax.dot_general(a, b, (((1,), (1,)), ((), ())), preferred_element_type=F32)


def dot_tn(a, b):
    return lax.dot_general(a, b, (((0,), (0,)), ((), ())), preferred_element_type=F32)


def halves(x):
    high = x.astype(BF16)
    return high, (x - high.astype(F32)).astype(BF16)


def loop(n, f):
    def body(k, _):
        f(k)
        return 0

    lax.fori_loop(0, n, body, 0)


def lanes(h):
    return pl.ds(pl.multiple_of(h * 256, 256), 256)


def wait_bytes(ref, sem):
    pltpu.make_async_copy(ref, ref, sem).wait()


def softplus_and_slope(y):
    t = jnp.exp2(-jnp.abs(y))
    u = 1.0 + t
    inv = pltpu.reciprocal(u, full_range=False)
    log = jnp.where(t < 2.0**-11, t * LOG2E, jnp.log2(u))
    return LN2 * (jnp.maximum(y, 0.0) + log), jnp.where(y >= 0, inv, t * inv)


def build_taps(w_ref, tf):
    spread = one_hot((iota((256, 32), 0) >> 3) == iota((256, 32), 1))
    widen = one_hot((iota((32, 256), 1) >> 3) == iota((32, 256), 0))
    s0, s1 = iota((256, 256), 0) & 7, iota((256, 256), 1) & 7
    same, above, below = s1 == s0, s1 == s0 + 4, s1 == s0 - 4
    for b in range(3):
        x = [dot(spread, dot(w_ref[3 * a + b], widen).astype(BF16)) for a in range(3)]
        tf[:, 256 * b : 256 * b + 256] = jnp.where(same, x[0], jnp.where(above, x[1], 0.0)).astype(BF16)
        tf[:, 768 + 256 * b : 1024 + 256 * b] = jnp.where(same, x[2], jnp.where(below, x[1], 0.0)).astype(BF16)


def mask_cotangent(r, c, cot_ref, move, mall, mt):
    for k in range(4):
        x = cot_ref[:, 16 * k : 16 * k + 16, :].astype(F32)
        row = r * 64 + 16 * k + iota((16, 256), 0)
        x = jnp.where((c * 256 + iota((16, 256), 1) >= row)[None], x, 0.0)
        for half in range(2):
            mall[:, lanes(2 * k + half)] = x[:, 8 * half : 8 * half + 8].reshape(256, 256).astype(BF16)
    for b in range(3):
        move[272 * b : 272 * b + 272, :] = one_hot(iota((272, 256), 0) - 4 * b == iota((272, 256), 1))
        mt[0, :, 256 * b : 256 * b + 256] = jnp.zeros((272, 256), BF16)
        mt[9, :, 256 * b : 256 * b + 256] = jnp.zeros((272, 256), BF16)

    def body(g):
        moved = dot_nt(move[...], mall[:, lanes(g)]).astype(BF16)
        for b in range(3):
            mt[g + 1, :, 256 * b : 256 * b + 256] = moved[272 * b : 272 * b + 272]

    loop(8, body)


def input_gradient(mt, tf, z):
    def body(h):
        z[h] = dot_nt_blocks(mt, tf, h)

    loop(9, body)


def dot_nt_blocks(mt, tf, h):
    left = jnp.concatenate([mt[h], mt[h + 1]], axis=1)
    right = jnp.concatenate(
        [tf[:, 768 * (1 - u) + 256 * b : 768 * (1 - u) + 256 * b + 256] for u in range(2) for b in range(3)], axis=0
    )
    return dot(left, right)


def features(rows, cols, rowf, colf):
    k, n = iota((128, 256), 0), iota((128, 256), 1) >> 3
    colf[...] = dot(cols, one_hot(k == n + 32)) * LOG2E
    x = dot(rows, one_hot(k == n))
    x = jnp.where((iota((128, 256), 0) & 7) == (iota((128, 256), 1) & 7), x, 0.0).astype(BF16)
    rowf[...] = dot(one_hot((iota((16, 128), 1) >> 3) == iota((16, 128), 0)), x) * LOG2E


def elementwise(rowf, colf, z, act, cacc, rsum):
    rsum[...] = jnp.zeros_like(rsum)

    def body(step):
        parts = [pl.ds(pl.multiple_of(24 * step + 8 * part, 8), 8) for part in range(3)]
        totals = [jnp.zeros((8, 256), F32)] * 3
        for h in range(9):
            left = rowf[h : h + 1, :]
            row = jnp.zeros((8, 256), F32)
            for k, rows in enumerate(parts):
                value, slope = softplus_and_slope(colf[rows, :] + left)
                act[h, rows, :] = value
                p = z[h, rows, :] * slope
                totals[k] += p
                row += p
            rsum[8 * h : 8 * h + 8, :] += row
        for k, rows in enumerate(parts):
            cacc[rows, :] = totals[k]

    loop(11, body)


def sums(cacc, rsum, cols, col_ends, row_main, row_ends):
    k, n = iota((256, 128), 0) >> 3, iota((256, 128), 1)
    picks = [one_hot(k + 32 * g == n) for g in range(4)]
    pick = jnp.concatenate(picks, axis=0)
    x = [
        jnp.concatenate([cacc[4 + 64 * q + 16 * g : 20 + 64 * q + 16 * g, :] for g in range(4)], axis=1) for q in range(4)
    ]
    high, low = halves(jnp.concatenate(x, axis=0))
    x = dot(high, pick) + dot(low, pick)
    for q in range(4):
        cols[q] = x[16 * q : 16 * q + 16]
    sub, lane = iota((16, 128), 0), iota((16, 128), 1)
    ends = jnp.concatenate([cacc[0:8, :], cacc[256:264, :]], axis=0)
    high, low = halves(ends)
    first = dot(high, picks[3]) + dot(low, picks[3])
    second = dot(high, picks[0]) + dot(low, picks[0])
    col_ends[0] = jnp.where(sub >= 12, pltpu.roll(first, 12, 0), 0.0)
    col_ends[1] = jnp.where(sub < 4, pltpu.roll(second, 4, 0), 0.0)
    x = jnp.concatenate([rsum[...], jnp.zeros((56, 256), F32)], axis=0)
    by_group = one_hot((iota((80, 128), 0) >> 3) == (iota((80, 128), 1) >> 3))
    high, low = halves(x)
    x = dot(by_group, high) + dot(by_group, low)
    x = jnp.where((iota((80, 256), 0) & 7) == (iota((80, 256), 1) & 7), x, 0.0)
    high, low = halves(jnp.concatenate([x[4 + 16 * g : 20 + 16 * g] for g in range(4)], axis=1))
    row_main[...] = dot(high, pick) + dot(low, pick)
    ends = jnp.concatenate([x[0:8], x[64:72]], axis=0)
    high, low = halves(ends)
    first = dot(high, picks[3]) + dot(low, picks[3])
    second = dot(high, picks[0]) + dot(low, picks[0])
    row_ends[0] = jnp.where(sub >= 12, pltpu.roll(first, 12, 0), 0.0)
    row_ends[1] = jnp.where(sub < 4, pltpu.roll(second, 4, 0), 0.0)


def build_windows(act, a3):
    def body(h):
        at = pl.ds(pl.multiple_of(256 * h, 256), 256)
        for b in range(3):
            a3[at, 256 * b : 256 * b + 256] = act[h, 4 * b : 4 * b + 256, :].astype(BF16)

    loop(9, body)


def convolve(r, c, k, a3, tf, out_ref):
    parts = []
    for g in (2 * k, 2 * k + 1):
        both = jnp.concatenate([a3[256 * (g + u) : 256 * (g + u) + 256, :] for u in range(2)], axis=1)
        parts.append(dot_nt(tf[...], both).reshape(32, 8, 256))
    y = jnp.concatenate(parts, axis=1)
    row = r * 64 + 16 * k + iota((16, 256), 0)
    col = c * 256 + iota((16, 256), 1)
    out_ref[:, 16 * k : 16 * k + 16, :] = jnp.where((col >= row)[None], y, 0.0).astype(BF16)


def build_picks(picks):
    for s in range(8):
        k, n = iota((256, 128), 0), iota((256, 128), 1)
        for which, wanted in enumerate((s, (s + 4) % 8)):
            picks[which, 256 * s : 256 * s + 256, :] = one_hot(k == 8 * n + wanted)


def tap_gradient(mall, a3, picks, gram, taps):
    for u in range(2):
        x = dot(mall[...], a3[256 * u : 256 * u + 2048, :])
        for k in range(6):
            gram[6 * u + k] = x[:, 128 * k : 128 * k + 128]

    def part(s, u, b):
        return jnp.concatenate([gram[6 * u + 2 * b + k, pl.ds(s, 32, stride=8), :] for k in range(2)], axis=1)

    def folded(x, which):
        high, low = halves(x)
        y = dot(jnp.concatenate([high, low], axis=0), picks[which])
        return y[0 : x.shape[0]] + y[x.shape[0] :]

    outer = [jnp.concatenate([part(s, u, b) for s in range(8)], axis=1) for u in range(2) for b in range(3)]
    outer = folded(jnp.concatenate(outer, axis=0), 0)
    inner = [jnp.concatenate([part(s, s // 4, b) for s in range(8)], axis=1) for b in range(3)]
    inner = folded(jnp.concatenate(inner, axis=0), 1)
    rows = [outer[32 * b : 32 * b + 32] for b in range(3)]
    rows += [inner[32 * b : 32 * b + 32] for b in range(3)]
    rows += [outer[96 + 32 * b : 128 + 32 * b] for b in range(3)]
    lane = iota((32, 128), 1)
    for q in range(3):
        total = jnp.zeros((32, 128), F32)
        for k, x in enumerate(rows[4 * q : 4 * q + 4]):
            total = jnp.where((lane >> 5) == k, pltpu.roll(x, 32 * k, 1) if k else x, total)
        taps[32 * q : 32 * q + 32, :] = total


LOCAL_SCRATCH = [
    pltpu.VMEM((16, 256), F32),
    pltpu.VMEM((272, 256), F32),
    pltpu.VMEM((96, 128), F32),
    pltpu.VMEM((256, 2048), BF16),
    pltpu.VMEM((10, 272, 768), BF16),
    pltpu.VMEM((9, 272, 256), F32),
    pltpu.VMEM((2304, 768), BF16),
    pltpu.VMEM((9, 272, 256), F32),
    pltpu.VMEM((256, 1536), BF16),
    pltpu.VMEM((816, 256), BF16),
    pltpu.VMEM((2, 2048, 128), BF16),
    pltpu.VMEM((12, 256, 128), F32),
    pltpu.VMEM((272, 256), F32),
    pltpu.VMEM((72, 256), F32),
    pltpu.VMEM((4, 16, 128), F32),
    pltpu.VMEM((2, 16, 128), F32),
    pltpu.VMEM((16, 128), F32),
    pltpu.VMEM((2, 16, 128), F32),
]


class Place:
    def __init__(self, nr, nc):
        r, c = lax.axis_index("row"), lax.axis_index("col")
        self.r, self.c, self.nr, self.nc = r, c, nr, nc
        self.per = nr // nc
        self.rb, self.rm = lax.div(r, self.per), lax.rem(r, self.per)
        _, self.quad = self.group(((r, 1, 0), (r, 2, 0)))
        _, self.line = self.group(((c, 1, 1), (c, 2, 1), (c, 4, 1)))
        self.k1, self.group1 = self.group(((r, 1, 0), (r, 8, 0), (r, 16, 0), (c, 2, 1), (c, 4, 1)))
        self.k2, self.group2 = self.group(((r, 2, 0), (r, 4, 0), (c, 1, 1)))
        self.has_up, self.has_down = r > 0, r < nr - 1
        self.has_left, self.has_right = c > 0, c < nc - 1
        self.ends_block = (self.rm == self.per - 1) & (self.rb < nc - 1)
        self.starts_block = (self.rm == 0) & (self.rb > 0)
        self.in_others = self.rb == c

    def group(self, bits):
        number, turns = 0, []
        for k, (x, weight, is_col) in enumerate(bits):
            bit = lax.rem(lax.div(x, weight), 2)
            number = number + bit * (1 << k)
            sign = 1 - 2 * bit
            turns.append((sign * weight, is_col, sign * (1 << k)))
        members = [(self.r, self.c, number)]
        for move, is_col, step in turns:
            members += [
                (a, b + move, n + step) if is_col else (a + move, b, n + step) for a, b, n in members
            ]
        return number, members[:0:-1]

    def other(self, k):
        return self.per * self.c + k, self.rb

    def targets(self, col):
        return [(lax.rem(self.r + self.per * k, self.nr), col) for k in range(self.nr // self.per)]

    def greet(self):
        r, c, nc, per, rb, rm = self.r, self.c, self.nc, self.per, self.rb, self.rm
        barrier = pltpu.get_barrier_semaphore()

        def signal(a, b):
            pl.semaphore_signal(barrier, inc=1, device_id=(a, b), device_id_type=MESH)

        def signal_all(col):
            for k in range(per):
                signal(per * c + k, col)

        is_first, is_last = c == 0, c == nc - 1
        before_is_me = is_last & (rb == nc - 2)
        after_is_me = is_first & (rb == 1)
        for a, b, _ in self.quad + self.line:
            signal(a, b)
        pl.when(jnp.logical_not(self.in_others))(lambda: signal(per * c + rm, c))
        for _, b, _ in self.line:
            signal(per * c + rm, b)
        pl.when(self.has_up)(lambda: signal(r - 1, nc - 1))
        pl.when(self.has_down)(lambda: signal(r + 1, 0))
        pl.when(self.has_left & jnp.logical_not(before_is_me))(lambda: signal(per * (c - 1) + rm, nc - 1))
        pl.when(self.has_right & jnp.logical_not(after_is_me))(lambda: signal(per * (c + 1) + rm, 0))
        pl.when(jnp.logical_not(self.in_others))(lambda: signal(per * c + rm, rb))
        for a, _, _ in self.quad:
            signal(per * (c - rb) + a, rb)
        pl.when(self.has_up)(lambda: signal(r - 1, c))
        pl.when(self.has_down)(lambda: signal(r + 1, c))
        pl.when(self.ends_block)(lambda: signal_all(rb + 1))
        pl.when(self.starts_block)(lambda: signal_all(rb - 1))
        for a, b, _ in self.group1 + self.group2:
            signal(a, b)
        n = len(self.quad + self.line + self.group1 + self.group2) + nc + per
        up, down = self.has_up, self.has_down
        for cond, m in (
            (self.in_others, -2), (is_last & down, nc), (is_first & up, nc),
            (is_last & (rb < nc - 1), nc), (before_is_me, -1), (is_first & (rb > 0), nc), (after_is_me, -1),
            (up, 1), (down, 1), (self.has_left, 1), (self.has_right, 1),
        ):
            n = n + jnp.where(cond, m, 0)
        return n

    def senders(self, send, recv):
        def put(src, dst_r, dst_c, dst, sem):
            pltpu.make_async_remote_copy(
                src, dst, send.at[sem], recv.at[sem], device_id=(dst_r, dst_c), device_id_type=MESH
            ).start()

        def put_other(src, k, dst, sem):
            a, b = self.other(k)
            mine = (a == self.r) & (b == self.c)
            pl.when(mine)(lambda: pltpu.make_async_copy(src, dst, recv.at[sem]).start())
            pl.when(jnp.logical_not(mine))(lambda: put(src, a, b, dst, sem))

        return put, put_other


def pair_kernel(
    nr, nc, e_hbm, lpt_hbm, rpt_hbm, w_hbm, cot_hbm,
    out_hbm, sums_hbm, eg_hbm,
    rowf, colf, taps, mall, mt, act, a3, z, tf, move, picks, gram, cacc, rsum, cols, col_ends, row_main, row_ends,
    out_ref, eg_ref, feats, e_ref, w_ref, cot_ref, own, quad, proj, es, eb, el, eh, blocks, row_feats, col_feats,
    cparts, cends, rends, turned, gparts, buf, r1, r2, r3, mid, fin, recv, send, loads, stores,
):
    ins = ((e_hbm, e_ref), (w_hbm, w_ref), (lpt_hbm, proj.at[0:32]), (rpt_hbm, proj.at[32:64]), (cot_hbm, cot_ref))
    ins = [pltpu.make_async_copy(src, dst, loads.at[k]) for k, (src, dst) in enumerate(ins)]
    for copy in ins:
        copy.start()
    p = Place(nr, nc)
    r, c, per, rb, rm, k1, k2 = p.r, p.c, p.per, p.rb, p.rm, p.k1, p.k2
    greeted = p.greet()
    put, put_other = p.senders(send, recv)
    rows8, rows7 = gparts, gparts.at[0 : nc - 1]

    proj[64:128, :] = jnp.zeros((64, 512), BF16)
    ins[0].wait()
    e = e_ref[...].astype(F32)
    es[...] = jnp.concatenate([e[:, 0:256], e[:, 256:512]], axis=0).astype(BF16)
    ins[2].wait()
    ins[3].wait()
    own[...] = dot_nt(e_ref[...], proj[...]).astype(BF16).astype(F32)
    ins[1].wait()
    build_taps(w_ref, tf)
    ins[4].wait()
    mask_cotangent(r, c, cot_ref, move, mall, mt)
    pl.semaphore_wait(pltpu.get_barrier_semaphore(), greeted)

    for a, b, _ in p.quad:
        put(own, a, b, quad.at[rm], 1)
    pltpu.make_async_copy(own, quad.at[rm], recv.at[1]).start()

    def put_line(row, dst, sem):
        for k in range(nc):
            put(own, row, k, dst, sem)

    is_first, is_last = c == 0, c == nc - 1
    row_after, row_before = is_last & p.has_down, is_first & p.has_up
    pl.when(row_after)(lambda: put_line(r + 1, row_feats.at[0], 2))
    pl.when(row_before)(lambda: put_line(r - 1, row_feats.at[1], 3))
    for a, b, _ in p.line:
        put(es, a, b, eb.at[c], 0)
    pltpu.make_async_copy(es, eb.at[c], recv.at[0]).start()

    def put_targets(src, col, dst, sem):
        first, *rest = p.targets(col)
        mine = c == col
        pl.when(mine)(lambda: pltpu.make_async_copy(src, dst, recv.at[sem]).start())
        pl.when(jnp.logical_not(mine))(lambda: put(src, *first, dst, sem))
        for a, b in rest:
            put(src, a, b, dst, sem)

    col_after, col_before = is_last & (rb < nc - 1), is_first & (rb > 0)
    wait_bytes(quad, recv.at[1])
    put_targets(quad, rb, blocks.at[c], 15)
    pl.when(col_after)(lambda: put_targets(quad.at[per - 1], rb + 1, col_feats.at[0], 4))
    pl.when(col_before)(lambda: put_targets(quad.at[0], rb - 1, col_feats.at[1], 5))
    input_gradient(mt, tf, z)
    build_picks(picks)

    wait_bytes(eb, recv.at[0])
    e = eb[...].astype(F32)
    el[...] = e[:, 0:8].reshape(64, 256).astype(BF16)
    eh[...] = e[:, 8:16].reshape(64, 256).astype(BF16)
    feats[8:72, :] = dot_nt(el[...], proj[:, 0:256]) + dot_nt(eh[...], proj[:, 256:512])

    def arrive(cond, ref, sem):
        pl.when(cond)(lambda: wait_bytes(ref, sem))
        pl.when(jnp.logical_not(cond))(lambda: ref.__setitem__(..., jnp.full(ref.shape, OUTSIDE, F32)))

    arrive(p.has_up, row_feats.at[0], recv.at[2])
    arrive(p.has_down, row_feats.at[1], recv.at[3])
    arrive(p.has_left, col_feats.at[0], recv.at[4])
    arrive(p.has_right, col_feats.at[1], recv.at[5])
    wait_bytes(blocks, recv.at[15])
    feats[0:8, :] = row_feats[0]
    feats[72:80, :] = row_feats[1]
    feats[80:136, :] = jnp.zeros((56, 128), F32)
    feats[136:144, :] = col_feats[0]
    for k in range(per):
        for q in range(nc):
            at = 144 + 8 * (nc * k + q)
            feats[at : at + 8, :] = blocks[q, k]
    feats[400:408, :] = col_feats[1]
    feats[408:416, :] = jnp.zeros((8, 128), F32)
    features(feats[4:132, :].astype(BF16), feats[140:412, :].astype(BF16), rowf, colf)
    elementwise(rowf, colf, z, act, cacc, rsum)
    sums(cacc, rsum, cols, col_ends, row_main, row_ends)

    for k in range(per):
        put_other(cols.at[k], k, cparts.at[rm], 6)
    pl.when(p.has_up)(lambda: put(row_ends.at[0], r - 1, c, rends.at[0], 7))
    pl.when(p.has_down)(lambda: put(row_ends.at[1], r + 1, c, rends.at[1], 8))
    pl.when(p.has_left)(lambda: put(col_ends.at[0], per * c - 1, rb, cends.at[0, rm], 9))
    pl.when(p.has_right)(lambda: put(col_ends.at[1], per * c + per, rb, cends.at[1, rm], 10))

    build_windows(act, a3)
    tap_gradient(mall, a3, picks, gram, taps)
    def gather_sum(cond, ref, sem):
        pl.when(cond)(lambda: wait_bytes(ref, sem))
        pl.when(jnp.logical_not(cond))(lambda: ref.__setitem__(..., jnp.zeros(ref.shape, F32)))

    gather_sum(p.has_down, rends.at[0], recv.at[7])
    gather_sum(p.has_up, rends.at[1], recv.at[8])
    gather_sum(p.ends_block, cends.at[0], recv.at[9])
    gather_sum(p.starts_block, cends.at[1], recv.at[10])
    wait_bytes(cparts, recv.at[6])
    grads = (
        row_main[...] + rends[0] + rends[1],
        jnp.sum(cparts[...], axis=0) + jnp.sum(cends[0], axis=0) + jnp.sum(cends[1], axis=0),
    )
    lane = iota((16, 128), 1)
    spread = []
    for g in range(4):
        parts = [x if turn % 128 == 0 else pltpu.roll(x, turn % 128, 1) for x, turn in zip(grads, (-32 * g, 32 - 32 * g))]
        spread.append(jnp.where(lane < 32, parts[0], jnp.where(lane < 64, parts[1], 0.0)))
    turned[...] = jnp.concatenate(spread, axis=0)

    high, low = halves(turned[...])
    for half, ref in enumerate((el, eh)):
        part = dot_tn(high, ref[...]) + dot_tn(low, ref[...])
        for k in range(16):
            at = 4 * (k // 2) + 2 * half + k % 2
            x = part[8 * (k // 2) : 8 * (k // 2) + 8, 128 * (k % 2) : 128 * (k % 2) + 128]
            y = taps[8 * at : 8 * at + 8, :] if at < 12 else jnp.zeros((8, 128), F32)
            buf[at] = jnp.concatenate([x, y], axis=0).astype(BF16)

    for a, b, at in p.group1:
        put(buf.at[at], a, b, r1.at[k1], 11)
    pltpu.make_async_copy(buf.at[k1], r1.at[k1], recv.at[11]).start()

    for a, b, _ in p.line:
        put(turned.at[pl.ds(pl.multiple_of(8 * b, 8), 8)], a, b, gparts.at[c], 14)
    pltpu.make_async_copy(turned.at[pl.ds(pl.multiple_of(8 * c, 8), 8)], gparts.at[c], recv.at[14]).start()

    outs = [
        pltpu.make_async_copy(out_ref.at[:, 16 * q : 16 * q + 16, :], out_hbm.at[:, 16 * q : 16 * q + 16, :], stores.at[q])
        for q in range(4)
    ]
    convolve(r, c, 0, a3, tf, out_ref)
    outs[0].start()
    convolve(r, c, 1, a3, tf, out_ref)
    outs[1].start()
    wait_bytes(r1, recv.at[11])
    mid[...] = jnp.sum(r1[...].astype(F32), axis=0).astype(BF16)
    for a, b, _ in p.group2:
        put(mid, a, b, r2.at[k2], 12)
    pltpu.make_async_copy(mid, r2.at[k2], recv.at[12]).start()

    convolve(r, c, 2, a3, tf, out_ref)
    outs[2].start()
    convolve(r, c, 3, a3, tf, out_ref)
    outs[3].start()
    wait_bytes(r2, recv.at[12])
    fin[...] = jnp.sum(r2[...].astype(F32), axis=0).astype(BF16)
    for a, b, _ in p.group1:
        put(fin, a, b, r3.at[k1], 13)
    pltpu.make_async_copy(fin, r3.at[k1], recv.at[13]).start()

    wait_bytes(gparts, recv.at[14])
    high, low = halves(jnp.sum(gparts[...], axis=0))
    eg_ref[...] = dot(high, proj[...]) + dot(low, proj[...])
    outs.append(pltpu.make_async_copy(eg_ref, eg_hbm, stores.at[4]))
    outs[4].start()

    for copy in outs:
        copy.wait()
    wait_bytes(eb.at[0 : nc - 1], send.at[0])
    wait_bytes(quad.at[0 : per - 1], send.at[1])
    pl.when(row_after)(lambda: wait_bytes(rows8, send.at[2]))
    pl.when(row_before)(lambda: wait_bytes(rows8, send.at[3]))

    def sent_targets(cond, mine, eight, seven, sem):
        pl.when(cond & mine)(lambda: wait_bytes(seven, send.at[sem]))
        pl.when(cond & jnp.logical_not(mine))(lambda: wait_bytes(eight, send.at[sem]))

    sent_targets(col_after, rb + 1 == c, rows8, rows7, 4)
    sent_targets(col_before, rb - 1 == c, rows8, rows7, 5)
    sent_targets(rb >= 0, p.in_others, blocks, blocks.at[0 : nc - 1], 15)
    pl.when(p.in_others)(lambda: wait_bytes(cparts.at[0 : per - 1], send.at[6]))
    pl.when(jnp.logical_not(p.in_others))(lambda: wait_bytes(cparts, send.at[6]))
    pl.when(p.has_up)(lambda: wait_bytes(row_ends.at[0], send.at[7]))
    pl.when(p.has_down)(lambda: wait_bytes(row_ends.at[1], send.at[8]))
    pl.when(p.has_left)(lambda: wait_bytes(col_ends.at[0], send.at[9]))
    pl.when(p.has_right)(lambda: wait_bytes(col_ends.at[1], send.at[10]))
    wait_bytes(r1.at[0 : r1.shape[0] - 1], send.at[11])
    wait_bytes(r2.at[0 : r2.shape[0] - 1], send.at[12])
    wait_bytes(gparts.at[0 : nc - 1], send.at[14])

    wait_bytes(r3, recv.at[13])
    last = pltpu.make_async_copy(r3, sums_hbm, stores.at[5])
    last.start()
    wait_bytes(r3.at[0 : r3.shape[0] - 1], send.at[13])
    last.wait()


def finish_kernel(
    scale, sums_in, eg_in, pair_in, conv_out, left_out, right_out, eg_out, pair_out,
    sums_ref, eg_ref, held, conv_ref, left_ref, right_ref, loads, stores,
):
    def piece(k):
        return slice(8 * k, 8 * k + 8)

    ins = [pltpu.make_async_copy(sums_in, sums_ref, loads.at[0]), pltpu.make_async_copy(eg_in, eg_ref, loads.at[1])]
    ins += [pltpu.make_async_copy(pair_in.at[piece(k)], held.at[piece(k)], loads.at[2 + k]) for k in range(4)]
    outs = [
        pltpu.make_async_copy(conv_ref, conv_out, stores.at[0]),
        pltpu.make_async_copy(left_ref, left_out, stores.at[1]),
        pltpu.make_async_copy(right_ref, right_out, stores.at[2]),
        pltpu.make_async_copy(eg_ref, eg_out, stores.at[3]),
    ]
    outs += [pltpu.make_async_copy(held.at[piece(k)], pair_out.at[piece(k)], stores.at[4 + k]) for k in range(4)]
    for copy in ins:
        copy.start()
    ins[0].wait()
    for ref, first, at in ((left_ref, 0, 1), (right_ref, 16, 2)):
        for k in range(16):
            x = sums_ref[first + k].astype(F32)[0:8]
            ref[8 * (k // 4) : 8 * (k // 4) + 8, 128 * (k % 4) : 128 * (k % 4) + 128] = x * scale
        outs[at].start()
    ins[1].wait()
    outs[3].start()
    for k in range(4):
        ins[2 + k].wait()
        outs[4 + k].start()
    for k in range(9):
        q, at = divmod(k, 4)
        for part in range(4):
            x = sums_ref[4 * q + part].astype(F32)
            conv_ref[k, 8 * part : 8 * part + 8, :] = x[8:16, 32 * at : 32 * at + 32] * scale
    outs[0].start()
    for copy in outs:
        copy.wait()


def shards(nr, nc, embed, left_proj, right_proj, conv_w, cotangent):
    per = nr // nc
    pair_out, totals, embed_grad = pl.pallas_call(
        functools.partial(pair_kernel, nr, nc),
        out_shape=(
            jax.ShapeDtypeStruct((32, 64, 256), BF16),
            jax.ShapeDtypeStruct((32, 16, 128), BF16),
            jax.ShapeDtypeStruct((8, 512), F32),
        ),
        in_specs=[HBM] * 5,
        out_specs=(HBM,) * 3,
        scratch_shapes=LOCAL_SCRATCH
        + [
            pltpu.VMEM((32, 64, 256), BF16),
            pltpu.VMEM((8, 512), F32),
            pltpu.VMEM((416, 128), F32),
            pltpu.VMEM((8, 512), BF16),
            pltpu.VMEM((9, 32, 32), BF16),
            pltpu.VMEM((32, 64, 256), BF16),
            pltpu.VMEM((8, 128), F32),
            pltpu.VMEM((per, 8, 128), F32),
            pltpu.VMEM((128, 512), BF16),
            pltpu.VMEM((16, 256), BF16),
            pltpu.VMEM((nc, 16, 256), BF16),
            pltpu.VMEM((64, 256), BF16),
            pltpu.VMEM((64, 256), BF16),
            pltpu.VMEM((nc, per, 8, 128), F32),
            pltpu.VMEM((2, 8, 128), F32),
            pltpu.VMEM((2, 8, 128), F32),
            pltpu.VMEM((per, 16, 128), F32),
            pltpu.VMEM((2, per, 16, 128), F32),
            pltpu.VMEM((2, 16, 128), F32),
            pltpu.VMEM((64, 128), F32),
            pltpu.VMEM((nc, 8, 128), F32),
            pltpu.VMEM((32, 16, 128), BF16),
            pltpu.VMEM((32, 16, 128), BF16),
            pltpu.VMEM((8, 16, 128), BF16),
            pltpu.VMEM((32, 16, 128), BF16),
            pltpu.VMEM((16, 128), BF16),
            pltpu.VMEM((16, 128), BF16),
            pltpu.SemaphoreType.DMA((16,)),
            pltpu.SemaphoreType.DMA((16,)),
            pltpu.SemaphoreType.DMA((5,)),
            pltpu.SemaphoreType.DMA((6,)),
        ],
        compiler_params=pltpu.CompilerParams(
            collective_id=0, has_side_effects=True, vmem_limit_bytes=60 * 1024 * 1024
        ),
        name="pair_kernel",
    )(embed, left_proj.T, right_proj.T, conv_w, cotangent)
    conv_grad, left_t, right_t, embed_grad, pair_out = pl.pallas_call(
        functools.partial(finish_kernel, 32.0 / (8 * nr * nc)),
        out_shape=(
            jax.ShapeDtypeStruct((9, 32, 32), F32),
            jax.ShapeDtypeStruct((32, 512), F32),
            jax.ShapeDtypeStruct((32, 512), F32),
            jax.ShapeDtypeStruct((8, 512), F32),
            jax.ShapeDtypeStruct((32, 64, 256), BF16),
        ),
        in_specs=[HBM] * 3,
        out_specs=(HBM,) * 5,
        scratch_shapes=[
            pltpu.VMEM((32, 16, 128), BF16),
            pltpu.VMEM((8, 512), F32),
            pltpu.VMEM((32, 64, 256), BF16),
            pltpu.VMEM((9, 32, 32), F32),
            pltpu.VMEM((32, 512), F32),
            pltpu.VMEM((32, 512), F32),
            pltpu.SemaphoreType.DMA((6,)),
            pltpu.SemaphoreType.DMA((8,)),
        ],
        compiler_params=pltpu.CompilerParams(vmem_limit_bytes=60 * 1024 * 1024),
        name="finish",
    )(totals, embed_grad, pair_out)
    return pair_out, conv_grad, left_t.T, right_t.T, embed_grad


def solution(mesh):
    body = functools.partial(shards, mesh.shape["row"], mesh.shape["col"])
    in_specs = (P(("row", "col"), None), P(), P(), P(), P(None, "row", "col"))
    out_specs = (P(None, "row", "col"), P(), P(), P(), P(("row", "col"), None))
    return jax.shard_map(body, mesh=mesh, in_specs=in_specs, out_specs=out_specs, check_vma=False)
```

```python
import functools

import jax
import jax.numpy as jnp
from jax import lax
from jax.experimental import pallas as pl
from jax.experimental.pallas import tpu as pltpu
from jax.sharding import PartitionSpec as P

MESH = pl.DeviceIdType.MESH
OUTSIDE = -1e30
LOG2E = 1.4426950408889634
LN2 = 0.6931471805599453
F32 = jnp.float32
BF16 = jnp.bfloat16
VMEM = pl.BlockSpec(memory_space=pltpu.VMEM)
HBM = pl.BlockSpec(memory_space=pltpu.HBM)


def iota(shape, dim):
    return lax.broadcasted_iota(jnp.int32, shape, dim)


def one_hot(cond):
    return jnp.where(cond, 1.0, 0.0).astype(BF16)


def dot(a, b):
    return jnp.dot(a, b, preferred_element_type=F32)


def dot_nt(a, b):
    return lax.dot_general(a, b, (((1,), (1,)), ((), ())), preferred_element_type=F32)


def dot_tn(a, b):
    return lax.dot_general(a, b, (((0,), (0,)), ((), ())), preferred_element_type=F32)


def halves(x):
    high = x.astype(BF16)
    return high, (x - high.astype(F32)).astype(BF16)


def loop(n, f):
    def body(k, _):
        f(k)
        return 0

    lax.fori_loop(0, n, body, 0)


def lanes(h):
    return pl.ds(pl.multiple_of(h * 256, 256), 256)


def wait_bytes(ref, sem):
    pltpu.make_async_copy(ref, ref, sem).wait()


def softplus_and_slope(y):
    t = jnp.exp2(-jnp.abs(y))
    u = 1.0 + t
    inv = pltpu.reciprocal(u, full_range=False)
    log = jnp.where(t < 2.0**-11, t * LOG2E, jnp.log2(u))
    return LN2 * (jnp.maximum(y, 0.0) + log), jnp.where(y >= 0, inv, t * inv)


def build_taps(w_ref, tf):
    spread = one_hot((iota((256, 32), 0) >> 3) == iota((256, 32), 1))
    widen = one_hot((iota((32, 256), 1) >> 3) == iota((32, 256), 0))
    s0, s1 = iota((256, 256), 0) & 7, iota((256, 256), 1) & 7
    same, above, below = s1 == s0, s1 == s0 + 4, s1 == s0 - 4
    for b in range(3):
        x = [dot(spread, dot(w_ref[3 * a + b], widen).astype(BF16)) for a in range(3)]
        tf[:, 256 * b : 256 * b + 256] = jnp.where(same, x[0], jnp.where(above, x[1], 0.0)).astype(BF16)
        tf[:, 768 + 256 * b : 1024 + 256 * b] = jnp.where(same, x[2], jnp.where(below, x[1], 0.0)).astype(BF16)


def mask_cotangent(r, c, cot_ref, move, mall, mt):
    for k in range(4):
        x = cot_ref[:, 16 * k : 16 * k + 16, :].astype(F32)
        row = r * 64 + 16 * k + iota((16, 256), 0)
        x = jnp.where((c * 256 + iota((16, 256), 1) >= row)[None], x, 0.0)
        for half in range(2):
            mall[:, lanes(2 * k + half)] = x[:, 8 * half : 8 * half + 8].reshape(256, 256).astype(BF16)
    for b in range(3):
        move[272 * b : 272 * b + 272, :] = one_hot(iota((272, 256), 0) - 4 * b == iota((272, 256), 1))
        mt[0, :, 256 * b : 256 * b + 256] = jnp.zeros((272, 256), BF16)
        mt[9, :, 256 * b : 256 * b + 256] = jnp.zeros((272, 256), BF16)

    def body(g):
        moved = dot_nt(move[...], mall[:, lanes(g)]).astype(BF16)
        for b in range(3):
            mt[g + 1, :, 256 * b : 256 * b + 256] = moved[272 * b : 272 * b + 272]

    loop(8, body)


def input_gradient(mt, tf, z, groups):
    def body(h, _):
        z[h] = group_gradient(mt, tf, h)
        return 0

    lax.fori_loop(*groups, body, 0)


def group_gradient(mt, tf, h):
    left = jnp.concatenate([mt[h], mt[h + 1]], axis=1)
    right = jnp.concatenate(
        [tf[:, 768 * (1 - u) + 256 * b : 768 * (1 - u) + 256 * b + 256] for u in range(2) for b in range(3)], axis=0
    )
    return dot(left, right)


def features(rows, cols, rowf, colf):
    k, n = iota((128, 256), 0), iota((128, 256), 1) >> 3
    colf[...] = dot(cols, one_hot(k == n + 32)) * LOG2E
    x = dot(rows, one_hot(k == n))
    x = jnp.where((iota((128, 256), 0) & 7) == (iota((128, 256), 1) & 7), x, 0.0).astype(BF16)
    rowf[...] = dot(one_hot((iota((16, 128), 1) >> 3) == iota((16, 128), 0)), x) * LOG2E


def elementwise(rowf, colf, z, act, cacc, rsum):
    rsum[...] = jnp.zeros_like(rsum)

    def body(step):
        parts = [pl.ds(pl.multiple_of(24 * step + 8 * part, 8), 8) for part in range(3)]
        totals = [jnp.zeros((8, 256), F32)] * 3
        for h in range(9):
            left = rowf[h : h + 1, :]
            row = jnp.zeros((8, 256), F32)
            for k, rows in enumerate(parts):
                value, slope = softplus_and_slope(colf[rows, :] + left)
                act[h, rows, :] = value
                p = z[h, rows, :] * slope
                totals[k] += p
                row += p
            rsum[8 * h : 8 * h + 8, :] += row
        for k, rows in enumerate(parts):
            cacc[rows, :] = totals[k]

    loop(11, body)


def sums(cacc, rsum, cols, col_ends, row_main, row_ends):
    k, n = iota((256, 128), 0) >> 3, iota((256, 128), 1)
    picks = [one_hot(k + 32 * g == n) for g in range(4)]
    pick = jnp.concatenate(picks, axis=0)
    x = [
        jnp.concatenate([cacc[4 + 64 * q + 16 * g : 20 + 64 * q + 16 * g, :] for g in range(4)], axis=1) for q in range(4)
    ]
    high, low = halves(jnp.concatenate(x, axis=0))
    x = dot(high, pick) + dot(low, pick)
    for q in range(4):
        cols[q] = x[16 * q : 16 * q + 16]
    sub, lane = iota((16, 128), 0), iota((16, 128), 1)
    ends = jnp.concatenate([cacc[0:8, :], cacc[256:264, :]], axis=0)
    high, low = halves(ends)
    first = dot(high, picks[3]) + dot(low, picks[3])
    second = dot(high, picks[0]) + dot(low, picks[0])
    col_ends[0] = jnp.where(sub >= 12, pltpu.roll(first, 12, 0), 0.0)
    col_ends[1] = jnp.where(sub < 4, pltpu.roll(second, 4, 0), 0.0)
    x = jnp.concatenate([rsum[...], jnp.zeros((56, 256), F32)], axis=0)
    by_group = one_hot((iota((80, 128), 0) >> 3) == (iota((80, 128), 1) >> 3))
    high, low = halves(x)
    x = dot(by_group, high) + dot(by_group, low)
    x = jnp.where((iota((80, 256), 0) & 7) == (iota((80, 256), 1) & 7), x, 0.0)
    high, low = halves(jnp.concatenate([x[4 + 16 * g : 20 + 16 * g] for g in range(4)], axis=1))
    row_main[...] = dot(high, pick) + dot(low, pick)
    ends = jnp.concatenate([x[0:8], x[64:72]], axis=0)
    high, low = halves(ends)
    first = dot(high, picks[3]) + dot(low, picks[3])
    second = dot(high, picks[0]) + dot(low, picks[0])
    row_ends[0] = jnp.where(sub >= 12, pltpu.roll(first, 12, 0), 0.0)
    row_ends[1] = jnp.where(sub < 4, pltpu.roll(second, 4, 0), 0.0)


def build_windows(act, a3):
    def body(h):
        at = pl.ds(pl.multiple_of(256 * h, 256), 256)
        for b in range(3):
            a3[at, 256 * b : 256 * b + 256] = act[h, 4 * b : 4 * b + 256, :].astype(BF16)

    loop(9, body)


def convolve(r, c, k, a3, tf, out_ref):
    parts = []
    for g in (2 * k, 2 * k + 1):
        both = jnp.concatenate([a3[256 * (g + u) : 256 * (g + u) + 256, :] for u in range(2)], axis=1)
        parts.append(dot_nt(tf[...], both).reshape(32, 8, 256))
    y = jnp.concatenate(parts, axis=1)
    row = r * 64 + 16 * k + iota((16, 256), 0)
    col = c * 256 + iota((16, 256), 1)
    out_ref[:, 16 * k : 16 * k + 16, :] = jnp.where((col >= row)[None], y, 0.0).astype(BF16)


def tap_gradient(mall, a3, gram, taps):
    for u in range(2):
        x = dot(mall[...], a3[256 * u : 256 * u + 2048, :])
        for k in range(6):
            gram[6 * u + k] = x[:, 128 * k : 128 * k + 128]
    lane = iota((32, 128), 1)

    def along(b, k, sources):
        total = jnp.zeros((32, 128), F32)
        for at, (s, u) in enumerate(sources):
            total = jnp.where((lane & 7) == at, gram[6 * u + 2 * b + k, pl.ds(s, 32, stride=8), :], total)
        return total

    sources = (
        [(s, 0) for s in range(8)],
        [((s + 4) % 8, 1 - s // 4) for s in range(8)],
        [(s, 1) for s in range(8)],
    )
    x = [jnp.concatenate([along(b, k, sources[a]) for k in range(2)], axis=1) for a in range(3) for b in range(3)]
    y = dot(jnp.concatenate(halves(jnp.concatenate(x, axis=0)), axis=0), one_hot((iota((256, 128), 0) >> 3) == iota((256, 128), 1)))
    y = y[0:288] + y[288:576]
    for q in range(3):
        total = jnp.zeros((32, 128), F32)
        for k in range(min(4, 9 - 4 * q)):
            tap = y[32 * (4 * q + k) : 32 * (4 * q + k) + 32]
            total = jnp.where((lane >> 5) == k, pltpu.roll(tap, 32 * k, 1) if k else tap, total)
        taps[32 * q : 32 * q + 32, :] = total


LOCAL_SCRATCH = [
    pltpu.VMEM((16, 256), F32),
    pltpu.VMEM((272, 256), F32),
    pltpu.VMEM((96, 128), F32),
    pltpu.VMEM((256, 2048), BF16),
    pltpu.VMEM((10, 272, 768), BF16),
    pltpu.VMEM((9, 272, 256), F32),
    pltpu.VMEM((2304, 768), BF16),
    pltpu.VMEM((9, 272, 256), F32),
    pltpu.VMEM((256, 1536), BF16),
    pltpu.VMEM((816, 256), BF16),
    pltpu.VMEM((12, 256, 128), F32),
    pltpu.VMEM((272, 256), F32),
    pltpu.VMEM((72, 256), F32),
    pltpu.VMEM((4, 16, 128), F32),
    pltpu.VMEM((2, 16, 128), F32),
    pltpu.VMEM((16, 128), F32),
    pltpu.VMEM((2, 16, 128), F32),
]


class Place:
    def __init__(self, nr, nc):
        r, c = lax.axis_index("row"), lax.axis_index("col")
        self.r, self.c, self.nr, self.nc = r, c, nr, nc
        self.per = nr // nc
        self.rb, self.rm = lax.div(r, self.per), lax.rem(r, self.per)
        _, self.quad = self.group(((r, 1, 0), (r, 2, 0)))
        _, self.line = self.group(((c, 1, 1), (c, 2, 1), (c, 4, 1)))
        self.k1, self.group1 = self.group(((r, 1, 0), (r, 8, 0), (r, 16, 0), (c, 2, 1), (c, 4, 1)))
        self.k2, self.group2 = self.group(((r, 2, 0), (r, 4, 0), (c, 1, 1)))
        self.has_up, self.has_down = r > 0, r < nr - 1
        self.has_left, self.has_right = c > 0, c < nc - 1
        self.ends_block = (self.rm == self.per - 1) & (self.rb < nc - 1)
        self.starts_block = (self.rm == 0) & (self.rb > 0)
        self.in_others = self.rb == c

    def group(self, bits):
        number, turns = 0, []
        for k, (x, weight, is_col) in enumerate(bits):
            bit = lax.rem(lax.div(x, weight), 2)
            number = number + bit * (1 << k)
            sign = 1 - 2 * bit
            turns.append((sign * weight, is_col, sign * (1 << k)))
        members = [(self.r, self.c, number)]
        for move, is_col, step in turns:
            members += [
                (a, b + move, n + step) if is_col else (a + move, b, n + step) for a, b, n in members
            ]
        return number, members[:0:-1]

    def other(self, k):
        return self.per * self.c + k, self.rb

    def targets(self, col):
        return [(lax.rem(self.r + self.per * k, self.nr), col) for k in range(self.nr // self.per)]

    def greet(self):
        r, c, nc, per, rb, rm = self.r, self.c, self.nc, self.per, self.rb, self.rm
        barrier = pltpu.get_barrier_semaphore()

        def signal(a, b):
            pl.semaphore_signal(barrier, inc=1, device_id=(a, b), device_id_type=MESH)

        def signal_all(col):
            for k in range(per):
                signal(per * c + k, col)

        is_first, is_last = c == 0, c == nc - 1
        before_is_me = is_last & (rb == nc - 2)
        after_is_me = is_first & (rb == 1)
        for a, b, _ in self.quad + self.line:
            signal(a, b)
        pl.when(jnp.logical_not(self.in_others))(lambda: signal(per * c + rm, c))
        for _, b, _ in self.line:
            signal(per * c + rm, b)
        pl.when(self.has_up)(lambda: signal(r - 1, nc - 1))
        pl.when(self.has_down)(lambda: signal(r + 1, 0))
        pl.when(self.has_left & jnp.logical_not(before_is_me))(lambda: signal(per * (c - 1) + rm, nc - 1))
        pl.when(self.has_right & jnp.logical_not(after_is_me))(lambda: signal(per * (c + 1) + rm, 0))
        pl.when(jnp.logical_not(self.in_others))(lambda: signal(per * c + rm, rb))
        for a, _, _ in self.quad:
            signal(per * (c - rb) + a, rb)
        pl.when(self.has_up)(lambda: signal(r - 1, c))
        pl.when(self.has_down)(lambda: signal(r + 1, c))
        pl.when(self.ends_block)(lambda: signal_all(rb + 1))
        pl.when(self.starts_block)(lambda: signal_all(rb - 1))
        for a, b, _ in self.group1 + self.group2:
            signal(a, b)
        n = len(self.quad + self.line + self.group1 + self.group2) + nc + per
        up, down = self.has_up, self.has_down
        for cond, m in (
            (self.in_others, -2), (is_last & down, nc), (is_first & up, nc),
            (is_last & (rb < nc - 1), nc), (before_is_me, -1), (is_first & (rb > 0), nc), (after_is_me, -1),
            (up, 1), (down, 1), (self.has_left, 1), (self.has_right, 1),
        ):
            n = n + jnp.where(cond, m, 0)
        return n

    def senders(self, send, recv):
        def put(src, dst_r, dst_c, dst, sem):
            pltpu.make_async_remote_copy(
                src, dst, send.at[sem], recv.at[sem], device_id=(dst_r, dst_c), device_id_type=MESH
            ).start()

        def put_other(src, k, dst, sem):
            a, b = self.other(k)
            mine = (a == self.r) & (b == self.c)
            pl.when(mine)(lambda: pltpu.make_async_copy(src, dst, recv.at[sem]).start())
            pl.when(jnp.logical_not(mine))(lambda: put(src, a, b, dst, sem))

        return put, put_other


def pair_kernel(
    nr, nc, e_hbm, lpt_hbm, rpt_hbm, w_hbm, cot_hbm,
    out_hbm, sums_hbm, eg_hbm,
    rowf, colf, taps, mall, mt, act, a3, z, tf, move, gram, cacc, rsum, cols, col_ends, row_main, row_ends,
    out_ref, eg_ref, feats, e_ref, w_ref, cot_ref, own, quad, proj, es, eb, el, eh, blocks, row_feats, col_feats,
    cparts, cends, rends, turned, gparts, buf, r1, r2, mid, fin, recv, send, loads, stores,
):
    ins = ((e_hbm, e_ref), (w_hbm, w_ref), (lpt_hbm, proj.at[0:32]), (rpt_hbm, proj.at[32:64]), (cot_hbm, cot_ref))
    ins = [pltpu.make_async_copy(src, dst, loads.at[k]) for k, (src, dst) in enumerate(ins)]
    for copy in ins:
        copy.start()
    p = Place(nr, nc)
    r, c, per, rb, rm, k1, k2 = p.r, p.c, p.per, p.rb, p.rm, p.k1, p.k2
    greeted = p.greet()
    put, put_other = p.senders(send, recv)
    rows8, rows7 = gparts, gparts.at[0 : nc - 1]

    proj[64:128, :] = jnp.zeros((64, 512), BF16)
    ins[0].wait()
    e = e_ref[...].astype(F32)
    es[...] = jnp.concatenate([e[:, 0:256], e[:, 256:512]], axis=0).astype(BF16)
    ins[2].wait()
    ins[3].wait()
    own[...] = dot_nt(e_ref[...], proj[...]).astype(BF16).astype(F32)
    ins[1].wait()
    build_taps(w_ref, tf)
    ins[4].wait()
    mask_cotangent(r, c, cot_ref, move, mall, mt)
    pl.semaphore_wait(pltpu.get_barrier_semaphore(), greeted)

    for a, b, _ in p.quad:
        put(own, a, b, quad.at[rm], 1)
    pltpu.make_async_copy(own, quad.at[rm], recv.at[1]).start()

    def put_line(row, dst, sem):
        for k in range(nc):
            put(own, row, k, dst, sem)

    is_first, is_last = c == 0, c == nc - 1
    row_after, row_before = is_last & p.has_down, is_first & p.has_up
    pl.when(row_after)(lambda: put_line(r + 1, row_feats.at[0], 2))
    pl.when(row_before)(lambda: put_line(r - 1, row_feats.at[1], 3))
    for a, b, _ in p.line:
        put(es, a, b, eb.at[c], 0)
    pltpu.make_async_copy(es, eb.at[c], recv.at[0]).start()

    def put_targets(src, col, dst, sem):
        first, *rest = p.targets(col)
        mine = c == col
        pl.when(mine)(lambda: pltpu.make_async_copy(src, dst, recv.at[sem]).start())
        pl.when(jnp.logical_not(mine))(lambda: put(src, *first, dst, sem))
        for a, b in rest:
            put(src, a, b, dst, sem)

    col_after, col_before = is_last & (rb < nc - 1), is_first & (rb > 0)
    input_gradient(mt, tf, z, (0, 5))
    wait_bytes(quad, recv.at[1])
    put_targets(quad, rb, blocks.at[c], 15)
    pl.when(col_after)(lambda: put_targets(quad.at[per - 1], rb + 1, col_feats.at[0], 4))
    pl.when(col_before)(lambda: put_targets(quad.at[0], rb - 1, col_feats.at[1], 5))
    input_gradient(mt, tf, z, (5, 9))

    wait_bytes(eb, recv.at[0])
    e = eb[...].astype(F32)
    el[...] = e[:, 0:8].reshape(64, 256).astype(BF16)
    eh[...] = e[:, 8:16].reshape(64, 256).astype(BF16)
    feats[8:72, :] = dot_nt(el[...], proj[:, 0:256]) + dot_nt(eh[...], proj[:, 256:512])

    def arrive(cond, ref, sem):
        pl.when(cond)(lambda: wait_bytes(ref, sem))
        pl.when(jnp.logical_not(cond))(lambda: ref.__setitem__(..., jnp.full(ref.shape, OUTSIDE, F32)))

    arrive(p.has_up, row_feats.at[0], recv.at[2])
    arrive(p.has_down, row_feats.at[1], recv.at[3])
    arrive(p.has_left, col_feats.at[0], recv.at[4])
    arrive(p.has_right, col_feats.at[1], recv.at[5])
    wait_bytes(blocks, recv.at[15])
    feats[0:8, :] = row_feats[0]
    feats[72:80, :] = row_feats[1]
    feats[80:136, :] = jnp.zeros((56, 128), F32)
    feats[136:144, :] = col_feats[0]
    for k in range(per):
        for q in range(nc):
            at = 144 + 8 * (nc * k + q)
            feats[at : at + 8, :] = blocks[q, k]
    feats[400:408, :] = col_feats[1]
    feats[408:416, :] = jnp.zeros((8, 128), F32)
    features(feats[4:132, :].astype(BF16), feats[140:412, :].astype(BF16), rowf, colf)
    elementwise(rowf, colf, z, act, cacc, rsum)
    sums(cacc, rsum, cols, col_ends, row_main, row_ends)

    for k in range(per):
        put_other(cols.at[k], k, cparts.at[rm], 6)
    pl.when(p.has_up)(lambda: put(row_ends.at[0], r - 1, c, rends.at[0], 7))
    pl.when(p.has_down)(lambda: put(row_ends.at[1], r + 1, c, rends.at[1], 8))
    pl.when(p.has_left)(lambda: put(col_ends.at[0], per * c - 1, rb, cends.at[0, rm], 9))
    pl.when(p.has_right)(lambda: put(col_ends.at[1], per * c + per, rb, cends.at[1, rm], 10))

    build_windows(act, a3)
    tap_gradient(mall, a3, gram, taps)
    def gather_sum(cond, ref, sem):
        pl.when(cond)(lambda: wait_bytes(ref, sem))
        pl.when(jnp.logical_not(cond))(lambda: ref.__setitem__(..., jnp.zeros(ref.shape, F32)))

    gather_sum(p.has_down, rends.at[0], recv.at[7])
    gather_sum(p.has_up, rends.at[1], recv.at[8])
    gather_sum(p.ends_block, cends.at[0], recv.at[9])
    gather_sum(p.starts_block, cends.at[1], recv.at[10])
    wait_bytes(cparts, recv.at[6])
    grads = (
        row_main[...] + rends[0] + rends[1],
        jnp.sum(cparts[...], axis=0) + jnp.sum(cends[0], axis=0) + jnp.sum(cends[1], axis=0),
    )
    lane = iota((16, 128), 1)
    spread = []
    for g in range(4):
        parts = [x if turn % 128 == 0 else pltpu.roll(x, turn % 128, 1) for x, turn in zip(grads, (-32 * g, 32 - 32 * g))]
        spread.append(jnp.where(lane < 32, parts[0], jnp.where(lane < 64, parts[1], 0.0)))
    turned[...] = jnp.concatenate(spread, axis=0)

    high, low = halves(turned[...])
    for half, ref in enumerate((el, eh)):
        part = dot_tn(high, ref[...]) + dot_tn(low, ref[...])
        for k in range(16):
            at = 4 * (k // 2) + 2 * half + k % 2
            x = part[8 * (k // 2) : 8 * (k // 2) + 8, 128 * (k % 2) : 128 * (k % 2) + 128]
            y = taps[8 * at : 8 * at + 8, :] if at < 12 else jnp.zeros((8, 128), F32)
            buf[at] = jnp.concatenate([x, y], axis=0).astype(BF16)

    for a, b, at in p.group1:
        put(buf.at[at], a, b, r1.at[k1], 11)
    pltpu.make_async_copy(buf.at[k1], r1.at[k1], recv.at[11]).start()

    for a, b, _ in p.line:
        put(turned.at[pl.ds(pl.multiple_of(8 * b, 8), 8)], a, b, gparts.at[c], 14)
    pltpu.make_async_copy(turned.at[pl.ds(pl.multiple_of(8 * c, 8), 8)], gparts.at[c], recv.at[14]).start()

    outs = [
        pltpu.make_async_copy(out_ref.at[:, 16 * q : 16 * q + 16, :], out_hbm.at[:, 16 * q : 16 * q + 16, :], stores.at[q])
        for q in range(4)
    ]
    convolve(r, c, 0, a3, tf, out_ref)
    outs[0].start()
    convolve(r, c, 1, a3, tf, out_ref)
    outs[1].start()
    wait_bytes(r1, recv.at[11])
    mid[...] = jnp.sum(r1[...].astype(F32), axis=0).astype(BF16)
    for a, b, _ in p.group2:
        put(mid, a, b, r2.at[k2], 12)
    pltpu.make_async_copy(mid, r2.at[k2], recv.at[12]).start()

    convolve(r, c, 2, a3, tf, out_ref)
    outs[2].start()
    convolve(r, c, 3, a3, tf, out_ref)
    outs[3].start()
    wait_bytes(r2, recv.at[12])
    fin[...] = jnp.sum(r2[...].astype(F32), axis=0).astype(BF16)
    for a, b, _ in p.group1:
        put(fin, a, b, sums_hbm.at[k1], 13)
    pltpu.make_async_copy(fin, sums_hbm.at[k1], recv.at[13]).start()

    wait_bytes(gparts, recv.at[14])
    high, low = halves(jnp.sum(gparts[...], axis=0))
    eg_ref[...] = dot(high, proj[...]) + dot(low, proj[...])
    outs.append(pltpu.make_async_copy(eg_ref, eg_hbm, stores.at[4]))
    outs[4].start()

    for copy in outs:
        copy.wait()
    wait_bytes(eb.at[0 : nc - 1], send.at[0])
    wait_bytes(quad.at[0 : per - 1], send.at[1])
    pl.when(row_after)(lambda: wait_bytes(rows8, send.at[2]))
    pl.when(row_before)(lambda: wait_bytes(rows8, send.at[3]))

    def sent_targets(cond, mine, eight, seven, sem):
        pl.when(cond & mine)(lambda: wait_bytes(seven, send.at[sem]))
        pl.when(cond & jnp.logical_not(mine))(lambda: wait_bytes(eight, send.at[sem]))

    sent_targets(col_after, rb + 1 == c, rows8, rows7, 4)
    sent_targets(col_before, rb - 1 == c, rows8, rows7, 5)
    sent_targets(rb >= 0, p.in_others, blocks, blocks.at[0 : nc - 1], 15)
    pl.when(p.in_others)(lambda: wait_bytes(cparts.at[0 : per - 1], send.at[6]))
    pl.when(jnp.logical_not(p.in_others))(lambda: wait_bytes(cparts, send.at[6]))
    pl.when(p.has_up)(lambda: wait_bytes(row_ends.at[0], send.at[7]))
    pl.when(p.has_down)(lambda: wait_bytes(row_ends.at[1], send.at[8]))
    pl.when(p.has_left)(lambda: wait_bytes(col_ends.at[0], send.at[9]))
    pl.when(p.has_right)(lambda: wait_bytes(col_ends.at[1], send.at[10]))
    wait_bytes(r1.at[0 : r1.shape[0] - 1], send.at[11])
    wait_bytes(r2.at[0 : r2.shape[0] - 1], send.at[12])
    wait_bytes(gparts.at[0 : nc - 1], send.at[14])

    wait_bytes(r1.at[0 : r1.shape[0] - 1], send.at[13])
    wait_bytes(sums_hbm, recv.at[13])


def finish_kernel(
    scale, sums_in, eg_in, pair_in, conv_out, left_out, right_out, eg_out, pair_out,
    sums_ref, eg_ref, held, conv_ref, left_ref, right_ref, loads, stores,
):
    def piece(k):
        return slice(8 * k, 8 * k + 8)

    ins = [pltpu.make_async_copy(sums_in, sums_ref, loads.at[0]), pltpu.make_async_copy(eg_in, eg_ref, loads.at[1])]
    ins += [pltpu.make_async_copy(pair_in.at[piece(k)], held.at[piece(k)], loads.at[2 + k]) for k in range(4)]
    outs = [
        pltpu.make_async_copy(conv_ref, conv_out, stores.at[0]),
        pltpu.make_async_copy(left_ref, left_out, stores.at[1]),
        pltpu.make_async_copy(right_ref, right_out, stores.at[2]),
        pltpu.make_async_copy(eg_ref, eg_out, stores.at[3]),
    ]
    outs += [pltpu.make_async_copy(held.at[piece(k)], pair_out.at[piece(k)], stores.at[4 + k]) for k in range(4)]
    for copy in ins:
        copy.start()
    ins[0].wait()
    for ref, first, at in ((left_ref, 0, 1), (right_ref, 16, 2)):
        for k in range(16):
            x = sums_ref[first + k].astype(F32)[0:8]
            ref[8 * (k // 4) : 8 * (k // 4) + 8, 128 * (k % 4) : 128 * (k % 4) + 128] = x * scale
        outs[at].start()
    ins[1].wait()
    outs[3].start()
    for k in range(4):
        ins[2 + k].wait()
        outs[4 + k].start()
    for k in range(9):
        q, at = divmod(k, 4)
        for part in range(4):
            x = sums_ref[4 * q + part].astype(F32)
            conv_ref[k, 8 * part : 8 * part + 8, :] = x[8:16, 32 * at : 32 * at + 32] * scale
    outs[0].start()
    for copy in outs:
        copy.wait()


def shards(nr, nc, embed, left_proj, right_proj, conv_w, cotangent):
    per = nr // nc
    pair_out, totals, embed_grad = pl.pallas_call(
        functools.partial(pair_kernel, nr, nc),
        out_shape=(
            jax.ShapeDtypeStruct((32, 64, 256), BF16),
            jax.ShapeDtypeStruct((32, 16, 128), BF16),
            jax.ShapeDtypeStruct((8, 512), F32),
        ),
        in_specs=[HBM] * 5,
        out_specs=(HBM,) * 3,
        scratch_shapes=LOCAL_SCRATCH
        + [
            pltpu.VMEM((32, 64, 256), BF16),
            pltpu.VMEM((8, 512), F32),
            pltpu.VMEM((416, 128), F32),
            pltpu.VMEM((8, 512), BF16),
            pltpu.VMEM((9, 32, 32), BF16),
            pltpu.VMEM((32, 64, 256), BF16),
            pltpu.VMEM((8, 128), F32),
            pltpu.VMEM((per, 8, 128), F32),
            pltpu.VMEM((128, 512), BF16),
            pltpu.VMEM((16, 256), BF16),
            pltpu.VMEM((nc, 16, 256), BF16),
            pltpu.VMEM((64, 256), BF16),
            pltpu.VMEM((64, 256), BF16),
            pltpu.VMEM((nc, per, 8, 128), F32),
            pltpu.VMEM((2, 8, 128), F32),
            pltpu.VMEM((2, 8, 128), F32),
            pltpu.VMEM((per, 16, 128), F32),
            pltpu.VMEM((2, per, 16, 128), F32),
            pltpu.VMEM((2, 16, 128), F32),
            pltpu.VMEM((64, 128), F32),
            pltpu.VMEM((nc, 8, 128), F32),
            pltpu.VMEM((32, 16, 128), BF16),
            pltpu.VMEM((32, 16, 128), BF16),
            pltpu.VMEM((8, 16, 128), BF16),
            pltpu.VMEM((16, 128), BF16),
            pltpu.VMEM((16, 128), BF16),
            pltpu.SemaphoreType.DMA((16,)),
            pltpu.SemaphoreType.DMA((16,)),
            pltpu.SemaphoreType.DMA((5,)),
            pltpu.SemaphoreType.DMA((6,)),
        ],
        compiler_params=pltpu.CompilerParams(
            collective_id=0, has_side_effects=True, vmem_limit_bytes=60 * 1024 * 1024
        ),
        name="pair_kernel",
    )(embed, left_proj.T, right_proj.T, conv_w, cotangent)
    conv_grad, left_t, right_t, embed_grad, pair_out = pl.pallas_call(
        functools.partial(finish_kernel, 32.0 / (8 * nr * nc)),
        out_shape=(
            jax.ShapeDtypeStruct((9, 32, 32), F32),
            jax.ShapeDtypeStruct((32, 512), F32),
            jax.ShapeDtypeStruct((32, 512), F32),
            jax.ShapeDtypeStruct((8, 512), F32),
            jax.ShapeDtypeStruct((32, 64, 256), BF16),
        ),
        in_specs=[HBM] * 3,
        out_specs=(HBM,) * 5,
        scratch_shapes=[
            pltpu.VMEM((32, 16, 128), BF16),
            pltpu.VMEM((8, 512), F32),
            pltpu.VMEM((32, 64, 256), BF16),
            pltpu.VMEM((9, 32, 32), F32),
            pltpu.VMEM((32, 512), F32),
            pltpu.VMEM((32, 512), F32),
            pltpu.SemaphoreType.DMA((6,)),
            pltpu.SemaphoreType.DMA((8,)),
        ],
        compiler_params=pltpu.CompilerParams(vmem_limit_bytes=60 * 1024 * 1024),
        name="finish",
    )(totals, embed_grad, pair_out)
    return pair_out, conv_grad, left_t.T, right_t.T, embed_grad


def solution(mesh):
    body = functools.partial(shards, mesh.shape["row"], mesh.shape["col"])
    in_specs = (P(("row", "col"), None), P(), P(), P(), P(None, "row", "col"))
    out_specs = (P(None, "row", "col"), P(), P(), P(), P(("row", "col"), None))
    return jax.shard_map(body, mesh=mesh, in_specs=in_specs, out_specs=out_specs, check_vma=False)
```

```python
import functools

import jax
import jax.numpy as jnp
from jax import lax
from jax.experimental import pallas as pl
from jax.experimental.pallas import tpu as pltpu
from jax.sharding import PartitionSpec as P

MESH = pl.DeviceIdType.MESH
OUTSIDE = -1e30
LOG2E = 1.4426950408889634
LN2 = 0.6931471805599453
F32 = jnp.float32
BF16 = jnp.bfloat16
VMEM = pl.BlockSpec(memory_space=pltpu.VMEM)
HBM = pl.BlockSpec(memory_space=pltpu.HBM)


def iota(shape, dim):
    return lax.broadcasted_iota(jnp.int32, shape, dim)


def one_hot(cond):
    return jnp.where(cond, 1.0, 0.0).astype(BF16)


def dot(a, b):
    return jnp.dot(a, b, preferred_element_type=F32)


def dot_nt(a, b):
    return lax.dot_general(a, b, (((1,), (1,)), ((), ())), preferred_element_type=F32)


def dot_tn(a, b):
    return lax.dot_general(a, b, (((0,), (0,)), ((), ())), preferred_element_type=F32)


def halves(x):
    high = x.astype(BF16)
    return high, (x - high.astype(F32)).astype(BF16)


def loop(n, f):
    def body(k, _):
        f(k)
        return 0

    lax.fori_loop(0, n, body, 0)


def lanes(h):
    return pl.ds(pl.multiple_of(h * 256, 256), 256)


def wait_bytes(ref, sem):
    pltpu.make_async_copy(ref, ref, sem).wait()


def softplus_and_slope(y):
    t = jnp.exp2(-jnp.abs(y))
    u = 1.0 + t
    inv = pltpu.reciprocal(u, full_range=False)
    log = jnp.where(t < 2.0**-11, t * LOG2E, jnp.log2(u))
    return LN2 * (jnp.maximum(y, 0.0) + log), jnp.where(y >= 0, inv, t * inv)


def build_taps(w_ref, tf):
    spread = one_hot((iota((256, 32), 0) >> 3) == iota((256, 32), 1))
    widen = one_hot((iota((32, 256), 1) >> 3) == iota((32, 256), 0))
    s0, s1 = iota((256, 256), 0) & 7, iota((256, 256), 1) & 7
    same, above, below = s1 == s0, s1 == s0 + 4, s1 == s0 - 4
    for b in range(3):
        x = [dot(spread, dot(w_ref[3 * a + b], widen).astype(BF16)) for a in range(3)]
        tf[:, 256 * b : 256 * b + 256] = jnp.where(same, x[0], jnp.where(above, x[1], 0.0)).astype(BF16)
        tf[:, 768 + 256 * b : 1024 + 256 * b] = jnp.where(same, x[2], jnp.where(below, x[1], 0.0)).astype(BF16)


def mask_cotangent(r, c, cot_ref, move, mall, mt):
    for k in range(4):
        x = cot_ref[:, 16 * k : 16 * k + 16, :].astype(F32)
        row = r * 64 + 16 * k + iota((16, 256), 0)
        x = jnp.where((c * 256 + iota((16, 256), 1) >= row)[None], x, 0.0)
        for half in range(2):
            mall[:, lanes(2 * k + half)] = x[:, 8 * half : 8 * half + 8].reshape(256, 256).astype(BF16)
    for b in range(3):
        move[272 * b : 272 * b + 272, :] = one_hot(iota((272, 256), 0) - 4 * b == iota((272, 256), 1))
        mt[0, :, 256 * b : 256 * b + 256] = jnp.zeros((272, 256), BF16)
        mt[9, :, 256 * b : 256 * b + 256] = jnp.zeros((272, 256), BF16)

    def body(g):
        moved = dot_nt(move[...], mall[:, lanes(g)]).astype(BF16)
        for b in range(3):
            mt[g + 1, :, 256 * b : 256 * b + 256] = moved[272 * b : 272 * b + 272]

    loop(8, body)


def input_gradient(mt, tf, z, groups):
    def body(h, _):
        z[h] = group_gradient(mt, tf, h)
        return 0

    lax.fori_loop(*groups, body, 0)


def group_gradient(mt, tf, h):
    left = jnp.concatenate([mt[h], mt[h + 1]], axis=1)
    right = jnp.concatenate(
        [tf[:, 768 * (1 - u) + 256 * b : 768 * (1 - u) + 256 * b + 256] for u in range(2) for b in range(3)], axis=0
    )
    return dot(left, right)


def features(rows, blocks, before, after, rowf, colf):
    k, n = iota((128, 256), 0), iota((128, 256), 1) >> 3
    picks = [one_hot(k == n + 32 * at) for at in range(4)]
    first = dot(before, picks[3])
    last = dot(after, picks[0])
    x = [first[4:8]] + [dot(blocks, pick) for pick in picks] + [last[0:4], jnp.zeros((8, 256), F32)]
    colf[...] = jnp.concatenate(x, axis=0) * LOG2E
    x = dot(rows, picks[0])
    x = jnp.where((iota((128, 256), 0) & 7) == (iota((128, 256), 1) & 7), x, 0.0).astype(BF16)
    rowf[...] = dot(one_hot((iota((16, 128), 1) >> 3) == iota((16, 128), 0)), x) * LOG2E


def elementwise(rowf, colf, z, act, cacc, rsum):
    rsum[...] = jnp.zeros_like(rsum)

    def body(step):
        parts = [pl.ds(pl.multiple_of(24 * step + 8 * part, 8), 8) for part in range(3)]
        totals = [jnp.zeros((8, 256), F32)] * 3
        for h in range(9):
            left = rowf[h : h + 1, :]
            row = jnp.zeros((8, 256), F32)
            for k, rows in enumerate(parts):
                value, slope = softplus_and_slope(colf[rows, :] + left)
                act[h, rows, :] = value
                p = z[h, rows, :] * slope
                totals[k] += p
                row += p
            rsum[8 * h : 8 * h + 8, :] += row
        for k, rows in enumerate(parts):
            cacc[rows, :] = totals[k]

    loop(11, body)


def sums(cacc, rsum, cols, col_ends, row_main, row_ends):
    k, n = iota((256, 128), 0) >> 3, iota((256, 128), 1)
    picks = [one_hot(k + 32 * g == n) for g in range(4)]
    pick = jnp.concatenate(picks, axis=0)
    x = [
        jnp.concatenate([cacc[4 + 64 * q + 16 * g : 20 + 64 * q + 16 * g, :] for g in range(4)], axis=1) for q in range(4)
    ]
    high, low = halves(jnp.concatenate(x, axis=0))
    x = dot(high, pick) + dot(low, pick)
    for q in range(4):
        cols[q] = x[16 * q : 16 * q + 16]
    sub, lane = iota((16, 128), 0), iota((16, 128), 1)
    ends = jnp.concatenate([cacc[0:8, :], cacc[256:264, :]], axis=0)
    high, low = halves(ends)
    first = dot(high, picks[3]) + dot(low, picks[3])
    second = dot(high, picks[0]) + dot(low, picks[0])
    col_ends[0] = jnp.where(sub >= 12, pltpu.roll(first, 12, 0), 0.0)
    col_ends[1] = jnp.where(sub < 4, pltpu.roll(second, 4, 0), 0.0)
    x = jnp.concatenate([rsum[...], jnp.zeros((56, 256), F32)], axis=0)
    by_group = one_hot((iota((80, 128), 0) >> 3) == (iota((80, 128), 1) >> 3))
    high, low = halves(x)
    x = dot(by_group, high) + dot(by_group, low)
    x = jnp.where((iota((80, 256), 0) & 7) == (iota((80, 256), 1) & 7), x, 0.0)
    high, low = halves(jnp.concatenate([x[4 + 16 * g : 20 + 16 * g] for g in range(4)], axis=1))
    row_main[...] = dot(high, pick) + dot(low, pick)
    ends = jnp.concatenate([x[0:8], x[64:72]], axis=0)
    high, low = halves(ends)
    first = dot(high, picks[3]) + dot(low, picks[3])
    second = dot(high, picks[0]) + dot(low, picks[0])
    row_ends[0] = jnp.where(sub >= 12, pltpu.roll(first, 12, 0), 0.0)
    row_ends[1] = jnp.where(sub < 4, pltpu.roll(second, 4, 0), 0.0)


def build_windows(act, a3):
    def body(h):
        at = pl.ds(pl.multiple_of(256 * h, 256), 256)
        for b in range(3):
            a3[at, 256 * b : 256 * b + 256] = act[h, 4 * b : 4 * b + 256, :].astype(BF16)

    loop(9, body)


def convolve(r, c, k, a3, tf, out_ref):
    parts = []
    for g in (2 * k, 2 * k + 1):
        both = jnp.concatenate([a3[256 * (g + u) : 256 * (g + u) + 256, :] for u in range(2)], axis=1)
        parts.append(dot_nt(tf[...], both).reshape(32, 8, 256))
    y = jnp.concatenate(parts, axis=1)
    row = r * 64 + 16 * k + iota((16, 256), 0)
    col = c * 256 + iota((16, 256), 1)
    out_ref[:, 16 * k : 16 * k + 16, :] = jnp.where((col >= row)[None], y, 0.0).astype(BF16)


def tap_gradient(mall, a3, gram, taps):
    for u in range(2):
        x = dot(mall[...], a3[256 * u : 256 * u + 2048, :])
        for k in range(6):
            gram[6 * u + k] = x[:, 128 * k : 128 * k + 128]
    lane = iota((32, 128), 1)

    def along(b, k, sources):
        total = jnp.zeros((32, 128), F32)
        for at, (s, u) in enumerate(sources):
            total = jnp.where((lane & 7) == at, gram[6 * u + 2 * b + k, pl.ds(s, 32, stride=8), :], total)
        return total

    sources = (
        [(s, 0) for s in range(8)],
        [((s + 4) % 8, 1 - s // 4) for s in range(8)],
        [(s, 1) for s in range(8)],
    )
    x = [jnp.concatenate([along(b, k, sources[a]) for k in range(2)], axis=1) for a in range(3) for b in range(3)]
    y = dot(jnp.concatenate(halves(jnp.concatenate(x, axis=0)), axis=0), one_hot((iota((256, 128), 0) >> 3) == iota((256, 128), 1)))
    y = y[0:288] + y[288:576]
    for q in range(3):
        total = jnp.zeros((32, 128), F32)
        for k in range(min(4, 9 - 4 * q)):
            tap = y[32 * (4 * q + k) : 32 * (4 * q + k) + 32]
            total = jnp.where((lane >> 5) == k, pltpu.roll(tap, 32 * k, 1) if k else tap, total)
        taps[32 * q : 32 * q + 32, :] = total


LOCAL_SCRATCH = [
    pltpu.VMEM((16, 256), F32),
    pltpu.VMEM((272, 256), F32),
    pltpu.VMEM((96, 128), F32),
    pltpu.VMEM((256, 2048), BF16),
    pltpu.VMEM((10, 272, 768), BF16),
    pltpu.VMEM((9, 272, 256), F32),
    pltpu.VMEM((2304, 768), BF16),
    pltpu.VMEM((9, 272, 256), F32),
    pltpu.VMEM((256, 1536), BF16),
    pltpu.VMEM((816, 256), BF16),
    pltpu.VMEM((12, 256, 128), F32),
    pltpu.VMEM((272, 256), F32),
    pltpu.VMEM((72, 256), F32),
    pltpu.VMEM((4, 16, 128), F32),
    pltpu.VMEM((2, 16, 128), F32),
    pltpu.VMEM((16, 128), F32),
    pltpu.VMEM((2, 16, 128), F32),
]


class Place:
    def __init__(self, nr, nc):
        r, c = lax.axis_index("row"), lax.axis_index("col")
        self.r, self.c, self.nr, self.nc = r, c, nr, nc
        self.per = nr // nc
        self.rb, self.rm = lax.div(r, self.per), lax.rem(r, self.per)
        _, self.quad = self.group(((r, 1, 0), (r, 2, 0)))
        _, self.line = self.group(((c, 1, 1), (c, 2, 1), (c, 4, 1)))
        self.k1, self.group1 = self.group(((r, 1, 0), (r, 8, 0), (r, 16, 0), (c, 2, 1), (c, 4, 1)))
        self.k2, self.group2 = self.group(((r, 2, 0), (r, 4, 0), (c, 1, 1)))
        self.has_up, self.has_down = r > 0, r < nr - 1
        self.has_left, self.has_right = c > 0, c < nc - 1
        self.ends_block = (self.rm == self.per - 1) & (self.rb < nc - 1)
        self.starts_block = (self.rm == 0) & (self.rb > 0)
        self.in_others = self.rb == c

    def group(self, bits):
        number, turns = 0, []
        for k, (x, weight, is_col) in enumerate(bits):
            bit = lax.rem(lax.div(x, weight), 2)
            number = number + bit * (1 << k)
            sign = 1 - 2 * bit
            turns.append((sign * weight, is_col, sign * (1 << k)))
        members = [(self.r, self.c, number)]
        for move, is_col, step in turns:
            members += [
                (a, b + move, n + step) if is_col else (a + move, b, n + step) for a, b, n in members
            ]
        return number, members[:0:-1]

    def other(self, k):
        return self.per * self.c + k, self.rb

    def targets(self, col):
        return [(lax.rem(self.r + self.per * k, self.nr), col) for k in range(self.nr // self.per)]

    def greet(self):
        r, c, nc, per, rb, rm = self.r, self.c, self.nc, self.per, self.rb, self.rm
        barrier = pltpu.get_barrier_semaphore()

        def signal(a, b):
            pl.semaphore_signal(barrier, inc=1, device_id=(a, b), device_id_type=MESH)

        def signal_all(col):
            for k in range(per):
                signal(per * c + k, col)

        is_first, is_last = c == 0, c == nc - 1
        before_is_me = is_last & (rb == nc - 2)
        after_is_me = is_first & (rb == 1)
        for a, b, _ in self.quad + self.line:
            signal(a, b)
        pl.when(jnp.logical_not(self.in_others))(lambda: signal(per * c + rm, c))
        for _, b, _ in self.line:
            signal(per * c + rm, b)
        pl.when(self.has_up)(lambda: signal(r - 1, nc - 1))
        pl.when(self.has_down)(lambda: signal(r + 1, 0))
        pl.when(self.has_left & jnp.logical_not(before_is_me))(lambda: signal(per * (c - 1) + rm, nc - 1))
        pl.when(self.has_right & jnp.logical_not(after_is_me))(lambda: signal(per * (c + 1) + rm, 0))
        pl.when(jnp.logical_not(self.in_others))(lambda: signal(per * c + rm, rb))
        for a, _, _ in self.quad:
            signal(per * (c - rb) + a, rb)
        pl.when(self.has_up)(lambda: signal(r - 1, c))
        pl.when(self.has_down)(lambda: signal(r + 1, c))
        pl.when(self.ends_block)(lambda: signal_all(rb + 1))
        pl.when(self.starts_block)(lambda: signal_all(rb - 1))
        for a, b, _ in self.group1 + self.group2:
            signal(a, b)
        n = len(self.quad + self.line + self.group1 + self.group2) + nc + per
        up, down = self.has_up, self.has_down
        for cond, m in (
            (self.in_others, -2), (is_last & down, nc), (is_first & up, nc),
            (is_last & (rb < nc - 1), nc), (before_is_me, -1), (is_first & (rb > 0), nc), (after_is_me, -1),
            (up, 1), (down, 1), (self.has_left, 1), (self.has_right, 1),
        ):
            n = n + jnp.where(cond, m, 0)
        return n

    def senders(self, send, recv):
        def put(src, dst_r, dst_c, dst, sem):
            pltpu.make_async_remote_copy(
                src, dst, send.at[sem], recv.at[sem], device_id=(dst_r, dst_c), device_id_type=MESH
            ).start()

        def put_other(src, k, dst, sem):
            a, b = self.other(k)
            mine = (a == self.r) & (b == self.c)
            pl.when(mine)(lambda: pltpu.make_async_copy(src, dst, recv.at[sem]).start())
            pl.when(jnp.logical_not(mine))(lambda: put(src, a, b, dst, sem))

        return put, put_other


def pair_kernel(
    nr, nc, e_hbm, lpt_hbm, rpt_hbm, w_hbm, cot_hbm,
    out_hbm, sums_hbm, eg_hbm,
    rowf, colf, taps, mall, mt, act, a3, z, tf, move, gram, cacc, rsum, cols, col_ends, row_main, row_ends,
    out_ref, eg_ref, feats, e_ref, w_ref, cot_ref, own, right, packed, quad, proj, es, eb, el, eh, blocks, row_feats, col_feats,
    cparts, cends, rends, turned, gparts, buf, r1, r2, mid, fin, recv, send, loads, stores,
):
    ins = ((e_hbm, e_ref), (w_hbm, w_ref), (lpt_hbm, proj.at[0:32]), (rpt_hbm, proj.at[32:64]), (cot_hbm, cot_ref))
    ins = [pltpu.make_async_copy(src, dst, loads.at[k]) for k, (src, dst) in enumerate(ins)]
    for copy in ins:
        copy.start()
    p = Place(nr, nc)
    r, c, per, rb, rm, k1, k2 = p.r, p.c, p.per, p.rb, p.rm, p.k1, p.k2
    greeted = p.greet()
    put, put_other = p.senders(send, recv)
    rows8, rows7 = gparts, gparts.at[0 : nc - 1]

    proj[64:128, :] = jnp.zeros((64, 512), BF16)
    ins[0].wait()
    e = e_ref[...].astype(F32)
    es[...] = jnp.concatenate([e[:, 0:256], e[:, 256:512]], axis=0).astype(BF16)
    ins[2].wait()
    ins[3].wait()
    own[...] = dot_nt(e_ref[...], proj[...]).astype(BF16).astype(F32)
    group = iota((8, 128), 1) >> 5
    right[...] = jnp.where(group == rm, pltpu.roll(own[...], lax.rem(32 * rm + 96, 128), 1), 0.0)
    ins[1].wait()
    build_taps(w_ref, tf)
    ins[4].wait()
    mask_cotangent(r, c, cot_ref, move, mall, mt)
    pl.semaphore_wait(pltpu.get_barrier_semaphore(), greeted)

    for a, b, _ in p.quad:
        put(right, a, b, quad.at[rm], 1)
    pltpu.make_async_copy(right, quad.at[rm], recv.at[1]).start()

    def put_line(row, dst, sem):
        for k in range(nc):
            put(own, row, k, dst, sem)

    is_first, is_last = c == 0, c == nc - 1
    row_after, row_before = is_last & p.has_down, is_first & p.has_up
    pl.when(row_after)(lambda: put_line(r + 1, row_feats.at[0], 2))
    pl.when(row_before)(lambda: put_line(r - 1, row_feats.at[1], 3))
    for a, b, _ in p.line:
        put(es, a, b, eb.at[c], 0)
    pltpu.make_async_copy(es, eb.at[c], recv.at[0]).start()

    def put_targets(src, col, dst, sem):
        first, *rest = p.targets(col)
        mine = c == col
        pl.when(mine)(lambda: pltpu.make_async_copy(src, dst, recv.at[sem]).start())
        pl.when(jnp.logical_not(mine))(lambda: put(src, *first, dst, sem))
        for a, b in rest:
            put(src, a, b, dst, sem)

    col_after, col_before = is_last & (rb < nc - 1), is_first & (rb > 0)
    input_gradient(mt, tf, z, (0, 5))
    wait_bytes(quad, recv.at[1])
    packed[...] = jnp.sum(quad[...], axis=0)
    put_targets(packed, rb, blocks.at[c], 15)
    pl.when(col_after)(lambda: put_targets(packed, rb + 1, col_feats.at[0], 4))
    pl.when(col_before)(lambda: put_targets(packed, rb - 1, col_feats.at[1], 5))
    input_gradient(mt, tf, z, (5, 9))

    wait_bytes(eb, recv.at[0])
    e = eb[...].astype(F32)
    el[...] = e[:, 0:8].reshape(64, 256).astype(BF16)
    eh[...] = e[:, 8:16].reshape(64, 256).astype(BF16)
    feats[8:72, :] = dot_nt(el[...], proj[:, 0:256]) + dot_nt(eh[...], proj[:, 256:512])

    def arrive(cond, ref, sem):
        pl.when(cond)(lambda: wait_bytes(ref, sem))
        pl.when(jnp.logical_not(cond))(lambda: ref.__setitem__(..., jnp.full(ref.shape, OUTSIDE, F32)))

    arrive(p.has_up, row_feats.at[0], recv.at[2])
    arrive(p.has_down, row_feats.at[1], recv.at[3])
    arrive(p.has_left, col_feats.at[0], recv.at[4])
    arrive(p.has_right, col_feats.at[1], recv.at[5])
    wait_bytes(blocks, recv.at[15])
    feats[0:8, :] = row_feats[0]
    feats[72:80, :] = row_feats[1]
    feats[80:136, :] = jnp.zeros((56, 128), F32)
    ends = [jnp.concatenate([col_feats[k], jnp.zeros((8, 128), F32)], axis=0).astype(BF16) for k in range(2)]
    features(feats[4:132, :].astype(BF16), blocks[...].reshape(8 * nc, 128).astype(BF16), *ends, rowf, colf)
    elementwise(rowf, colf, z, act, cacc, rsum)
    sums(cacc, rsum, cols, col_ends, row_main, row_ends)

    for k in range(per):
        put_other(cols.at[k], k, cparts.at[rm], 6)
    pl.when(p.has_up)(lambda: put(row_ends.at[0], r - 1, c, rends.at[0], 7))
    pl.when(p.has_down)(lambda: put(row_ends.at[1], r + 1, c, rends.at[1], 8))
    pl.when(p.has_left)(lambda: put(col_ends.at[0], per * c - 1, rb, cends.at[0, rm], 9))
    pl.when(p.has_right)(lambda: put(col_ends.at[1], per * c + per, rb, cends.at[1, rm], 10))

    build_windows(act, a3)
    tap_gradient(mall, a3, gram, taps)
    def gather_sum(cond, ref, sem):
        pl.when(cond)(lambda: wait_bytes(ref, sem))
        pl.when(jnp.logical_not(cond))(lambda: ref.__setitem__(..., jnp.zeros(ref.shape, F32)))

    gather_sum(p.has_down, rends.at[0], recv.at[7])
    gather_sum(p.has_up, rends.at[1], recv.at[8])
    gather_sum(p.ends_block, cends.at[0], recv.at[9])
    gather_sum(p.starts_block, cends.at[1], recv.at[10])
    wait_bytes(cparts, recv.at[6])
    grads = (
        row_main[...] + rends[0] + rends[1],
        jnp.sum(cparts[...], axis=0) + jnp.sum(cends[0], axis=0) + jnp.sum(cends[1], axis=0),
    )
    lane = iota((16, 128), 1)
    spread = []
    for g in range(4):
        parts = [x if turn % 128 == 0 else pltpu.roll(x, turn % 128, 1) for x, turn in zip(grads, (-32 * g, 32 - 32 * g))]
        spread.append(jnp.where(lane < 32, parts[0], jnp.where(lane < 64, parts[1], 0.0)))
    turned[...] = jnp.concatenate(spread, axis=0)

    high, low = halves(turned[...])
    for half, ref in enumerate((el, eh)):
        part = dot_tn(high, ref[...]) + dot_tn(low, ref[...])
        for k in range(16):
            at = 4 * (k // 2) + 2 * half + k % 2
            x = part[8 * (k // 2) : 8 * (k // 2) + 8, 128 * (k % 2) : 128 * (k % 2) + 128]
            y = taps[8 * at : 8 * at + 8, :] if at < 12 else jnp.zeros((8, 128), F32)
            buf[at] = jnp.concatenate([x, y], axis=0).astype(BF16)

    for a, b, at in p.group1:
        put(buf.at[at], a, b, r1.at[k1], 11)
    pltpu.make_async_copy(buf.at[k1], r1.at[k1], recv.at[11]).start()

    for a, b, _ in p.line:
        put(turned.at[pl.ds(pl.multiple_of(8 * b, 8), 8)], a, b, gparts.at[c], 14)
    pltpu.make_async_copy(turned.at[pl.ds(pl.multiple_of(8 * c, 8), 8)], gparts.at[c], recv.at[14]).start()

    outs = [
        pltpu.make_async_copy(out_ref.at[:, 16 * q : 16 * q + 16, :], out_hbm.at[:, 16 * q : 16 * q + 16, :], stores.at[q])
        for q in range(4)
    ]
    convolve(r, c, 0, a3, tf, out_ref)
    outs[0].start()
    convolve(r, c, 1, a3, tf, out_ref)
    outs[1].start()
    wait_bytes(r1, recv.at[11])
    mid[...] = jnp.sum(r1[...].astype(F32), axis=0).astype(BF16)
    for a, b, _ in p.group2:
        put(mid, a, b, r2.at[k2], 12)
    pltpu.make_async_copy(mid, r2.at[k2], recv.at[12]).start()

    convolve(r, c, 2, a3, tf, out_ref)
    outs[2].start()
    convolve(r, c, 3, a3, tf, out_ref)
    outs[3].start()
    wait_bytes(r2, recv.at[12])
    fin[...] = jnp.sum(r2[...].astype(F32), axis=0).astype(BF16)
    for a, b, _ in p.group1:
        put(fin, a, b, sums_hbm.at[k1], 13)
    pltpu.make_async_copy(fin, sums_hbm.at[k1], recv.at[13]).start()

    wait_bytes(gparts, recv.at[14])
    high, low = halves(jnp.sum(gparts[...], axis=0))
    eg_ref[...] = dot(high, proj[...]) + dot(low, proj[...])
    outs.append(pltpu.make_async_copy(eg_ref, eg_hbm, stores.at[4]))
    outs[4].start()

    for copy in outs:
        copy.wait()
    wait_bytes(eb.at[0 : nc - 1], send.at[0])
    wait_bytes(quad.at[0 : per - 1], send.at[1])
    pl.when(row_after)(lambda: wait_bytes(rows8, send.at[2]))
    pl.when(row_before)(lambda: wait_bytes(rows8, send.at[3]))

    def sent_targets(cond, mine, eight, seven, sem):
        pl.when(cond & mine)(lambda: wait_bytes(seven, send.at[sem]))
        pl.when(cond & jnp.logical_not(mine))(lambda: wait_bytes(eight, send.at[sem]))

    sent_targets(col_after, rb + 1 == c, rows8, rows7, 4)
    sent_targets(col_before, rb - 1 == c, rows8, rows7, 5)
    sent_targets(rb >= 0, p.in_others, blocks, blocks.at[0 : nc - 1], 15)
    pl.when(p.in_others)(lambda: wait_bytes(cparts.at[0 : per - 1], send.at[6]))
    pl.when(jnp.logical_not(p.in_others))(lambda: wait_bytes(cparts, send.at[6]))
    pl.when(p.has_up)(lambda: wait_bytes(row_ends.at[0], send.at[7]))
    pl.when(p.has_down)(lambda: wait_bytes(row_ends.at[1], send.at[8]))
    pl.when(p.has_left)(lambda: wait_bytes(col_ends.at[0], send.at[9]))
    pl.when(p.has_right)(lambda: wait_bytes(col_ends.at[1], send.at[10]))
    wait_bytes(r1.at[0 : r1.shape[0] - 1], send.at[11])
    wait_bytes(r2.at[0 : r2.shape[0] - 1], send.at[12])
    wait_bytes(gparts.at[0 : nc - 1], send.at[14])

    wait_bytes(r1.at[0 : r1.shape[0] - 1], send.at[13])
    wait_bytes(sums_hbm, recv.at[13])


def finish_kernel(
    scale, sums_in, eg_in, pair_in, conv_out, left_out, right_out, eg_out, pair_out,
    sums_ref, eg_ref, held, conv_ref, left_ref, right_ref, loads, stores,
):
    def piece(k):
        return slice(8 * k, 8 * k + 8)

    ins = [pltpu.make_async_copy(sums_in, sums_ref, loads.at[0]), pltpu.make_async_copy(eg_in, eg_ref, loads.at[1])]
    ins += [pltpu.make_async_copy(pair_in.at[piece(k)], held.at[piece(k)], loads.at[2 + k]) for k in range(4)]
    outs = [
        pltpu.make_async_copy(conv_ref, conv_out, stores.at[0]),
        pltpu.make_async_copy(left_ref, left_out, stores.at[1]),
        pltpu.make_async_copy(right_ref, right_out, stores.at[2]),
        pltpu.make_async_copy(eg_ref, eg_out, stores.at[3]),
    ]
    outs += [pltpu.make_async_copy(held.at[piece(k)], pair_out.at[piece(k)], stores.at[4 + k]) for k in range(4)]
    for copy in ins:
        copy.start()
    ins[0].wait()
    for ref, first, at in ((left_ref, 0, 1), (right_ref, 16, 2)):
        for k in range(16):
            x = sums_ref[first + k].astype(F32)[0:8]
            ref[8 * (k // 4) : 8 * (k // 4) + 8, 128 * (k % 4) : 128 * (k % 4) + 128] = x * scale
        outs[at].start()
    ins[1].wait()
    outs[3].start()
    for k in range(4):
        ins[2 + k].wait()
        outs[4 + k].start()
    for k in range(9):
        q, at = divmod(k, 4)
        for part in range(4):
            x = sums_ref[4 * q + part].astype(F32)
            conv_ref[k, 8 * part : 8 * part + 8, :] = x[8:16, 32 * at : 32 * at + 32] * scale
    outs[0].start()
    for copy in outs:
        copy.wait()


def shards(nr, nc, embed, left_proj, right_proj, conv_w, cotangent):
    per = nr // nc
    pair_out, totals, embed_grad = pl.pallas_call(
        functools.partial(pair_kernel, nr, nc),
        out_shape=(
            jax.ShapeDtypeStruct((32, 64, 256), BF16),
            jax.ShapeDtypeStruct((32, 16, 128), BF16),
            jax.ShapeDtypeStruct((8, 512), F32),
        ),
        in_specs=[HBM] * 5,
        out_specs=(HBM,) * 3,
        scratch_shapes=LOCAL_SCRATCH
        + [
            pltpu.VMEM((32, 64, 256), BF16),
            pltpu.VMEM((8, 512), F32),
            pltpu.VMEM((136, 128), F32),
            pltpu.VMEM((8, 512), BF16),
            pltpu.VMEM((9, 32, 32), BF16),
            pltpu.VMEM((32, 64, 256), BF16),
            pltpu.VMEM((8, 128), F32),
            pltpu.VMEM((8, 128), F32),
            pltpu.VMEM((8, 128), F32),
            pltpu.VMEM((per, 8, 128), F32),
            pltpu.VMEM((128, 512), BF16),
            pltpu.VMEM((16, 256), BF16),
            pltpu.VMEM((nc, 16, 256), BF16),
            pltpu.VMEM((64, 256), BF16),
            pltpu.VMEM((64, 256), BF16),
            pltpu.VMEM((nc, 8, 128), F32),
            pltpu.VMEM((2, 8, 128), F32),
            pltpu.VMEM((2, 8, 128), F32),
            pltpu.VMEM((per, 16, 128), F32),
            pltpu.VMEM((2, per, 16, 128), F32),
            pltpu.VMEM((2, 16, 128), F32),
            pltpu.VMEM((64, 128), F32),
            pltpu.VMEM((nc, 8, 128), F32),
            pltpu.VMEM((32, 16, 128), BF16),
            pltpu.VMEM((32, 16, 128), BF16),
            pltpu.VMEM((8, 16, 128), BF16),
            pltpu.VMEM((16, 128), BF16),
            pltpu.VMEM((16, 128), BF16),
            pltpu.SemaphoreType.DMA((16,)),
            pltpu.SemaphoreType.DMA((16,)),
            pltpu.SemaphoreType.DMA((5,)),
            pltpu.SemaphoreType.DMA((6,)),
        ],
        compiler_params=pltpu.CompilerParams(
            collective_id=0, has_side_effects=True, vmem_limit_bytes=60 * 1024 * 1024
        ),
        name="pair_kernel",
    )(embed, left_proj.T, right_proj.T, conv_w, cotangent)
    conv_grad, left_t, right_t, embed_grad, pair_out = pl.pallas_call(
        functools.partial(finish_kernel, 32.0 / (8 * nr * nc)),
        out_shape=(
            jax.ShapeDtypeStruct((9, 32, 32), F32),
            jax.ShapeDtypeStruct((32, 512), F32),
            jax.ShapeDtypeStruct((32, 512), F32),
            jax.ShapeDtypeStruct((8, 512), F32),
            jax.ShapeDtypeStruct((32, 64, 256), BF16),
        ),
        in_specs=[HBM] * 3,
        out_specs=(HBM,) * 5,
        scratch_shapes=[
            pltpu.VMEM((32, 16, 128), BF16),
            pltpu.VMEM((8, 512), F32),
            pltpu.VMEM((32, 64, 256), BF16),
            pltpu.VMEM((9, 32, 32), F32),
            pltpu.VMEM((32, 512), F32),
            pltpu.VMEM((32, 512), F32),
            pltpu.SemaphoreType.DMA((6,)),
            pltpu.SemaphoreType.DMA((8,)),
        ],
        compiler_params=pltpu.CompilerParams(vmem_limit_bytes=60 * 1024 * 1024),
        name="finish",
    )(totals, embed_grad, pair_out)
    return pair_out, conv_grad, left_t.T, right_t.T, embed_grad


def solution(mesh):
    body = functools.partial(shards, mesh.shape["row"], mesh.shape["col"])
    in_specs = (P(("row", "col"), None), P(), P(), P(), P(None, "row", "col"))
    out_specs = (P(None, "row", "col"), P(), P(), P(), P(("row", "col"), None))
    return jax.shard_map(body, mesh=mesh, in_specs=in_specs, out_specs=out_specs, check_vma=False)
```

```python
import functools

import jax
import jax.numpy as jnp
from jax import lax
from jax.experimental import pallas as pl
from jax.experimental.pallas import tpu as pltpu
from jax.sharding import PartitionSpec as P

MESH = pl.DeviceIdType.MESH
OUTSIDE = -1e30
LOG2E = 1.4426950408889634
LN2 = 0.6931471805599453
PIECES = 22
F32 = jnp.float32
BF16 = jnp.bfloat16
VMEM = pl.BlockSpec(memory_space=pltpu.VMEM)
HBM = pl.BlockSpec(memory_space=pltpu.HBM)


def iota(shape, dim):
    return lax.broadcasted_iota(jnp.int32, shape, dim)


def one_hot(cond):
    return jnp.where(cond, 1.0, 0.0).astype(BF16)


def dot(a, b):
    return jnp.dot(a, b, preferred_element_type=F32)


def dot_nt(a, b):
    return lax.dot_general(a, b, (((1,), (1,)), ((), ())), preferred_element_type=F32)


def dot_tn(a, b):
    return lax.dot_general(a, b, (((0,), (0,)), ((), ())), preferred_element_type=F32)


def halves(x):
    high = x.astype(BF16)
    return high, (x - high.astype(F32)).astype(BF16)


def loop(n, f):
    def body(k, _):
        f(k)
        return 0

    lax.fori_loop(0, n, body, 0)


def lanes(h):
    return pl.ds(pl.multiple_of(h * 256, 256), 256)


def wait_bytes(ref, sem):
    pltpu.make_async_copy(ref, ref, sem).wait()


def softplus_and_slope(y):
    t = jnp.exp2(-jnp.abs(y))
    u = 1.0 + t
    inv = pltpu.reciprocal(u, full_range=False)
    log = jnp.where(t < 2.0**-11, t * LOG2E, jnp.log2(u))
    return LN2 * (jnp.maximum(y, 0.0) + log), jnp.where(y >= 0, inv, t * inv)


def build_taps(w_ref, tf):
    spread = one_hot((iota((256, 32), 0) >> 3) == iota((256, 32), 1))
    widen = one_hot((iota((32, 256), 1) >> 3) == iota((32, 256), 0))
    s0, s1 = iota((256, 256), 0) & 7, iota((256, 256), 1) & 7
    same, above, below = s1 == s0, s1 == s0 + 4, s1 == s0 - 4
    for b in range(3):
        x = [dot(spread, dot(w_ref[3 * a + b], widen).astype(BF16)) for a in range(3)]
        tf[:, 256 * b : 256 * b + 256] = jnp.where(same, x[0], jnp.where(above, x[1], 0.0)).astype(BF16)
        tf[:, 768 + 256 * b : 1024 + 256 * b] = jnp.where(same, x[2], jnp.where(below, x[1], 0.0)).astype(BF16)


def mask_cotangent(r, c, cot_ref, move, mall, mt):
    for k in range(4):
        x = cot_ref[:, 16 * k : 16 * k + 16, :].astype(F32)
        row = r * 64 + 16 * k + iota((16, 256), 0)
        x = jnp.where((c * 256 + iota((16, 256), 1) >= row)[None], x, 0.0)
        for half in range(2):
            mall[:, lanes(2 * k + half)] = x[:, 8 * half : 8 * half + 8].reshape(256, 256).astype(BF16)
    for b in range(3):
        move[272 * b : 272 * b + 272, :] = one_hot(iota((272, 256), 0) - 4 * b == iota((272, 256), 1))
        mt[0, :, 256 * b : 256 * b + 256] = jnp.zeros((272, 256), BF16)
        mt[9, :, 256 * b : 256 * b + 256] = jnp.zeros((272, 256), BF16)

    def body(g):
        moved = dot_nt(move[...], mall[:, lanes(g)]).astype(BF16)
        for b in range(3):
            mt[g + 1, :, 256 * b : 256 * b + 256] = moved[272 * b : 272 * b + 272]

    loop(8, body)


def input_gradient(mt, tf, z, groups):
    def body(h, _):
        z[h] = group_gradient(mt, tf, h)
        return 0

    lax.fori_loop(*groups, body, 0)


def group_gradient(mt, tf, h):
    left = jnp.concatenate([mt[h], mt[h + 1]], axis=1)
    right = jnp.concatenate(
        [tf[:, 768 * (1 - u) + 256 * b : 768 * (1 - u) + 256 * b + 256] for u in range(2) for b in range(3)], axis=0
    )
    return dot(left, right)


def features(rows, blocks, before, after, rowf, colf):
    k, n = iota((128, 256), 0), iota((128, 256), 1) >> 3
    picks = [one_hot(k == n + 32 * at) for at in range(4)]
    first = dot(before, picks[3])
    last = dot(after, picks[0])
    x = [first[4:8]] + [dot(blocks, pick) for pick in picks] + [last[0:4], jnp.zeros((8, 256), F32)]
    colf[...] = jnp.concatenate(x, axis=0) * LOG2E
    x = dot(rows, picks[0])
    x = jnp.where((iota((128, 256), 0) & 7) == (iota((128, 256), 1) & 7), x, 0.0).astype(BF16)
    rowf[...] = dot(one_hot((iota((16, 128), 1) >> 3) == iota((16, 128), 0)), x) * LOG2E


def elementwise(rowf, colf, z, act, cacc, rsum):
    rsum[...] = jnp.zeros_like(rsum)

    def body(step):
        parts = [pl.ds(pl.multiple_of(24 * step + 8 * part, 8), 8) for part in range(3)]
        totals = [jnp.zeros((8, 256), F32)] * 3
        for h in range(9):
            left = rowf[h : h + 1, :]
            row = jnp.zeros((8, 256), F32)
            for k, rows in enumerate(parts):
                value, slope = softplus_and_slope(colf[rows, :] + left)
                act[h, rows, :] = value
                p = z[h, rows, :] * slope
                totals[k] += p
                row += p
            rsum[8 * h : 8 * h + 8, :] += row
        for k, rows in enumerate(parts):
            cacc[rows, :] = totals[k]

    loop(11, body)


def sums(cacc, rsum, cols, col_ends, row_main, row_ends):
    k, n = iota((256, 128), 0) >> 3, iota((256, 128), 1)
    picks = [one_hot(k + 32 * g == n) for g in range(4)]
    pick = jnp.concatenate(picks, axis=0)
    x = [
        jnp.concatenate([cacc[4 + 64 * q + 16 * g : 20 + 64 * q + 16 * g, :] for g in range(4)], axis=1) for q in range(4)
    ]
    high, low = halves(jnp.concatenate(x, axis=0))
    x = dot(high, pick) + dot(low, pick)
    for q in range(4):
        cols[q] = x[16 * q : 16 * q + 16]
    sub, lane = iota((16, 128), 0), iota((16, 128), 1)
    ends = jnp.concatenate([cacc[0:8, :], cacc[256:264, :]], axis=0)
    high, low = halves(ends)
    first = dot(high, picks[3]) + dot(low, picks[3])
    second = dot(high, picks[0]) + dot(low, picks[0])
    col_ends[0] = jnp.where(sub >= 12, pltpu.roll(first, 12, 0), 0.0)
    col_ends[1] = jnp.where(sub < 4, pltpu.roll(second, 4, 0), 0.0)
    x = jnp.concatenate([rsum[...], jnp.zeros((56, 256), F32)], axis=0)
    by_group = one_hot((iota((80, 128), 0) >> 3) == (iota((80, 128), 1) >> 3))
    high, low = halves(x)
    x = dot(by_group, high) + dot(by_group, low)
    x = jnp.where((iota((80, 256), 0) & 7) == (iota((80, 256), 1) & 7), x, 0.0)
    high, low = halves(jnp.concatenate([x[4 + 16 * g : 20 + 16 * g] for g in range(4)], axis=1))
    row_main[...] = dot(high, pick) + dot(low, pick)
    ends = jnp.concatenate([x[0:8], x[64:72]], axis=0)
    high, low = halves(ends)
    first = dot(high, picks[3]) + dot(low, picks[3])
    second = dot(high, picks[0]) + dot(low, picks[0])
    row_ends[0] = jnp.where(sub >= 12, pltpu.roll(first, 12, 0), 0.0)
    row_ends[1] = jnp.where(sub < 4, pltpu.roll(second, 4, 0), 0.0)


def build_windows(act, a3):
    def body(h):
        at = pl.ds(pl.multiple_of(256 * h, 256), 256)
        for b in range(3):
            a3[at, 256 * b : 256 * b + 256] = act[h, 4 * b : 4 * b + 256, :].astype(BF16)

    loop(9, body)


def convolve(r, c, k, a3, tf, out_ref):
    parts = []
    for g in (2 * k, 2 * k + 1):
        both = jnp.concatenate([a3[256 * (g + u) : 256 * (g + u) + 256, :] for u in range(2)], axis=1)
        parts.append(dot_nt(tf[...], both).reshape(32, 8, 256))
    y = jnp.concatenate(parts, axis=1)
    row = r * 64 + 16 * k + iota((16, 256), 0)
    col = c * 256 + iota((16, 256), 1)
    out_ref[:, 16 * k : 16 * k + 16, :] = jnp.where((col >= row)[None], y, 0.0).astype(BF16)


def tap_gradient(mall, a3, gram, taps):
    for u in range(2):
        x = dot(mall[...], a3[256 * u : 256 * u + 2048, :])
        for k in range(6):
            gram[6 * u + k] = x[:, 128 * k : 128 * k + 128]
    lane = iota((32, 128), 1)

    def along(b, k, sources):
        total = jnp.zeros((32, 128), F32)
        for at, (s, u) in enumerate(sources):
            total = jnp.where((lane & 7) == at, gram[6 * u + 2 * b + k, pl.ds(s, 32, stride=8), :], total)
        return total

    sources = (
        [(s, 0) for s in range(8)],
        [((s + 4) % 8, 1 - s // 4) for s in range(8)],
        [(s, 1) for s in range(8)],
    )
    x = [jnp.concatenate([along(b, k, sources[a]) for k in range(2)], axis=1) for a in range(3) for b in range(3)]
    y = dot(jnp.concatenate(halves(jnp.concatenate(x, axis=0)), axis=0), one_hot((iota((256, 128), 0) >> 3) == iota((256, 128), 1)))
    y = y[0:288] + y[288:576]
    for q in range(3):
        total = jnp.zeros((32, 128), F32)
        for k in range(min(4, 9 - 4 * q)):
            tap = y[32 * (4 * q + k) : 32 * (4 * q + k) + 32]
            total = jnp.where((lane >> 5) == k, pltpu.roll(tap, 32 * k, 1) if k else tap, total)
        taps[32 * q : 32 * q + 32, :] = total


LOCAL_SCRATCH = [
    pltpu.VMEM((16, 256), F32),
    pltpu.VMEM((272, 256), F32),
    pltpu.VMEM((96, 128), F32),
    pltpu.VMEM((256, 2048), BF16),
    pltpu.VMEM((10, 272, 768), BF16),
    pltpu.VMEM((9, 272, 256), F32),
    pltpu.VMEM((2304, 768), BF16),
    pltpu.VMEM((9, 272, 256), F32),
    pltpu.VMEM((256, 1536), BF16),
    pltpu.VMEM((816, 256), BF16),
    pltpu.VMEM((12, 256, 128), F32),
    pltpu.VMEM((272, 256), F32),
    pltpu.VMEM((72, 256), F32),
    pltpu.VMEM((4, 16, 128), F32),
    pltpu.VMEM((2, 16, 128), F32),
    pltpu.VMEM((16, 128), F32),
    pltpu.VMEM((2, 16, 128), F32),
]


class Place:
    def __init__(self, nr, nc):
        r, c = lax.axis_index("row"), lax.axis_index("col")
        self.r, self.c, self.nr, self.nc = r, c, nr, nc
        self.per = nr // nc
        self.rb, self.rm = lax.div(r, self.per), lax.rem(r, self.per)
        _, self.quad = self.group(((r, 1, 0), (r, 2, 0)))
        _, self.line = self.group(((c, 1, 1), (c, 2, 1), (c, 4, 1)))
        self.plane = ((r, 8, 0), (r, 16, 0), (c, 2, 1), (c, 4, 1), (r, 1, 0))
        self.k1, self.group1 = self.group(self.plane)
        self.k2, self.group2 = self.group(((r, 2, 0), (r, 4, 0), (c, 1, 1)))
        self.has_up, self.has_down = r > 0, r < nr - 1
        self.has_left, self.has_right = c > 0, c < nc - 1
        self.ends_block = (self.rm == self.per - 1) & (self.rb < nc - 1)
        self.starts_block = (self.rm == 0) & (self.rb > 0)
        self.in_others = self.rb == c

    def group(self, bits):
        number, turns = 0, []
        for k, (x, weight, is_col) in enumerate(bits):
            bit = lax.rem(lax.div(x, weight), 2)
            number = number + bit * (1 << k)
            sign = 1 - 2 * bit
            turns.append((sign * weight, is_col, sign * (1 << k)))
        members = [(self.r, self.c, number)]
        for move, is_col, step in turns:
            members += [
                (a, b + move, n + step) if is_col else (a + move, b, n + step) for a, b, n in members
            ]
        return number, members[:0:-1]

    def plane_member(self, k):
        a, b = self.r, self.c
        for at, (x, weight, is_col) in enumerate(self.plane):
            move = weight * (k >> at & 1) - weight * lax.rem(lax.div(x, weight), 2)
            a, b = (a, b + move) if is_col else (a + move, b)
        return a, b

    def other(self, k):
        return self.per * self.c + k, self.rb

    def targets(self, col):
        return [(lax.rem(self.r + self.per * k, self.nr), col) for k in range(self.nr // self.per)]

    def greet(self):
        r, c, nc, per, rb, rm = self.r, self.c, self.nc, self.per, self.rb, self.rm
        barrier = pltpu.get_barrier_semaphore()

        def signal(a, b):
            pl.semaphore_signal(barrier, inc=1, device_id=(a, b), device_id_type=MESH)

        def signal_all(col):
            for k in range(per):
                signal(per * c + k, col)

        is_first, is_last = c == 0, c == nc - 1
        before_is_me = is_last & (rb == nc - 2)
        after_is_me = is_first & (rb == 1)
        for a, b, _ in self.quad + self.line:
            signal(a, b)
        pl.when(jnp.logical_not(self.in_others))(lambda: signal(per * c + rm, c))
        for _, b, _ in self.line:
            signal(per * c + rm, b)
        pl.when(self.has_up)(lambda: signal(r - 1, nc - 1))
        pl.when(self.has_down)(lambda: signal(r + 1, 0))
        pl.when(self.has_left & jnp.logical_not(before_is_me))(lambda: signal(per * (c - 1) + rm, nc - 1))
        pl.when(self.has_right & jnp.logical_not(after_is_me))(lambda: signal(per * (c + 1) + rm, 0))
        pl.when(jnp.logical_not(self.in_others))(lambda: signal(per * c + rm, rb))
        for a, _, _ in self.quad:
            signal(per * (c - rb) + a, rb)
        pl.when(self.has_up)(lambda: signal(r - 1, c))
        pl.when(self.has_down)(lambda: signal(r + 1, c))
        pl.when(self.ends_block)(lambda: signal_all(rb + 1))
        pl.when(self.starts_block)(lambda: signal_all(rb - 1))
        for a, b, _ in self.group1 + self.group2:
            signal(a, b)
        n = len(self.quad + self.line + self.group1 + self.group2) + nc + per
        up, down = self.has_up, self.has_down
        for cond, m in (
            (self.in_others, -2), (is_last & down, nc), (is_first & up, nc),
            (is_last & (rb < nc - 1), nc), (before_is_me, -1), (is_first & (rb > 0), nc), (after_is_me, -1),
            (up, 1), (down, 1), (self.has_left, 1), (self.has_right, 1),
        ):
            n = n + jnp.where(cond, m, 0)
        return n

    def senders(self, send, recv):
        def put(src, dst_r, dst_c, dst, sem):
            pltpu.make_async_remote_copy(
                src, dst, send.at[sem], recv.at[sem], device_id=(dst_r, dst_c), device_id_type=MESH
            ).start()

        def put_other(src, k, dst, sem):
            a, b = self.other(k)
            mine = (a == self.r) & (b == self.c)
            pl.when(mine)(lambda: pltpu.make_async_copy(src, dst, recv.at[sem]).start())
            pl.when(jnp.logical_not(mine))(lambda: put(src, a, b, dst, sem))

        return put, put_other


def pair_kernel(
    nr, nc, e_hbm, lpt_hbm, rpt_hbm, w_hbm, cot_hbm,
    out_hbm, sums_hbm, eg_hbm,
    rowf, colf, taps, mall, mt, act, a3, z, tf, move, gram, cacc, rsum, cols, col_ends, row_main, row_ends,
    out_ref, eg_ref, feats, e_ref, w_ref, cot_ref, own, right, packed, quad, line, proj, es, eb, el, eh, blocks, row_feats, col_feats,
    cparts, cends, rends, turned, gparts, buf, r1, r2, mid, fin, recv, send, loads, stores,
):
    ins = ((e_hbm, e_ref), (w_hbm, w_ref), (lpt_hbm, proj.at[0:32]), (rpt_hbm, proj.at[32:64]), (cot_hbm, cot_ref))
    ins = [pltpu.make_async_copy(src, dst, loads.at[k]) for k, (src, dst) in enumerate(ins)]
    for copy in ins:
        copy.start()
    p = Place(nr, nc)
    r, c, per, rb, rm, k1, k2 = p.r, p.c, p.per, p.rb, p.rm, p.k1, p.k2
    greeted = p.greet()
    put, put_other = p.senders(send, recv)
    rows8, rows7 = gparts, gparts.at[0 : nc - 1]

    proj[64:128, :] = jnp.zeros((64, 512), BF16)
    ins[0].wait()
    e = e_ref[...].astype(F32)
    es[...] = jnp.concatenate([e[:, 0:256], e[:, 256:512]], axis=0).astype(BF16)
    ins[2].wait()
    ins[3].wait()
    own[...] = dot_nt(e_ref[...], proj[...]).astype(BF16).astype(F32)
    group = iota((8, 128), 1) >> 5
    right[...] = jnp.where(group == rm, pltpu.roll(own[...], lax.rem(32 * rm + 96, 128), 1), 0.0)
    ins[1].wait()
    build_taps(w_ref, tf)
    ins[4].wait()
    mask_cotangent(r, c, cot_ref, move, mall, mt)
    pl.semaphore_wait(pltpu.get_barrier_semaphore(), greeted)

    for a, b, _ in p.quad:
        put(right, a, b, quad.at[rm], 1)
    pltpu.make_async_copy(right, quad.at[rm], recv.at[1]).start()

    def put_line(row, dst, sem):
        for k in range(nc):
            put(own, row, k, dst, sem)

    is_first, is_last = c == 0, c == nc - 1
    row_after, row_before = is_last & p.has_down, is_first & p.has_up
    pl.when(row_after)(lambda: put_line(r + 1, row_feats.at[0], 2))
    pl.when(row_before)(lambda: put_line(r - 1, row_feats.at[1], 3))
    for a, b, _ in p.line:
        put(own, a, b, line.at[c], 16)
    pltpu.make_async_copy(own, line.at[c], recv.at[16]).start()

    def put_targets(src, col, dst, sem):
        first, *rest = p.targets(col)
        mine = c == col
        pl.when(mine)(lambda: pltpu.make_async_copy(src, dst, recv.at[sem]).start())
        pl.when(jnp.logical_not(mine))(lambda: put(src, *first, dst, sem))
        for a, b in rest:
            put(src, a, b, dst, sem)

    col_after, col_before = is_last & (rb < nc - 1), is_first & (rb > 0)
    input_gradient(mt, tf, z, (0, 5))
    wait_bytes(quad, recv.at[1])
    packed[...] = jnp.sum(quad[...], axis=0)
    put_targets(packed, rb, blocks.at[c], 15)
    pl.when(col_after)(lambda: put_targets(packed, rb + 1, col_feats.at[0], 4))
    pl.when(col_before)(lambda: put_targets(packed, rb - 1, col_feats.at[1], 5))
    input_gradient(mt, tf, z, (5, 9))

    def arrive(cond, ref, sem):
        pl.when(cond)(lambda: wait_bytes(ref, sem))
        pl.when(jnp.logical_not(cond))(lambda: ref.__setitem__(..., jnp.full(ref.shape, OUTSIDE, F32)))

    arrive(p.has_up, row_feats.at[0], recv.at[2])
    arrive(p.has_down, row_feats.at[1], recv.at[3])
    arrive(p.has_left, col_feats.at[0], recv.at[4])
    arrive(p.has_right, col_feats.at[1], recv.at[5])
    wait_bytes(line, recv.at[16])
    wait_bytes(blocks, recv.at[15])
    feats[8:72, :] = line[...].reshape(8 * nc, 128)
    feats[0:8, :] = row_feats[0]
    feats[72:80, :] = row_feats[1]
    feats[80:136, :] = jnp.zeros((56, 128), F32)
    ends = [jnp.concatenate([col_feats[k], jnp.zeros((8, 128), F32)], axis=0).astype(BF16) for k in range(2)]
    features(feats[4:132, :].astype(BF16), blocks[...].reshape(8 * nc, 128).astype(BF16), *ends, rowf, colf)
    for a, b, _ in p.line:
        put(es, a, b, eb.at[c], 0)
    pltpu.make_async_copy(es, eb.at[c], recv.at[0]).start()
    elementwise(rowf, colf, z, act, cacc, rsum)
    sums(cacc, rsum, cols, col_ends, row_main, row_ends)

    for k in range(per):
        put_other(cols.at[k], k, cparts.at[rm], 6)
    pl.when(p.has_up)(lambda: put(row_ends.at[0], r - 1, c, rends.at[0], 7))
    pl.when(p.has_down)(lambda: put(row_ends.at[1], r + 1, c, rends.at[1], 8))
    pl.when(p.has_left)(lambda: put(col_ends.at[0], per * c - 1, rb, cends.at[0, rm], 9))
    pl.when(p.has_right)(lambda: put(col_ends.at[1], per * c + per, rb, cends.at[1, rm], 10))

    build_windows(act, a3)
    tap_gradient(mall, a3, gram, taps)
    def gather_sum(cond, ref, sem):
        pl.when(cond)(lambda: wait_bytes(ref, sem))
        pl.when(jnp.logical_not(cond))(lambda: ref.__setitem__(..., jnp.zeros(ref.shape, F32)))

    gather_sum(p.has_down, rends.at[0], recv.at[7])
    gather_sum(p.has_up, rends.at[1], recv.at[8])
    gather_sum(p.ends_block, cends.at[0], recv.at[9])
    gather_sum(p.starts_block, cends.at[1], recv.at[10])
    wait_bytes(cparts, recv.at[6])
    grads = (
        row_main[...] + rends[0] + rends[1],
        jnp.sum(cparts[...], axis=0) + jnp.sum(cends[0], axis=0) + jnp.sum(cends[1], axis=0),
    )
    lane = iota((16, 128), 1)
    spread = []
    for g in range(4):
        parts = [x if turn % 128 == 0 else pltpu.roll(x, turn % 128, 1) for x, turn in zip(grads, (-32 * g, 32 - 32 * g))]
        spread.append(jnp.where(lane < 32, parts[0], jnp.where(lane < 64, parts[1], 0.0)))
    turned[...] = jnp.concatenate(spread, axis=0)

    wait_bytes(eb, recv.at[0])
    e = eb[...].astype(F32)
    el[...] = e[:, 0:8].reshape(64, 256).astype(BF16)
    eh[...] = e[:, 8:16].reshape(64, 256).astype(BF16)

    high, low = halves(turned[...])
    for half, ref in enumerate((el, eh)):
        part = dot_tn(high, ref[...]) + dot_tn(low, ref[...])
        for k in range(8):
            at = slice(16 * (k // 2), 16 * (k // 2) + 16), slice(128 * (k % 2), 128 * (k % 2) + 128)
            buf[4 * (k // 2) + 2 * half + k % 2] = part[at].astype(BF16)
    for k in range(PIECES - 16):
        buf[16 + k] = taps[16 * k : 16 * k + 16, :].astype(BF16)

    owner = k1 < PIECES
    for k in range(PIECES):
        pl.when(k1 != k)(lambda k=k: put(buf.at[k], *p.plane_member(k), r1.at[k1], 11))
    pl.when(owner)(lambda: pltpu.make_async_copy(buf.at[k1], r1.at[k1], recv.at[11]).start())

    for a, b, _ in p.line:
        put(turned.at[pl.ds(pl.multiple_of(8 * b, 8), 8)], a, b, gparts.at[c], 14)
    pltpu.make_async_copy(turned.at[pl.ds(pl.multiple_of(8 * c, 8), 8)], gparts.at[c], recv.at[14]).start()

    outs = [
        pltpu.make_async_copy(out_ref.at[:, 16 * q : 16 * q + 16, :], out_hbm.at[:, 16 * q : 16 * q + 16, :], stores.at[q])
        for q in range(4)
    ]
    convolve(r, c, 0, a3, tf, out_ref)
    outs[0].start()
    convolve(r, c, 1, a3, tf, out_ref)
    outs[1].start()

    @pl.when(owner)
    def _():
        wait_bytes(r1, recv.at[11])
        mid[...] = jnp.sum(r1[...].astype(F32), axis=0).astype(BF16)
        for a, b, _ in p.group2:
            put(mid, a, b, r2.at[k2], 12)
        pltpu.make_async_copy(mid, r2.at[k2], recv.at[12]).start()

    convolve(r, c, 2, a3, tf, out_ref)
    outs[2].start()
    convolve(r, c, 3, a3, tf, out_ref)
    outs[3].start()

    @pl.when(owner)
    def _():
        wait_bytes(r2, recv.at[12])
        fin[...] = jnp.sum(r2[...].astype(F32), axis=0).astype(BF16)
        for a, b, _ in p.group1:
            put(fin, a, b, sums_hbm.at[k1], 13)
        pltpu.make_async_copy(fin, sums_hbm.at[k1], recv.at[13]).start()

    wait_bytes(gparts, recv.at[14])
    high, low = halves(jnp.sum(gparts[...], axis=0))
    eg_ref[...] = dot(high, proj[...]) + dot(low, proj[...])
    outs.append(pltpu.make_async_copy(eg_ref, eg_hbm, stores.at[4]))
    outs[4].start()

    for copy in outs:
        copy.wait()
    wait_bytes(eb.at[0 : nc - 1], send.at[0])
    wait_bytes(quad.at[0 : per - 1], send.at[1])
    pl.when(row_after)(lambda: wait_bytes(rows8, send.at[2]))
    pl.when(row_before)(lambda: wait_bytes(rows8, send.at[3]))

    def sent_targets(cond, mine, eight, seven, sem):
        pl.when(cond & mine)(lambda: wait_bytes(seven, send.at[sem]))
        pl.when(cond & jnp.logical_not(mine))(lambda: wait_bytes(eight, send.at[sem]))

    sent_targets(col_after, rb + 1 == c, rows8, rows7, 4)
    sent_targets(col_before, rb - 1 == c, rows8, rows7, 5)
    sent_targets(rb >= 0, p.in_others, blocks, blocks.at[0 : nc - 1], 15)
    pl.when(p.in_others)(lambda: wait_bytes(cparts.at[0 : per - 1], send.at[6]))
    pl.when(jnp.logical_not(p.in_others))(lambda: wait_bytes(cparts, send.at[6]))
    pl.when(p.has_up)(lambda: wait_bytes(row_ends.at[0], send.at[7]))
    pl.when(p.has_down)(lambda: wait_bytes(row_ends.at[1], send.at[8]))
    pl.when(p.has_left)(lambda: wait_bytes(col_ends.at[0], send.at[9]))
    pl.when(p.has_right)(lambda: wait_bytes(col_ends.at[1], send.at[10]))
    wait_bytes(line.at[0 : nc - 1], send.at[16])
    pl.when(owner)(lambda: wait_bytes(r1.at[0 : PIECES - 1], send.at[11]))
    pl.when(jnp.logical_not(owner))(lambda: wait_bytes(r1.at[0:PIECES], send.at[11]))
    pl.when(owner)(lambda: wait_bytes(r2.at[0 : r2.shape[0] - 1], send.at[12]))
    wait_bytes(gparts.at[0 : nc - 1], send.at[14])

    pl.when(owner)(lambda: wait_bytes(r1.at[0 : r1.shape[0] - 1], send.at[13]))
    wait_bytes(sums_hbm, recv.at[13])


def finish_kernel(
    scale, sums_in, eg_in, pair_in, conv_out, left_out, right_out, eg_out, pair_out,
    sums_ref, eg_ref, held, conv_ref, left_ref, right_ref, loads, stores,
):
    def piece(k):
        return slice(8 * k, 8 * k + 8)

    ins = [pltpu.make_async_copy(sums_in, sums_ref, loads.at[0]), pltpu.make_async_copy(eg_in, eg_ref, loads.at[1])]
    ins += [pltpu.make_async_copy(pair_in.at[piece(k)], held.at[piece(k)], loads.at[2 + k]) for k in range(4)]
    outs = [
        pltpu.make_async_copy(conv_ref, conv_out, stores.at[0]),
        pltpu.make_async_copy(left_ref, left_out, stores.at[1]),
        pltpu.make_async_copy(right_ref, right_out, stores.at[2]),
        pltpu.make_async_copy(eg_ref, eg_out, stores.at[3]),
    ]
    outs += [pltpu.make_async_copy(held.at[piece(k)], pair_out.at[piece(k)], stores.at[4 + k]) for k in range(4)]
    for copy in ins:
        copy.start()
    ins[0].wait()
    for ref, first, at in ((left_ref, 0, 1), (right_ref, 8, 2)):
        for k in range(8):
            x = sums_ref[first + k].astype(F32)
            ref[16 * (k // 4) : 16 * (k // 4) + 16, 128 * (k % 4) : 128 * (k % 4) + 128] = x * scale
        outs[at].start()
    ins[1].wait()
    outs[3].start()
    for k in range(4):
        ins[2 + k].wait()
        outs[4 + k].start()
    for k in range(9):
        q, at = divmod(k, 4)
        for part in range(2):
            x = sums_ref[16 + 2 * q + part].astype(F32)
            conv_ref[k, 16 * part : 16 * part + 16, :] = x[:, 32 * at : 32 * at + 32] * scale
    outs[0].start()
    for copy in outs:
        copy.wait()


def shards(nr, nc, embed, left_proj, right_proj, conv_w, cotangent):
    per = nr // nc
    pair_out, totals, embed_grad = pl.pallas_call(
        functools.partial(pair_kernel, nr, nc),
        out_shape=(
            jax.ShapeDtypeStruct((32, 64, 256), BF16),
            jax.ShapeDtypeStruct((PIECES, 16, 128), BF16),
            jax.ShapeDtypeStruct((8, 512), F32),
        ),
        in_specs=[HBM] * 5,
        out_specs=(HBM,) * 3,
        scratch_shapes=LOCAL_SCRATCH
        + [
            pltpu.VMEM((32, 64, 256), BF16),
            pltpu.VMEM((8, 512), F32),
            pltpu.VMEM((136, 128), F32),
            pltpu.VMEM((8, 512), BF16),
            pltpu.VMEM((9, 32, 32), BF16),
            pltpu.VMEM((32, 64, 256), BF16),
            pltpu.VMEM((8, 128), F32),
            pltpu.VMEM((8, 128), F32),
            pltpu.VMEM((8, 128), F32),
            pltpu.VMEM((per, 8, 128), F32),
            pltpu.VMEM((nc, 8, 128), F32),
            pltpu.VMEM((128, 512), BF16),
            pltpu.VMEM((16, 256), BF16),
            pltpu.VMEM((nc, 16, 256), BF16),
            pltpu.VMEM((64, 256), BF16),
            pltpu.VMEM((64, 256), BF16),
            pltpu.VMEM((nc, 8, 128), F32),
            pltpu.VMEM((2, 8, 128), F32),
            pltpu.VMEM((2, 8, 128), F32),
            pltpu.VMEM((per, 16, 128), F32),
            pltpu.VMEM((2, per, 16, 128), F32),
            pltpu.VMEM((2, 16, 128), F32),
            pltpu.VMEM((64, 128), F32),
            pltpu.VMEM((nc, 8, 128), F32),
            pltpu.VMEM((PIECES, 16, 128), BF16),
            pltpu.VMEM((32, 16, 128), BF16),
            pltpu.VMEM((8, 16, 128), BF16),
            pltpu.VMEM((16, 128), BF16),
            pltpu.VMEM((16, 128), BF16),
            pltpu.SemaphoreType.DMA((17,)),
            pltpu.SemaphoreType.DMA((17,)),
            pltpu.SemaphoreType.DMA((5,)),
            pltpu.SemaphoreType.DMA((6,)),
        ],
        compiler_params=pltpu.CompilerParams(
            collective_id=0, has_side_effects=True, vmem_limit_bytes=60 * 1024 * 1024
        ),
        name="pair_kernel",
    )(embed, left_proj.T, right_proj.T, conv_w, cotangent)
    conv_grad, left_t, right_t, embed_grad, pair_out = pl.pallas_call(
        functools.partial(finish_kernel, 32.0 / (8 * nr * nc)),
        out_shape=(
            jax.ShapeDtypeStruct((9, 32, 32), F32),
            jax.ShapeDtypeStruct((32, 512), F32),
            jax.ShapeDtypeStruct((32, 512), F32),
            jax.ShapeDtypeStruct((8, 512), F32),
            jax.ShapeDtypeStruct((32, 64, 256), BF16),
        ),
        in_specs=[HBM] * 3,
        out_specs=(HBM,) * 5,
        scratch_shapes=[
            pltpu.VMEM((PIECES, 16, 128), BF16),
            pltpu.VMEM((8, 512), F32),
            pltpu.VMEM((32, 64, 256), BF16),
            pltpu.VMEM((9, 32, 32), F32),
            pltpu.VMEM((32, 512), F32),
            pltpu.VMEM((32, 512), F32),
            pltpu.SemaphoreType.DMA((6,)),
            pltpu.SemaphoreType.DMA((8,)),
        ],
        compiler_params=pltpu.CompilerParams(vmem_limit_bytes=60 * 1024 * 1024),
        name="finish",
    )(totals, embed_grad, pair_out)
    return pair_out, conv_grad, left_t.T, right_t.T, embed_grad


def solution(mesh):
    body = functools.partial(shards, mesh.shape["row"], mesh.shape["col"])
    in_specs = (P(("row", "col"), None), P(), P(), P(), P(None, "row", "col"))
    out_specs = (P(None, "row", "col"), P(), P(), P(), P(("row", "col"), None))
    return jax.shard_map(body, mesh=mesh, in_specs=in_specs, out_specs=out_specs, check_vma=False)
```

```python
import functools

import jax
import jax.numpy as jnp
from jax import lax
from jax.experimental import pallas as pl
from jax.experimental.pallas import tpu as pltpu
from jax.sharding import PartitionSpec as P

MESH = pl.DeviceIdType.MESH
OUTSIDE = -1e30
LOG2E = 1.4426950408889634
LN2 = 0.6931471805599453
PIECES = 22
F32 = jnp.float32
BF16 = jnp.bfloat16
VMEM = pl.BlockSpec(memory_space=pltpu.VMEM)
HBM = pl.BlockSpec(memory_space=pltpu.HBM)


def iota(shape, dim):
    return lax.broadcasted_iota(jnp.int32, shape, dim)


def one_hot(cond):
    return jnp.where(cond, 1.0, 0.0).astype(BF16)


def dot(a, b):
    return jnp.dot(a, b, preferred_element_type=F32)


def dot_nt(a, b):
    return lax.dot_general(a, b, (((1,), (1,)), ((), ())), preferred_element_type=F32)


def dot_tn(a, b):
    return lax.dot_general(a, b, (((0,), (0,)), ((), ())), preferred_element_type=F32)


def halves(x):
    high = x.astype(BF16)
    return high, (x - high.astype(F32)).astype(BF16)


def loop(n, f):
    def body(k, _):
        f(k)
        return 0

    lax.fori_loop(0, n, body, 0)


def lanes(h):
    return pl.ds(pl.multiple_of(h * 256, 256), 256)


def wait_bytes(ref, sem):
    pltpu.make_async_copy(ref, ref, sem).wait()


def softplus_and_slope(y):
    t = jnp.exp2(-jnp.abs(y))
    u = 1.0 + t
    inv = pltpu.reciprocal(u, full_range=False)
    log = jnp.where(t < 2.0**-11, t * LOG2E, jnp.log2(u))
    return LN2 * (jnp.maximum(y, 0.0) + log), jnp.where(y >= 0, inv, t * inv)


def build_taps(w_ref, tf):
    spread = one_hot((iota((256, 32), 0) >> 3) == iota((256, 32), 1))
    widen = one_hot((iota((32, 256), 1) >> 3) == iota((32, 256), 0))
    s0, s1 = iota((256, 256), 0) & 7, iota((256, 256), 1) & 7
    same, above, below = s1 == s0, s1 == s0 + 4, s1 == s0 - 4
    x = dot(w_ref[...].reshape(288, 32), widen).astype(BF16)
    for b in range(3):
        x0, x1, x2 = (dot(spread, x[96 * a + 32 * b : 96 * a + 32 * b + 32]) for a in range(3))
        tf[:, 256 * b : 256 * b + 256] = jnp.where(same, x0, jnp.where(above, x1, 0.0)).astype(BF16)
        tf[:, 768 + 256 * b : 1024 + 256 * b] = jnp.where(same, x2, jnp.where(below, x1, 0.0)).astype(BF16)


def mask_cotangent(r, c, cot_ref, move, mall, mt):
    mall[0:256, 2048:2304] = jnp.zeros((256, 256), BF16)
    mall[256:512, 0:256] = jnp.zeros((256, 256), BF16)
    for k in range(4):
        x = cot_ref[:, 16 * k : 16 * k + 16, :].astype(F32)
        row = r * 64 + 16 * k + iota((16, 256), 0)
        x = jnp.where((c * 256 + iota((16, 256), 1) >= row)[None], x, 0.0)
        for half in range(2):
            m = x[:, 8 * half : 8 * half + 8].reshape(256, 256).astype(BF16)
            mall[0:256, lanes(2 * k + half)] = m
            mall[256:512, lanes(2 * k + half + 1)] = m
    for b in range(2):
        move[272 * b : 272 * b + 272, :] = one_hot(iota((272, 256), 0) - 4 * b == iota((272, 256), 1))
    mt[0] = jnp.zeros((272, 768), BF16)
    mt[9] = jnp.zeros((272, 768), BF16)
    none = jnp.zeros((8, 256), F32)

    def body(g):
        moved = dot_nt(move[...], mall[0:256, lanes(g)])
        mt[g + 1, :, 0:256] = moved[0:272].astype(BF16)
        mt[g + 1, :, 256:512] = moved[272:544].astype(BF16)
        mt[g + 1, :, 512:768] = jnp.concatenate([none, moved[0:264]], axis=0).astype(BF16)

    loop(8, body)


def input_gradient(mt, tf, z, steps):
    def body(step, _):
        left = [jnp.concatenate([mt[3 * step + k], mt[3 * step + k + 1]], axis=1) for k in range(3)]
        right = jnp.concatenate(
            [tf[:, 768 * (1 - u) + 256 * b : 768 * (1 - u) + 256 * b + 256] for u in range(2) for b in range(3)], axis=0
        )
        x = dot(jnp.concatenate(left, axis=0), right)
        for k in range(3):
            z[3 * step + k] = x[272 * k : 272 * k + 272]
        return 0

    lax.fori_loop(*steps, body, 0)


def features(rows, blocks, before, after, rowf, colf):
    k, n = iota((128, 256), 0), iota((128, 256), 1) >> 3
    picks = [one_hot(k == n + 32 * at) for at in range(4)]
    first = dot(before, picks[3])
    last = dot(after, picks[0])
    x = [first[4:8]] + [dot(blocks, pick) for pick in picks] + [last[0:4], jnp.zeros((8, 256), F32)]
    colf[...] = jnp.concatenate(x, axis=0) * LOG2E
    x = dot(rows, picks[0])
    x = jnp.where((iota((128, 256), 0) & 7) == (iota((128, 256), 1) & 7), x, 0.0).astype(BF16)
    rowf[...] = dot(one_hot((iota((16, 128), 1) >> 3) == iota((16, 128), 0)), x) * LOG2E


def elementwise(rowf, colf, z, act, cacc, rsum):
    rsum[...] = jnp.zeros_like(rsum)

    def body(step):
        parts = [pl.ds(pl.multiple_of(24 * step + 8 * part, 8), 8) for part in range(3)]
        totals = [jnp.zeros((8, 256), F32)] * 3
        for h in range(9):
            left = rowf[h : h + 1, :]
            row = jnp.zeros((8, 256), F32)
            for k, rows in enumerate(parts):
                value, slope = softplus_and_slope(colf[rows, :] + left)
                act[h, rows, :] = value
                p = z[h, rows, :] * slope
                totals[k] += p
                row += p
            rsum[8 * h : 8 * h + 8, :] += row
        for k, rows in enumerate(parts):
            cacc[rows, :] = totals[k]

    loop(11, body)


def sums(cacc, rsum, cols, col_ends, row_main, row_ends):
    k, n = iota((256, 128), 0) >> 3, iota((256, 128), 1)
    picks = [one_hot(k + 32 * g == n) for g in range(4)]
    pick = jnp.concatenate(picks, axis=0)
    x = [
        jnp.concatenate([cacc[4 + 64 * q + 16 * g : 20 + 64 * q + 16 * g, :] for g in range(4)], axis=1) for q in range(4)
    ]
    high, low = halves(jnp.concatenate(x, axis=0))
    x = dot(high, pick) + dot(low, pick)
    for q in range(4):
        cols[q] = x[16 * q : 16 * q + 16]
    sub, lane = iota((16, 128), 0), iota((16, 128), 1)
    ends = jnp.concatenate([cacc[0:8, :], cacc[256:264, :]], axis=0)
    high, low = halves(ends)
    first = dot(high, picks[3]) + dot(low, picks[3])
    second = dot(high, picks[0]) + dot(low, picks[0])
    col_ends[0] = jnp.where(sub >= 12, pltpu.roll(first, 12, 0), 0.0)
    col_ends[1] = jnp.where(sub < 4, pltpu.roll(second, 4, 0), 0.0)
    x = jnp.concatenate([rsum[...], jnp.zeros((56, 256), F32)], axis=0)
    by_group = one_hot((iota((80, 128), 0) >> 3) == (iota((80, 128), 1) >> 3))
    high, low = halves(x)
    x = dot(by_group, high) + dot(by_group, low)
    x = jnp.where((iota((80, 256), 0) & 7) == (iota((80, 256), 1) & 7), x, 0.0)
    high, low = halves(jnp.concatenate([x[4 + 16 * g : 20 + 16 * g] for g in range(4)], axis=1))
    row_main[...] = dot(high, pick) + dot(low, pick)
    ends = jnp.concatenate([x[0:8], x[64:72]], axis=0)
    high, low = halves(ends)
    first = dot(high, picks[3]) + dot(low, picks[3])
    second = dot(high, picks[0]) + dot(low, picks[0])
    row_ends[0] = jnp.where(sub >= 12, pltpu.roll(first, 12, 0), 0.0)
    row_ends[1] = jnp.where(sub < 4, pltpu.roll(second, 4, 0), 0.0)


def build_windows(act, a3):
    def body(h):
        at = pl.ds(pl.multiple_of(256 * h, 256), 256)
        for b in range(3):
            a3[at, 256 * b : 256 * b + 256] = act[h, 4 * b : 4 * b + 256, :].astype(BF16)

    loop(9, body)


def convolve(r, c, k, a3, tf, out_ref):
    parts = []
    for g in (2 * k, 2 * k + 1):
        both = jnp.concatenate([a3[256 * (g + u) : 256 * (g + u) + 256, :] for u in range(2)], axis=1)
        parts.append(dot_nt(tf[...], both).reshape(32, 8, 256))
    y = jnp.concatenate(parts, axis=1)
    row = r * 64 + 16 * k + iota((16, 256), 0)
    col = c * 256 + iota((16, 256), 1)
    out_ref[:, 16 * k : 16 * k + 16, :] = jnp.where((col >= row)[None], y, 0.0).astype(BF16)


def tap_gradient(mall, a3, gram, taps):
    x = dot(mall[...], a3[...])
    for u in range(2):
        for k in range(6):
            gram[6 * u + k] = x[256 * u : 256 * u + 256, 128 * k : 128 * k + 128]
    lane = iota((32, 128), 1)

    def along(b, k, sources):
        total = jnp.zeros((32, 128), F32)
        for at, (s, u) in enumerate(sources):
            total = jnp.where((lane & 7) == at, gram[6 * u + 2 * b + k, pl.ds(s, 32, stride=8), :], total)
        return total

    sources = (
        [(s, 0) for s in range(8)],
        [((s + 4) % 8, 1 - s // 4) for s in range(8)],
        [(s, 1) for s in range(8)],
    )
    x = [jnp.concatenate([along(b, k, sources[a]) for k in range(2)], axis=1) for a in range(3) for b in range(3)]
    y = dot(jnp.concatenate(halves(jnp.concatenate(x, axis=0)), axis=0), one_hot((iota((256, 128), 0) >> 3) == iota((256, 128), 1)))
    y = y[0:288] + y[288:576]
    for q in range(3):
        total = jnp.zeros((32, 128), F32)
        for k in range(min(4, 9 - 4 * q)):
            tap = y[32 * (4 * q + k) : 32 * (4 * q + k) + 32]
            total = jnp.where((lane >> 5) == k, pltpu.roll(tap, 32 * k, 1) if k else tap, total)
        taps[32 * q : 32 * q + 32, :] = total


LOCAL_SCRATCH = [
    pltpu.VMEM((16, 256), F32),
    pltpu.VMEM((272, 256), F32),
    pltpu.VMEM((96, 128), F32),
    pltpu.VMEM((512, 2304), BF16),
    pltpu.VMEM((10, 272, 768), BF16),
    pltpu.VMEM((9, 272, 256), F32),
    pltpu.VMEM((2304, 768), BF16),
    pltpu.VMEM((9, 272, 256), F32),
    pltpu.VMEM((256, 1536), BF16),
    pltpu.VMEM((544, 256), BF16),
    pltpu.VMEM((12, 256, 128), F32),
    pltpu.VMEM((272, 256), F32),
    pltpu.VMEM((72, 256), F32),
    pltpu.VMEM((4, 16, 128), F32),
    pltpu.VMEM((2, 16, 128), F32),
    pltpu.VMEM((16, 128), F32),
    pltpu.VMEM((2, 16, 128), F32),
]


class Place:
    def __init__(self, nr, nc):
        r, c = lax.axis_index("row"), lax.axis_index("col")
        self.r, self.c, self.nr, self.nc = r, c, nr, nc
        self.per = nr // nc
        self.rb, self.rm = lax.div(r, self.per), lax.rem(r, self.per)
        _, self.quad = self.group(((r, 1, 0), (r, 2, 0)))
        _, self.line = self.group(((c, 1, 1), (c, 2, 1), (c, 4, 1)))
        self.plane = ((r, 1, 0), (r, 8, 0), (c, 2, 1), (r, 16, 0), (c, 4, 1))
        self.k1, self.group1 = self.group(self.plane)
        self.k2, self.group2 = self.group(((r, 2, 0), (r, 4, 0), (c, 1, 1)))
        self.has_up, self.has_down = r > 0, r < nr - 1
        self.has_left, self.has_right = c > 0, c < nc - 1
        self.ends_block = (self.rm == self.per - 1) & (self.rb < nc - 1)
        self.starts_block = (self.rm == 0) & (self.rb > 0)
        self.in_others = self.rb == c

    def group(self, bits):
        number, turns = 0, []
        for k, (x, weight, is_col) in enumerate(bits):
            bit = lax.rem(lax.div(x, weight), 2)
            number = number + bit * (1 << k)
            sign = 1 - 2 * bit
            turns.append((sign * weight, is_col, sign * (1 << k)))
        members = [(self.r, self.c, number)]
        for move, is_col, step in turns:
            members += [
                (a, b + move, n + step) if is_col else (a + move, b, n + step) for a, b, n in members
            ]
        return number, members[:0:-1]

    def plane_member(self, k):
        a, b = self.r, self.c
        for at, (x, weight, is_col) in enumerate(self.plane):
            move = weight * (k >> at & 1) - weight * lax.rem(lax.div(x, weight), 2)
            a, b = (a, b + move) if is_col else (a + move, b)
        return a, b

    def other(self, k):
        return self.per * self.c + k, self.rb

    def targets(self, col):
        return [(lax.rem(self.r + self.per * k, self.nr), col) for k in range(self.nr // self.per)]

    def greet(self):
        r, c, nc, per, rb, rm = self.r, self.c, self.nc, self.per, self.rb, self.rm
        barrier = pltpu.get_barrier_semaphore()

        def signal(a, b):
            pl.semaphore_signal(barrier, inc=1, device_id=(a, b), device_id_type=MESH)

        def signal_all(col):
            for k in range(per):
                signal(per * c + k, col)

        is_first, is_last = c == 0, c == nc - 1
        before_is_me = is_last & (rb == nc - 2)
        after_is_me = is_first & (rb == 1)
        for a, b, _ in self.quad + self.line:
            signal(a, b)
        pl.when(jnp.logical_not(self.in_others))(lambda: signal(per * c + rm, c))
        for _, b, _ in self.line:
            signal(per * c + rm, b)
        pl.when(self.has_up)(lambda: signal(r - 1, nc - 1))
        pl.when(self.has_down)(lambda: signal(r + 1, 0))
        pl.when(self.has_left & jnp.logical_not(before_is_me))(lambda: signal(per * (c - 1) + rm, nc - 1))
        pl.when(self.has_right & jnp.logical_not(after_is_me))(lambda: signal(per * (c + 1) + rm, 0))
        pl.when(jnp.logical_not(self.in_others))(lambda: signal(per * c + rm, rb))
        for a, _, _ in self.quad:
            signal(per * (c - rb) + a, rb)
        pl.when(self.has_up)(lambda: signal(r - 1, c))
        pl.when(self.has_down)(lambda: signal(r + 1, c))
        pl.when(self.ends_block)(lambda: signal_all(rb + 1))
        pl.when(self.starts_block)(lambda: signal_all(rb - 1))
        owner = self.k1 < PIECES

        @pl.when(owner)
        def _():
            for a, b, _ in self.group1 + self.group2:
                signal(a, b)

        @pl.when(jnp.logical_not(owner))
        def _():
            for k in range(PIECES):
                signal(*self.plane_member(k))

        n = len(self.quad + self.line) + nc + per
        n = n + jnp.where(owner, len(self.group1 + self.group2), PIECES)
        up, down = self.has_up, self.has_down
        for cond, m in (
            (self.in_others, -2), (is_last & down, nc), (is_first & up, nc),
            (is_last & (rb < nc - 1), nc), (before_is_me, -1), (is_first & (rb > 0), nc), (after_is_me, -1),
            (up, 1), (down, 1), (self.has_left, 1), (self.has_right, 1),
        ):
            n = n + jnp.where(cond, m, 0)
        return n

    def senders(self, send, recv):
        def put(src, dst_r, dst_c, dst, sem):
            pltpu.make_async_remote_copy(
                src, dst, send.at[sem], recv.at[sem], device_id=(dst_r, dst_c), device_id_type=MESH
            ).start()

        def put_other(src, k, dst, sem):
            a, b = self.other(k)
            mine = (a == self.r) & (b == self.c)
            pl.when(mine)(lambda: pltpu.make_async_copy(src, dst, recv.at[sem]).start())
            pl.when(jnp.logical_not(mine))(lambda: put(src, a, b, dst, sem))

        return put, put_other


def pair_kernel(
    nr, nc, e_hbm, lpt_hbm, rpt_hbm, w_hbm, cot_hbm,
    out_hbm, sums_hbm, eg_hbm,
    rowf, colf, taps, mall, mt, act, a3, z, tf, move, gram, cacc, rsum, cols, col_ends, row_main, row_ends,
    out_ref, eg_ref, feats, e_ref, w_ref, cot_ref, own, right, packed, quad, line, proj, es, eb, el, eh, blocks, row_feats, col_feats,
    cparts, cends, rends, turned, gparts, buf, r1, r2, mid, fin, recv, send, loads, stores,
):
    ins = ((e_hbm, e_ref), (w_hbm, w_ref), (lpt_hbm, proj.at[0:32]), (rpt_hbm, proj.at[32:64]), (cot_hbm, cot_ref))
    ins = [pltpu.make_async_copy(src, dst, loads.at[k]) for k, (src, dst) in enumerate(ins)]
    for copy in ins:
        copy.start()
    p = Place(nr, nc)
    r, c, per, rb, rm, k1, k2 = p.r, p.c, p.per, p.rb, p.rm, p.k1, p.k2
    greeted = p.greet()
    put, put_other = p.senders(send, recv)
    rows8, rows7 = gparts, gparts.at[0 : nc - 1]

    proj[64:128, :] = jnp.zeros((64, 512), BF16)
    ins[0].wait()
    e = e_ref[...].astype(F32)
    es[...] = jnp.concatenate([e[:, 0:256], e[:, 256:512]], axis=0).astype(BF16)
    ins[2].wait()
    ins[3].wait()
    own[...] = dot_nt(e_ref[...], proj[...]).astype(BF16).astype(F32)
    group = iota((8, 128), 1) >> 5
    right[...] = jnp.where(group == rm, pltpu.roll(own[...], lax.rem(32 * rm + 96, 128), 1), 0.0)
    ins[1].wait()
    build_taps(w_ref, tf)
    ins[4].wait()
    mask_cotangent(r, c, cot_ref, move, mall, mt)
    pl.semaphore_wait(pltpu.get_barrier_semaphore(), greeted)

    for a, b, _ in p.quad:
        put(right, a, b, quad.at[rm], 1)
    pltpu.make_async_copy(right, quad.at[rm], recv.at[1]).start()

    def put_line(row, dst, sem):
        for k in range(nc):
            put(own, row, k, dst, sem)

    is_first, is_last = c == 0, c == nc - 1
    row_after, row_before = is_last & p.has_down, is_first & p.has_up
    pl.when(row_after)(lambda: put_line(r + 1, row_feats.at[0], 2))
    pl.when(row_before)(lambda: put_line(r - 1, row_feats.at[1], 3))
    for a, b, _ in p.line:
        put(own, a, b, line.at[c], 16)
    pltpu.make_async_copy(own, line.at[c], recv.at[16]).start()

    def put_targets(src, col, dst, sem):
        first, *rest = p.targets(col)
        mine = c == col
        pl.when(mine)(lambda: pltpu.make_async_copy(src, dst, recv.at[sem]).start())
        pl.when(jnp.logical_not(mine))(lambda: put(src, *first, dst, sem))
        for a, b in rest:
            put(src, a, b, dst, sem)

    col_after, col_before = is_last & (rb < nc - 1), is_first & (rb > 0)
    input_gradient(mt, tf, z, (0, 1))
    wait_bytes(quad, recv.at[1])
    packed[...] = jnp.sum(quad[...], axis=0)
    put_targets(packed, rb, blocks.at[c], 15)
    pl.when(col_after)(lambda: put_targets(packed, rb + 1, col_feats.at[0], 4))
    pl.when(col_before)(lambda: put_targets(packed, rb - 1, col_feats.at[1], 5))
    input_gradient(mt, tf, z, (1, 3))

    def arrive(cond, ref, sem):
        pl.when(cond)(lambda: wait_bytes(ref, sem))
        pl.when(jnp.logical_not(cond))(lambda: ref.__setitem__(..., jnp.full(ref.shape, OUTSIDE, F32)))

    arrive(p.has_up, row_feats.at[0], recv.at[2])
    arrive(p.has_down, row_feats.at[1], recv.at[3])
    arrive(p.has_left, col_feats.at[0], recv.at[4])
    arrive(p.has_right, col_feats.at[1], recv.at[5])
    wait_bytes(line, recv.at[16])
    wait_bytes(blocks, recv.at[15])
    feats[8:72, :] = line[...].reshape(8 * nc, 128)
    feats[0:8, :] = row_feats[0]
    feats[72:80, :] = row_feats[1]
    feats[80:136, :] = jnp.zeros((56, 128), F32)
    ends = [jnp.concatenate([col_feats[k], jnp.zeros((8, 128), F32)], axis=0).astype(BF16) for k in range(2)]
    features(feats[4:132, :].astype(BF16), blocks[...].reshape(8 * nc, 128).astype(BF16), *ends, rowf, colf)
    for a, b, _ in p.line:
        put(es, a, b, eb.at[c], 0)
    pltpu.make_async_copy(es, eb.at[c], recv.at[0]).start()
    elementwise(rowf, colf, z, act, cacc, rsum)
    sums(cacc, rsum, cols, col_ends, row_main, row_ends)

    for k in range(per):
        put_other(cols.at[k], k, cparts.at[rm], 6)
    pl.when(p.has_up)(lambda: put(row_ends.at[0], r - 1, c, rends.at[0], 7))
    pl.when(p.has_down)(lambda: put(row_ends.at[1], r + 1, c, rends.at[1], 8))
    pl.when(p.has_left)(lambda: put(col_ends.at[0], per * c - 1, rb, cends.at[0, rm], 9))
    pl.when(p.has_right)(lambda: put(col_ends.at[1], per * c + per, rb, cends.at[1, rm], 10))

    build_windows(act, a3)
    tap_gradient(mall, a3, gram, taps)
    def gather_sum(cond, ref, sem):
        pl.when(cond)(lambda: wait_bytes(ref, sem))
        pl.when(jnp.logical_not(cond))(lambda: ref.__setitem__(..., jnp.zeros(ref.shape, F32)))

    gather_sum(p.has_down, rends.at[0], recv.at[7])
    gather_sum(p.has_up, rends.at[1], recv.at[8])
    gather_sum(p.ends_block, cends.at[0], recv.at[9])
    gather_sum(p.starts_block, cends.at[1], recv.at[10])
    wait_bytes(cparts, recv.at[6])
    grads = (
        row_main[...] + rends[0] + rends[1],
        jnp.sum(cparts[...], axis=0) + jnp.sum(cends[0], axis=0) + jnp.sum(cends[1], axis=0),
    )
    lane = iota((16, 128), 1)
    spread = []
    for g in range(4):
        parts = [x if turn % 128 == 0 else pltpu.roll(x, turn % 128, 1) for x, turn in zip(grads, (-32 * g, 32 - 32 * g))]
        spread.append(jnp.where(lane < 32, parts[0], jnp.where(lane < 64, parts[1], 0.0)))
    turned[...] = jnp.concatenate(spread, axis=0)

    wait_bytes(eb, recv.at[0])
    e = eb[...].astype(F32)
    el[...] = e[:, 0:8].reshape(64, 256).astype(BF16)
    eh[...] = e[:, 8:16].reshape(64, 256).astype(BF16)

    high, low = halves(turned[...])
    for half, ref in enumerate((el, eh)):
        part = dot_tn(high, ref[...]) + dot_tn(low, ref[...])
        for k in range(8):
            at = slice(16 * (k // 2), 16 * (k // 2) + 16), slice(128 * (k % 2), 128 * (k % 2) + 128)
            buf[4 * (k // 2) + 2 * half + k % 2] = part[at].astype(BF16)
    for k in range(PIECES - 16):
        buf[16 + k] = taps[16 * k : 16 * k + 16, :].astype(BF16)

    owner = k1 < PIECES
    for k in range(PIECES):
        pl.when(k1 != k)(lambda k=k: put(buf.at[k], *p.plane_member(k), r1.at[k1], 11))
    pl.when(owner)(lambda: pltpu.make_async_copy(buf.at[k1], r1.at[k1], recv.at[11]).start())

    for a, b, _ in p.line:
        put(turned.at[pl.ds(pl.multiple_of(8 * b, 8), 8)], a, b, gparts.at[c], 14)
    pltpu.make_async_copy(turned.at[pl.ds(pl.multiple_of(8 * c, 8), 8)], gparts.at[c], recv.at[14]).start()

    outs = [
        pltpu.make_async_copy(out_ref.at[:, 16 * q : 16 * q + 16, :], out_hbm.at[:, 16 * q : 16 * q + 16, :], stores.at[q])
        for q in range(4)
    ]
    convolve(r, c, 0, a3, tf, out_ref)
    outs[0].start()
    convolve(r, c, 1, a3, tf, out_ref)
    outs[1].start()

    @pl.when(owner)
    def _():
        wait_bytes(r1, recv.at[11])
        mid[...] = jnp.sum(r1[...].astype(F32), axis=0).astype(BF16)
        for a, b, _ in p.group2:
            put(mid, a, b, r2.at[k2], 12)
        pltpu.make_async_copy(mid, r2.at[k2], recv.at[12]).start()

    convolve(r, c, 2, a3, tf, out_ref)
    outs[2].start()
    convolve(r, c, 3, a3, tf, out_ref)
    outs[3].start()

    @pl.when(owner)
    def _():
        wait_bytes(r2, recv.at[12])
        fin[...] = jnp.sum(r2[...].astype(F32), axis=0).astype(BF16)
        for a, b, _ in p.group1:
            put(fin, a, b, sums_hbm.at[k1], 13)
        pltpu.make_async_copy(fin, sums_hbm.at[k1], recv.at[13]).start()

    wait_bytes(gparts, recv.at[14])
    high, low = halves(jnp.sum(gparts[...], axis=0))
    eg_ref[...] = dot(high, proj[...]) + dot(low, proj[...])
    outs.append(pltpu.make_async_copy(eg_ref, eg_hbm, stores.at[4]))
    outs[4].start()

    for copy in outs:
        copy.wait()
    wait_bytes(eb.at[0 : nc - 1], send.at[0])
    wait_bytes(quad.at[0 : per - 1], send.at[1])
    pl.when(row_after)(lambda: wait_bytes(rows8, send.at[2]))
    pl.when(row_before)(lambda: wait_bytes(rows8, send.at[3]))

    def sent_targets(cond, mine, eight, seven, sem):
        pl.when(cond & mine)(lambda: wait_bytes(seven, send.at[sem]))
        pl.when(cond & jnp.logical_not(mine))(lambda: wait_bytes(eight, send.at[sem]))

    sent_targets(col_after, rb + 1 == c, rows8, rows7, 4)
    sent_targets(col_before, rb - 1 == c, rows8, rows7, 5)
    sent_targets(rb >= 0, p.in_others, blocks, blocks.at[0 : nc - 1], 15)
    pl.when(p.in_others)(lambda: wait_bytes(cparts.at[0 : per - 1], send.at[6]))
    pl.when(jnp.logical_not(p.in_others))(lambda: wait_bytes(cparts, send.at[6]))
    pl.when(p.has_up)(lambda: wait_bytes(row_ends.at[0], send.at[7]))
    pl.when(p.has_down)(lambda: wait_bytes(row_ends.at[1], send.at[8]))
    pl.when(p.has_left)(lambda: wait_bytes(col_ends.at[0], send.at[9]))
    pl.when(p.has_right)(lambda: wait_bytes(col_ends.at[1], send.at[10]))
    wait_bytes(line.at[0 : nc - 1], send.at[16])
    pl.when(owner)(lambda: wait_bytes(r1.at[0 : PIECES - 1], send.at[11]))
    pl.when(jnp.logical_not(owner))(lambda: wait_bytes(r1.at[0:PIECES], send.at[11]))
    pl.when(owner)(lambda: wait_bytes(r2.at[0 : r2.shape[0] - 1], send.at[12]))
    wait_bytes(gparts.at[0 : nc - 1], send.at[14])

    pl.when(owner)(lambda: wait_bytes(r1.at[0 : r1.shape[0] - 1], send.at[13]))
    wait_bytes(sums_hbm, recv.at[13])


def finish_kernel(
    scale, sums_in, eg_in, pair_in, conv_out, left_out, right_out, eg_out, pair_out,
    sums_ref, eg_ref, held, conv_ref, left_ref, right_ref, loads, stores,
):
    def piece(k):
        return slice(8 * k, 8 * k + 8)

    ins = [pltpu.make_async_copy(sums_in, sums_ref, loads.at[0]), pltpu.make_async_copy(eg_in, eg_ref, loads.at[1])]
    ins += [pltpu.make_async_copy(pair_in.at[piece(k)], held.at[piece(k)], loads.at[2 + k]) for k in range(4)]
    outs = [
        pltpu.make_async_copy(conv_ref, conv_out, stores.at[0]),
        pltpu.make_async_copy(left_ref, left_out, stores.at[1]),
        pltpu.make_async_copy(right_ref, right_out, stores.at[2]),
        pltpu.make_async_copy(eg_ref, eg_out, stores.at[3]),
    ]
    outs += [pltpu.make_async_copy(held.at[piece(k)], pair_out.at[piece(k)], stores.at[4 + k]) for k in range(4)]
    for copy in ins:
        copy.start()
    ins[0].wait()
    for ref, first, at in ((left_ref, 0, 1), (right_ref, 8, 2)):
        for k in range(8):
            x = sums_ref[first + k].astype(F32)
            ref[16 * (k // 4) : 16 * (k // 4) + 16, 128 * (k % 4) : 128 * (k % 4) + 128] = x * scale
        outs[at].start()
    ins[1].wait()
    outs[3].start()
    for k in range(4):
        ins[2 + k].wait()
        outs[4 + k].start()
    for k in range(9):
        q, at = divmod(k, 4)
        for part in range(2):
            x = sums_ref[16 + 2 * q + part].astype(F32)
            conv_ref[k, 16 * part : 16 * part + 16, :] = x[:, 32 * at : 32 * at + 32] * scale
    outs[0].start()
    for copy in outs:
        copy.wait()


def shards(nr, nc, embed, left_proj, right_proj, conv_w, cotangent):
    per = nr // nc
    pair_out, totals, embed_grad = pl.pallas_call(
        functools.partial(pair_kernel, nr, nc),
        out_shape=(
            jax.ShapeDtypeStruct((32, 64, 256), BF16),
            jax.ShapeDtypeStruct((PIECES, 16, 128), BF16),
            jax.ShapeDtypeStruct((8, 512), F32),
        ),
        in_specs=[HBM] * 5,
        out_specs=(HBM,) * 3,
        scratch_shapes=LOCAL_SCRATCH
        + [
            pltpu.VMEM((32, 64, 256), BF16),
            pltpu.VMEM((8, 512), F32),
            pltpu.VMEM((136, 128), F32),
            pltpu.VMEM((8, 512), BF16),
            pltpu.VMEM((9, 32, 32), BF16),
            pltpu.VMEM((32, 64, 256), BF16),
            pltpu.VMEM((8, 128), F32),
            pltpu.VMEM((8, 128), F32),
            pltpu.VMEM((8, 128), F32),
            pltpu.VMEM((per, 8, 128), F32),
            pltpu.VMEM((nc, 8, 128), F32),
            pltpu.VMEM((128, 512), BF16),
            pltpu.VMEM((16, 256), BF16),
            pltpu.VMEM((nc, 16, 256), BF16),
            pltpu.VMEM((64, 256), BF16),
            pltpu.VMEM((64, 256), BF16),
            pltpu.VMEM((nc, 8, 128), F32),
            pltpu.VMEM((2, 8, 128), F32),
            pltpu.VMEM((2, 8, 128), F32),
            pltpu.VMEM((per, 16, 128), F32),
            pltpu.VMEM((2, per, 16, 128), F32),
            pltpu.VMEM((2, 16, 128), F32),
            pltpu.VMEM((64, 128), F32),
            pltpu.VMEM((nc, 8, 128), F32),
            pltpu.VMEM((PIECES, 16, 128), BF16),
            pltpu.VMEM((32, 16, 128), BF16),
            pltpu.VMEM((8, 16, 128), BF16),
            pltpu.VMEM((16, 128), BF16),
            pltpu.VMEM((16, 128), BF16),
            pltpu.SemaphoreType.DMA((17,)),
            pltpu.SemaphoreType.DMA((17,)),
            pltpu.SemaphoreType.DMA((5,)),
            pltpu.SemaphoreType.DMA((6,)),
        ],
        compiler_params=pltpu.CompilerParams(
            collective_id=0, has_side_effects=True, vmem_limit_bytes=60 * 1024 * 1024
        ),
        name="pair_kernel",
    )(embed, left_proj.T, right_proj.T, conv_w, cotangent)
    conv_grad, left_t, right_t, embed_grad, pair_out = pl.pallas_call(
        functools.partial(finish_kernel, 32.0 / (8 * nr * nc)),
        out_shape=(
            jax.ShapeDtypeStruct((9, 32, 32), F32),
            jax.ShapeDtypeStruct((32, 512), F32),
            jax.ShapeDtypeStruct((32, 512), F32),
            jax.ShapeDtypeStruct((8, 512), F32),
            jax.ShapeDtypeStruct((32, 64, 256), BF16),
        ),
        in_specs=[HBM] * 3,
        out_specs=(HBM,) * 5,
        scratch_shapes=[
            pltpu.VMEM((PIECES, 16, 128), BF16),
            pltpu.VMEM((8, 512), F32),
            pltpu.VMEM((32, 64, 256), BF16),
            pltpu.VMEM((9, 32, 32), F32),
            pltpu.VMEM((32, 512), F32),
            pltpu.VMEM((32, 512), F32),
            pltpu.SemaphoreType.DMA((6,)),
            pltpu.SemaphoreType.DMA((8,)),
        ],
        compiler_params=pltpu.CompilerParams(vmem_limit_bytes=60 * 1024 * 1024),
        name="finish",
    )(totals, embed_grad, pair_out)
    return pair_out, conv_grad, left_t.T, right_t.T, embed_grad


def solution(mesh):
    body = functools.partial(shards, mesh.shape["row"], mesh.shape["col"])
    in_specs = (P(("row", "col"), None), P(), P(), P(), P(None, "row", "col"))
    out_specs = (P(None, "row", "col"), P(), P(), P(), P(("row", "col"), None))
    return jax.shard_map(body, mesh=mesh, in_specs=in_specs, out_specs=out_specs, check_vma=False)
```

```python
import functools

import jax
import jax.numpy as jnp
from jax import lax
from jax.experimental import pallas as pl
from jax.experimental.pallas import tpu as pltpu
from jax.sharding import PartitionSpec as P

MESH = pl.DeviceIdType.MESH
OUTSIDE = -1e30
LOG2E = 1.4426950408889634
LN2 = 0.6931471805599453
PIECES = 22
F32 = jnp.float32
BF16 = jnp.bfloat16
VMEM = pl.BlockSpec(memory_space=pltpu.VMEM)
HBM = pl.BlockSpec(memory_space=pltpu.HBM)


def iota(shape, dim):
    return lax.broadcasted_iota(jnp.int32, shape, dim)


def one_hot(cond):
    return jnp.where(cond, 1.0, 0.0).astype(BF16)


def dot(a, b):
    return jnp.dot(a, b, preferred_element_type=F32)


def dot_nt(a, b):
    return lax.dot_general(a, b, (((1,), (1,)), ((), ())), preferred_element_type=F32)


def dot_tn(a, b):
    return lax.dot_general(a, b, (((0,), (0,)), ((), ())), preferred_element_type=F32)


def halves(x):
    high = x.astype(BF16)
    return high, (x - high.astype(F32)).astype(BF16)


def loop(n, f):
    def body(k, _):
        f(k)
        return 0

    lax.fori_loop(0, n, body, 0)


def lanes(h):
    return pl.ds(pl.multiple_of(h * 256, 256), 256)


def wait_bytes(ref, sem):
    pltpu.make_async_copy(ref, ref, sem).wait()


def softplus_and_slope(y):
    t = jnp.exp2(-jnp.abs(y))
    u = 1.0 + t
    inv = pltpu.reciprocal(u, full_range=False)
    log = jnp.where(t < 2.0**-11, t * LOG2E, jnp.log2(u))
    return LN2 * (jnp.maximum(y, 0.0) + log), jnp.where(y >= 0, inv, t * inv)


def build_taps(w_ref, tf):
    spread = one_hot((iota((256, 32), 0) >> 3) == iota((256, 32), 1))
    widen = one_hot((iota((32, 256), 1) >> 3) == iota((32, 256), 0))
    s0, s1 = iota((256, 256), 0) & 7, iota((256, 256), 1) & 7
    same, above, below = s1 == s0, s1 == s0 + 4, s1 == s0 - 4
    x = dot(w_ref[...].reshape(288, 32), widen).astype(BF16)
    for b in range(3):
        x0, x1, x2 = (dot(spread, x[96 * a + 32 * b : 96 * a + 32 * b + 32]) for a in range(3))
        tf[:, 256 * b : 256 * b + 256] = jnp.where(same, x0, jnp.where(above, x1, 0.0)).astype(BF16)
        tf[:, 768 + 256 * b : 1024 + 256 * b] = jnp.where(same, x2, jnp.where(below, x1, 0.0)).astype(BF16)


def mask_cotangent(r, c, cot_ref, move, mall, mt):
    mall[0:256, 2048:2304] = jnp.zeros((256, 256), BF16)
    mall[256:512, 0:256] = jnp.zeros((256, 256), BF16)
    for k in range(4):
        x = cot_ref[:, 16 * k : 16 * k + 16, :].astype(F32)
        row = r * 64 + 16 * k + iota((16, 256), 0)
        x = jnp.where((c * 256 + iota((16, 256), 1) >= row)[None], x, 0.0)
        for half in range(2):
            m = x[:, 8 * half : 8 * half + 8].reshape(256, 256).astype(BF16)
            mall[0:256, lanes(2 * k + half)] = m
            mall[256:512, lanes(2 * k + half + 1)] = m
    for b in range(2):
        move[272 * b : 272 * b + 272, :] = one_hot(iota((272, 256), 0) - 4 * b == iota((272, 256), 1))
    mt[0] = jnp.zeros((272, 768), BF16)
    mt[9] = jnp.zeros((272, 768), BF16)
    none = jnp.zeros((8, 256), F32)

    def body(g):
        moved = dot_nt(move[...], mall[0:256, lanes(g)])
        mt[g + 1, :, 0:256] = moved[0:272].astype(BF16)
        mt[g + 1, :, 256:512] = moved[272:544].astype(BF16)
        mt[g + 1, :, 512:768] = jnp.concatenate([none, moved[0:264]], axis=0).astype(BF16)

    loop(8, body)


def input_gradient(mt, tf, z, steps):
    def body(step, _):
        left = [jnp.concatenate([mt[3 * step + k], mt[3 * step + k + 1]], axis=1) for k in range(3)]
        right = jnp.concatenate(
            [tf[:, 768 * (1 - u) + 256 * b : 768 * (1 - u) + 256 * b + 256] for u in range(2) for b in range(3)], axis=0
        )
        x = dot(jnp.concatenate(left, axis=0), right)
        for k in range(3):
            z[3 * step + k] = x[272 * k : 272 * k + 272]
        return 0

    lax.fori_loop(*steps, body, 0)


def features(rows, blocks, before, after, onto, rowf, colf):
    picks = [onto[:, 256 * at : 256 * at + 256] for at in range(4)]
    first = dot(before, picks[3])
    last = dot(after, picks[0])
    x = [first[4:8]] + [dot(blocks, pick) for pick in picks] + [last[0:4], jnp.zeros((8, 256), F32)]
    colf[...] = jnp.concatenate(x, axis=0) * LOG2E
    x = dot(rows, picks[0])
    x = jnp.where((iota((128, 256), 0) & 7) == (iota((128, 256), 1) & 7), x, 0.0).astype(BF16)
    rowf[...] = dot(one_hot((iota((16, 128), 1) >> 3) == iota((16, 128), 0)), x) * LOG2E


def elementwise(rowf, colf, z, act, cacc, rsum):
    rsum[...] = jnp.zeros_like(rsum)

    def body(step):
        parts = [pl.ds(pl.multiple_of(24 * step + 8 * part, 8), 8) for part in range(3)]
        totals = [jnp.zeros((8, 256), F32)] * 3
        for h in range(9):
            left = rowf[h : h + 1, :]
            row = jnp.zeros((8, 256), F32)
            for k, rows in enumerate(parts):
                value, slope = softplus_and_slope(colf[rows, :] + left)
                act[h, rows, :] = value
                p = z[h, rows, :] * slope
                totals[k] += p
                row += p
            rsum[8 * h : 8 * h + 8, :] += row
        for k, rows in enumerate(parts):
            cacc[rows, :] = totals[k]

    loop(11, body)


def build_constants(onto, pick, by_group):
    k, n = iota((128, 256), 0), iota((128, 256), 1) >> 3
    for at in range(4):
        onto[:, 256 * at : 256 * at + 256] = one_hot(k == n + 32 * at)
    k, n = iota((256, 128), 0) >> 3, iota((256, 128), 1)
    for g in range(4):
        pick[256 * g : 256 * g + 256, :] = one_hot(k + 32 * g == n)
    by_group[...] = one_hot((iota((80, 128), 0) >> 3) == (iota((80, 128), 1) >> 3))


def ends_of(x, pick, ends):
    sub = iota((16, 128), 0)
    high, low = halves(x)
    first = dot(high, pick[768:1024]) + dot(low, pick[768:1024])
    second = dot(high, pick[0:256]) + dot(low, pick[0:256])
    ends[0] = jnp.where(sub >= 12, pltpu.roll(first, 12, 0), 0.0)
    ends[1] = jnp.where(sub < 4, pltpu.roll(second, 4, 0), 0.0)


def column_sums(cacc, pick, cols):
    x = [
        jnp.concatenate([cacc[4 + 64 * q + 16 * g : 20 + 64 * q + 16 * g, :] for g in range(4)], axis=1) for q in range(4)
    ]
    high, low = halves(jnp.concatenate(x, axis=0))
    x = dot(high, pick[...]) + dot(low, pick[...])
    for q in range(4):
        cols[q] = x[16 * q : 16 * q + 16]


def column_end_sums(cacc, pick, col_ends):
    ends_of(jnp.concatenate([cacc[0:8, :], cacc[256:264, :]], axis=0), pick, col_ends)


def row_sums(rsum, pick, by_group, row_main, row_ends):
    x = jnp.concatenate([rsum[...], jnp.zeros((56, 256), F32)], axis=0)
    high, low = halves(x)
    x = dot(by_group[...], high) + dot(by_group[...], low)
    x = jnp.where((iota((80, 256), 0) & 7) == (iota((80, 256), 1) & 7), x, 0.0)
    ends_of(jnp.concatenate([x[0:8], x[64:72]], axis=0), pick, row_ends)
    high, low = halves(jnp.concatenate([x[4 + 16 * g : 20 + 16 * g] for g in range(4)], axis=1))
    row_main[...] = dot(high, pick[...]) + dot(low, pick[...])


def build_windows(act, a3):
    def body(h):
        at = pl.ds(pl.multiple_of(256 * h, 256), 256)
        for b in range(3):
            a3[at, 256 * b : 256 * b + 256] = act[h, 4 * b : 4 * b + 256, :].astype(BF16)

    loop(9, body)


def convolve(r, c, k, a3, tf, out_ref):
    parts = []
    for g in (2 * k, 2 * k + 1):
        both = jnp.concatenate([a3[256 * (g + u) : 256 * (g + u) + 256, :] for u in range(2)], axis=1)
        parts.append(dot_nt(tf[...], both).reshape(32, 8, 256))
    y = jnp.concatenate(parts, axis=1)
    row = r * 64 + 16 * k + iota((16, 256), 0)
    col = c * 256 + iota((16, 256), 1)
    out_ref[:, 16 * k : 16 * k + 16, :] = jnp.where((col >= row)[None], y, 0.0).astype(BF16)


def tap_gradient(mall, a3, pick, gram, taps):
    x = dot(mall[...], a3[...])
    for u in range(2):
        for k in range(6):
            gram[6 * u + k] = x[256 * u : 256 * u + 256, 128 * k : 128 * k + 128]
    lane = iota((32, 128), 1)

    def along(b, k, sources):
        total = jnp.zeros((32, 128), F32)
        for at, (s, u) in enumerate(sources):
            total = jnp.where((lane & 7) == at, gram[6 * u + 2 * b + k, pl.ds(s, 32, stride=8), :], total)
        return total

    sources = (
        [(s, 0) for s in range(8)],
        [((s + 4) % 8, 1 - s // 4) for s in range(8)],
        [(s, 1) for s in range(8)],
    )
    x = [jnp.concatenate([along(b, k, sources[a]) for k in range(2)], axis=1) for a in range(3) for b in range(3)]
    y = dot(jnp.concatenate(halves(jnp.concatenate(x, axis=0)), axis=0), pick[0:256])
    y = y[0:288] + y[288:576]
    for q in range(3):
        total = jnp.zeros((32, 128), F32)
        for k in range(min(4, 9 - 4 * q)):
            tap = y[32 * (4 * q + k) : 32 * (4 * q + k) + 32]
            total = jnp.where((lane >> 5) == k, pltpu.roll(tap, 32 * k, 1) if k else tap, total)
        taps[32 * q : 32 * q + 32, :] = total


LOCAL_SCRATCH = [
    pltpu.VMEM((16, 256), F32),
    pltpu.VMEM((272, 256), F32),
    pltpu.VMEM((96, 128), F32),
    pltpu.VMEM((512, 2304), BF16),
    pltpu.VMEM((10, 272, 768), BF16),
    pltpu.VMEM((9, 272, 256), F32),
    pltpu.VMEM((2304, 768), BF16),
    pltpu.VMEM((9, 272, 256), F32),
    pltpu.VMEM((256, 1536), BF16),
    pltpu.VMEM((544, 256), BF16),
    pltpu.VMEM((128, 1024), BF16),
    pltpu.VMEM((1024, 128), BF16),
    pltpu.VMEM((80, 128), BF16),
    pltpu.VMEM((12, 256, 128), F32),
    pltpu.VMEM((272, 256), F32),
    pltpu.VMEM((72, 256), F32),
    pltpu.VMEM((4, 16, 128), F32),
    pltpu.VMEM((2, 16, 128), F32),
    pltpu.VMEM((16, 128), F32),
    pltpu.VMEM((2, 16, 128), F32),
]


class Place:
    def __init__(self, nr, nc):
        r, c = lax.axis_index("row"), lax.axis_index("col")
        self.r, self.c, self.nr, self.nc = r, c, nr, nc
        self.per = nr // nc
        self.rb, self.rm = lax.div(r, self.per), lax.rem(r, self.per)
        _, self.quad = self.group(((r, 1, 0), (r, 2, 0)))
        _, self.line = self.group(((c, 1, 1), (c, 2, 1), (c, 4, 1)))
        self.plane = ((r, 1, 0), (r, 8, 0), (c, 2, 1), (r, 16, 0), (c, 4, 1))
        self.k1, self.group1 = self.group(self.plane)
        self.k2, self.group2 = self.group(((r, 2, 0), (r, 4, 0), (c, 1, 1)))
        self.has_up, self.has_down = r > 0, r < nr - 1
        self.has_left, self.has_right = c > 0, c < nc - 1
        self.ends_block = (self.rm == self.per - 1) & (self.rb < nc - 1)
        self.starts_block = (self.rm == 0) & (self.rb > 0)
        self.in_others = self.rb == c

    def group(self, bits):
        number, turns = 0, []
        for k, (x, weight, is_col) in enumerate(bits):
            bit = lax.rem(lax.div(x, weight), 2)
            number = number + bit * (1 << k)
            sign = 1 - 2 * bit
            turns.append((sign * weight, is_col, sign * (1 << k)))
        members = [(self.r, self.c, number)]
        for move, is_col, step in turns:
            members += [
                (a, b + move, n + step) if is_col else (a + move, b, n + step) for a, b, n in members
            ]
        return number, members[:0:-1]

    def plane_member(self, k):
        a, b = self.r, self.c
        for at, (x, weight, is_col) in enumerate(self.plane):
            move = weight * (k >> at & 1) - weight * lax.rem(lax.div(x, weight), 2)
            a, b = (a, b + move) if is_col else (a + move, b)
        return a, b

    def other(self, k):
        return self.per * self.c + k, self.rb

    def targets(self, col):
        return [(lax.rem(self.r + self.per * k, self.nr), col) for k in range(self.nr // self.per)]

    def greet(self):
        r, c, nc, per, rb, rm = self.r, self.c, self.nc, self.per, self.rb, self.rm
        barrier = pltpu.get_barrier_semaphore()

        def signal(a, b):
            pl.semaphore_signal(barrier, inc=1, device_id=(a, b), device_id_type=MESH)

        def signal_all(col):
            for k in range(per):
                signal(per * c + k, col)

        is_first, is_last = c == 0, c == nc - 1
        before_is_me = is_last & (rb == nc - 2)
        after_is_me = is_first & (rb == 1)
        for a, b, _ in self.quad + self.line:
            signal(a, b)
        pl.when(jnp.logical_not(self.in_others))(lambda: signal(per * c + rm, c))
        for _, b, _ in self.line:
            signal(per * c + rm, b)
        pl.when(self.has_up)(lambda: signal(r - 1, nc - 1))
        pl.when(self.has_down)(lambda: signal(r + 1, 0))
        pl.when(self.has_left & jnp.logical_not(before_is_me))(lambda: signal(per * (c - 1) + rm, nc - 1))
        pl.when(self.has_right & jnp.logical_not(after_is_me))(lambda: signal(per * (c + 1) + rm, 0))
        pl.when(jnp.logical_not(self.in_others))(lambda: signal(per * c + rm, rb))
        for a, _, _ in self.quad:
            signal(per * (c - rb) + a, rb)
        pl.when(self.has_up)(lambda: signal(r - 1, c))
        pl.when(self.has_down)(lambda: signal(r + 1, c))
        pl.when(self.ends_block)(lambda: signal_all(rb + 1))
        pl.when(self.starts_block)(lambda: signal_all(rb - 1))
        owner = self.k1 < PIECES

        @pl.when(owner)
        def _():
            for a, b, _ in self.group1 + self.group2:
                signal(a, b)

        @pl.when(jnp.logical_not(owner))
        def _():
            for k in range(PIECES):
                signal(*self.plane_member(k))

        n = len(self.quad + self.line) + nc + per
        n = n + jnp.where(owner, len(self.group1 + self.group2), PIECES)
        up, down = self.has_up, self.has_down
        for cond, m in (
            (self.in_others, -2), (is_last & down, nc), (is_first & up, nc),
            (is_last & (rb < nc - 1), nc), (before_is_me, -1), (is_first & (rb > 0), nc), (after_is_me, -1),
            (up, 1), (down, 1), (self.has_left, 1), (self.has_right, 1),
        ):
            n = n + jnp.where(cond, m, 0)
        return n

    def senders(self, send, recv):
        def put(src, dst_r, dst_c, dst, sem):
            pltpu.make_async_remote_copy(
                src, dst, send.at[sem], recv.at[sem], device_id=(dst_r, dst_c), device_id_type=MESH
            ).start()

        def put_other(src, k, dst, sem):
            a, b = self.other(k)
            mine = (a == self.r) & (b == self.c)
            pl.when(mine)(lambda: pltpu.make_async_copy(src, dst, recv.at[sem]).start())
            pl.when(jnp.logical_not(mine))(lambda: put(src, a, b, dst, sem))

        return put, put_other


def pair_kernel(
    nr, nc, e_hbm, lpt_hbm, rpt_hbm, w_hbm, cot_hbm,
    out_hbm, sums_hbm, eg_hbm,
    rowf, colf, taps, mall, mt, act, a3, z, tf, move, onto, pick, by_group, gram, cacc, rsum, cols, col_ends, row_main, row_ends,
    out_ref, eg_ref, feats, e_ref, w_ref, cot_ref, own, right, packed, quad, line, proj, es, eb, el, eh, blocks, row_feats, col_feats,
    cparts, cends, rends, turned, gparts, buf, r1, r2, mid, fin, recv, send, loads, stores,
):
    ins = ((e_hbm, e_ref), (w_hbm, w_ref), (lpt_hbm, proj.at[0:32]), (rpt_hbm, proj.at[32:64]), (cot_hbm, cot_ref))
    ins = [pltpu.make_async_copy(src, dst, loads.at[k]) for k, (src, dst) in enumerate(ins)]
    for copy in ins:
        copy.start()
    p = Place(nr, nc)
    r, c, per, rb, rm, k1, k2 = p.r, p.c, p.per, p.rb, p.rm, p.k1, p.k2
    greeted = p.greet()
    put, put_other = p.senders(send, recv)
    rows8, rows7 = gparts, gparts.at[0 : nc - 1]

    proj[64:128, :] = jnp.zeros((64, 512), BF16)
    ins[0].wait()
    e = e_ref[...].astype(F32)
    es[...] = jnp.concatenate([e[:, 0:256], e[:, 256:512]], axis=0).astype(BF16)
    ins[2].wait()
    ins[3].wait()
    own[...] = dot_nt(e_ref[...], proj[...]).astype(BF16).astype(F32)
    group = iota((8, 128), 1) >> 5
    right[...] = jnp.where(group == rm, pltpu.roll(own[...], lax.rem(32 * rm + 96, 128), 1), 0.0)
    ins[1].wait()
    build_taps(w_ref, tf)
    ins[4].wait()
    mask_cotangent(r, c, cot_ref, move, mall, mt)
    pl.semaphore_wait(pltpu.get_barrier_semaphore(), greeted)

    for a, b, _ in p.quad:
        put(right, a, b, quad.at[rm], 1)
    pltpu.make_async_copy(right, quad.at[rm], recv.at[1]).start()

    def put_line(row, dst, sem):
        for k in range(nc):
            put(own, row, k, dst, sem)

    is_first, is_last = c == 0, c == nc - 1
    row_after, row_before = is_last & p.has_down, is_first & p.has_up
    pl.when(row_after)(lambda: put_line(r + 1, row_feats.at[0], 2))
    pl.when(row_before)(lambda: put_line(r - 1, row_feats.at[1], 3))
    for a, b, _ in p.line:
        put(own, a, b, line.at[c], 16)
    pltpu.make_async_copy(own, line.at[c], recv.at[16]).start()

    def put_targets(src, col, dst, sem):
        first, *rest = p.targets(col)
        mine = c == col
        pl.when(mine)(lambda: pltpu.make_async_copy(src, dst, recv.at[sem]).start())
        pl.when(jnp.logical_not(mine))(lambda: put(src, *first, dst, sem))
        for a, b in rest:
            put(src, a, b, dst, sem)

    col_after, col_before = is_last & (rb < nc - 1), is_first & (rb > 0)
    input_gradient(mt, tf, z, (0, 1))
    wait_bytes(quad, recv.at[1])
    packed[...] = jnp.sum(quad[...], axis=0)
    put_targets(packed, rb, blocks.at[c], 15)
    pl.when(col_after)(lambda: put_targets(packed, rb + 1, col_feats.at[0], 4))
    pl.when(col_before)(lambda: put_targets(packed, rb - 1, col_feats.at[1], 5))
    input_gradient(mt, tf, z, (1, 3))
    build_constants(onto, pick, by_group)

    def arrive(cond, ref, sem):
        pl.when(cond)(lambda: wait_bytes(ref, sem))
        pl.when(jnp.logical_not(cond))(lambda: ref.__setitem__(..., jnp.full(ref.shape, OUTSIDE, F32)))

    arrive(p.has_up, row_feats.at[0], recv.at[2])
    arrive(p.has_down, row_feats.at[1], recv.at[3])
    arrive(p.has_left, col_feats.at[0], recv.at[4])
    arrive(p.has_right, col_feats.at[1], recv.at[5])
    wait_bytes(line, recv.at[16])
    wait_bytes(blocks, recv.at[15])
    feats[8:72, :] = line[...].reshape(8 * nc, 128)
    feats[0:8, :] = row_feats[0]
    feats[72:80, :] = row_feats[1]
    feats[80:136, :] = jnp.zeros((56, 128), F32)
    ends = [jnp.concatenate([col_feats[k], jnp.zeros((8, 128), F32)], axis=0).astype(BF16) for k in range(2)]
    features(feats[4:132, :].astype(BF16), blocks[...].reshape(8 * nc, 128).astype(BF16), *ends, onto, rowf, colf)
    for a, b, _ in p.line:
        put(es, a, b, eb.at[c], 0)
    pltpu.make_async_copy(es, eb.at[c], recv.at[0]).start()
    elementwise(rowf, colf, z, act, cacc, rsum)

    column_sums(cacc, pick, cols)
    for k in range(per):
        put_other(cols.at[k], k, cparts.at[rm], 6)
    column_end_sums(cacc, pick, col_ends)
    pl.when(p.has_left)(lambda: put(col_ends.at[0], per * c - 1, rb, cends.at[0, rm], 9))
    pl.when(p.has_right)(lambda: put(col_ends.at[1], per * c + per, rb, cends.at[1, rm], 10))
    row_sums(rsum, pick, by_group, row_main, row_ends)
    pl.when(p.has_up)(lambda: put(row_ends.at[0], r - 1, c, rends.at[0], 7))
    pl.when(p.has_down)(lambda: put(row_ends.at[1], r + 1, c, rends.at[1], 8))

    build_windows(act, a3)
    tap_gradient(mall, a3, pick, gram, taps)
    for k in range(PIECES - 16):
        buf[16 + k] = taps[16 * k : 16 * k + 16, :].astype(BF16)

    def put_piece(k):
        pl.when(k1 != k)(lambda: put(buf.at[k], *p.plane_member(k), r1.at[k1], 11))

    for k in range(16, PIECES):
        put_piece(k)
    wait_bytes(eb, recv.at[0])
    e = eb[...].astype(F32)
    el[...] = e[:, 0:8].reshape(64, 256).astype(BF16)
    eh[...] = e[:, 8:16].reshape(64, 256).astype(BF16)
    def gather_sum(cond, ref, sem):
        pl.when(cond)(lambda: wait_bytes(ref, sem))
        pl.when(jnp.logical_not(cond))(lambda: ref.__setitem__(..., jnp.zeros(ref.shape, F32)))

    gather_sum(p.has_down, rends.at[0], recv.at[7])
    gather_sum(p.has_up, rends.at[1], recv.at[8])
    gather_sum(p.ends_block, cends.at[0], recv.at[9])
    gather_sum(p.starts_block, cends.at[1], recv.at[10])
    wait_bytes(cparts, recv.at[6])
    grads = (
        row_main[...] + rends[0] + rends[1],
        jnp.sum(cparts[...], axis=0) + jnp.sum(cends[0], axis=0) + jnp.sum(cends[1], axis=0),
    )
    lane = iota((16, 128), 1)
    spread = []
    for g in range(4):
        parts = [x if turn % 128 == 0 else pltpu.roll(x, turn % 128, 1) for x, turn in zip(grads, (-32 * g, 32 - 32 * g))]
        spread.append(jnp.where(lane < 32, parts[0], jnp.where(lane < 64, parts[1], 0.0)))
    turned[...] = jnp.concatenate(spread, axis=0)

    high, low = halves(turned[...])
    for half, ref in enumerate((el, eh)):
        part = dot_tn(high, ref[...]) + dot_tn(low, ref[...])
        for k in range(8):
            at = slice(16 * (k // 2), 16 * (k // 2) + 16), slice(128 * (k % 2), 128 * (k % 2) + 128)
            buf[4 * (k // 2) + 2 * half + k % 2] = part[at].astype(BF16)

    owner = k1 < PIECES
    for k in range(16):
        put_piece(k)
    pl.when(owner)(lambda: pltpu.make_async_copy(buf.at[k1], r1.at[k1], recv.at[11]).start())

    for a, b, _ in p.line:
        put(turned.at[pl.ds(pl.multiple_of(8 * b, 8), 8)], a, b, gparts.at[c], 14)
    pltpu.make_async_copy(turned.at[pl.ds(pl.multiple_of(8 * c, 8), 8)], gparts.at[c], recv.at[14]).start()

    outs = [
        pltpu.make_async_copy(out_ref.at[:, 16 * q : 16 * q + 16, :], out_hbm.at[:, 16 * q : 16 * q + 16, :], stores.at[q])
        for q in range(4)
    ]
    convolve(r, c, 0, a3, tf, out_ref)
    outs[0].start()
    convolve(r, c, 1, a3, tf, out_ref)
    outs[1].start()

    @pl.when(owner)
    def _():
        wait_bytes(r1, recv.at[11])
        mid[...] = jnp.sum(r1[...].astype(F32), axis=0).astype(BF16)
        for a, b, _ in p.group2:
            put(mid, a, b, r2.at[k2], 12)
        pltpu.make_async_copy(mid, r2.at[k2], recv.at[12]).start()

    convolve(r, c, 2, a3, tf, out_ref)
    outs[2].start()
    convolve(r, c, 3, a3, tf, out_ref)
    outs[3].start()

    @pl.when(owner)
    def _():
        wait_bytes(r2, recv.at[12])
        fin[...] = jnp.sum(r2[...].astype(F32), axis=0).astype(BF16)
        for a, b, _ in p.group1:
            put(fin, a, b, sums_hbm.at[k1], 13)
        pltpu.make_async_copy(fin, sums_hbm.at[k1], recv.at[13]).start()

    wait_bytes(gparts, recv.at[14])
    high, low = halves(jnp.sum(gparts[...], axis=0))
    eg_ref[...] = dot(high, proj[...]) + dot(low, proj[...])
    outs.append(pltpu.make_async_copy(eg_ref, eg_hbm, stores.at[4]))
    outs[4].start()

    for copy in outs:
        copy.wait()
    wait_bytes(eb.at[0 : nc - 1], send.at[0])
    wait_bytes(quad.at[0 : per - 1], send.at[1])
    pl.when(row_after)(lambda: wait_bytes(rows8, send.at[2]))
    pl.when(row_before)(lambda: wait_bytes(rows8, send.at[3]))

    def sent_targets(cond, mine, eight, seven, sem):
        pl.when(cond & mine)(lambda: wait_bytes(seven, send.at[sem]))
        pl.when(cond & jnp.logical_not(mine))(lambda: wait_bytes(eight, send.at[sem]))

    sent_targets(col_after, rb + 1 == c, rows8, rows7, 4)
    sent_targets(col_before, rb - 1 == c, rows8, rows7, 5)
    sent_targets(rb >= 0, p.in_others, blocks, blocks.at[0 : nc - 1], 15)
    pl.when(p.in_others)(lambda: wait_bytes(cparts.at[0 : per - 1], send.at[6]))
    pl.when(jnp.logical_not(p.in_others))(lambda: wait_bytes(cparts, send.at[6]))
    pl.when(p.has_up)(lambda: wait_bytes(row_ends.at[0], send.at[7]))
    pl.when(p.has_down)(lambda: wait_bytes(row_ends.at[1], send.at[8]))
    pl.when(p.has_left)(lambda: wait_bytes(col_ends.at[0], send.at[9]))
    pl.when(p.has_right)(lambda: wait_bytes(col_ends.at[1], send.at[10]))
    wait_bytes(line.at[0 : nc - 1], send.at[16])
    pl.when(owner)(lambda: wait_bytes(r1.at[0 : PIECES - 1], send.at[11]))
    pl.when(jnp.logical_not(owner))(lambda: wait_bytes(r1.at[0:PIECES], send.at[11]))
    pl.when(owner)(lambda: wait_bytes(r2.at[0 : r2.shape[0] - 1], send.at[12]))
    wait_bytes(gparts.at[0 : nc - 1], send.at[14])

    pl.when(owner)(lambda: wait_bytes(r1.at[0 : r1.shape[0] - 1], send.at[13]))
    wait_bytes(sums_hbm, recv.at[13])


def finish_kernel(
    scale, sums_in, eg_in, pair_in, conv_out, left_out, right_out, eg_out, pair_out,
    sums_ref, eg_ref, held, conv_ref, left_ref, right_ref, loads, stores,
):
    def piece(k):
        return slice(8 * k, 8 * k + 8)

    ins = [pltpu.make_async_copy(sums_in, sums_ref, loads.at[0]), pltpu.make_async_copy(eg_in, eg_ref, loads.at[1])]
    ins += [pltpu.make_async_copy(pair_in.at[piece(k)], held.at[piece(k)], loads.at[2 + k]) for k in range(4)]
    outs = [
        pltpu.make_async_copy(conv_ref, conv_out, stores.at[0]),
        pltpu.make_async_copy(left_ref, left_out, stores.at[1]),
        pltpu.make_async_copy(right_ref, right_out, stores.at[2]),
        pltpu.make_async_copy(eg_ref, eg_out, stores.at[3]),
    ]
    outs += [pltpu.make_async_copy(held.at[piece(k)], pair_out.at[piece(k)], stores.at[4 + k]) for k in range(4)]
    for copy in ins:
        copy.start()
    ins[0].wait()
    for ref, first, at in ((left_ref, 0, 1), (right_ref, 8, 2)):
        for k in range(8):
            x = sums_ref[first + k].astype(F32)
            ref[16 * (k // 4) : 16 * (k // 4) + 16, 128 * (k % 4) : 128 * (k % 4) + 128] = x * scale
        outs[at].start()
    ins[1].wait()
    outs[3].start()
    for k in range(4):
        ins[2 + k].wait()
        outs[4 + k].start()
    for k in range(9):
        q, at = divmod(k, 4)
        for part in range(2):
            x = sums_ref[16 + 2 * q + part].astype(F32)
            conv_ref[k, 16 * part : 16 * part + 16, :] = x[:, 32 * at : 32 * at + 32] * scale
    outs[0].start()
    for copy in outs:
        copy.wait()


def shards(nr, nc, embed, left_proj, right_proj, conv_w, cotangent):
    per = nr // nc
    pair_out, totals, embed_grad = pl.pallas_call(
        functools.partial(pair_kernel, nr, nc),
        out_shape=(
            jax.ShapeDtypeStruct((32, 64, 256), BF16),
            jax.ShapeDtypeStruct((PIECES, 16, 128), BF16),
            jax.ShapeDtypeStruct((8, 512), F32),
        ),
        in_specs=[HBM] * 5,
        out_specs=(HBM,) * 3,
        scratch_shapes=LOCAL_SCRATCH
        + [
            pltpu.VMEM((32, 64, 256), BF16),
            pltpu.VMEM((8, 512), F32),
            pltpu.VMEM((136, 128), F32),
            pltpu.VMEM((8, 512), BF16),
            pltpu.VMEM((9, 32, 32), BF16),
            pltpu.VMEM((32, 64, 256), BF16),
            pltpu.VMEM((8, 128), F32),
            pltpu.VMEM((8, 128), F32),
            pltpu.VMEM((8, 128), F32),
            pltpu.VMEM((per, 8, 128), F32),
            pltpu.VMEM((nc, 8, 128), F32),
            pltpu.VMEM((128, 512), BF16),
            pltpu.VMEM((16, 256), BF16),
            pltpu.VMEM((nc, 16, 256), BF16),
            pltpu.VMEM((64, 256), BF16),
            pltpu.VMEM((64, 256), BF16),
            pltpu.VMEM((nc, 8, 128), F32),
            pltpu.VMEM((2, 8, 128), F32),
            pltpu.VMEM((2, 8, 128), F32),
            pltpu.VMEM((per, 16, 128), F32),
            pltpu.VMEM((2, per, 16, 128), F32),
            pltpu.VMEM((2, 16, 128), F32),
            pltpu.VMEM((64, 128), F32),
            pltpu.VMEM((nc, 8, 128), F32),
            pltpu.VMEM((PIECES, 16, 128), BF16),
            pltpu.VMEM((32, 16, 128), BF16),
            pltpu.VMEM((8, 16, 128), BF16),
            pltpu.VMEM((16, 128), BF16),
            pltpu.VMEM((16, 128), BF16),
            pltpu.SemaphoreType.DMA((17,)),
            pltpu.SemaphoreType.DMA((17,)),
            pltpu.SemaphoreType.DMA((5,)),
            pltpu.SemaphoreType.DMA((6,)),
        ],
        compiler_params=pltpu.CompilerParams(
            collective_id=0, has_side_effects=True, vmem_limit_bytes=60 * 1024 * 1024
        ),
        name="pair_kernel",
    )(embed, left_proj.T, right_proj.T, conv_w, cotangent)
    conv_grad, left_t, right_t, embed_grad, pair_out = pl.pallas_call(
        functools.partial(finish_kernel, 32.0 / (8 * nr * nc)),
        out_shape=(
            jax.ShapeDtypeStruct((9, 32, 32), F32),
            jax.ShapeDtypeStruct((32, 512), F32),
            jax.ShapeDtypeStruct((32, 512), F32),
            jax.ShapeDtypeStruct((8, 512), F32),
            jax.ShapeDtypeStruct((32, 64, 256), BF16),
        ),
        in_specs=[HBM] * 3,
        out_specs=(HBM,) * 5,
        scratch_shapes=[
            pltpu.VMEM((PIECES, 16, 128), BF16),
            pltpu.VMEM((8, 512), F32),
            pltpu.VMEM((32, 64, 256), BF16),
            pltpu.VMEM((9, 32, 32), F32),
            pltpu.VMEM((32, 512), F32),
            pltpu.VMEM((32, 512), F32),
            pltpu.SemaphoreType.DMA((6,)),
            pltpu.SemaphoreType.DMA((8,)),
        ],
        compiler_params=pltpu.CompilerParams(vmem_limit_bytes=60 * 1024 * 1024),
        name="finish",
    )(totals, embed_grad, pair_out)
    return pair_out, conv_grad, left_t.T, right_t.T, embed_grad


def solution(mesh):
    body = functools.partial(shards, mesh.shape["row"], mesh.shape["col"])
    in_specs = (P(("row", "col"), None), P(), P(), P(), P(None, "row", "col"))
    out_specs = (P(None, "row", "col"), P(), P(), P(), P(("row", "col"), None))
    return jax.shard_map(body, mesh=mesh, in_specs=in_specs, out_specs=out_specs, check_vma=False)
```

```python
import functools

import jax
import jax.numpy as jnp
from jax import lax
from jax.experimental import pallas as pl
from jax.experimental.pallas import tpu as pltpu
from jax.sharding import PartitionSpec as P

MESH = pl.DeviceIdType.MESH
OUTSIDE = -1e30
LOG2E = 1.4426950408889634
LN2 = 0.6931471805599453
PIECES = 22
F32 = jnp.float32
BF16 = jnp.bfloat16
VMEM = pl.BlockSpec(memory_space=pltpu.VMEM)
HBM = pl.BlockSpec(memory_space=pltpu.HBM)


def iota(shape, dim):
    return lax.broadcasted_iota(jnp.int32, shape, dim)


def one_hot(cond):
    return jnp.where(cond, 1.0, 0.0).astype(BF16)


def dot(a, b):
    return jnp.dot(a, b, preferred_element_type=F32)


def dot_nt(a, b):
    return lax.dot_general(a, b, (((1,), (1,)), ((), ())), preferred_element_type=F32)


def dot_tn(a, b):
    return lax.dot_general(a, b, (((0,), (0,)), ((), ())), preferred_element_type=F32)


def halves(x):
    high = x.astype(BF16)
    return high, (x - high.astype(F32)).astype(BF16)


def loop(n, f):
    def body(k, _):
        f(k)
        return 0

    lax.fori_loop(0, n, body, 0)


def lanes(h):
    return pl.ds(pl.multiple_of(h * 256, 256), 256)


def wait_bytes(ref, sem):
    pltpu.make_async_copy(ref, ref, sem).wait()


def softplus_and_slope(y):
    t = jnp.exp2(-jnp.abs(y))
    u = 1.0 + t
    inv = pltpu.reciprocal(u, full_range=False)
    log = jnp.where(t < 2.0**-11, t * LOG2E, jnp.log2(u))
    return jnp.maximum(y, 0.0) + log, jnp.where(y >= 0, inv, t * inv)


def build_taps(w_ref, tf):
    spread = one_hot((iota((256, 32), 0) >> 3) == iota((256, 32), 1))
    widen = one_hot((iota((32, 256), 1) >> 3) == iota((32, 256), 0))
    s0, s1 = iota((256, 256), 0) & 7, iota((256, 256), 1) & 7
    same, above, below = s1 == s0, s1 == s0 + 4, s1 == s0 - 4
    x = dot(w_ref[...].reshape(288, 32), widen).astype(BF16)
    for b in range(3):
        x0, x1, x2 = (dot(spread, x[96 * a + 32 * b : 96 * a + 32 * b + 32]) for a in range(3))
        tf[:, 256 * b : 256 * b + 256] = jnp.where(same, x0, jnp.where(above, x1, 0.0)).astype(BF16)
        tf[:, 768 + 256 * b : 1024 + 256 * b] = jnp.where(same, x2, jnp.where(below, x1, 0.0)).astype(BF16)


def mask_cotangent(r, c, cot_ref, move, mall, mt):
    mall[0:256, 2048:2304] = jnp.zeros((256, 256), BF16)
    mall[256:512, 0:256] = jnp.zeros((256, 256), BF16)
    for k in range(4):
        x = cot_ref[:, 16 * k : 16 * k + 16, :].astype(F32)
        row = r * 64 + 16 * k + iota((16, 256), 0)
        x = jnp.where((c * 256 + iota((16, 256), 1) >= row)[None], x, 0.0)
        for half in range(2):
            m = x[:, 8 * half : 8 * half + 8].reshape(256, 256).astype(BF16)
            mall[0:256, lanes(2 * k + half)] = m
            mall[256:512, lanes(2 * k + half + 1)] = m
    for b in range(2):
        move[272 * b : 272 * b + 272, :] = one_hot(iota((272, 256), 0) - 4 * b == iota((272, 256), 1))
    mt[0] = jnp.zeros((272, 768), BF16)
    mt[9] = jnp.zeros((272, 768), BF16)
    none = jnp.zeros((8, 256), F32)

    def body(g):
        moved = dot_nt(move[...], mall[0:256, lanes(g)])
        mt[g + 1, :, 0:256] = moved[0:272].astype(BF16)
        mt[g + 1, :, 256:512] = moved[272:544].astype(BF16)
        mt[g + 1, :, 512:768] = jnp.concatenate([none, moved[0:264]], axis=0).astype(BF16)

    loop(8, body)


def input_gradient(mt, tf, z, steps):
    def body(step, _):
        left = [jnp.concatenate([mt[3 * step + k], mt[3 * step + k + 1]], axis=1) for k in range(3)]
        right = jnp.concatenate(
            [tf[:, 768 * (1 - u) + 256 * b : 768 * (1 - u) + 256 * b + 256] for u in range(2) for b in range(3)], axis=0
        )
        x = dot(jnp.concatenate(left, axis=0), right)
        for k in range(3):
            z[3 * step + k] = x[272 * k : 272 * k + 272]
        return 0

    lax.fori_loop(*steps, body, 0)


def features(rows, blocks, before, after, onto, rowf, colf):
    picks = [onto[:, 256 * at : 256 * at + 256] for at in range(4)]
    first = dot(before, picks[3])
    last = dot(after, picks[0])
    x = [first[4:8]] + [dot(blocks, pick) for pick in picks] + [last[0:4], jnp.zeros((8, 256), F32)]
    colf[...] = jnp.concatenate(x, axis=0) * LOG2E
    x = dot(rows, picks[0])
    x = jnp.where((iota((128, 256), 0) & 7) == (iota((128, 256), 1) & 7), x, 0.0).astype(BF16)
    rowf[...] = dot(one_hot((iota((16, 128), 1) >> 3) == iota((16, 128), 0)), x) * LOG2E


def elementwise(rowf, colf, z, act, cacc, rsum):
    rsum[...] = jnp.zeros_like(rsum)

    def body(step):
        parts = [pl.ds(pl.multiple_of(24 * step + 8 * part, 8), 8) for part in range(3)]
        totals = [jnp.zeros((8, 256), F32)] * 3
        for h in range(9):
            left = rowf[h : h + 1, :]
            row = jnp.zeros((8, 256), F32)
            for k, rows in enumerate(parts):
                value, slope = softplus_and_slope(colf[rows, :] + left)
                act[h, rows, :] = value
                p = z[h, rows, :] * slope
                totals[k] += p
                row += p
            rsum[8 * h : 8 * h + 8, :] += row
        for k, rows in enumerate(parts):
            cacc[rows, :] = totals[k]

    loop(11, body)


def build_constants(onto, pick, by_group):
    k, n = iota((128, 256), 0), iota((128, 256), 1) >> 3
    for at in range(4):
        onto[:, 256 * at : 256 * at + 256] = one_hot(k == n + 32 * at)
    k, n = iota((256, 128), 0) >> 3, iota((256, 128), 1)
    for g in range(4):
        pick[256 * g : 256 * g + 256, :] = one_hot(k + 32 * g == n)
    by_group[...] = one_hot((iota((80, 128), 0) >> 3) == (iota((80, 128), 1) >> 3))


def ends_of(x, pick, ends):
    sub = iota((16, 128), 0)
    high, low = halves(x)
    first = dot(high, pick[768:1024]) + dot(low, pick[768:1024])
    second = dot(high, pick[0:256]) + dot(low, pick[0:256])
    ends[0] = jnp.where(sub >= 12, pltpu.roll(first, 12, 0), 0.0)
    ends[1] = jnp.where(sub < 4, pltpu.roll(second, 4, 0), 0.0)


def column_sums(cacc, pick, cols):
    x = [
        jnp.concatenate([cacc[4 + 64 * q + 16 * g : 20 + 64 * q + 16 * g, :] for g in range(4)], axis=1) for q in range(4)
    ]
    high, low = halves(jnp.concatenate(x, axis=0))
    x = dot(high, pick[...]) + dot(low, pick[...])
    for q in range(4):
        cols[q] = x[16 * q : 16 * q + 16]


def column_end_sums(cacc, pick, col_ends):
    ends_of(jnp.concatenate([cacc[0:8, :], cacc[256:264, :]], axis=0), pick, col_ends)


def row_sums(rsum, pick, by_group, row_main, row_ends):
    x = jnp.concatenate([rsum[...], jnp.zeros((56, 256), F32)], axis=0)
    high, low = halves(x)
    x = dot(by_group[...], high) + dot(by_group[...], low)
    x = jnp.where((iota((80, 256), 0) & 7) == (iota((80, 256), 1) & 7), x, 0.0)
    ends_of(jnp.concatenate([x[0:8], x[64:72]], axis=0), pick, row_ends)
    high, low = halves(jnp.concatenate([x[4 + 16 * g : 20 + 16 * g] for g in range(4)], axis=1))
    row_main[...] = dot(high, pick[...]) + dot(low, pick[...])


def build_windows(act, a3):
    def body(h):
        at = pl.ds(pl.multiple_of(256 * h, 256), 256)
        for b in range(3):
            a3[at, 256 * b : 256 * b + 256] = (act[h, 4 * b : 4 * b + 256, :] * LN2).astype(BF16)

    loop(9, body)


def convolve(r, c, k, a3, tf, out_ref):
    parts = []
    for g in (2 * k, 2 * k + 1):
        both = jnp.concatenate([a3[256 * (g + u) : 256 * (g + u) + 256, :] for u in range(2)], axis=1)
        parts.append(dot_nt(tf[...], both).reshape(32, 8, 256))
    y = jnp.concatenate(parts, axis=1)
    row = r * 64 + 16 * k + iota((16, 256), 0)
    col = c * 256 + iota((16, 256), 1)
    out_ref[:, 16 * k : 16 * k + 16, :] = jnp.where((col >= row)[None], y, 0.0).astype(BF16)


def tap_gradient(mall, a3, pick, gram, taps):
    x = dot(mall[...], a3[...])
    for u in range(2):
        for k in range(6):
            gram[6 * u + k] = x[256 * u : 256 * u + 256, 128 * k : 128 * k + 128]
    lane = iota((32, 128), 1)

    def along(b, k, sources):
        total = jnp.zeros((32, 128), F32)
        for at, (s, u) in enumerate(sources):
            total = jnp.where((lane & 7) == at, gram[6 * u + 2 * b + k, pl.ds(s, 32, stride=8), :], total)
        return total

    sources = (
        [(s, 0) for s in range(8)],
        [((s + 4) % 8, 1 - s // 4) for s in range(8)],
        [(s, 1) for s in range(8)],
    )
    x = [jnp.concatenate([along(b, k, sources[a]) for k in range(2)], axis=1) for a in range(3) for b in range(3)]
    y = dot(jnp.concatenate(halves(jnp.concatenate(x, axis=0)), axis=0), pick[0:256])
    y = y[0:288] + y[288:576]
    for q in range(3):
        total = jnp.zeros((32, 128), F32)
        for k in range(min(4, 9 - 4 * q)):
            tap = y[32 * (4 * q + k) : 32 * (4 * q + k) + 32]
            total = jnp.where((lane >> 5) == k, pltpu.roll(tap, 32 * k, 1) if k else tap, total)
        taps[32 * q : 32 * q + 32, :] = total


LOCAL_SCRATCH = [
    pltpu.VMEM((16, 256), F32),
    pltpu.VMEM((272, 256), F32),
    pltpu.VMEM((96, 128), F32),
    pltpu.VMEM((512, 2304), BF16),
    pltpu.VMEM((10, 272, 768), BF16),
    pltpu.VMEM((9, 272, 256), F32),
    pltpu.VMEM((2304, 768), BF16),
    pltpu.VMEM((9, 272, 256), F32),
    pltpu.VMEM((256, 1536), BF16),
    pltpu.VMEM((544, 256), BF16),
    pltpu.VMEM((128, 1024), BF16),
    pltpu.VMEM((1024, 128), BF16),
    pltpu.VMEM((80, 128), BF16),
    pltpu.VMEM((12, 256, 128), F32),
    pltpu.VMEM((272, 256), F32),
    pltpu.VMEM((72, 256), F32),
    pltpu.VMEM((4, 16, 128), F32),
    pltpu.VMEM((2, 16, 128), F32),
    pltpu.VMEM((16, 128), F32),
    pltpu.VMEM((2, 16, 128), F32),
]


class Place:
    def __init__(self, nr, nc):
        r, c = lax.axis_index("row"), lax.axis_index("col")
        self.r, self.c, self.nr, self.nc = r, c, nr, nc
        self.per = nr // nc
        self.rb, self.rm = lax.div(r, self.per), lax.rem(r, self.per)
        _, self.quad = self.group(((r, 1, 0), (r, 2, 0)))
        _, self.line = self.group(((c, 1, 1), (c, 2, 1), (c, 4, 1)))
        self.plane = ((r, 1, 0), (r, 8, 0), (c, 2, 1), (r, 16, 0), (c, 4, 1))
        self.k1, self.group1 = self.group(self.plane)
        self.z_line = ((r, 2, 0), (r, 4, 0), (c, 1, 1))
        self.k2, self.group2 = self.group(self.z_line)
        self.has_up, self.has_down = r > 0, r < nr - 1
        self.has_left, self.has_right = c > 0, c < nc - 1
        self.ends_block = (self.rm == self.per - 1) & (self.rb < nc - 1)
        self.starts_block = (self.rm == 0) & (self.rb > 0)
        self.in_others = self.rb == c

    def group(self, bits):
        number, turns = 0, []
        for k, (x, weight, is_col) in enumerate(bits):
            bit = lax.rem(lax.div(x, weight), 2)
            number = number + bit * (1 << k)
            sign = 1 - 2 * bit
            turns.append((sign * weight, is_col, sign * (1 << k)))
        members = [(self.r, self.c, number)]
        for move, is_col, step in turns:
            members += [
                (a, b + move, n + step) if is_col else (a + move, b, n + step) for a, b, n in members
            ]
        return number, members[:0:-1]

    def member(self, bits, k):
        a, b = self.r, self.c
        for at, (x, weight, is_col) in enumerate(bits):
            move = weight * (k >> at & 1) - weight * lax.rem(lax.div(x, weight), 2)
            a, b = (a, b + move) if is_col else (a + move, b)
        return a, b

    def other(self, k):
        return self.per * self.c + k, self.rb

    def targets(self, col):
        return [(lax.rem(self.r + self.per * k, self.nr), col) for k in range(self.nr // self.per)]

    def greet(self):
        r, c, nc, per, rb, rm = self.r, self.c, self.nc, self.per, self.rb, self.rm
        barrier = pltpu.get_barrier_semaphore()

        def signal(a, b):
            pl.semaphore_signal(barrier, inc=1, device_id=(a, b), device_id_type=MESH)

        def signal_all(col):
            for k in range(per):
                signal(per * c + k, col)

        is_first, is_last = c == 0, c == nc - 1
        before_is_me = is_last & (rb == nc - 2)
        after_is_me = is_first & (rb == 1)
        for a, b, _ in self.quad + self.line:
            signal(a, b)
        pl.when(jnp.logical_not(self.in_others))(lambda: signal(per * c + rm, c))
        for _, b, _ in self.line:
            signal(per * c + rm, b)
        pl.when(self.has_up)(lambda: signal(r - 1, nc - 1))
        pl.when(self.has_down)(lambda: signal(r + 1, 0))
        pl.when(self.has_left & jnp.logical_not(before_is_me))(lambda: signal(per * (c - 1) + rm, nc - 1))
        pl.when(self.has_right & jnp.logical_not(after_is_me))(lambda: signal(per * (c + 1) + rm, 0))
        pl.when(jnp.logical_not(self.in_others))(lambda: signal(per * c + rm, rb))
        for a, _, _ in self.quad:
            signal(per * (c - rb) + a, rb)
        pl.when(self.has_up)(lambda: signal(r - 1, c))
        pl.when(self.has_down)(lambda: signal(r + 1, c))
        pl.when(self.ends_block)(lambda: signal_all(rb + 1))
        pl.when(self.starts_block)(lambda: signal_all(rb - 1))
        owner = self.k1 < PIECES

        @pl.when(owner)
        def _():
            for a, b, _ in self.group1 + self.group2:
                signal(a, b)

        @pl.when(jnp.logical_not(owner))
        def _():
            for k in range(PIECES):
                signal(*self.member(self.plane, k))

        n = len(self.quad + self.line) + nc + per
        n = n + jnp.where(owner, len(self.group1 + self.group2), PIECES)
        up, down = self.has_up, self.has_down
        for cond, m in (
            (self.in_others, -2), (is_last & down, nc), (is_first & up, nc),
            (is_last & (rb < nc - 1), nc), (before_is_me, -1), (is_first & (rb > 0), nc), (after_is_me, -1),
            (up, 1), (down, 1), (self.has_left, 1), (self.has_right, 1),
        ):
            n = n + jnp.where(cond, m, 0)
        return n

    def senders(self, send, recv):
        def put(src, dst_r, dst_c, dst, sem):
            pltpu.make_async_remote_copy(
                src, dst, send.at[sem], recv.at[sem], device_id=(dst_r, dst_c), device_id_type=MESH
            ).start()

        def put_other(src, k, dst, sem):
            a, b = self.other(k)
            mine = (a == self.r) & (b == self.c)
            pl.when(mine)(lambda: pltpu.make_async_copy(src, dst, recv.at[sem]).start())
            pl.when(jnp.logical_not(mine))(lambda: put(src, a, b, dst, sem))

        return put, put_other


def pair_kernel(
    nr, nc, e_hbm, lpt_hbm, rpt_hbm, w_hbm, cot_hbm,
    out_hbm, sums_hbm, eg_hbm,
    rowf, colf, taps, mall, mt, act, a3, z, tf, move, onto, pick, by_group, gram, cacc, rsum, cols, col_ends, row_main, row_ends,
    out_ref, eg_ref, feats, e_ref, w_ref, cot_ref, own, right, packed, quad, line, proj, es, eb, el, eh, blocks, row_feats, col_feats,
    cparts, cends, rends, turned, gparts, buf, r1, r2, mid, fin, recv, send, loads, stores,
):
    ins = ((e_hbm, e_ref), (w_hbm, w_ref), (lpt_hbm, proj.at[0:32]), (rpt_hbm, proj.at[32:64]), (cot_hbm, cot_ref))
    ins = [pltpu.make_async_copy(src, dst, loads.at[k]) for k, (src, dst) in enumerate(ins)]
    for copy in ins:
        copy.start()
    p = Place(nr, nc)
    r, c, per, rb, rm, k1, k2 = p.r, p.c, p.per, p.rb, p.rm, p.k1, p.k2
    greeted = p.greet()
    put, put_other = p.senders(send, recv)
    rows8, rows7 = gparts, gparts.at[0 : nc - 1]

    proj[64:128, :] = jnp.zeros((64, 512), BF16)
    ins[0].wait()
    e = e_ref[...].astype(F32)
    es[...] = jnp.concatenate([e[:, 0:256], e[:, 256:512]], axis=0).astype(BF16)
    ins[2].wait()
    ins[3].wait()
    own[...] = dot_nt(e_ref[...], proj[...]).astype(BF16).astype(F32)
    group = iota((8, 128), 1) >> 5
    right[...] = jnp.where(group == rm, pltpu.roll(own[...], lax.rem(32 * rm + 96, 128), 1), 0.0)
    ins[1].wait()
    build_taps(w_ref, tf)
    ins[4].wait()
    mask_cotangent(r, c, cot_ref, move, mall, mt)
    pl.semaphore_wait(pltpu.get_barrier_semaphore(), greeted)

    for a, b, _ in p.quad:
        put(right, a, b, quad.at[rm], 1)
    pltpu.make_async_copy(right, quad.at[rm], recv.at[1]).start()

    def put_line(row, dst, sem):
        for k in range(nc):
            put(own, row, k, dst, sem)

    is_first, is_last = c == 0, c == nc - 1
    row_after, row_before = is_last & p.has_down, is_first & p.has_up
    pl.when(row_after)(lambda: put_line(r + 1, row_feats.at[0], 2))
    pl.when(row_before)(lambda: put_line(r - 1, row_feats.at[1], 3))
    for a, b, _ in p.line:
        put(own, a, b, line.at[c], 16)
    pltpu.make_async_copy(own, line.at[c], recv.at[16]).start()

    def put_targets(src, col, dst, sem):
        first, *rest = p.targets(col)
        mine = c == col
        pl.when(mine)(lambda: pltpu.make_async_copy(src, dst, recv.at[sem]).start())
        pl.when(jnp.logical_not(mine))(lambda: put(src, *first, dst, sem))
        for a, b in rest:
            put(src, a, b, dst, sem)

    col_after, col_before = is_last & (rb < nc - 1), is_first & (rb > 0)
    input_gradient(mt, tf, z, (0, 1))
    wait_bytes(quad, recv.at[1])
    packed[...] = jnp.sum(quad[...], axis=0)
    put_targets(packed, rb, blocks.at[c], 15)
    pl.when(col_after)(lambda: put_targets(packed, rb + 1, col_feats.at[0], 4))
    pl.when(col_before)(lambda: put_targets(packed, rb - 1, col_feats.at[1], 5))
    input_gradient(mt, tf, z, (1, 3))
    build_constants(onto, pick, by_group)

    def arrive(cond, ref, sem):
        pl.when(cond)(lambda: wait_bytes(ref, sem))
        pl.when(jnp.logical_not(cond))(lambda: ref.__setitem__(..., jnp.full(ref.shape, OUTSIDE, F32)))

    arrive(p.has_up, row_feats.at[0], recv.at[2])
    arrive(p.has_down, row_feats.at[1], recv.at[3])
    arrive(p.has_left, col_feats.at[0], recv.at[4])
    arrive(p.has_right, col_feats.at[1], recv.at[5])
    wait_bytes(line, recv.at[16])
    wait_bytes(blocks, recv.at[15])
    feats[8:72, :] = line[...].reshape(8 * nc, 128)
    feats[0:8, :] = row_feats[0]
    feats[72:80, :] = row_feats[1]
    feats[80:136, :] = jnp.zeros((56, 128), F32)
    ends = [jnp.concatenate([col_feats[k], jnp.zeros((8, 128), F32)], axis=0).astype(BF16) for k in range(2)]
    features(feats[4:132, :].astype(BF16), blocks[...].reshape(8 * nc, 128).astype(BF16), *ends, onto, rowf, colf)
    for a, b, _ in p.line:
        put(es, a, b, eb.at[c], 0)
    pltpu.make_async_copy(es, eb.at[c], recv.at[0]).start()
    elementwise(rowf, colf, z, act, cacc, rsum)

    column_sums(cacc, pick, cols)
    for k in range(per):
        put_other(cols.at[k], k, cparts.at[rm], 6)
    column_end_sums(cacc, pick, col_ends)
    pl.when(p.has_left)(lambda: put(col_ends.at[0], per * c - 1, rb, cends.at[0, rm], 9))
    pl.when(p.has_right)(lambda: put(col_ends.at[1], per * c + per, rb, cends.at[1, rm], 10))
    row_sums(rsum, pick, by_group, row_main, row_ends)
    pl.when(p.has_up)(lambda: put(row_ends.at[0], r - 1, c, rends.at[0], 7))
    pl.when(p.has_down)(lambda: put(row_ends.at[1], r + 1, c, rends.at[1], 8))

    build_windows(act, a3)
    tap_gradient(mall, a3, pick, gram, taps)
    for k in range(PIECES - 16):
        buf[16 + k] = taps[16 * k : 16 * k + 16, :].astype(BF16)

    def put_piece(k):
        pl.when(k1 != k)(lambda: put(buf.at[k], *p.member(p.plane, k), r1.at[k1], 11))

    for k in range(16, PIECES):
        put_piece(k)
    wait_bytes(eb, recv.at[0])
    e = eb[...].astype(F32)
    el[...] = e[:, 0:8].reshape(64, 256).astype(BF16)
    eh[...] = e[:, 8:16].reshape(64, 256).astype(BF16)
    def gather_sum(cond, ref, sem):
        pl.when(cond)(lambda: wait_bytes(ref, sem))
        pl.when(jnp.logical_not(cond))(lambda: ref.__setitem__(..., jnp.zeros(ref.shape, F32)))

    gather_sum(p.has_down, rends.at[0], recv.at[7])
    gather_sum(p.has_up, rends.at[1], recv.at[8])
    gather_sum(p.ends_block, cends.at[0], recv.at[9])
    gather_sum(p.starts_block, cends.at[1], recv.at[10])
    wait_bytes(cparts, recv.at[6])
    grads = (
        row_main[...] + rends[0] + rends[1],
        jnp.sum(cparts[...], axis=0) + jnp.sum(cends[0], axis=0) + jnp.sum(cends[1], axis=0),
    )
    lane = iota((16, 128), 1)
    spread = []
    for g in range(4):
        parts = [x if turn % 128 == 0 else pltpu.roll(x, turn % 128, 1) for x, turn in zip(grads, (-32 * g, 32 - 32 * g))]
        spread.append(jnp.where(lane < 32, parts[0], jnp.where(lane < 64, parts[1], 0.0)))
    turned[...] = jnp.concatenate(spread, axis=0)

    high, low = halves(turned[...])
    for half, ref in enumerate((el, eh)):
        part = dot_tn(high, ref[...]) + dot_tn(low, ref[...])
        for k in range(8):
            at = slice(16 * (k // 2), 16 * (k // 2) + 16), slice(128 * (k % 2), 128 * (k % 2) + 128)
            buf[4 * (k // 2) + 2 * half + k % 2] = part[at].astype(BF16)

    owner = k1 < PIECES
    for k in range(16):
        put_piece(k)
    pl.when(owner)(lambda: pltpu.make_async_copy(buf.at[k1], r1.at[k1], recv.at[11]).start())

    for a, b, _ in p.line:
        put(turned.at[pl.ds(pl.multiple_of(8 * b, 8), 8)], a, b, gparts.at[c], 14)
    pltpu.make_async_copy(turned.at[pl.ds(pl.multiple_of(8 * c, 8), 8)], gparts.at[c], recv.at[14]).start()

    outs = [
        pltpu.make_async_copy(out_ref.at[:, 16 * q : 16 * q + 16, :], out_hbm.at[:, 16 * q : 16 * q + 16, :], stores.at[q])
        for q in range(4)
    ]
    convolve(r, c, 0, a3, tf, out_ref)
    outs[0].start()
    convolve(r, c, 1, a3, tf, out_ref)
    outs[1].start()

    @pl.when(owner)
    def _():
        wait_bytes(r1, recv.at[11])
        mid[...] = jnp.sum(r1[...].astype(F32), axis=0).astype(BF16)
        for k in range(8):
            pl.when(k2 != k)(lambda k=k: put(mid, *p.member(p.z_line, k), r2.at[k2], 12))
        pltpu.make_async_copy(mid, r2.at[k2], recv.at[12]).start()

    convolve(r, c, 2, a3, tf, out_ref)
    outs[2].start()
    convolve(r, c, 3, a3, tf, out_ref)
    outs[3].start()

    @pl.when(owner)
    def _():
        wait_bytes(r2, recv.at[12])
        fin[...] = jnp.sum(r2[...].astype(F32), axis=0).astype(BF16)
        for k in (1, 0, *range(2, 32)):
            pl.when(k1 != k)(lambda k=k: put(fin, *p.member(p.plane, k), sums_hbm.at[k1], 13))
        pltpu.make_async_copy(fin, sums_hbm.at[k1], recv.at[13]).start()

    wait_bytes(gparts, recv.at[14])
    high, low = halves(jnp.sum(gparts[...], axis=0))
    eg_ref[...] = dot(high, proj[...]) + dot(low, proj[...])
    outs.append(pltpu.make_async_copy(eg_ref, eg_hbm, stores.at[4]))
    outs[4].start()

    for copy in outs:
        copy.wait()
    wait_bytes(eb.at[0 : nc - 1], send.at[0])
    wait_bytes(quad.at[0 : per - 1], send.at[1])
    pl.when(row_after)(lambda: wait_bytes(rows8, send.at[2]))
    pl.when(row_before)(lambda: wait_bytes(rows8, send.at[3]))

    def sent_targets(cond, mine, eight, seven, sem):
        pl.when(cond & mine)(lambda: wait_bytes(seven, send.at[sem]))
        pl.when(cond & jnp.logical_not(mine))(lambda: wait_bytes(eight, send.at[sem]))

    sent_targets(col_after, rb + 1 == c, rows8, rows7, 4)
    sent_targets(col_before, rb - 1 == c, rows8, rows7, 5)
    sent_targets(rb >= 0, p.in_others, blocks, blocks.at[0 : nc - 1], 15)
    pl.when(p.in_others)(lambda: wait_bytes(cparts.at[0 : per - 1], send.at[6]))
    pl.when(jnp.logical_not(p.in_others))(lambda: wait_bytes(cparts, send.at[6]))
    pl.when(p.has_up)(lambda: wait_bytes(row_ends.at[0], send.at[7]))
    pl.when(p.has_down)(lambda: wait_bytes(row_ends.at[1], send.at[8]))
    pl.when(p.has_left)(lambda: wait_bytes(col_ends.at[0], send.at[9]))
    pl.when(p.has_right)(lambda: wait_bytes(col_ends.at[1], send.at[10]))
    wait_bytes(line.at[0 : nc - 1], send.at[16])
    pl.when(owner)(lambda: wait_bytes(r1.at[0 : PIECES - 1], send.at[11]))
    pl.when(jnp.logical_not(owner))(lambda: wait_bytes(r1.at[0:PIECES], send.at[11]))
    pl.when(owner)(lambda: wait_bytes(r2.at[0 : r2.shape[0] - 1], send.at[12]))
    wait_bytes(gparts.at[0 : nc - 1], send.at[14])

    pl.when(owner)(lambda: wait_bytes(r1.at[0 : r1.shape[0] - 1], send.at[13]))
    wait_bytes(sums_hbm, recv.at[13])


def finish_kernel(
    scale, sums_in, eg_in, pair_in, conv_out, left_out, right_out, eg_out, pair_out,
    sums_ref, eg_ref, held, conv_ref, left_ref, right_ref, loads, stores,
):
    def piece(k):
        return slice(8 * k, 8 * k + 8)

    ins = [pltpu.make_async_copy(sums_in, sums_ref, loads.at[0]), pltpu.make_async_copy(eg_in, eg_ref, loads.at[1])]
    ins += [pltpu.make_async_copy(pair_in.at[piece(k)], held.at[piece(k)], loads.at[2 + k]) for k in range(4)]
    outs = [
        pltpu.make_async_copy(conv_ref, conv_out, stores.at[0]),
        pltpu.make_async_copy(left_ref, left_out, stores.at[1]),
        pltpu.make_async_copy(right_ref, right_out, stores.at[2]),
        pltpu.make_async_copy(eg_ref, eg_out, stores.at[3]),
    ]
    outs += [pltpu.make_async_copy(held.at[piece(k)], pair_out.at[piece(k)], stores.at[4 + k]) for k in range(4)]
    for copy in ins:
        copy.start()
    ins[0].wait()
    for ref, first, at in ((left_ref, 0, 1), (right_ref, 8, 2)):
        for k in range(8):
            x = sums_ref[first + k].astype(F32)
            ref[16 * (k // 4) : 16 * (k // 4) + 16, 128 * (k % 4) : 128 * (k % 4) + 128] = x * scale
        outs[at].start()
    ins[1].wait()
    outs[3].start()
    for k in range(4):
        ins[2 + k].wait()
        outs[4 + k].start()
    for k in range(9):
        q, at = divmod(k, 4)
        for part in range(2):
            x = sums_ref[16 + 2 * q + part].astype(F32)
            conv_ref[k, 16 * part : 16 * part + 16, :] = x[:, 32 * at : 32 * at + 32] * scale
    outs[0].start()
    for copy in outs:
        copy.wait()


def shards(nr, nc, embed, left_proj, right_proj, conv_w, cotangent):
    per = nr // nc
    pair_out, totals, embed_grad = pl.pallas_call(
        functools.partial(pair_kernel, nr, nc),
        out_shape=(
            jax.ShapeDtypeStruct((32, 64, 256), BF16),
            jax.ShapeDtypeStruct((PIECES, 16, 128), BF16),
            jax.ShapeDtypeStruct((8, 512), F32),
        ),
        in_specs=[HBM] * 5,
        out_specs=(HBM,) * 3,
        scratch_shapes=LOCAL_SCRATCH
        + [
            pltpu.VMEM((32, 64, 256), BF16),
            pltpu.VMEM((8, 512), F32),
            pltpu.VMEM((136, 128), F32),
            pltpu.VMEM((8, 512), BF16),
            pltpu.VMEM((9, 32, 32), BF16),
            pltpu.VMEM((32, 64, 256), BF16),
            pltpu.VMEM((8, 128), F32),
            pltpu.VMEM((8, 128), F32),
            pltpu.VMEM((8, 128), F32),
            pltpu.VMEM((per, 8, 128), F32),
            pltpu.VMEM((nc, 8, 128), F32),
            pltpu.VMEM((128, 512), BF16),
            pltpu.VMEM((16, 256), BF16),
            pltpu.VMEM((nc, 16, 256), BF16),
            pltpu.VMEM((64, 256), BF16),
            pltpu.VMEM((64, 256), BF16),
            pltpu.VMEM((nc, 8, 128), F32),
            pltpu.VMEM((2, 8, 128), F32),
            pltpu.VMEM((2, 8, 128), F32),
            pltpu.VMEM((per, 16, 128), F32),
            pltpu.VMEM((2, per, 16, 128), F32),
            pltpu.VMEM((2, 16, 128), F32),
            pltpu.VMEM((64, 128), F32),
            pltpu.VMEM((nc, 8, 128), F32),
            pltpu.VMEM((PIECES, 16, 128), BF16),
            pltpu.VMEM((32, 16, 128), BF16),
            pltpu.VMEM((8, 16, 128), BF16),
            pltpu.VMEM((16, 128), BF16),
            pltpu.VMEM((16, 128), BF16),
            pltpu.SemaphoreType.DMA((17,)),
            pltpu.SemaphoreType.DMA((17,)),
            pltpu.SemaphoreType.DMA((5,)),
            pltpu.SemaphoreType.DMA((6,)),
        ],
        compiler_params=pltpu.CompilerParams(
            collective_id=0, has_side_effects=True, vmem_limit_bytes=60 * 1024 * 1024
        ),
        name="pair_kernel",
    )(embed, left_proj.T, right_proj.T, conv_w, cotangent)
    conv_grad, left_t, right_t, embed_grad, pair_out = pl.pallas_call(
        functools.partial(finish_kernel, 32.0 / (8 * nr * nc)),
        out_shape=(
            jax.ShapeDtypeStruct((9, 32, 32), F32),
            jax.ShapeDtypeStruct((32, 512), F32),
            jax.ShapeDtypeStruct((32, 512), F32),
            jax.ShapeDtypeStruct((8, 512), F32),
            jax.ShapeDtypeStruct((32, 64, 256), BF16),
        ),
        in_specs=[HBM] * 3,
        out_specs=(HBM,) * 5,
        scratch_shapes=[
            pltpu.VMEM((PIECES, 16, 128), BF16),
            pltpu.VMEM((8, 512), F32),
            pltpu.VMEM((32, 64, 256), BF16),
            pltpu.VMEM((9, 32, 32), F32),
            pltpu.VMEM((32, 512), F32),
            pltpu.VMEM((32, 512), F32),
            pltpu.SemaphoreType.DMA((6,)),
            pltpu.SemaphoreType.DMA((8,)),
        ],
        compiler_params=pltpu.CompilerParams(vmem_limit_bytes=60 * 1024 * 1024),
        name="finish",
    )(totals, embed_grad, pair_out)
    return pair_out, conv_grad, left_t.T, right_t.T, embed_grad


def solution(mesh):
    body = functools.partial(shards, mesh.shape["row"], mesh.shape["col"])
    in_specs = (P(("row", "col"), None), P(), P(), P(), P(None, "row", "col"))
    out_specs = (P(None, "row", "col"), P(), P(), P(), P(("row", "col"), None))
    return jax.shard_map(body, mesh=mesh, in_specs=in_specs, out_specs=out_specs, check_vma=False)
```

```python
import functools

import jax
import jax.numpy as jnp
from jax import lax
from jax.experimental import pallas as pl
from jax.experimental.pallas import tpu as pltpu
from jax.sharding import PartitionSpec as P

MESH = pl.DeviceIdType.MESH
OUTSIDE = -1e30
LOG2E = 1.4426950408889634
LN2 = 0.6931471805599453
PIECES = 22
F32 = jnp.float32
BF16 = jnp.bfloat16
VMEM = pl.BlockSpec(memory_space=pltpu.VMEM)
HBM = pl.BlockSpec(memory_space=pltpu.HBM)


def iota(shape, dim):
    return lax.broadcasted_iota(jnp.int32, shape, dim)


def one_hot(cond):
    return jnp.where(cond, 1.0, 0.0).astype(BF16)


def dot(a, b):
    return jnp.dot(a, b, preferred_element_type=F32)


def dot_nt(a, b):
    return lax.dot_general(a, b, (((1,), (1,)), ((), ())), preferred_element_type=F32)


def dot_tn(a, b):
    return lax.dot_general(a, b, (((0,), (0,)), ((), ())), preferred_element_type=F32)


def halves(x):
    high = x.astype(BF16)
    return high, (x - high.astype(F32)).astype(BF16)


def loop(n, f):
    def body(k, _):
        f(k)
        return 0

    lax.fori_loop(0, n, body, 0)


def lanes(h):
    return pl.ds(pl.multiple_of(h * 256, 256), 256)


def wait_bytes(ref, sem):
    pltpu.make_async_copy(ref, ref, sem).wait()


def softplus_and_slope(y):
    t = jnp.exp2(-jnp.abs(y))
    u = 1.0 + t
    inv = pltpu.reciprocal(u, full_range=False)
    log = jnp.where(t < 2.0**-11, t * LOG2E, jnp.log2(u))
    return jnp.maximum(y, 0.0) + log, jnp.where(y >= 0, inv, t * inv)


def build_taps(w_ref, tf):
    spread = one_hot((iota((256, 32), 0) >> 3) == iota((256, 32), 1))
    widen = one_hot((iota((32, 256), 1) >> 3) == iota((32, 256), 0))
    s0, s1 = iota((256, 256), 0) & 7, iota((256, 256), 1) & 7
    same, above, below = s1 == s0, s1 == s0 + 4, s1 == s0 - 4
    x = dot(w_ref[...].reshape(288, 32), widen).astype(BF16)
    for b in range(3):
        x0, x1, x2 = (dot(spread, x[96 * a + 32 * b : 96 * a + 32 * b + 32]) for a in range(3))
        tf[:, 256 * b : 256 * b + 256] = jnp.where(same, x0, jnp.where(above, x1, 0.0)).astype(BF16)
        tf[:, 768 + 256 * b : 1024 + 256 * b] = jnp.where(same, x2, jnp.where(below, x1, 0.0)).astype(BF16)


def mask_cotangent(r, c, cot_ref, move, mall, mt):
    mall[0:256, 2048:2304] = jnp.zeros((256, 256), BF16)
    mall[256:512, 0:256] = jnp.zeros((256, 256), BF16)
    for k in range(4):
        x = cot_ref[:, 16 * k : 16 * k + 16, :].astype(F32)
        row = r * 64 + 16 * k + iota((16, 256), 0)
        x = jnp.where((c * 256 + iota((16, 256), 1) >= row)[None], x, 0.0)
        for half in range(2):
            m = x[:, 8 * half : 8 * half + 8].reshape(256, 256).astype(BF16)
            mall[0:256, lanes(2 * k + half)] = m
            mall[256:512, lanes(2 * k + half + 1)] = m
    for b in range(2):
        move[272 * b : 272 * b + 272, :] = one_hot(iota((272, 256), 0) - 4 * b == iota((272, 256), 1))
    mt[0] = jnp.zeros((272, 768), BF16)
    mt[9] = jnp.zeros((272, 768), BF16)
    none = jnp.zeros((8, 256), F32)

    def body(g):
        moved = dot_nt(move[...], mall[0:256, lanes(g)])
        mt[g + 1, :, 0:256] = moved[0:272].astype(BF16)
        mt[g + 1, :, 256:512] = moved[272:544].astype(BF16)
        mt[g + 1, :, 512:768] = jnp.concatenate([none, moved[0:264]], axis=0).astype(BF16)

    loop(8, body)


def input_gradient(mt, tf, z, steps):
    def body(step, _):
        left = [jnp.concatenate([mt[3 * step + k], mt[3 * step + k + 1]], axis=1) for k in range(3)]
        right = jnp.concatenate(
            [tf[:, 768 * (1 - u) + 256 * b : 768 * (1 - u) + 256 * b + 256] for u in range(2) for b in range(3)], axis=0
        )
        x = dot(jnp.concatenate(left, axis=0), right)
        for k in range(3):
            z[3 * step + k] = x[272 * k : 272 * k + 272]
        return 0

    lax.fori_loop(*steps, body, 0)


def features(rows, blocks, before, after, onto, rowf, colf):
    picks = [onto[:, 256 * at : 256 * at + 256] for at in range(4)]
    first = dot(before, picks[3])
    last = dot(after, picks[0])
    x = [first[4:8]] + [dot(blocks, pick) for pick in picks] + [last[0:4], jnp.zeros((8, 256), F32)]
    colf[...] = jnp.concatenate(x, axis=0) * LOG2E
    x = dot(rows, picks[0])
    x = jnp.where((iota((128, 256), 0) & 7) == (iota((128, 256), 1) & 7), x, 0.0).astype(BF16)
    rowf[...] = dot(one_hot((iota((16, 128), 1) >> 3) == iota((16, 128), 0)), x) * LOG2E


def elementwise(rowf, colf, z, act, cacc, rsum):
    rsum[...] = jnp.zeros_like(rsum)

    def body(step):
        parts = [pl.ds(pl.multiple_of(24 * step + 8 * part, 8), 8) for part in range(3)]
        totals = [jnp.zeros((8, 256), F32)] * 3
        for h in range(9):
            left = rowf[h : h + 1, :]
            row = jnp.zeros((8, 256), F32)
            for k, rows in enumerate(parts):
                value, slope = softplus_and_slope(colf[rows, :] + left)
                act[h, rows, :] = value
                p = z[h, rows, :] * slope
                totals[k] += p
                row += p
            rsum[8 * h : 8 * h + 8, :] += row
        for k, rows in enumerate(parts):
            cacc[rows, :] = totals[k]

    loop(11, body)


def build_constants(onto, pick, by_group):
    k, n = iota((128, 256), 0), iota((128, 256), 1) >> 3
    for at in range(4):
        onto[:, 256 * at : 256 * at + 256] = one_hot(k == n + 32 * at)
    k, n = iota((256, 128), 0) >> 3, iota((256, 128), 1)
    for g in range(4):
        pick[256 * g : 256 * g + 256, :] = one_hot(k + 32 * g == n)
    by_group[...] = one_hot((iota((80, 128), 0) >> 3) == (iota((80, 128), 1) >> 3))


def ends_of(x, pick, ends):
    sub = iota((16, 128), 0)
    high, low = halves(x)
    first = dot(high, pick[768:1024]) + dot(low, pick[768:1024])
    second = dot(high, pick[0:256]) + dot(low, pick[0:256])
    ends[0] = jnp.where(sub >= 12, pltpu.roll(first, 12, 0), 0.0)[8:16]
    ends[1] = jnp.where(sub < 4, pltpu.roll(second, 4, 0), 0.0)[0:8]


def column_sums(cacc, pick, cols):
    x = [
        jnp.concatenate([cacc[4 + 64 * q + 16 * g : 20 + 64 * q + 16 * g, :] for g in range(4)], axis=1) for q in range(4)
    ]
    high, low = halves(jnp.concatenate(x, axis=0))
    x = dot(high, pick[...]) + dot(low, pick[...])
    for q in range(4):
        cols[q] = x[16 * q : 16 * q + 16]


def column_end_sums(cacc, pick, col_ends):
    ends_of(jnp.concatenate([cacc[0:8, :], cacc[256:264, :]], axis=0), pick, col_ends)


def row_sums(rsum, pick, by_group, row_main, row_ends):
    x = jnp.concatenate([rsum[...], jnp.zeros((56, 256), F32)], axis=0)
    high, low = halves(x)
    x = dot(by_group[...], high) + dot(by_group[...], low)
    x = jnp.where((iota((80, 256), 0) & 7) == (iota((80, 256), 1) & 7), x, 0.0)
    ends_of(jnp.concatenate([x[0:8], x[64:72]], axis=0), pick, row_ends)
    high, low = halves(jnp.concatenate([x[4 + 16 * g : 20 + 16 * g] for g in range(4)], axis=1))
    row_main[...] = dot(high, pick[...]) + dot(low, pick[...])


def build_windows(act, a3):
    def body(h):
        at = pl.ds(pl.multiple_of(256 * h, 256), 256)
        for b in range(3):
            a3[at, 256 * b : 256 * b + 256] = (act[h, 4 * b : 4 * b + 256, :] * LN2).astype(BF16)

    loop(9, body)


def convolve(r, c, k, a3, tf, out_ref):
    parts = []
    for g in (2 * k, 2 * k + 1):
        both = jnp.concatenate([a3[256 * (g + u) : 256 * (g + u) + 256, :] for u in range(2)], axis=1)
        parts.append(dot_nt(tf[...], both).reshape(32, 8, 256))
    y = jnp.concatenate(parts, axis=1)
    row = r * 64 + 16 * k + iota((16, 256), 0)
    col = c * 256 + iota((16, 256), 1)
    out_ref[:, 16 * k : 16 * k + 16, :] = jnp.where((col >= row)[None], y, 0.0).astype(BF16)


def tap_gradient(mall, a3, pick, gram, taps):
    x = dot(mall[...], a3[...])
    for u in range(2):
        for k in range(6):
            gram[6 * u + k] = x[256 * u : 256 * u + 256, 128 * k : 128 * k + 128]
    lane = iota((32, 128), 1)

    def along(b, k, sources):
        total = jnp.zeros((32, 128), F32)
        for at, (s, u) in enumerate(sources):
            total = jnp.where((lane & 7) == at, gram[6 * u + 2 * b + k, pl.ds(s, 32, stride=8), :], total)
        return total

    sources = (
        [(s, 0) for s in range(8)],
        [((s + 4) % 8, 1 - s // 4) for s in range(8)],
        [(s, 1) for s in range(8)],
    )
    x = [jnp.concatenate([along(b, k, sources[a]) for k in range(2)], axis=1) for a in range(3) for b in range(3)]
    y = dot(jnp.concatenate(halves(jnp.concatenate(x, axis=0)), axis=0), pick[0:256])
    y = y[0:288] + y[288:576]
    for q in range(3):
        total = jnp.zeros((32, 128), F32)
        for k in range(min(4, 9 - 4 * q)):
            tap = y[32 * (4 * q + k) : 32 * (4 * q + k) + 32]
            total = jnp.where((lane >> 5) == k, pltpu.roll(tap, 32 * k, 1) if k else tap, total)
        taps[32 * q : 32 * q + 32, :] = total


LOCAL_SCRATCH = [
    pltpu.VMEM((16, 256), F32),
    pltpu.VMEM((272, 256), F32),
    pltpu.VMEM((96, 128), F32),
    pltpu.VMEM((512, 2304), BF16),
    pltpu.VMEM((10, 272, 768), BF16),
    pltpu.VMEM((9, 272, 256), F32),
    pltpu.VMEM((2304, 768), BF16),
    pltpu.VMEM((9, 272, 256), F32),
    pltpu.VMEM((256, 1536), BF16),
    pltpu.VMEM((544, 256), BF16),
    pltpu.VMEM((128, 1024), BF16),
    pltpu.VMEM((1024, 128), BF16),
    pltpu.VMEM((80, 128), BF16),
    pltpu.VMEM((12, 256, 128), F32),
    pltpu.VMEM((272, 256), F32),
    pltpu.VMEM((72, 256), F32),
    pltpu.VMEM((4, 16, 128), F32),
    pltpu.VMEM((2, 8, 128), F32),
    pltpu.VMEM((16, 128), F32),
    pltpu.VMEM((2, 8, 128), F32),
]


class Place:
    def __init__(self, nr, nc):
        r, c = lax.axis_index("row"), lax.axis_index("col")
        self.r, self.c, self.nr, self.nc = r, c, nr, nc
        self.per = nr // nc
        self.rb, self.rm = lax.div(r, self.per), lax.rem(r, self.per)
        _, self.quad = self.group(((r, 1, 0), (r, 2, 0)))
        _, self.line = self.group(((c, 1, 1), (c, 2, 1), (c, 4, 1)))
        self.plane = ((r, 1, 0), (r, 8, 0), (c, 2, 1), (r, 16, 0), (c, 4, 1))
        self.k1, self.group1 = self.group(self.plane)
        self.z_line = ((r, 2, 0), (r, 4, 0), (c, 1, 1))
        self.k2, self.group2 = self.group(self.z_line)
        self.has_up, self.has_down = r > 0, r < nr - 1
        self.has_left, self.has_right = c > 0, c < nc - 1
        self.ends_block = (self.rm == self.per - 1) & (self.rb < nc - 1)
        self.starts_block = (self.rm == 0) & (self.rb > 0)
        self.in_others = self.rb == c

    def group(self, bits):
        number, turns = 0, []
        for k, (x, weight, is_col) in enumerate(bits):
            bit = lax.rem(lax.div(x, weight), 2)
            number = number + bit * (1 << k)
            sign = 1 - 2 * bit
            turns.append((sign * weight, is_col, sign * (1 << k)))
        members = [(self.r, self.c, number)]
        for move, is_col, step in turns:
            members += [
                (a, b + move, n + step) if is_col else (a + move, b, n + step) for a, b, n in members
            ]
        return number, members[:0:-1]

    def member(self, bits, k):
        a, b = self.r, self.c
        for at, (x, weight, is_col) in enumerate(bits):
            move = weight * (k >> at & 1) - weight * lax.rem(lax.div(x, weight), 2)
            a, b = (a, b + move) if is_col else (a + move, b)
        return a, b

    def other(self, k):
        return self.per * self.c + k, self.rb

    def targets(self, col):
        return [(lax.rem(self.r + self.per * k, self.nr), col) for k in range(self.nr // self.per)]

    def greet(self):
        r, c, nc, per, rb, rm = self.r, self.c, self.nc, self.per, self.rb, self.rm
        barrier = pltpu.get_barrier_semaphore()

        def signal(a, b):
            pl.semaphore_signal(barrier, inc=1, device_id=(a, b), device_id_type=MESH)

        def signal_all(col):
            for k in range(per):
                signal(per * c + k, col)

        is_first, is_last = c == 0, c == nc - 1
        before_is_me = is_last & (rb == nc - 2)
        after_is_me = is_first & (rb == 1)
        for a, b, _ in self.quad + self.line:
            signal(a, b)
        pl.when(jnp.logical_not(self.in_others))(lambda: signal(per * c + rm, c))
        for _, b, _ in self.line:
            signal(per * c + rm, b)
        pl.when(self.has_up)(lambda: signal(r - 1, nc - 1))
        pl.when(self.has_down)(lambda: signal(r + 1, 0))
        pl.when(self.has_left & jnp.logical_not(before_is_me))(lambda: signal(per * (c - 1) + rm, nc - 1))
        pl.when(self.has_right & jnp.logical_not(after_is_me))(lambda: signal(per * (c + 1) + rm, 0))
        pl.when(jnp.logical_not(self.in_others))(lambda: signal(per * c + rm, rb))
        for a, _, _ in self.quad:
            signal(per * (c - rb) + a, rb)
        pl.when(self.has_up)(lambda: signal(r - 1, c))
        pl.when(self.has_down)(lambda: signal(r + 1, c))
        pl.when(self.ends_block)(lambda: signal_all(rb + 1))
        pl.when(self.starts_block)(lambda: signal_all(rb - 1))
        owner = self.k1 < PIECES

        @pl.when(owner)
        def _():
            for a, b, _ in self.group1 + self.group2:
                signal(a, b)

        @pl.when(jnp.logical_not(owner))
        def _():
            for k in range(PIECES):
                signal(*self.member(self.plane, k))

        n = len(self.quad + self.line) + nc + per
        n = n + jnp.where(owner, len(self.group1 + self.group2), PIECES)
        up, down = self.has_up, self.has_down
        for cond, m in (
            (self.in_others, -2), (is_last & down, nc), (is_first & up, nc),
            (is_last & (rb < nc - 1), nc), (before_is_me, -1), (is_first & (rb > 0), nc), (after_is_me, -1),
            (up, 1), (down, 1), (self.has_left, 1), (self.has_right, 1),
        ):
            n = n + jnp.where(cond, m, 0)
        return n

    def senders(self, send, recv):
        def put(src, dst_r, dst_c, dst, sem):
            pltpu.make_async_remote_copy(
                src, dst, send.at[sem], recv.at[sem], device_id=(dst_r, dst_c), device_id_type=MESH
            ).start()

        def put_other(src, k, dst, sem):
            a, b = self.other(k)
            mine = (a == self.r) & (b == self.c)
            pl.when(mine)(lambda: pltpu.make_async_copy(src, dst, recv.at[sem]).start())
            pl.when(jnp.logical_not(mine))(lambda: put(src, a, b, dst, sem))

        return put, put_other


def pair_kernel(
    nr, nc, e_hbm, lpt_hbm, rpt_hbm, w_hbm, cot_hbm,
    out_hbm, sums_hbm, eg_hbm,
    rowf, colf, taps, mall, mt, act, a3, z, tf, move, onto, pick, by_group, gram, cacc, rsum, cols, col_ends, row_main, row_ends,
    out_ref, eg_ref, feats, e_ref, w_ref, cot_ref, own, right, packed, quad, line, proj, es, eb, twice, blocks, row_feats, col_feats,
    cparts, cends, rends, turned, gparts, buf, r1, r2, mid, fin, recv, send, loads, stores,
):
    ins = ((e_hbm, e_ref), (w_hbm, w_ref), (lpt_hbm, proj.at[0:32]), (rpt_hbm, proj.at[32:64]), (cot_hbm, cot_ref))
    ins = [pltpu.make_async_copy(src, dst, loads.at[k]) for k, (src, dst) in enumerate(ins)]
    for copy in ins:
        copy.start()
    p = Place(nr, nc)
    r, c, per, rb, rm, k1, k2 = p.r, p.c, p.per, p.rb, p.rm, p.k1, p.k2
    greeted = p.greet()
    put, put_other = p.senders(send, recv)
    rows8, rows7 = gparts, gparts.at[0 : nc - 1]

    proj[64:128, :] = jnp.zeros((64, 512), BF16)
    ins[0].wait()
    e = e_ref[...].astype(F32)
    es[...] = jnp.concatenate([e[:, 0:256], e[:, 256:512]], axis=0).astype(BF16)
    ins[2].wait()
    ins[3].wait()
    own[...] = dot_nt(e_ref[...], proj[...]).astype(BF16).astype(F32)
    group = iota((8, 128), 1) >> 5
    right[...] = jnp.where(group == rm, pltpu.roll(own[...], lax.rem(32 * rm + 96, 128), 1), 0.0)
    ins[1].wait()
    build_taps(w_ref, tf)
    ins[4].wait()
    mask_cotangent(r, c, cot_ref, move, mall, mt)
    pl.semaphore_wait(pltpu.get_barrier_semaphore(), greeted)

    for a, b, _ in p.quad:
        put(right, a, b, quad.at[rm], 1)
    pltpu.make_async_copy(right, quad.at[rm], recv.at[1]).start()

    def put_line(row, dst, sem):
        for k in range(nc):
            put(own, row, k, dst, sem)

    is_first, is_last = c == 0, c == nc - 1
    row_after, row_before = is_last & p.has_down, is_first & p.has_up
    pl.when(row_after)(lambda: put_line(r + 1, row_feats.at[0], 2))
    pl.when(row_before)(lambda: put_line(r - 1, row_feats.at[1], 3))
    for a, b, _ in p.line:
        put(own, a, b, line.at[c], 16)
    pltpu.make_async_copy(own, line.at[c], recv.at[16]).start()

    def put_targets(src, col, dst, sem):
        first, *rest = p.targets(col)
        mine = c == col
        pl.when(mine)(lambda: pltpu.make_async_copy(src, dst, recv.at[sem]).start())
        pl.when(jnp.logical_not(mine))(lambda: put(src, *first, dst, sem))
        for a, b in rest:
            put(src, a, b, dst, sem)

    col_after, col_before = is_last & (rb < nc - 1), is_first & (rb > 0)
    input_gradient(mt, tf, z, (0, 1))
    wait_bytes(quad, recv.at[1])
    packed[...] = jnp.sum(quad[...], axis=0)
    put_targets(packed, rb, blocks.at[c], 15)
    pl.when(col_after)(lambda: put_targets(packed, rb + 1, col_feats.at[0], 4))
    pl.when(col_before)(lambda: put_targets(packed, rb - 1, col_feats.at[1], 5))
    input_gradient(mt, tf, z, (1, 3))
    build_constants(onto, pick, by_group)

    def arrive(cond, ref, sem):
        pl.when(cond)(lambda: wait_bytes(ref, sem))
        pl.when(jnp.logical_not(cond))(lambda: ref.__setitem__(..., jnp.full(ref.shape, OUTSIDE, F32)))

    arrive(p.has_up, row_feats.at[0], recv.at[2])
    arrive(p.has_down, row_feats.at[1], recv.at[3])
    arrive(p.has_left, col_feats.at[0], recv.at[4])
    arrive(p.has_right, col_feats.at[1], recv.at[5])
    wait_bytes(line, recv.at[16])
    wait_bytes(blocks, recv.at[15])
    feats[8:72, :] = line[...].reshape(8 * nc, 128)
    feats[0:8, :] = row_feats[0]
    feats[72:80, :] = row_feats[1]
    feats[80:136, :] = jnp.zeros((56, 128), F32)
    ends = [jnp.concatenate([col_feats[k], jnp.zeros((8, 128), F32)], axis=0).astype(BF16) for k in range(2)]
    features(feats[4:132, :].astype(BF16), blocks[...].reshape(8 * nc, 128).astype(BF16), *ends, onto, rowf, colf)
    for a, b, _ in p.line:
        put(es, a, b, eb.at[c], 0)
    pltpu.make_async_copy(es, eb.at[c], recv.at[0]).start()
    elementwise(rowf, colf, z, act, cacc, rsum)

    column_sums(cacc, pick, cols)
    for k in range(per):
        put_other(cols.at[k], k, cparts.at[rm], 6)
    column_end_sums(cacc, pick, col_ends)
    pl.when(p.has_left)(lambda: put(col_ends.at[0], per * c - 1, rb, cends.at[0, rm], 9))
    pl.when(p.has_right)(lambda: put(col_ends.at[1], per * c + per, rb, cends.at[1, rm], 10))
    row_sums(rsum, pick, by_group, row_main, row_ends)
    pl.when(p.has_up)(lambda: put(row_ends.at[0], r - 1, c, rends.at[0], 7))
    pl.when(p.has_down)(lambda: put(row_ends.at[1], r + 1, c, rends.at[1], 8))

    build_windows(act, a3)
    tap_gradient(mall, a3, pick, gram, taps)
    for k in range(PIECES - 16):
        buf[16 + k] = taps[16 * k : 16 * k + 16, :].astype(BF16)

    def put_piece(k):
        pl.when(k1 != k)(lambda: put(buf.at[k], *p.member(p.plane, k), r1.at[k1], 11))

    for k in range(16, PIECES):
        put_piece(k)
    wait_bytes(eb, recv.at[0])
    e = eb[...].astype(F32)
    e = jnp.concatenate([e[:, 0:8].reshape(64, 256), e[:, 8:16].reshape(64, 256)], axis=1).astype(BF16)
    twice[...] = jnp.concatenate([e, e], axis=0)

    def gather_sum(cond, ref, sem):
        pl.when(cond)(lambda: wait_bytes(ref, sem))
        pl.when(jnp.logical_not(cond))(lambda: ref.__setitem__(..., jnp.zeros(ref.shape, F32)))

    gather_sum(p.has_down, rends.at[0], recv.at[7])
    gather_sum(p.has_up, rends.at[1], recv.at[8])
    gather_sum(p.ends_block, cends.at[0], recv.at[9])
    gather_sum(p.starts_block, cends.at[1], recv.at[10])
    wait_bytes(cparts, recv.at[6])
    grads = (
        row_main[...] + jnp.concatenate([rends[1], rends[0]], axis=0),
        jnp.sum(cparts[...], axis=0)
        + jnp.concatenate([jnp.sum(cends[1], axis=0), jnp.sum(cends[0], axis=0)], axis=0),
    )
    lane = iota((16, 128), 1)
    spread = []
    for g in range(4):
        parts = [x if turn % 128 == 0 else pltpu.roll(x, turn % 128, 1) for x, turn in zip(grads, (-32 * g, 32 - 32 * g))]
        spread.append(jnp.where(lane < 32, parts[0], jnp.where(lane < 64, parts[1], 0.0)))
    turned[...] = jnp.concatenate(spread, axis=0)

    part = dot_tn(jnp.concatenate(halves(turned[...]), axis=0), twice[...])
    for k in range(16):
        at = slice(16 * (k // 4), 16 * (k // 4) + 16), slice(128 * (k % 4), 128 * (k % 4) + 128)
        buf[k] = part[at].astype(BF16)

    owner = k1 < PIECES
    for k in range(16):
        put_piece(k)
    pl.when(owner)(lambda: pltpu.make_async_copy(buf.at[k1], r1.at[k1], recv.at[11]).start())

    outs = [
        pltpu.make_async_copy(out_ref.at[:, 16 * q : 16 * q + 16, :], out_hbm.at[:, 16 * q : 16 * q + 16, :], stores.at[q])
        for q in range(4)
    ]
    convolve(r, c, 0, a3, tf, out_ref)
    outs[0].start()
    for a, b, _ in p.line:
        put(turned.at[pl.ds(pl.multiple_of(8 * b, 8), 8)], a, b, gparts.at[c], 14)
    pltpu.make_async_copy(turned.at[pl.ds(pl.multiple_of(8 * c, 8), 8)], gparts.at[c], recv.at[14]).start()
    convolve(r, c, 1, a3, tf, out_ref)
    outs[1].start()

    @pl.when(owner)
    def _():
        wait_bytes(r1, recv.at[11])
        mid[...] = jnp.sum(r1[...].astype(F32), axis=0).astype(BF16)
        for k in range(8):
            pl.when(k2 != k)(lambda k=k: put(mid, *p.member(p.z_line, k), r2.at[k2], 12))
        pltpu.make_async_copy(mid, r2.at[k2], recv.at[12]).start()

    convolve(r, c, 2, a3, tf, out_ref)
    outs[2].start()
    convolve(r, c, 3, a3, tf, out_ref)
    outs[3].start()

    @pl.when(owner)
    def _():
        wait_bytes(r2, recv.at[12])
        fin[...] = jnp.sum(r2[...].astype(F32), axis=0).astype(BF16)
        for k in (1, 0, *range(2, 32)):
            pl.when(k1 != k)(lambda k=k: put(fin, *p.member(p.plane, k), sums_hbm.at[k1], 13))
        pltpu.make_async_copy(fin, sums_hbm.at[k1], recv.at[13]).start()

    wait_bytes(gparts, recv.at[14])
    high, low = halves(jnp.sum(gparts[...], axis=0))
    eg_ref[...] = dot(high, proj[...]) + dot(low, proj[...])
    outs.append(pltpu.make_async_copy(eg_ref, eg_hbm, stores.at[4]))
    outs[4].start()

    for copy in outs:
        copy.wait()
    wait_bytes(eb.at[0 : nc - 1], send.at[0])
    wait_bytes(quad.at[0 : per - 1], send.at[1])
    pl.when(row_after)(lambda: wait_bytes(rows8, send.at[2]))
    pl.when(row_before)(lambda: wait_bytes(rows8, send.at[3]))

    def sent_targets(cond, mine, eight, seven, sem):
        pl.when(cond & mine)(lambda: wait_bytes(seven, send.at[sem]))
        pl.when(cond & jnp.logical_not(mine))(lambda: wait_bytes(eight, send.at[sem]))

    sent_targets(col_after, rb + 1 == c, rows8, rows7, 4)
    sent_targets(col_before, rb - 1 == c, rows8, rows7, 5)
    sent_targets(rb >= 0, p.in_others, blocks, blocks.at[0 : nc - 1], 15)
    pl.when(p.in_others)(lambda: wait_bytes(cparts.at[0 : per - 1], send.at[6]))
    pl.when(jnp.logical_not(p.in_others))(lambda: wait_bytes(cparts, send.at[6]))
    pl.when(p.has_up)(lambda: wait_bytes(row_ends.at[0], send.at[7]))
    pl.when(p.has_down)(lambda: wait_bytes(row_ends.at[1], send.at[8]))
    pl.when(p.has_left)(lambda: wait_bytes(col_ends.at[0], send.at[9]))
    pl.when(p.has_right)(lambda: wait_bytes(col_ends.at[1], send.at[10]))
    wait_bytes(line.at[0 : nc - 1], send.at[16])
    pl.when(owner)(lambda: wait_bytes(r1.at[0 : PIECES - 1], send.at[11]))
    pl.when(jnp.logical_not(owner))(lambda: wait_bytes(r1.at[0:PIECES], send.at[11]))
    pl.when(owner)(lambda: wait_bytes(r2.at[0 : r2.shape[0] - 1], send.at[12]))
    wait_bytes(gparts.at[0 : nc - 1], send.at[14])

    pl.when(owner)(lambda: wait_bytes(r1.at[0 : r1.shape[0] - 1], send.at[13]))
    wait_bytes(sums_hbm, recv.at[13])


def finish_kernel(
    scale, sums_in, eg_in, pair_in, conv_out, left_out, right_out, eg_out, pair_out,
    sums_ref, eg_ref, held, conv_ref, left_ref, right_ref, loads, stores,
):
    def piece(k):
        return slice(8 * k, 8 * k + 8)

    ins = [pltpu.make_async_copy(sums_in, sums_ref, loads.at[0]), pltpu.make_async_copy(eg_in, eg_ref, loads.at[1])]
    ins += [pltpu.make_async_copy(pair_in.at[piece(k)], held.at[piece(k)], loads.at[2 + k]) for k in range(4)]
    outs = [
        pltpu.make_async_copy(conv_ref, conv_out, stores.at[0]),
        pltpu.make_async_copy(left_ref, left_out, stores.at[1]),
        pltpu.make_async_copy(right_ref, right_out, stores.at[2]),
        pltpu.make_async_copy(eg_ref, eg_out, stores.at[3]),
    ]
    outs += [pltpu.make_async_copy(held.at[piece(k)], pair_out.at[piece(k)], stores.at[4 + k]) for k in range(4)]
    for copy in ins:
        copy.start()
    ins[0].wait()
    for ref, first, at in ((left_ref, 0, 1), (right_ref, 8, 2)):
        for k in range(8):
            x = sums_ref[first + k].astype(F32)
            ref[16 * (k // 4) : 16 * (k // 4) + 16, 128 * (k % 4) : 128 * (k % 4) + 128] = x * scale
        outs[at].start()
    ins[1].wait()
    outs[3].start()
    for k in range(4):
        ins[2 + k].wait()
        outs[4 + k].start()
    for k in range(9):
        q, at = divmod(k, 4)
        for part in range(2):
            x = sums_ref[16 + 2 * q + part].astype(F32)
            conv_ref[k, 16 * part : 16 * part + 16, :] = x[:, 32 * at : 32 * at + 32] * scale
    outs[0].start()
    for copy in outs:
        copy.wait()


def shards(nr, nc, embed, left_proj, right_proj, conv_w, cotangent):
    per = nr // nc
    pair_out, totals, embed_grad = pl.pallas_call(
        functools.partial(pair_kernel, nr, nc),
        out_shape=(
            jax.ShapeDtypeStruct((32, 64, 256), BF16),
            jax.ShapeDtypeStruct((PIECES, 16, 128), BF16),
            jax.ShapeDtypeStruct((8, 512), F32),
        ),
        in_specs=[HBM] * 5,
        out_specs=(HBM,) * 3,
        scratch_shapes=LOCAL_SCRATCH
        + [
            pltpu.VMEM((32, 64, 256), BF16),
            pltpu.VMEM((8, 512), F32),
            pltpu.VMEM((136, 128), F32),
            pltpu.VMEM((8, 512), BF16),
            pltpu.VMEM((9, 32, 32), BF16),
            pltpu.VMEM((32, 64, 256), BF16),
            pltpu.VMEM((8, 128), F32),
            pltpu.VMEM((8, 128), F32),
            pltpu.VMEM((8, 128), F32),
            pltpu.VMEM((per, 8, 128), F32),
            pltpu.VMEM((nc, 8, 128), F32),
            pltpu.VMEM((128, 512), BF16),
            pltpu.VMEM((16, 256), BF16),
            pltpu.VMEM((nc, 16, 256), BF16),
            pltpu.VMEM((128, 512), BF16),
            pltpu.VMEM((nc, 8, 128), F32),
            pltpu.VMEM((2, 8, 128), F32),
            pltpu.VMEM((2, 8, 128), F32),
            pltpu.VMEM((per, 16, 128), F32),
            pltpu.VMEM((2, per, 8, 128), F32),
            pltpu.VMEM((2, 8, 128), F32),
            pltpu.VMEM((64, 128), F32),
            pltpu.VMEM((nc, 8, 128), F32),
            pltpu.VMEM((PIECES, 16, 128), BF16),
            pltpu.VMEM((32, 16, 128), BF16),
            pltpu.VMEM((8, 16, 128), BF16),
            pltpu.VMEM((16, 128), BF16),
            pltpu.VMEM((16, 128), BF16),
            pltpu.SemaphoreType.DMA((17,)),
            pltpu.SemaphoreType.DMA((17,)),
            pltpu.SemaphoreType.DMA((5,)),
            pltpu.SemaphoreType.DMA((6,)),
        ],
        compiler_params=pltpu.CompilerParams(
            collective_id=0, has_side_effects=True, vmem_limit_bytes=60 * 1024 * 1024
        ),
        name="pair_kernel",
    )(embed, left_proj.T, right_proj.T, conv_w, cotangent)
    conv_grad, left_t, right_t, embed_grad, pair_out = pl.pallas_call(
        functools.partial(finish_kernel, 32.0 / (8 * nr * nc)),
        out_shape=(
            jax.ShapeDtypeStruct((9, 32, 32), F32),
            jax.ShapeDtypeStruct((32, 512), F32),
            jax.ShapeDtypeStruct((32, 512), F32),
            jax.ShapeDtypeStruct((8, 512), F32),
            jax.ShapeDtypeStruct((32, 64, 256), BF16),
        ),
        in_specs=[HBM] * 3,
        out_specs=(HBM,) * 5,
        scratch_shapes=[
            pltpu.VMEM((PIECES, 16, 128), BF16),
            pltpu.VMEM((8, 512), F32),
            pltpu.VMEM((32, 64, 256), BF16),
            pltpu.VMEM((9, 32, 32), F32),
            pltpu.VMEM((32, 512), F32),
            pltpu.VMEM((32, 512), F32),
            pltpu.SemaphoreType.DMA((6,)),
            pltpu.SemaphoreType.DMA((8,)),
        ],
        compiler_params=pltpu.CompilerParams(vmem_limit_bytes=60 * 1024 * 1024),
        name="finish",
    )(totals, embed_grad, pair_out)
    return pair_out, conv_grad, left_t.T, right_t.T, embed_grad


def solution(mesh):
    body = functools.partial(shards, mesh.shape["row"], mesh.shape["col"])
    in_specs = (P(("row", "col"), None), P(), P(), P(), P(None, "row", "col"))
    out_specs = (P(None, "row", "col"), P(), P(), P(), P(("row", "col"), None))
    return jax.shard_map(body, mesh=mesh, in_specs=in_specs, out_specs=out_specs, check_vma=False)
```

```python
import functools

import jax
import jax.numpy as jnp
from jax import lax
from jax.experimental import pallas as pl
from jax.experimental.pallas import tpu as pltpu
from jax.sharding import PartitionSpec as P

MESH = pl.DeviceIdType.MESH
OUTSIDE = -1e30
LOG2E = 1.4426950408889634
LN2 = 0.6931471805599453
PIECES = 22
F32 = jnp.float32
BF16 = jnp.bfloat16
VMEM = pl.BlockSpec(memory_space=pltpu.VMEM)
HBM = pl.BlockSpec(memory_space=pltpu.HBM)


def iota(shape, dim):
    return lax.broadcasted_iota(jnp.int32, shape, dim)


def one_hot(cond):
    return jnp.where(cond, 1.0, 0.0).astype(BF16)


def dot(a, b):
    return jnp.dot(a, b, preferred_element_type=F32)


def dot_nt(a, b):
    return lax.dot_general(a, b, (((1,), (1,)), ((), ())), preferred_element_type=F32)


def dot_tn(a, b):
    return lax.dot_general(a, b, (((0,), (0,)), ((), ())), preferred_element_type=F32)


def halves(x):
    high = x.astype(BF16)
    return high, (x - high.astype(F32)).astype(BF16)


def loop(n, f):
    def body(k, _):
        f(k)
        return 0

    lax.fori_loop(0, n, body, 0)


def lanes(h):
    return pl.ds(pl.multiple_of(h * 256, 256), 256)


def wait_bytes(ref, sem):
    pltpu.make_async_copy(ref, ref, sem).wait()


def softplus_and_slope(y):
    t = jnp.exp2(-jnp.abs(y))
    u = 1.0 + t
    inv = pltpu.reciprocal(u, full_range=False)
    log = jnp.where(t < 2.0**-11, t * LOG2E, jnp.log2(u))
    return jnp.maximum(y, 0.0) + log, jnp.where(y >= 0, inv, t * inv)


def build_taps(w_ref, tf):
    spread = one_hot((iota((256, 32), 0) >> 3) == iota((256, 32), 1))
    widen = one_hot((iota((32, 256), 1) >> 3) == iota((32, 256), 0))
    s0, s1 = iota((256, 256), 0) & 7, iota((256, 256), 1) & 7
    same, above, below = s1 == s0, s1 == s0 + 4, s1 == s0 - 4
    x = dot(w_ref[...].reshape(288, 32), widen).astype(BF16)
    for b in range(3):
        x0, x1, x2 = (dot(spread, x[96 * a + 32 * b : 96 * a + 32 * b + 32]) for a in range(3))
        tf[:, 256 * b : 256 * b + 256] = jnp.where(same, x0, jnp.where(above, x1, 0.0)).astype(BF16)
        tf[:, 768 + 256 * b : 1024 + 256 * b] = jnp.where(same, x2, jnp.where(below, x1, 0.0)).astype(BF16)


def mask_cotangent(r, c, cot_ref, move, mall, mt):
    mall[0:256, 2048:2304] = jnp.zeros((256, 256), BF16)
    mall[256:512, 0:256] = jnp.zeros((256, 256), BF16)
    for k in range(4):
        x = cot_ref[:, 16 * k : 16 * k + 16, :].astype(F32)
        row = r * 64 + 16 * k + iota((16, 256), 0)
        x = jnp.where((c * 256 + iota((16, 256), 1) >= row)[None], x, 0.0)
        for half in range(2):
            m = x[:, 8 * half : 8 * half + 8].reshape(256, 256).astype(BF16)
            mall[0:256, lanes(2 * k + half)] = m
            mall[256:512, lanes(2 * k + half + 1)] = m
    for b in range(2):
        move[272 * b : 272 * b + 272, :] = one_hot(iota((272, 256), 0) - 4 * b == iota((272, 256), 1))
    mt[0] = jnp.zeros((272, 768), BF16)
    mt[9] = jnp.zeros((272, 768), BF16)
    none = jnp.zeros((8, 256), F32)

    def body(g):
        moved = dot_nt(move[...], mall[0:256, lanes(g)])
        mt[g + 1, :, 0:256] = moved[0:272].astype(BF16)
        mt[g + 1, :, 256:512] = moved[272:544].astype(BF16)
        mt[g + 1, :, 512:768] = jnp.concatenate([none, moved[0:264]], axis=0).astype(BF16)

    loop(8, body)


def input_gradient(mt, tf, z, steps):
    def body(step, _):
        left = [jnp.concatenate([mt[3 * step + k], mt[3 * step + k + 1]], axis=1) for k in range(3)]
        right = jnp.concatenate(
            [tf[:, 768 * (1 - u) + 256 * b : 768 * (1 - u) + 256 * b + 256] for u in range(2) for b in range(3)], axis=0
        )
        x = dot(jnp.concatenate(left, axis=0), right)
        for k in range(3):
            z[3 * step + k] = x[272 * k : 272 * k + 272]
        return 0

    lax.fori_loop(*steps, body, 0)


def features(rows, blocks, before, after, onto, rowf, colf):
    picks = [onto[:, 256 * at : 256 * at + 256] for at in range(4)]
    first = dot(before, picks[3])
    last = dot(after, picks[0])
    x = [first[4:8]] + [dot(blocks, pick) for pick in picks] + [last[0:4], jnp.zeros((8, 256), F32)]
    colf[...] = jnp.concatenate(x, axis=0) * LOG2E
    x = dot(rows, picks[0])
    x = jnp.where((iota((128, 256), 0) & 7) == (iota((128, 256), 1) & 7), x, 0.0).astype(BF16)
    rowf[...] = dot(one_hot((iota((16, 128), 1) >> 3) == iota((16, 128), 0)), x) * LOG2E


def elementwise(rowf, colf, z, act, cacc, rsum):
    rsum[...] = jnp.zeros_like(rsum)

    def body(step):
        parts = [pl.ds(pl.multiple_of(24 * step + 8 * part, 8), 8) for part in range(3)]
        totals = [jnp.zeros((8, 256), F32)] * 3
        for h in range(9):
            left = rowf[h : h + 1, :]
            row = jnp.zeros((8, 256), F32)
            for k, rows in enumerate(parts):
                value, slope = softplus_and_slope(colf[rows, :] + left)
                act[h, rows, :] = value
                p = z[h, rows, :] * slope
                totals[k] += p
                row += p
            rsum[8 * h : 8 * h + 8, :] += row
        for k, rows in enumerate(parts):
            cacc[rows, :] = totals[k]

    loop(11, body)


def build_constants(onto, pick, by_group):
    k, n = iota((128, 256), 0), iota((128, 256), 1) >> 3
    for at in range(4):
        onto[:, 256 * at : 256 * at + 256] = one_hot(k == n + 32 * at)
    k, n = iota((256, 128), 0) >> 3, iota((256, 128), 1)
    for g in range(4):
        pick[256 * g : 256 * g + 256, :] = one_hot(k + 32 * g == n)
    by_group[...] = one_hot((iota((80, 128), 0) >> 3) == (iota((80, 128), 1) >> 3))


def ends_of(x, pick, ends):
    sub = iota((16, 128), 0)
    high, low = halves(x)
    first = dot(high, pick[768:1024]) + dot(low, pick[768:1024])
    second = dot(high, pick[0:256]) + dot(low, pick[0:256])
    ends[0] = jnp.where(sub >= 12, pltpu.roll(first, 12, 0), 0.0)[8:16]
    ends[1] = jnp.where(sub < 4, pltpu.roll(second, 4, 0), 0.0)[0:8]


def column_sums(cacc, pick, cols):
    x = [
        jnp.concatenate([cacc[4 + 64 * q + 16 * g : 20 + 64 * q + 16 * g, :] for g in range(4)], axis=1) for q in range(4)
    ]
    high, low = halves(jnp.concatenate(x, axis=0))
    x = dot(high, pick[...]) + dot(low, pick[...])
    for q in range(4):
        cols[q] = x[16 * q : 16 * q + 16]


def column_end_sums(cacc, pick, col_ends):
    ends_of(jnp.concatenate([cacc[0:8, :], cacc[256:264, :]], axis=0), pick, col_ends)


def row_sums(rsum, pick, by_group, row_main, row_ends):
    x = jnp.concatenate([rsum[...], jnp.zeros((56, 256), F32)], axis=0)
    high, low = halves(x)
    x = dot(by_group[...], high) + dot(by_group[...], low)
    x = jnp.where((iota((80, 256), 0) & 7) == (iota((80, 256), 1) & 7), x, 0.0)
    ends_of(jnp.concatenate([x[0:8], x[64:72]], axis=0), pick, row_ends)
    high, low = halves(jnp.concatenate([x[4 + 16 * g : 20 + 16 * g] for g in range(4)], axis=1))
    row_main[...] = dot(high, pick[...]) + dot(low, pick[...])


def build_windows(act, a3):
    def body(h):
        at = pl.ds(pl.multiple_of(256 * h, 256), 256)
        for b in range(3):
            a3[at, 256 * b : 256 * b + 256] = (act[h, 4 * b : 4 * b + 256, :] * LN2).astype(BF16)

    loop(9, body)


def convolve(r, c, k, a3, tf, out_ref):
    parts = []
    for g in (2 * k, 2 * k + 1):
        both = jnp.concatenate([a3[256 * (g + u) : 256 * (g + u) + 256, :] for u in range(2)], axis=1)
        parts.append(dot_nt(tf[...], both).reshape(32, 8, 256))
    y = jnp.concatenate(parts, axis=1)
    row = r * 64 + 16 * k + iota((16, 256), 0)
    col = c * 256 + iota((16, 256), 1)
    out_ref[:, 16 * k : 16 * k + 16, :] = jnp.where((col >= row)[None], y, 0.0).astype(BF16)


def tap_gradient(mall, a3, pick, gram, taps):
    x = dot(mall[...], a3[...])
    for u in range(2):
        for k in range(6):
            gram[6 * u + k] = x[256 * u : 256 * u + 256, 128 * k : 128 * k + 128]
    lane = iota((32, 128), 1)

    def along(b, k, sources):
        total = jnp.zeros((32, 128), F32)
        for at, (s, u) in enumerate(sources):
            total = jnp.where((lane & 7) == at, gram[6 * u + 2 * b + k, pl.ds(s, 32, stride=8), :], total)
        return total

    sources = (
        [(s, 0) for s in range(8)],
        [((s + 4) % 8, 1 - s // 4) for s in range(8)],
        [(s, 1) for s in range(8)],
    )
    x = [jnp.concatenate([along(b, k, sources[a]) for k in range(2)], axis=1) for a in range(3) for b in range(3)]
    y = dot(jnp.concatenate(halves(jnp.concatenate(x, axis=0)), axis=0), pick[0:256])
    y = y[0:288] + y[288:576]
    for q in range(3):
        total = jnp.zeros((32, 128), F32)
        for k in range(min(4, 9 - 4 * q)):
            tap = y[32 * (4 * q + k) : 32 * (4 * q + k) + 32]
            total = jnp.where((lane >> 5) == k, pltpu.roll(tap, 32 * k, 1) if k else tap, total)
        taps[32 * q : 32 * q + 32, :] = total


LOCAL_SCRATCH = [
    pltpu.VMEM((16, 256), F32),
    pltpu.VMEM((272, 256), F32),
    pltpu.VMEM((96, 128), F32),
    pltpu.VMEM((512, 2304), BF16),
    pltpu.VMEM((10, 272, 768), BF16),
    pltpu.VMEM((9, 272, 256), F32),
    pltpu.VMEM((2304, 768), BF16),
    pltpu.VMEM((9, 272, 256), F32),
    pltpu.VMEM((256, 1536), BF16),
    pltpu.VMEM((544, 256), BF16),
    pltpu.VMEM((128, 1024), BF16),
    pltpu.VMEM((1024, 128), BF16),
    pltpu.VMEM((80, 128), BF16),
    pltpu.VMEM((12, 256, 128), F32),
    pltpu.VMEM((272, 256), F32),
    pltpu.VMEM((72, 256), F32),
    pltpu.VMEM((4, 16, 128), F32),
    pltpu.VMEM((2, 8, 128), F32),
    pltpu.VMEM((16, 128), F32),
    pltpu.VMEM((2, 8, 128), F32),
]


class Place:
    def __init__(self, nr, nc):
        r, c = lax.axis_index("row"), lax.axis_index("col")
        self.r, self.c, self.nr, self.nc = r, c, nr, nc
        self.per = nr // nc
        self.rb, self.rm = lax.div(r, self.per), lax.rem(r, self.per)
        _, self.quad = self.group(((r, 1, 0), (r, 2, 0)))
        _, self.line = self.group(((c, 1, 1), (c, 2, 1), (c, 4, 1)))
        self.plane = ((r, 1, 0), (r, 8, 0), (c, 2, 1), (r, 16, 0), (c, 4, 1))
        self.k1, self.group1 = self.group(self.plane)
        self.z_line = ((r, 2, 0), (r, 4, 0), (c, 1, 1))
        self.k2, self.group2 = self.group(self.z_line)
        self.has_up, self.has_down = r > 0, r < nr - 1
        self.has_left, self.has_right = c > 0, c < nc - 1
        self.ends_block = (self.rm == self.per - 1) & (self.rb < nc - 1)
        self.starts_block = (self.rm == 0) & (self.rb > 0)
        self.in_others = self.rb == c

    def group(self, bits):
        number, turns = 0, []
        for k, (x, weight, is_col) in enumerate(bits):
            bit = lax.rem(lax.div(x, weight), 2)
            number = number + bit * (1 << k)
            sign = 1 - 2 * bit
            turns.append((sign * weight, is_col, sign * (1 << k)))
        members = [(self.r, self.c, number)]
        for move, is_col, step in turns:
            members += [
                (a, b + move, n + step) if is_col else (a + move, b, n + step) for a, b, n in members
            ]
        return number, members[:0:-1]

    def member(self, bits, k):
        a, b = self.r, self.c
        for at, (x, weight, is_col) in enumerate(bits):
            move = weight * (k >> at & 1) - weight * lax.rem(lax.div(x, weight), 2)
            a, b = (a, b + move) if is_col else (a + move, b)
        return a, b

    def other(self, k):
        return self.per * self.c + k, self.rb

    def targets(self, col):
        return [(lax.rem(self.r + self.per * k, self.nr), col) for k in range(self.nr // self.per)]

    def greet(self):
        r, c, nc, per, rb, rm = self.r, self.c, self.nc, self.per, self.rb, self.rm
        barrier = pltpu.get_barrier_semaphore()

        def signal(a, b):
            pl.semaphore_signal(barrier, inc=1, device_id=(a, b), device_id_type=MESH)

        def signal_all(col):
            for k in range(per):
                signal(per * c + k, col)

        is_first, is_last = c == 0, c == nc - 1
        before_is_me = is_last & (rb == nc - 2)
        after_is_me = is_first & (rb == 1)
        for a, b, _ in self.quad + self.line:
            signal(a, b)
        pl.when(jnp.logical_not(self.in_others))(lambda: signal(per * c + rm, c))
        for _, b, _ in self.line:
            signal(per * c + rm, b)
        pl.when(self.has_up)(lambda: signal(r - 1, nc - 1))
        pl.when(self.has_down)(lambda: signal(r + 1, 0))
        pl.when(self.has_left & jnp.logical_not(before_is_me))(lambda: signal(per * (c - 1) + rm, nc - 1))
        pl.when(self.has_right & jnp.logical_not(after_is_me))(lambda: signal(per * (c + 1) + rm, 0))
        pl.when(jnp.logical_not(self.in_others))(lambda: signal(per * c + rm, rb))
        for a, _, _ in self.quad:
            signal(per * (c - rb) + a, rb)
        pl.when(self.has_up)(lambda: signal(r - 1, c))
        pl.when(self.has_down)(lambda: signal(r + 1, c))
        pl.when(self.ends_block)(lambda: signal_all(rb + 1))
        pl.when(self.starts_block)(lambda: signal_all(rb - 1))
        owner = self.k1 < PIECES

        @pl.when(owner)
        def _():
            for a, b, _ in self.group1 + self.group2:
                signal(a, b)

        @pl.when(jnp.logical_not(owner))
        def _():
            for k in range(PIECES):
                signal(*self.member(self.plane, k))

        n = len(self.quad + self.line) + nc + per
        n = n + jnp.where(owner, len(self.group1 + self.group2), PIECES)
        up, down = self.has_up, self.has_down
        for cond, m in (
            (self.in_others, -2), (is_last & down, nc), (is_first & up, nc),
            (is_last & (rb < nc - 1), nc), (before_is_me, -1), (is_first & (rb > 0), nc), (after_is_me, -1),
            (up, 1), (down, 1), (self.has_left, 1), (self.has_right, 1),
        ):
            n = n + jnp.where(cond, m, 0)
        return n

    def senders(self, send, recv):
        def put(src, dst_r, dst_c, dst, sem):
            pltpu.make_async_remote_copy(
                src, dst, send.at[sem], recv.at[sem], device_id=(dst_r, dst_c), device_id_type=MESH
            ).start()

        def put_other(src, k, dst, sem):
            a, b = self.other(k)
            mine = (a == self.r) & (b == self.c)
            pl.when(mine)(lambda: pltpu.make_async_copy(src, dst, recv.at[sem]).start())
            pl.when(jnp.logical_not(mine))(lambda: put(src, a, b, dst, sem))

        return put, put_other


def pair_kernel(
    nr, nc, e_hbm, lpt_hbm, rpt_hbm, w_hbm, cot_hbm,
    out_hbm, sums_hbm, eg_hbm,
    rowf, colf, taps, mall, mt, act, a3, z, tf, move, onto, pick, by_group, gram, cacc, rsum, cols, col_ends, row_main, row_ends,
    out_ref, eg_ref, feats, e_ref, w_ref, cot_ref, own, right, packed, quad, line, proj, es, eb, twice, blocks, row_feats, col_feats,
    cparts, cends, rends, turned, gparts, buf, r1, r2, mid, fin, recv, send, loads, stores,
):
    ins = ((e_hbm, e_ref), (w_hbm, w_ref), (lpt_hbm, proj.at[0:32]), (rpt_hbm, proj.at[32:64]), (cot_hbm, cot_ref))
    ins = [pltpu.make_async_copy(src, dst, loads.at[k]) for k, (src, dst) in enumerate(ins)]
    for copy in ins:
        copy.start()
    p = Place(nr, nc)
    r, c, per, rb, rm, k1, k2 = p.r, p.c, p.per, p.rb, p.rm, p.k1, p.k2
    greeted = p.greet()
    put, put_other = p.senders(send, recv)
    rows8, rows7 = gparts, gparts.at[0 : nc - 1]

    proj[64:128, :] = jnp.zeros((64, 512), BF16)
    ins[0].wait()
    e = e_ref[...].astype(F32)
    es[...] = jnp.concatenate([e[:, 0:256], e[:, 256:512]], axis=0).astype(BF16)
    ins[2].wait()
    ins[3].wait()
    own[...] = dot_nt(e_ref[...], proj[...]).astype(BF16).astype(F32)
    group = iota((8, 128), 1) >> 5
    right[...] = jnp.where(group == rm, pltpu.roll(own[...], lax.rem(32 * rm + 96, 128), 1), 0.0)
    ins[1].wait()
    build_taps(w_ref, tf)
    ins[4].wait()
    mask_cotangent(r, c, cot_ref, move, mall, mt)
    pl.semaphore_wait(pltpu.get_barrier_semaphore(), greeted)

    for a, b, _ in p.quad:
        put(right, a, b, quad.at[rm], 1)
    pltpu.make_async_copy(right, quad.at[rm], recv.at[1]).start()

    def put_line(row, dst, sem):
        for k in range(nc):
            put(own, row, k, dst, sem)

    is_first, is_last = c == 0, c == nc - 1
    row_after, row_before = is_last & p.has_down, is_first & p.has_up
    pl.when(row_after)(lambda: put_line(r + 1, row_feats.at[0], 2))
    pl.when(row_before)(lambda: put_line(r - 1, row_feats.at[1], 3))
    for a, b, _ in p.line:
        put(own, a, b, line.at[c], 16)
    pltpu.make_async_copy(own, line.at[c], recv.at[16]).start()

    def put_targets(src, col, dst, sem):
        first, *rest = p.targets(col)
        mine = c == col
        pl.when(mine)(lambda: pltpu.make_async_copy(src, dst, recv.at[sem]).start())
        pl.when(jnp.logical_not(mine))(lambda: put(src, *first, dst, sem))
        for a, b in rest:
            put(src, a, b, dst, sem)

    col_after, col_before = is_last & (rb < nc - 1), is_first & (rb > 0)
    input_gradient(mt, tf, z, (0, 1))
    wait_bytes(quad, recv.at[1])
    packed[...] = jnp.sum(quad[...], axis=0)
    put_targets(packed, rb, blocks.at[c], 15)
    pl.when(col_after)(lambda: put_targets(packed, rb + 1, col_feats.at[0], 4))
    pl.when(col_before)(lambda: put_targets(packed, rb - 1, col_feats.at[1], 5))
    input_gradient(mt, tf, z, (1, 3))
    build_constants(onto, pick, by_group)

    def arrive(cond, ref, sem):
        pl.when(cond)(lambda: wait_bytes(ref, sem))
        pl.when(jnp.logical_not(cond))(lambda: ref.__setitem__(..., jnp.full(ref.shape, OUTSIDE, F32)))

    arrive(p.has_up, row_feats.at[0], recv.at[2])
    arrive(p.has_down, row_feats.at[1], recv.at[3])
    arrive(p.has_left, col_feats.at[0], recv.at[4])
    arrive(p.has_right, col_feats.at[1], recv.at[5])
    wait_bytes(line, recv.at[16])
    wait_bytes(blocks, recv.at[15])
    feats[8:72, :] = line[...].reshape(8 * nc, 128)
    feats[0:8, :] = row_feats[0]
    feats[72:80, :] = row_feats[1]
    feats[80:136, :] = jnp.zeros((56, 128), F32)
    ends = [jnp.concatenate([col_feats[k], jnp.zeros((8, 128), F32)], axis=0).astype(BF16) for k in range(2)]
    features(feats[4:132, :].astype(BF16), blocks[...].reshape(8 * nc, 128).astype(BF16), *ends, onto, rowf, colf)
    for a, b, _ in p.line:
        put(es, a, b, eb.at[c], 0)
    pltpu.make_async_copy(es, eb.at[c], recv.at[0]).start()
    elementwise(rowf, colf, z, act, cacc, rsum)

    column_sums(cacc, pick, cols)
    for k in range(per):
        put_other(cols.at[k], k, cparts.at[rm], 6)
    column_end_sums(cacc, pick, col_ends)
    pl.when(p.has_left)(lambda: put(col_ends.at[0], per * c - 1, rb, cends.at[0, rm], 9))
    pl.when(p.has_right)(lambda: put(col_ends.at[1], per * c + per, rb, cends.at[1, rm], 10))
    row_sums(rsum, pick, by_group, row_main, row_ends)
    pl.when(p.has_up)(lambda: put(row_ends.at[0], r - 1, c, rends.at[0], 7))
    pl.when(p.has_down)(lambda: put(row_ends.at[1], r + 1, c, rends.at[1], 8))

    build_windows(act, a3)
    tap_gradient(mall, a3, pick, gram, taps)
    for k in range(PIECES - 16):
        buf[16 + k] = taps[16 * k : 16 * k + 16, :].astype(BF16)

    owner = k1 < PIECES

    def put_pieces(ks):
        def piece(k):
            put(buf.at[k], *p.member(p.plane, k), r1.at[k1], 11)

        @pl.when(owner)
        def _():
            for k in ks:
                pl.when(k1 != k)(lambda k=k: piece(k))

        @pl.when(jnp.logical_not(owner))
        def _():
            for k in ks:
                piece(k)

    put_pieces(range(16, PIECES))
    wait_bytes(eb, recv.at[0])
    e = eb[...].astype(F32)
    e = jnp.concatenate([e[:, 0:8].reshape(64, 256), e[:, 8:16].reshape(64, 256)], axis=1).astype(BF16)
    twice[...] = jnp.concatenate([e, e], axis=0)

    def gather_sum(cond, ref, sem):
        pl.when(cond)(lambda: wait_bytes(ref, sem))
        pl.when(jnp.logical_not(cond))(lambda: ref.__setitem__(..., jnp.zeros(ref.shape, F32)))

    gather_sum(p.has_down, rends.at[0], recv.at[7])
    gather_sum(p.has_up, rends.at[1], recv.at[8])
    gather_sum(p.ends_block, cends.at[0], recv.at[9])
    gather_sum(p.starts_block, cends.at[1], recv.at[10])
    wait_bytes(cparts, recv.at[6])
    grads = (
        row_main[...] + jnp.concatenate([rends[1], rends[0]], axis=0),
        jnp.sum(cparts[...], axis=0)
        + jnp.concatenate([jnp.sum(cends[1], axis=0), jnp.sum(cends[0], axis=0)], axis=0),
    )
    lane = iota((16, 128), 1)
    spread = []
    for g in range(4):
        parts = [x if turn % 128 == 0 else pltpu.roll(x, turn % 128, 1) for x, turn in zip(grads, (-32 * g, 32 - 32 * g))]
        spread.append(jnp.where(lane < 32, parts[0], jnp.where(lane < 64, parts[1], 0.0)))
    turned[...] = jnp.concatenate(spread, axis=0)

    part = dot_tn(jnp.concatenate(halves(turned[...]), axis=0), twice[...])
    for k in range(16):
        at = slice(16 * (k // 4), 16 * (k // 4) + 16), slice(128 * (k % 4), 128 * (k % 4) + 128)
        buf[k] = part[at].astype(BF16)

    put_pieces(range(16))
    pl.when(owner)(lambda: pltpu.make_async_copy(buf.at[k1], r1.at[k1], recv.at[11]).start())

    outs = [
        pltpu.make_async_copy(out_ref.at[:, 16 * q : 16 * q + 16, :], out_hbm.at[:, 16 * q : 16 * q + 16, :], stores.at[q])
        for q in range(4)
    ]
    convolve(r, c, 0, a3, tf, out_ref)
    outs[0].start()
    for a, b, _ in p.line:
        put(turned.at[pl.ds(pl.multiple_of(8 * b, 8), 8)], a, b, gparts.at[c], 14)
    pltpu.make_async_copy(turned.at[pl.ds(pl.multiple_of(8 * c, 8), 8)], gparts.at[c], recv.at[14]).start()
    convolve(r, c, 1, a3, tf, out_ref)
    outs[1].start()

    @pl.when(owner)
    def _():
        wait_bytes(r1, recv.at[11])
        mid[...] = jnp.sum(r1[...].astype(F32), axis=0).astype(BF16)
        for k in range(8):
            pl.when(k2 != k)(lambda k=k: put(mid, *p.member(p.z_line, k), r2.at[k2], 12))
        pltpu.make_async_copy(mid, r2.at[k2], recv.at[12]).start()

    convolve(r, c, 2, a3, tf, out_ref)
    outs[2].start()
    convolve(r, c, 3, a3, tf, out_ref)
    outs[3].start()

    @pl.when(owner)
    def _():
        wait_bytes(r2, recv.at[12])
        fin[...] = jnp.sum(r2[...].astype(F32), axis=0).astype(BF16)
        for k in (1, 0, *range(2, 32)):
            pl.when(k1 != k)(lambda k=k: put(fin, *p.member(p.plane, k), sums_hbm.at[k1], 13))
        pltpu.make_async_copy(fin, sums_hbm.at[k1], recv.at[13]).start()

    wait_bytes(gparts, recv.at[14])
    high, low = halves(jnp.sum(gparts[...], axis=0))
    eg_ref[...] = dot(high, proj[...]) + dot(low, proj[...])
    outs.append(pltpu.make_async_copy(eg_ref, eg_hbm, stores.at[4]))
    outs[4].start()

    for copy in outs:
        copy.wait()
    wait_bytes(eb.at[0 : nc - 1], send.at[0])
    wait_bytes(quad.at[0 : per - 1], send.at[1])
    pl.when(row_after)(lambda: wait_bytes(rows8, send.at[2]))
    pl.when(row_before)(lambda: wait_bytes(rows8, send.at[3]))

    def sent_targets(cond, mine, eight, seven, sem):
        pl.when(cond & mine)(lambda: wait_bytes(seven, send.at[sem]))
        pl.when(cond & jnp.logical_not(mine))(lambda: wait_bytes(eight, send.at[sem]))

    sent_targets(col_after, rb + 1 == c, rows8, rows7, 4)
    sent_targets(col_before, rb - 1 == c, rows8, rows7, 5)
    sent_targets(rb >= 0, p.in_others, blocks, blocks.at[0 : nc - 1], 15)
    pl.when(p.in_others)(lambda: wait_bytes(cparts.at[0 : per - 1], send.at[6]))
    pl.when(jnp.logical_not(p.in_others))(lambda: wait_bytes(cparts, send.at[6]))
    pl.when(p.has_up)(lambda: wait_bytes(row_ends.at[0], send.at[7]))
    pl.when(p.has_down)(lambda: wait_bytes(row_ends.at[1], send.at[8]))
    pl.when(p.has_left)(lambda: wait_bytes(col_ends.at[0], send.at[9]))
    pl.when(p.has_right)(lambda: wait_bytes(col_ends.at[1], send.at[10]))
    wait_bytes(line.at[0 : nc - 1], send.at[16])
    pl.when(owner)(lambda: wait_bytes(r1.at[0 : PIECES - 1], send.at[11]))
    pl.when(jnp.logical_not(owner))(lambda: wait_bytes(r1.at[0:PIECES], send.at[11]))
    pl.when(owner)(lambda: wait_bytes(r2.at[0 : r2.shape[0] - 1], send.at[12]))
    wait_bytes(gparts.at[0 : nc - 1], send.at[14])

    pl.when(owner)(lambda: wait_bytes(r1.at[0 : r1.shape[0] - 1], send.at[13]))
    wait_bytes(sums_hbm, recv.at[13])


def finish_kernel(
    scale, sums_in, eg_in, pair_in, conv_out, left_out, right_out, eg_out, pair_out,
    sums_ref, eg_ref, held, conv_ref, left_ref, right_ref, loads, stores,
):
    def piece(k):
        return slice(8 * k, 8 * k + 8)

    ins = [pltpu.make_async_copy(sums_in, sums_ref, loads.at[0]), pltpu.make_async_copy(eg_in, eg_ref, loads.at[1])]
    ins += [pltpu.make_async_copy(pair_in.at[piece(k)], held.at[piece(k)], loads.at[2 + k]) for k in range(4)]
    outs = [
        pltpu.make_async_copy(conv_ref, conv_out, stores.at[0]),
        pltpu.make_async_copy(left_ref, left_out, stores.at[1]),
        pltpu.make_async_copy(right_ref, right_out, stores.at[2]),
        pltpu.make_async_copy(eg_ref, eg_out, stores.at[3]),
    ]
    outs += [pltpu.make_async_copy(held.at[piece(k)], pair_out.at[piece(k)], stores.at[4 + k]) for k in range(4)]
    for copy in ins:
        copy.start()
    ins[0].wait()
    for ref, first, at in ((left_ref, 0, 1), (right_ref, 8, 2)):
        for k in range(8):
            x = sums_ref[first + k].astype(F32)
            ref[16 * (k // 4) : 16 * (k // 4) + 16, 128 * (k % 4) : 128 * (k % 4) + 128] = x * scale
        outs[at].start()
    ins[1].wait()
    outs[3].start()
    for k in range(4):
        ins[2 + k].wait()
        outs[4 + k].start()
    for k in range(9):
        q, at = divmod(k, 4)
        for part in range(2):
            x = sums_ref[16 + 2 * q + part].astype(F32)
            conv_ref[k, 16 * part : 16 * part + 16, :] = x[:, 32 * at : 32 * at + 32] * scale
    outs[0].start()
    for copy in outs:
        copy.wait()


def shards(nr, nc, embed, left_proj, right_proj, conv_w, cotangent):
    per = nr // nc
    pair_out, totals, embed_grad = pl.pallas_call(
        functools.partial(pair_kernel, nr, nc),
        out_shape=(
            jax.ShapeDtypeStruct((32, 64, 256), BF16),
            jax.ShapeDtypeStruct((PIECES, 16, 128), BF16),
            jax.ShapeDtypeStruct((8, 512), F32),
        ),
        in_specs=[HBM] * 5,
        out_specs=(HBM,) * 3,
        scratch_shapes=LOCAL_SCRATCH
        + [
            pltpu.VMEM((32, 64, 256), BF16),
            pltpu.VMEM((8, 512), F32),
            pltpu.VMEM((136, 128), F32),
            pltpu.VMEM((8, 512), BF16),
            pltpu.VMEM((9, 32, 32), BF16),
            pltpu.VMEM((32, 64, 256), BF16),
            pltpu.VMEM((8, 128), F32),
            pltpu.VMEM((8, 128), F32),
            pltpu.VMEM((8, 128), F32),
            pltpu.VMEM((per, 8, 128), F32),
            pltpu.VMEM((nc, 8, 128), F32),
            pltpu.VMEM((128, 512), BF16),
            pltpu.VMEM((16, 256), BF16),
            pltpu.VMEM((nc, 16, 256), BF16),
            pltpu.VMEM((128, 512), BF16),
            pltpu.VMEM((nc, 8, 128), F32),
            pltpu.VMEM((2, 8, 128), F32),
            pltpu.VMEM((2, 8, 128), F32),
            pltpu.VMEM((per, 16, 128), F32),
            pltpu.VMEM((2, per, 8, 128), F32),
            pltpu.VMEM((2, 8, 128), F32),
            pltpu.VMEM((64, 128), F32),
            pltpu.VMEM((nc, 8, 128), F32),
            pltpu.VMEM((PIECES, 16, 128), BF16),
            pltpu.VMEM((32, 16, 128), BF16),
            pltpu.VMEM((8, 16, 128), BF16),
            pltpu.VMEM((16, 128), BF16),
            pltpu.VMEM((16, 128), BF16),
            pltpu.SemaphoreType.DMA((17,)),
            pltpu.SemaphoreType.DMA((17,)),
            pltpu.SemaphoreType.DMA((5,)),
            pltpu.SemaphoreType.DMA((6,)),
        ],
        compiler_params=pltpu.CompilerParams(
            collective_id=0, has_side_effects=True, vmem_limit_bytes=60 * 1024 * 1024
        ),
        name="pair_kernel",
    )(embed, left_proj.T, right_proj.T, conv_w, cotangent)
    conv_grad, left_t, right_t, embed_grad, pair_out = pl.pallas_call(
        functools.partial(finish_kernel, 32.0 / (8 * nr * nc)),
        out_shape=(
            jax.ShapeDtypeStruct((9, 32, 32), F32),
            jax.ShapeDtypeStruct((32, 512), F32),
            jax.ShapeDtypeStruct((32, 512), F32),
            jax.ShapeDtypeStruct((8, 512), F32),
            jax.ShapeDtypeStruct((32, 64, 256), BF16),
        ),
        in_specs=[HBM] * 3,
        out_specs=(HBM,) * 5,
        scratch_shapes=[
            pltpu.VMEM((PIECES, 16, 128), BF16),
            pltpu.VMEM((8, 512), F32),
            pltpu.VMEM((32, 64, 256), BF16),
            pltpu.VMEM((9, 32, 32), F32),
            pltpu.VMEM((32, 512), F32),
            pltpu.VMEM((32, 512), F32),
            pltpu.SemaphoreType.DMA((6,)),
            pltpu.SemaphoreType.DMA((8,)),
        ],
        compiler_params=pltpu.CompilerParams(vmem_limit_bytes=60 * 1024 * 1024),
        name="finish",
    )(totals, embed_grad, pair_out)
    return pair_out, conv_grad, left_t.T, right_t.T, embed_grad


def solution(mesh):
    body = functools.partial(shards, mesh.shape["row"], mesh.shape["col"])
    in_specs = (P(("row", "col"), None), P(), P(), P(), P(None, "row", "col"))
    out_specs = (P(None, "row", "col"), P(), P(), P(), P(("row", "col"), None))
    return jax.shard_map(body, mesh=mesh, in_specs=in_specs, out_specs=out_specs, check_vma=False)
```

```python
import functools

import jax
import jax.numpy as jnp
from jax import lax
from jax.experimental import pallas as pl
from jax.experimental.pallas import tpu as pltpu
from jax.sharding import PartitionSpec as P

MESH = pl.DeviceIdType.MESH
OUTSIDE = -1e30
LOG2E = 1.4426950408889634
LN2 = 0.6931471805599453
PIECES = 22
F32 = jnp.float32
BF16 = jnp.bfloat16
VMEM = pl.BlockSpec(memory_space=pltpu.VMEM)
HBM = pl.BlockSpec(memory_space=pltpu.HBM)


def iota(shape, dim):
    return lax.broadcasted_iota(jnp.int32, shape, dim)


def one_hot(cond):
    return jnp.where(cond, 1.0, 0.0).astype(BF16)


def dot(a, b):
    return jnp.dot(a, b, preferred_element_type=F32)


def dot_nt(a, b):
    return lax.dot_general(a, b, (((1,), (1,)), ((), ())), preferred_element_type=F32)


def dot_tn(a, b):
    return lax.dot_general(a, b, (((0,), (0,)), ((), ())), preferred_element_type=F32)


def halves(x):
    high = x.astype(BF16)
    return high, (x - high.astype(F32)).astype(BF16)


def loop(n, f):
    def body(k, _):
        f(k)
        return 0

    lax.fori_loop(0, n, body, 0)


def lanes(h):
    return pl.ds(pl.multiple_of(h * 256, 256), 256)


def wait_bytes(ref, sem):
    pltpu.make_async_copy(ref, ref, sem).wait()


def softplus_and_slope(y):
    t = jnp.exp2(-jnp.abs(y))
    u = 1.0 + t
    inv = pltpu.reciprocal(u, full_range=False)
    log = jnp.where(t < 2.0**-11, t * LOG2E, jnp.log2(u))
    return jnp.maximum(y, 0.0) + log, jnp.where(y >= 0, inv, t * inv)


def build_taps(w_ref, tf):
    spread = one_hot((iota((256, 32), 0) >> 3) == iota((256, 32), 1))
    widen = one_hot((iota((32, 256), 1) >> 3) == iota((32, 256), 0))
    s0, s1 = iota((256, 256), 0) & 7, iota((256, 256), 1) & 7
    same, above, below = s1 == s0, s1 == s0 + 4, s1 == s0 - 4
    x = dot(w_ref[...].reshape(288, 32), widen).astype(BF16)
    for b in range(3):
        x0, x1, x2 = (dot(spread, x[96 * a + 32 * b : 96 * a + 32 * b + 32]) for a in range(3))
        tf[:, 256 * b : 256 * b + 256] = jnp.where(same, x0, jnp.where(above, x1, 0.0)).astype(BF16)
        tf[:, 768 + 256 * b : 1024 + 256 * b] = jnp.where(same, x2, jnp.where(below, x1, 0.0)).astype(BF16)


def mask_cotangent(r, c, cot_ref, move, mall, mt):
    mall[0:256, 2048:2304] = jnp.zeros((256, 256), BF16)
    mall[256:512, 0:256] = jnp.zeros((256, 256), BF16)
    for k in range(4):
        x = cot_ref[:, 16 * k : 16 * k + 16, :].astype(F32)
        row = r * 64 + 16 * k + iota((16, 256), 0)
        x = jnp.where((c * 256 + iota((16, 256), 1) >= row)[None], x, 0.0)
        for half in range(2):
            m = x[:, 8 * half : 8 * half + 8].reshape(256, 256).astype(BF16)
            mall[0:256, lanes(2 * k + half)] = m
            mall[256:512, lanes(2 * k + half + 1)] = m
    for b in range(2):
        move[272 * b : 272 * b + 272, :] = one_hot(iota((272, 256), 0) - 4 * b == iota((272, 256), 1))
    mt[0] = jnp.zeros((272, 768), BF16)
    mt[9] = jnp.zeros((272, 768), BF16)
    none = jnp.zeros((8, 256), F32)

    def body(g):
        moved = dot_nt(move[...], mall[0:256, lanes(g)])
        mt[g + 1, :, 0:256] = moved[0:272].astype(BF16)
        mt[g + 1, :, 256:512] = moved[272:544].astype(BF16)
        mt[g + 1, :, 512:768] = jnp.concatenate([none, moved[0:264]], axis=0).astype(BF16)

    loop(8, body)


def input_gradient(mt, tf, z, steps):
    def body(step, _):
        left = [jnp.concatenate([mt[3 * step + k], mt[3 * step + k + 1]], axis=1) for k in range(3)]
        right = jnp.concatenate(
            [tf[:, 768 * (1 - u) + 256 * b : 768 * (1 - u) + 256 * b + 256] for u in range(2) for b in range(3)], axis=0
        )
        x = dot(jnp.concatenate(left, axis=0), right)
        for k in range(3):
            z[3 * step + k] = x[272 * k : 272 * k + 272]
        return 0

    lax.fori_loop(*steps, body, 0)


def features(rows, blocks, before, after, onto, rowf, colf):
    picks = [onto[:, 256 * at : 256 * at + 256] for at in range(4)]
    first = dot(before, picks[3])
    last = dot(after, picks[0])
    x = [first[4:8]] + [dot(blocks, pick) for pick in picks] + [last[0:4], jnp.zeros((8, 256), F32)]
    colf[...] = jnp.concatenate(x, axis=0) * LOG2E
    x = dot(rows, picks[0])
    x = jnp.where((iota((128, 256), 0) & 7) == (iota((128, 256), 1) & 7), x, 0.0).astype(BF16)
    rowf[...] = dot(one_hot((iota((16, 128), 1) >> 3) == iota((16, 128), 0)), x) * LOG2E


def elementwise(rowf, colf, z, act, cacc, rsum):
    rsum[...] = jnp.zeros_like(rsum)

    def body(step):
        parts = [pl.ds(pl.multiple_of(24 * step + 8 * part, 8), 8) for part in range(3)]
        totals = [jnp.zeros((8, 256), F32)] * 3
        for h in range(9):
            left = rowf[h : h + 1, :]
            row = jnp.zeros((8, 256), F32)
            for k, rows in enumerate(parts):
                value, slope = softplus_and_slope(colf[rows, :] + left)
                act[h, rows, :] = value
                p = z[h, rows, :] * slope
                totals[k] += p
                row += p
            rsum[8 * h : 8 * h + 8, :] += row
        for k, rows in enumerate(parts):
            cacc[rows, :] = totals[k]

    loop(11, body)


def build_constants(onto, pick, by_group):
    k, n = iota((128, 256), 0), iota((128, 256), 1) >> 3
    for at in range(4):
        onto[:, 256 * at : 256 * at + 256] = one_hot(k == n + 32 * at)
    k, n = iota((256, 128), 0) >> 3, iota((256, 128), 1)
    for g in range(4):
        pick[256 * g : 256 * g + 256, :] = one_hot(k + 32 * g == n)
    by_group[...] = one_hot((iota((80, 128), 0) >> 3) == (iota((80, 128), 1) >> 3))


def ends_of(x, pick, ends):
    sub = iota((16, 128), 0)
    high, low = halves(x)
    first = dot(high, pick[768:1024]) + dot(low, pick[768:1024])
    second = dot(high, pick[0:256]) + dot(low, pick[0:256])
    ends[0] = jnp.where(sub >= 12, pltpu.roll(first, 12, 0), 0.0)[8:16]
    ends[1] = jnp.where(sub < 4, pltpu.roll(second, 4, 0), 0.0)[0:8]


def column_sums(cacc, pick, cols):
    x = [
        jnp.concatenate([cacc[4 + 64 * q + 16 * g : 20 + 64 * q + 16 * g, :] for g in range(4)], axis=1) for q in range(4)
    ]
    high, low = halves(jnp.concatenate(x, axis=0))
    x = dot(high, pick[...]) + dot(low, pick[...])
    for q in range(4):
        cols[q] = x[16 * q : 16 * q + 16]


def column_end_sums(cacc, pick, col_ends):
    ends_of(jnp.concatenate([cacc[0:8, :], cacc[256:264, :]], axis=0), pick, col_ends)


def row_sums(rsum, pick, by_group, row_main, row_ends):
    x = jnp.concatenate([rsum[...], jnp.zeros((56, 256), F32)], axis=0)
    high, low = halves(x)
    x = dot(by_group[...], high) + dot(by_group[...], low)
    x = jnp.where((iota((80, 256), 0) & 7) == (iota((80, 256), 1) & 7), x, 0.0)
    ends_of(jnp.concatenate([x[0:8], x[64:72]], axis=0), pick, row_ends)
    high, low = halves(jnp.concatenate([x[4 + 16 * g : 20 + 16 * g] for g in range(4)], axis=1))
    row_main[...] = dot(high, pick[...]) + dot(low, pick[...])


def build_windows(act, a3):
    def body(h):
        at = pl.ds(pl.multiple_of(256 * h, 256), 256)
        for b in range(3):
            a3[at, 256 * b : 256 * b + 256] = (act[h, 4 * b : 4 * b + 256, :] * LN2).astype(BF16)

    loop(9, body)


def convolve(r, c, k, a3, tf, out_ref):
    parts = []
    for g in (2 * k, 2 * k + 1):
        both = jnp.concatenate([a3[256 * (g + u) : 256 * (g + u) + 256, :] for u in range(2)], axis=1)
        parts.append(dot_nt(tf[...], both).reshape(32, 8, 256))
    y = jnp.concatenate(parts, axis=1)
    row = r * 64 + 16 * k + iota((16, 256), 0)
    col = c * 256 + iota((16, 256), 1)
    out_ref[:, 16 * k : 16 * k + 16, :] = jnp.where((col >= row)[None], y, 0.0).astype(BF16)


def tap_gradient(mall, a3, pick, gram, taps):
    x = dot(mall[...], a3[...])
    for u in range(2):
        for k in range(6):
            gram[6 * u + k] = x[256 * u : 256 * u + 256, 128 * k : 128 * k + 128]
    lane = iota((32, 128), 1)

    def along(b, k, sources):
        total = jnp.zeros((32, 128), F32)
        for at, (s, u) in enumerate(sources):
            total = jnp.where((lane & 7) == at, gram[6 * u + 2 * b + k, pl.ds(s, 32, stride=8), :], total)
        return total

    sources = (
        [(s, 0) for s in range(8)],
        [((s + 4) % 8, 1 - s // 4) for s in range(8)],
        [(s, 1) for s in range(8)],
    )
    x = [jnp.concatenate([along(b, k, sources[a]) for k in range(2)], axis=1) for a in range(3) for b in range(3)]
    y = dot(jnp.concatenate(halves(jnp.concatenate(x, axis=0)), axis=0), pick[0:256])
    y = y[0:288] + y[288:576]
    for q in range(3):
        total = jnp.zeros((32, 128), F32)
        for k in range(min(4, 9 - 4 * q)):
            tap = y[32 * (4 * q + k) : 32 * (4 * q + k) + 32]
            total = jnp.where((lane >> 5) == k, pltpu.roll(tap, 32 * k, 1) if k else tap, total)
        taps[32 * q : 32 * q + 32, :] = total


LOCAL_SCRATCH = [
    pltpu.VMEM((16, 256), F32),
    pltpu.VMEM((272, 256), F32),
    pltpu.VMEM((96, 128), F32),
    pltpu.VMEM((512, 2304), BF16),
    pltpu.VMEM((10, 272, 768), BF16),
    pltpu.VMEM((9, 272, 256), F32),
    pltpu.VMEM((2304, 768), BF16),
    pltpu.VMEM((9, 272, 256), F32),
    pltpu.VMEM((256, 1536), BF16),
    pltpu.VMEM((544, 256), BF16),
    pltpu.VMEM((128, 1024), BF16),
    pltpu.VMEM((1024, 128), BF16),
    pltpu.VMEM((80, 128), BF16),
    pltpu.VMEM((12, 256, 128), F32),
    pltpu.VMEM((272, 256), F32),
    pltpu.VMEM((72, 256), F32),
    pltpu.VMEM((4, 16, 128), F32),
    pltpu.VMEM((2, 8, 128), F32),
    pltpu.VMEM((16, 128), F32),
    pltpu.VMEM((2, 8, 128), F32),
]


class Place:
    def __init__(self, nr, nc):
        r, c = lax.axis_index("row"), lax.axis_index("col")
        self.r, self.c, self.nr, self.nc = r, c, nr, nc
        self.per = nr // nc
        self.rb, self.rm = lax.div(r, self.per), lax.rem(r, self.per)
        _, self.quad = self.group(((r, 1, 0), (r, 2, 0)))
        _, self.line = self.group(((c, 1, 1), (c, 2, 1), (c, 4, 1)))
        self.plane = ((r, 1, 0), (r, 8, 0), (c, 2, 1), (r, 16, 0), (c, 4, 1))
        self.k1, self.group1 = self.group(self.plane)
        self.z_line = ((r, 2, 0), (r, 4, 0), (c, 1, 1))
        self.k2, self.group2 = self.group(self.z_line)
        self.has_up, self.has_down = r > 0, r < nr - 1
        self.has_left, self.has_right = c > 0, c < nc - 1
        self.ends_block = (self.rm == self.per - 1) & (self.rb < nc - 1)
        self.starts_block = (self.rm == 0) & (self.rb > 0)
        self.in_others = self.rb == c

    def group(self, bits):
        number, turns = 0, []
        for k, (x, weight, is_col) in enumerate(bits):
            bit = lax.rem(lax.div(x, weight), 2)
            number = number + bit * (1 << k)
            sign = 1 - 2 * bit
            turns.append((sign * weight, is_col, sign * (1 << k)))
        members = [(self.r, self.c, number)]
        for move, is_col, step in turns:
            members += [
                (a, b + move, n + step) if is_col else (a + move, b, n + step) for a, b, n in members
            ]
        return number, members[:0:-1]

    def member(self, bits, k):
        a, b = self.r, self.c
        for at, (x, weight, is_col) in enumerate(bits):
            move = weight * (k >> at & 1) - weight * lax.rem(lax.div(x, weight), 2)
            a, b = (a, b + move) if is_col else (a + move, b)
        return a, b

    def other(self, k):
        return self.per * self.c + k, self.rb

    def targets(self, col):
        return [(lax.rem(self.r + self.per * k, self.nr), col) for k in range(self.nr // self.per)]

    def greet(self):
        r, c, nc, per, rb, rm = self.r, self.c, self.nc, self.per, self.rb, self.rm
        barrier = pltpu.get_barrier_semaphore()

        def signal(a, b):
            pl.semaphore_signal(barrier, inc=1, device_id=(a, b), device_id_type=MESH)

        def signal_all(col):
            for k in range(per):
                signal(per * c + k, col)

        is_first, is_last = c == 0, c == nc - 1
        before_is_me = is_last & (rb == nc - 2)
        after_is_me = is_first & (rb == 1)
        for a, b, _ in self.quad + self.line:
            signal(a, b)
        pl.when(jnp.logical_not(self.in_others))(lambda: signal(per * c + rm, c))
        for _, b, _ in self.line:
            signal(per * c + rm, b)
        pl.when(self.has_up)(lambda: signal(r - 1, nc - 1))
        pl.when(self.has_down)(lambda: signal(r + 1, 0))
        pl.when(self.has_left & jnp.logical_not(before_is_me))(lambda: signal(per * (c - 1) + rm, nc - 1))
        pl.when(self.has_right & jnp.logical_not(after_is_me))(lambda: signal(per * (c + 1) + rm, 0))
        pl.when(jnp.logical_not(self.in_others))(lambda: signal(per * c + rm, rb))
        for a, _, _ in self.quad:
            signal(per * (c - rb) + a, rb)
        pl.when(self.has_up)(lambda: signal(r - 1, c))
        pl.when(self.has_down)(lambda: signal(r + 1, c))
        pl.when(self.ends_block)(lambda: signal_all(rb + 1))
        pl.when(self.starts_block)(lambda: signal_all(rb - 1))
        owner = self.k1 < PIECES

        @pl.when(owner)
        def _():
            for a, b, _ in self.group1 + self.group2:
                signal(a, b)

        @pl.when(jnp.logical_not(owner))
        def _():
            for k in range(PIECES):
                signal(*self.member(self.plane, k))

        n = len(self.quad + self.line) + nc + per
        n = n + jnp.where(owner, len(self.group1 + self.group2), PIECES)
        up, down = self.has_up, self.has_down
        for cond, m in (
            (self.in_others, -2), (is_last & down, nc), (is_first & up, nc),
            (is_last & (rb < nc - 1), nc), (before_is_me, -1), (is_first & (rb > 0), nc), (after_is_me, -1),
            (up, 1), (down, 1), (self.has_left, 1), (self.has_right, 1),
        ):
            n = n + jnp.where(cond, m, 0)
        return n

    def senders(self, send, recv):
        def put(src, dst_r, dst_c, dst, sem):
            pltpu.make_async_remote_copy(
                src, dst, send.at[sem], recv.at[sem], device_id=(dst_r, dst_c), device_id_type=MESH
            ).start()

        def put_other(src, k, dst, sem):
            a, b = self.other(k)
            mine = (a == self.r) & (b == self.c)
            pl.when(mine)(lambda: pltpu.make_async_copy(src, dst, recv.at[sem]).start())
            pl.when(jnp.logical_not(mine))(lambda: put(src, a, b, dst, sem))

        return put, put_other


def pair_kernel(
    nr, nc, e_hbm, lpt_hbm, rpt_hbm, w_hbm, cot_hbm,
    out_hbm, sums_hbm, eg_hbm,
    rowf, colf, taps, mall, mt, act, a3, z, tf, move, onto, pick, by_group, gram, cacc, rsum, cols, col_ends, row_main, row_ends,
    out_ref, eg_ref, feats, e_ref, w_ref, cot_ref, own, right, packed, quad, line, proj, es, eb, twice, blocks, row_feats, col_feats,
    cparts, cends, rends, turned, gparts, buf, r1, r2, mid, fin, recv, send, loads, stores,
):
    ins = ((e_hbm, e_ref), (w_hbm, w_ref), (lpt_hbm, proj.at[0:32]), (rpt_hbm, proj.at[32:64]), (cot_hbm, cot_ref))
    ins = [pltpu.make_async_copy(src, dst, loads.at[k]) for k, (src, dst) in enumerate(ins)]
    for copy in ins:
        copy.start()
    p = Place(nr, nc)
    r, c, per, rb, rm, k1, k2 = p.r, p.c, p.per, p.rb, p.rm, p.k1, p.k2
    greeted = p.greet()
    put, put_other = p.senders(send, recv)
    rows8, rows7 = gparts, gparts.at[0 : nc - 1]

    proj[64:128, :] = jnp.zeros((64, 512), BF16)
    ins[0].wait()
    e = e_ref[...].astype(F32)
    es[...] = jnp.concatenate([e[:, 0:256], e[:, 256:512]], axis=0).astype(BF16)
    ins[2].wait()
    ins[3].wait()
    own[...] = dot_nt(e_ref[...], proj[...]).astype(BF16).astype(F32)
    group = iota((8, 128), 1) >> 5
    right[...] = jnp.where(group == rm, pltpu.roll(own[...], lax.rem(32 * rm + 96, 128), 1), 0.0)
    ins[1].wait()
    build_taps(w_ref, tf)
    ins[4].wait()
    mask_cotangent(r, c, cot_ref, move, mall, mt)
    pl.semaphore_wait(pltpu.get_barrier_semaphore(), greeted)

    for a, b, _ in p.quad:
        put(right, a, b, quad.at[rm], 1)
    pltpu.make_async_copy(right, quad.at[rm], recv.at[1]).start()

    def put_line(row, dst, sem):
        for k in range(nc):
            put(own, row, k, dst, sem)

    is_first, is_last = c == 0, c == nc - 1
    row_after, row_before = is_last & p.has_down, is_first & p.has_up
    pl.when(row_after)(lambda: put_line(r + 1, row_feats.at[0], 2))
    pl.when(row_before)(lambda: put_line(r - 1, row_feats.at[1], 3))
    for a, b, _ in p.line:
        put(own, a, b, line.at[c], 16)
    pltpu.make_async_copy(own, line.at[c], recv.at[16]).start()

    def put_targets(src, col, dst, sem):
        first, *rest = p.targets(col)
        mine = c == col
        pl.when(mine)(lambda: pltpu.make_async_copy(src, dst, recv.at[sem]).start())
        pl.when(jnp.logical_not(mine))(lambda: put(src, *first, dst, sem))
        for a, b in rest:
            put(src, a, b, dst, sem)

    col_after, col_before = is_last & (rb < nc - 1), is_first & (rb > 0)
    input_gradient(mt, tf, z, (0, 1))
    wait_bytes(quad, recv.at[1])
    packed[...] = jnp.sum(quad[...], axis=0)
    put_targets(packed, rb, blocks.at[c], 15)
    pl.when(col_after)(lambda: put_targets(packed, rb + 1, col_feats.at[0], 4))
    pl.when(col_before)(lambda: put_targets(packed, rb - 1, col_feats.at[1], 5))
    input_gradient(mt, tf, z, (1, 3))
    build_constants(onto, pick, by_group)

    def arrive(cond, ref, sem):
        pl.when(cond)(lambda: wait_bytes(ref, sem))

    def fill(cond, ref, value):
        pl.when(jnp.logical_not(cond))(lambda: ref.__setitem__(..., jnp.full(ref.shape, value, F32)))

    for cond, feats_in, sums_in in (
        (p.has_up, row_feats.at[0], rends.at[1]),
        (p.has_down, row_feats.at[1], rends.at[0]),
        (p.has_left, col_feats.at[0], None),
        (p.has_right, col_feats.at[1], None),
    ):
        fill(cond, feats_in, OUTSIDE)
        if sums_in is not None:
            fill(cond, sums_in, 0.0)
    fill(p.ends_block, cends.at[0], 0.0)
    fill(p.starts_block, cends.at[1], 0.0)
    arrive(p.has_up, row_feats.at[0], recv.at[2])
    arrive(p.has_down, row_feats.at[1], recv.at[3])
    arrive(p.has_left, col_feats.at[0], recv.at[4])
    arrive(p.has_right, col_feats.at[1], recv.at[5])
    wait_bytes(line, recv.at[16])
    wait_bytes(blocks, recv.at[15])
    feats[8:72, :] = line[...].reshape(8 * nc, 128)
    feats[0:8, :] = row_feats[0]
    feats[72:80, :] = row_feats[1]
    feats[80:136, :] = jnp.zeros((56, 128), F32)
    ends = [jnp.concatenate([col_feats[k], jnp.zeros((8, 128), F32)], axis=0).astype(BF16) for k in range(2)]
    features(feats[4:132, :].astype(BF16), blocks[...].reshape(8 * nc, 128).astype(BF16), *ends, onto, rowf, colf)
    for a, b, _ in p.line:
        put(es, a, b, eb.at[c], 0)
    pltpu.make_async_copy(es, eb.at[c], recv.at[0]).start()
    elementwise(rowf, colf, z, act, cacc, rsum)

    column_sums(cacc, pick, cols)

    @pl.when(p.in_others)
    def _():
        for k in range(per):
            put_other(cols.at[k], k, cparts.at[rm], 6)

    @pl.when(jnp.logical_not(p.in_others))
    def _():
        for k in range(per):
            put(cols.at[k], *p.other(k), cparts.at[rm], 6)

    column_end_sums(cacc, pick, col_ends)
    pl.when(p.has_left)(lambda: put(col_ends.at[0], per * c - 1, rb, cends.at[0, rm], 9))
    pl.when(p.has_right)(lambda: put(col_ends.at[1], per * c + per, rb, cends.at[1, rm], 10))
    row_sums(rsum, pick, by_group, row_main, row_ends)
    pl.when(p.has_up)(lambda: put(row_ends.at[0], r - 1, c, rends.at[0], 7))
    pl.when(p.has_down)(lambda: put(row_ends.at[1], r + 1, c, rends.at[1], 8))

    build_windows(act, a3)
    tap_gradient(mall, a3, pick, gram, taps)
    for k in range(PIECES - 16):
        buf[16 + k] = taps[16 * k : 16 * k + 16, :].astype(BF16)

    owner = k1 < PIECES

    def put_pieces(ks):
        def piece(k):
            put(buf.at[k], *p.member(p.plane, k), r1.at[k1], 11)

        @pl.when(owner)
        def _():
            for k in ks:
                pl.when(k1 != k)(lambda k=k: piece(k))

        @pl.when(jnp.logical_not(owner))
        def _():
            for k in ks:
                piece(k)

    put_pieces(range(16, PIECES))
    wait_bytes(eb, recv.at[0])
    e = eb[...].astype(F32)
    e = jnp.concatenate([e[:, 0:8].reshape(64, 256), e[:, 8:16].reshape(64, 256)], axis=1).astype(BF16)
    twice[...] = jnp.concatenate([e, e], axis=0)

    arrive(p.has_down, rends.at[0], recv.at[7])
    arrive(p.has_up, rends.at[1], recv.at[8])
    arrive(p.ends_block, cends.at[0], recv.at[9])
    arrive(p.starts_block, cends.at[1], recv.at[10])
    wait_bytes(cparts, recv.at[6])
    grads = (
        row_main[...] + jnp.concatenate([rends[1], rends[0]], axis=0),
        jnp.sum(cparts[...], axis=0)
        + jnp.concatenate([jnp.sum(cends[1], axis=0), jnp.sum(cends[0], axis=0)], axis=0),
    )
    lane = iota((16, 128), 1)
    spread = []
    for g in range(4):
        parts = [x if turn % 128 == 0 else pltpu.roll(x, turn % 128, 1) for x, turn in zip(grads, (-32 * g, 32 - 32 * g))]
        spread.append(jnp.where(lane < 32, parts[0], jnp.where(lane < 64, parts[1], 0.0)))
    turned[...] = jnp.concatenate(spread, axis=0)

    part = dot_tn(jnp.concatenate(halves(turned[...]), axis=0), twice[...])
    for k in range(16):
        at = slice(16 * (k // 4), 16 * (k // 4) + 16), slice(128 * (k % 4), 128 * (k % 4) + 128)
        buf[k] = part[at].astype(BF16)

    put_pieces(range(16))
    pl.when(owner)(lambda: pltpu.make_async_copy(buf.at[k1], r1.at[k1], recv.at[11]).start())

    outs = [
        pltpu.make_async_copy(out_ref.at[:, 16 * q : 16 * q + 16, :], out_hbm.at[:, 16 * q : 16 * q + 16, :], stores.at[q])
        for q in range(4)
    ]
    convolve(r, c, 0, a3, tf, out_ref)
    outs[0].start()
    for a, b, _ in p.line:
        put(turned.at[pl.ds(pl.multiple_of(8 * b, 8), 8)], a, b, gparts.at[c], 14)
    pltpu.make_async_copy(turned.at[pl.ds(pl.multiple_of(8 * c, 8), 8)], gparts.at[c], recv.at[14]).start()
    convolve(r, c, 1, a3, tf, out_ref)
    outs[1].start()

    @pl.when(owner)
    def _():
        wait_bytes(r1, recv.at[11])
        mid[...] = jnp.sum(r1[...].astype(F32), axis=0).astype(BF16)
        for a, b, _ in p.group2:
            put(mid, a, b, r2.at[k2], 12)
        pltpu.make_async_copy(mid, r2.at[k2], recv.at[12]).start()

    convolve(r, c, 2, a3, tf, out_ref)
    outs[2].start()
    convolve(r, c, 3, a3, tf, out_ref)
    outs[3].start()

    @pl.when(owner)
    def _():
        wait_bytes(r2, recv.at[12])
        fin[...] = jnp.sum(r2[...].astype(F32), axis=0).astype(BF16)
        for k in (1, 0, *range(2, 32)):
            pl.when(k1 != k)(lambda k=k: put(fin, *p.member(p.plane, k), sums_hbm.at[k1], 13))
        pltpu.make_async_copy(fin, sums_hbm.at[k1], recv.at[13]).start()

    wait_bytes(gparts, recv.at[14])
    high, low = halves(jnp.sum(gparts[...], axis=0))
    eg_ref[...] = dot(high, proj[...]) + dot(low, proj[...])
    outs.append(pltpu.make_async_copy(eg_ref, eg_hbm, stores.at[4]))
    outs[4].start()

    for copy in outs:
        copy.wait()
    wait_bytes(eb.at[0 : nc - 1], send.at[0])
    wait_bytes(quad.at[0 : per - 1], send.at[1])
    pl.when(row_after)(lambda: wait_bytes(rows8, send.at[2]))
    pl.when(row_before)(lambda: wait_bytes(rows8, send.at[3]))

    def sent_targets(cond, mine, eight, seven, sem):
        pl.when(cond & mine)(lambda: wait_bytes(seven, send.at[sem]))
        pl.when(cond & jnp.logical_not(mine))(lambda: wait_bytes(eight, send.at[sem]))

    sent_targets(col_after, rb + 1 == c, rows8, rows7, 4)
    sent_targets(col_before, rb - 1 == c, rows8, rows7, 5)
    sent_targets(rb >= 0, p.in_others, blocks, blocks.at[0 : nc - 1], 15)
    pl.when(p.in_others)(lambda: wait_bytes(cparts.at[0 : per - 1], send.at[6]))
    pl.when(jnp.logical_not(p.in_others))(lambda: wait_bytes(cparts, send.at[6]))
    pl.when(p.has_up)(lambda: wait_bytes(row_ends.at[0], send.at[7]))
    pl.when(p.has_down)(lambda: wait_bytes(row_ends.at[1], send.at[8]))
    pl.when(p.has_left)(lambda: wait_bytes(col_ends.at[0], send.at[9]))
    pl.when(p.has_right)(lambda: wait_bytes(col_ends.at[1], send.at[10]))
    wait_bytes(line.at[0 : nc - 1], send.at[16])
    pl.when(owner)(lambda: wait_bytes(r1.at[0 : PIECES - 1], send.at[11]))
    pl.when(jnp.logical_not(owner))(lambda: wait_bytes(r1.at[0:PIECES], send.at[11]))
    pl.when(owner)(lambda: wait_bytes(r2.at[0 : r2.shape[0] - 1], send.at[12]))
    wait_bytes(gparts.at[0 : nc - 1], send.at[14])

    pl.when(owner)(lambda: wait_bytes(r1.at[0 : r1.shape[0] - 1], send.at[13]))
    wait_bytes(sums_hbm, recv.at[13])


def finish_kernel(
    scale, sums_in, eg_in, pair_in, conv_out, left_out, right_out, eg_out, pair_out,
    sums_ref, eg_ref, held, conv_ref, left_ref, right_ref, loads, stores,
):
    def piece(k):
        return slice(8 * k, 8 * k + 8)

    ins = [pltpu.make_async_copy(sums_in, sums_ref, loads.at[0]), pltpu.make_async_copy(eg_in, eg_ref, loads.at[1])]
    ins += [pltpu.make_async_copy(pair_in.at[piece(k)], held.at[piece(k)], loads.at[2 + k]) for k in range(4)]
    outs = [
        pltpu.make_async_copy(conv_ref, conv_out, stores.at[0]),
        pltpu.make_async_copy(left_ref, left_out, stores.at[1]),
        pltpu.make_async_copy(right_ref, right_out, stores.at[2]),
        pltpu.make_async_copy(eg_ref, eg_out, stores.at[3]),
    ]
    outs += [pltpu.make_async_copy(held.at[piece(k)], pair_out.at[piece(k)], stores.at[4 + k]) for k in range(4)]
    for copy in ins:
        copy.start()
    ins[0].wait()
    for ref, first, at in ((left_ref, 0, 1), (right_ref, 8, 2)):
        for k in range(8):
            x = sums_ref[first + k].astype(F32)
            ref[16 * (k // 4) : 16 * (k // 4) + 16, 128 * (k % 4) : 128 * (k % 4) + 128] = x * scale
        outs[at].start()
    ins[1].wait()
    outs[3].start()
    for k in range(4):
        ins[2 + k].wait()
        outs[4 + k].start()
    for k in range(9):
        q, at = divmod(k, 4)
        for part in range(2):
            x = sums_ref[16 + 2 * q + part].astype(F32)
            conv_ref[k, 16 * part : 16 * part + 16, :] = x[:, 32 * at : 32 * at + 32] * scale
    outs[0].start()
    for copy in outs:
        copy.wait()


def shards(nr, nc, embed, left_proj, right_proj, conv_w, cotangent):
    per = nr // nc
    pair_out, totals, embed_grad = pl.pallas_call(
        functools.partial(pair_kernel, nr, nc),
        out_shape=(
            jax.ShapeDtypeStruct((32, 64, 256), BF16),
            jax.ShapeDtypeStruct((PIECES, 16, 128), BF16),
            jax.ShapeDtypeStruct((8, 512), F32),
        ),
        in_specs=[HBM] * 5,
        out_specs=(HBM,) * 3,
        scratch_shapes=LOCAL_SCRATCH
        + [
            pltpu.VMEM((32, 64, 256), BF16),
            pltpu.VMEM((8, 512), F32),
            pltpu.VMEM((136, 128), F32),
            pltpu.VMEM((8, 512), BF16),
            pltpu.VMEM((9, 32, 32), BF16),
            pltpu.VMEM((32, 64, 256), BF16),
            pltpu.VMEM((8, 128), F32),
            pltpu.VMEM((8, 128), F32),
            pltpu.VMEM((8, 128), F32),
            pltpu.VMEM((per, 8, 128), F32),
            pltpu.VMEM((nc, 8, 128), F32),
            pltpu.VMEM((128, 512), BF16),
            pltpu.VMEM((16, 256), BF16),
            pltpu.VMEM((nc, 16, 256), BF16),
            pltpu.VMEM((128, 512), BF16),
            pltpu.VMEM((nc, 8, 128), F32),
            pltpu.VMEM((2, 8, 128), F32),
            pltpu.VMEM((2, 8, 128), F32),
            pltpu.VMEM((per, 16, 128), F32),
            pltpu.VMEM((2, per, 8, 128), F32),
            pltpu.VMEM((2, 8, 128), F32),
            pltpu.VMEM((64, 128), F32),
            pltpu.VMEM((nc, 8, 128), F32),
            pltpu.VMEM((PIECES, 16, 128), BF16),
            pltpu.VMEM((32, 16, 128), BF16),
            pltpu.VMEM((8, 16, 128), BF16),
            pltpu.VMEM((16, 128), BF16),
            pltpu.VMEM((16, 128), BF16),
            pltpu.SemaphoreType.DMA((17,)),
            pltpu.SemaphoreType.DMA((17,)),
            pltpu.SemaphoreType.DMA((5,)),
            pltpu.SemaphoreType.DMA((6,)),
        ],
        compiler_params=pltpu.CompilerParams(
            collective_id=0, has_side_effects=True, vmem_limit_bytes=60 * 1024 * 1024
        ),
        name="pair_kernel",
    )(embed, left_proj.T, right_proj.T, conv_w, cotangent)
    conv_grad, left_t, right_t, embed_grad, pair_out = pl.pallas_call(
        functools.partial(finish_kernel, 32.0 / (8 * nr * nc)),
        out_shape=(
            jax.ShapeDtypeStruct((9, 32, 32), F32),
            jax.ShapeDtypeStruct((32, 512), F32),
            jax.ShapeDtypeStruct((32, 512), F32),
            jax.ShapeDtypeStruct((8, 512), F32),
            jax.ShapeDtypeStruct((32, 64, 256), BF16),
        ),
        in_specs=[HBM] * 3,
        out_specs=(HBM,) * 5,
        scratch_shapes=[
            pltpu.VMEM((PIECES, 16, 128), BF16),
            pltpu.VMEM((8, 512), F32),
            pltpu.VMEM((32, 64, 256), BF16),
            pltpu.VMEM((9, 32, 32), F32),
            pltpu.VMEM((32, 512), F32),
            pltpu.VMEM((32, 512), F32),
            pltpu.SemaphoreType.DMA((6,)),
            pltpu.SemaphoreType.DMA((8,)),
        ],
        compiler_params=pltpu.CompilerParams(vmem_limit_bytes=60 * 1024 * 1024),
        name="finish",
    )(totals, embed_grad, pair_out)
    return pair_out, conv_grad, left_t.T, right_t.T, embed_grad


def solution(mesh):
    body = functools.partial(shards, mesh.shape["row"], mesh.shape["col"])
    in_specs = (P(("row", "col"), None), P(), P(), P(), P(None, "row", "col"))
    out_specs = (P(None, "row", "col"), P(), P(), P(), P(("row", "col"), None))
    return jax.shard_map(body, mesh=mesh, in_specs=in_specs, out_specs=out_specs, check_vma=False)
```

```python
import functools

import jax
import jax.numpy as jnp
from jax import lax
from jax.experimental import pallas as pl
from jax.experimental.pallas import tpu as pltpu
from jax.sharding import PartitionSpec as P

MESH = pl.DeviceIdType.MESH
OUTSIDE = -1e30
LOG2E = 1.4426950408889634
LN2 = 0.6931471805599453
PIECES = 22
F32 = jnp.float32
BF16 = jnp.bfloat16
VMEM = pl.BlockSpec(memory_space=pltpu.VMEM)
HBM = pl.BlockSpec(memory_space=pltpu.HBM)


def iota(shape, dim):
    return lax.broadcasted_iota(jnp.int32, shape, dim)


def one_hot(cond):
    return jnp.where(cond, 1.0, 0.0).astype(BF16)


def dot(a, b):
    return jnp.dot(a, b, preferred_element_type=F32)


def dot_nt(a, b):
    return lax.dot_general(a, b, (((1,), (1,)), ((), ())), preferred_element_type=F32)


def dot_tn(a, b):
    return lax.dot_general(a, b, (((0,), (0,)), ((), ())), preferred_element_type=F32)


def halves(x):
    high = x.astype(BF16)
    return high, (x - high.astype(F32)).astype(BF16)


def loop(n, f):
    def body(k, _):
        f(k)
        return 0

    lax.fori_loop(0, n, body, 0)


def lanes(h):
    return pl.ds(pl.multiple_of(h * 256, 256), 256)


def wait_bytes(ref, sem):
    pltpu.make_async_copy(ref, ref, sem).wait()


def softplus_and_slope(y):
    t = jnp.exp2(-jnp.abs(y))
    u = 1.0 + t
    inv = pltpu.reciprocal(u, full_range=False)
    log = jnp.where(t < 2.0**-11, t * LOG2E, jnp.log2(u))
    return jnp.maximum(y, 0.0) + log, jnp.where(y >= 0, inv, t * inv)


def build_taps(w_ref, tf):
    spread = one_hot((iota((256, 32), 0) >> 3) == iota((256, 32), 1))
    widen = one_hot((iota((32, 256), 1) >> 3) == iota((32, 256), 0))
    s0, s1 = iota((256, 256), 0) & 7, iota((256, 256), 1) & 7
    same, above, below = s1 == s0, s1 == s0 + 4, s1 == s0 - 4
    x = dot(w_ref[...].reshape(288, 32), widen).astype(BF16)
    for b in range(3):
        x0, x1, x2 = (dot(spread, x[96 * a + 32 * b : 96 * a + 32 * b + 32]) for a in range(3))
        tf[:, 256 * b : 256 * b + 256] = jnp.where(same, x0, jnp.where(above, x1, 0.0)).astype(BF16)
        tf[:, 768 + 256 * b : 1024 + 256 * b] = jnp.where(same, x2, jnp.where(below, x1, 0.0)).astype(BF16)


def mask_cotangent(r, c, cot_ref, move, mall, mt):
    mall[0:256, 2048:2304] = jnp.zeros((256, 256), BF16)
    mall[256:512, 0:256] = jnp.zeros((256, 256), BF16)
    for k in range(4):
        x = cot_ref[:, 16 * k : 16 * k + 16, :].astype(F32)
        row = r * 64 + 16 * k + iota((16, 256), 0)
        x = jnp.where((c * 256 + iota((16, 256), 1) >= row)[None], x, 0.0)
        for half in range(2):
            m = x[:, 8 * half : 8 * half + 8].reshape(256, 256).astype(BF16)
            mall[0:256, lanes(2 * k + half)] = m
            mall[256:512, lanes(2 * k + half + 1)] = m
    for b in range(2):
        move[272 * b : 272 * b + 272, :] = one_hot(iota((272, 256), 0) - 4 * b == iota((272, 256), 1))
    mt[0] = jnp.zeros((272, 768), BF16)
    mt[9] = jnp.zeros((272, 768), BF16)
    none = jnp.zeros((8, 256), F32)

    def body(g):
        moved = dot_nt(move[...], mall[0:256, lanes(g)])
        mt[g + 1, :, 0:256] = moved[0:272].astype(BF16)
        mt[g + 1, :, 256:512] = moved[272:544].astype(BF16)
        mt[g + 1, :, 512:768] = jnp.concatenate([none, moved[0:264]], axis=0).astype(BF16)

    loop(8, body)


def input_gradient(mt, tf, z, steps):
    def body(step, _):
        left = [jnp.concatenate([mt[3 * step + k], mt[3 * step + k + 1]], axis=1) for k in range(3)]
        right = jnp.concatenate(
            [tf[:, 768 * (1 - u) + 256 * b : 768 * (1 - u) + 256 * b + 256] for u in range(2) for b in range(3)], axis=0
        )
        x = dot(jnp.concatenate(left, axis=0), right)
        for k in range(3):
            z[3 * step + k] = x[272 * k : 272 * k + 272]
        return 0

    lax.fori_loop(*steps, body, 0)


def features(rows, blocks, before, after, onto, rowf, colf):
    picks = [onto[:, 256 * at : 256 * at + 256] for at in range(4)]
    first = dot(before, picks[3])
    last = dot(after, picks[0])
    x = [first[4:8]] + [dot(blocks, pick) for pick in picks] + [last[0:4], jnp.zeros((8, 256), F32)]
    colf[...] = jnp.concatenate(x, axis=0) * LOG2E
    x = dot(rows, picks[0])
    x = jnp.where((iota((128, 256), 0) & 7) == (iota((128, 256), 1) & 7), x, 0.0).astype(BF16)
    rowf[...] = dot(one_hot((iota((16, 128), 1) >> 3) == iota((16, 128), 0)), x) * LOG2E


def elementwise(rowf, colf, z, act, cacc, rsum):
    rsum[...] = jnp.zeros_like(rsum)

    def body(step):
        parts = [pl.ds(pl.multiple_of(24 * step + 8 * part, 8), 8) for part in range(3)]
        totals = [jnp.zeros((8, 256), F32)] * 3
        for h in range(9):
            left = rowf[h : h + 1, :]
            row = jnp.zeros((8, 256), F32)
            for k, rows in enumerate(parts):
                value, slope = softplus_and_slope(colf[rows, :] + left)
                act[h, rows, :] = value
                p = z[h, rows, :] * slope
                totals[k] += p
                row += p
            rsum[8 * h : 8 * h + 8, :] += row
        for k, rows in enumerate(parts):
            cacc[rows, :] = totals[k]

    loop(11, body)


def build_constants(onto, pick, by_group):
    k, n = iota((128, 256), 0), iota((128, 256), 1) >> 3
    for at in range(4):
        onto[:, 256 * at : 256 * at + 256] = one_hot(k == n + 32 * at)
    k, n = iota((256, 128), 0) >> 3, iota((256, 128), 1)
    for g in range(4):
        pick[256 * g : 256 * g + 256, :] = one_hot(k + 32 * g == n)
    by_group[...] = one_hot((iota((80, 128), 0) >> 3) == (iota((80, 128), 1) >> 3))


def ends_of(x, pick, ends):
    sub = iota((16, 128), 0)
    high, low = halves(x)
    first = dot(high, pick[768:1024]) + dot(low, pick[768:1024])
    second = dot(high, pick[0:256]) + dot(low, pick[0:256])
    ends[0] = jnp.where(sub >= 12, pltpu.roll(first, 12, 0), 0.0)[8:16]
    ends[1] = jnp.where(sub < 4, pltpu.roll(second, 4, 0), 0.0)[0:8]


def column_sums(cacc, pick, cols):
    x = [
        jnp.concatenate([cacc[4 + 64 * q + 16 * g : 20 + 64 * q + 16 * g, :] for g in range(4)], axis=1) for q in range(4)
    ]
    high, low = halves(jnp.concatenate(x, axis=0))
    x = dot(high, pick[...]) + dot(low, pick[...])
    for q in range(4):
        cols[q] = x[16 * q : 16 * q + 16]


def column_end_sums(cacc, pick, col_ends):
    ends_of(jnp.concatenate([cacc[0:8, :], cacc[256:264, :]], axis=0), pick, col_ends)


def row_sums(rsum, pick, by_group, row_main, row_ends):
    x = jnp.concatenate([rsum[...], jnp.zeros((56, 256), F32)], axis=0)
    high, low = halves(x)
    x = dot(by_group[...], high) + dot(by_group[...], low)
    x = jnp.where((iota((80, 256), 0) & 7) == (iota((80, 256), 1) & 7), x, 0.0)
    ends_of(jnp.concatenate([x[0:8], x[64:72]], axis=0), pick, row_ends)
    high, low = halves(jnp.concatenate([x[4 + 16 * g : 20 + 16 * g] for g in range(4)], axis=1))
    row_main[...] = dot(high, pick[...]) + dot(low, pick[...])


def build_windows(act, a3):
    def body(h):
        at = pl.ds(pl.multiple_of(256 * h, 256), 256)
        for b in range(3):
            a3[at, 256 * b : 256 * b + 256] = (act[h, 4 * b : 4 * b + 256, :] * LN2).astype(BF16)

    loop(9, body)


def convolve(r, c, k, a3, tf, out_ref):
    parts = []
    for g in (2 * k, 2 * k + 1):
        both = jnp.concatenate([a3[256 * (g + u) : 256 * (g + u) + 256, :] for u in range(2)], axis=1)
        parts.append(dot_nt(tf[...], both).reshape(32, 8, 256))
    y = jnp.concatenate(parts, axis=1)
    row = r * 64 + 16 * k + iota((16, 256), 0)
    col = c * 256 + iota((16, 256), 1)
    out_ref[:, 16 * k : 16 * k + 16, :] = jnp.where((col >= row)[None], y, 0.0).astype(BF16)


def tap_gradient(mall, a3, pick, gram, taps):
    x = dot(mall[...], a3[...])
    for u in range(2):
        for k in range(6):
            gram[6 * u + k] = x[256 * u : 256 * u + 256, 128 * k : 128 * k + 128]
    lane = iota((32, 128), 1)

    def along(b, k, sources):
        total = jnp.zeros((32, 128), F32)
        for at, (s, u) in enumerate(sources):
            total = jnp.where((lane & 7) == at, gram[6 * u + 2 * b + k, pl.ds(s, 32, stride=8), :], total)
        return total

    sources = (
        [(s, 0) for s in range(8)],
        [((s + 4) % 8, 1 - s // 4) for s in range(8)],
        [(s, 1) for s in range(8)],
    )
    x = [jnp.concatenate([along(b, k, sources[a]) for k in range(2)], axis=1) for a in range(3) for b in range(3)]
    y = dot(jnp.concatenate(halves(jnp.concatenate(x, axis=0)), axis=0), pick[0:256])
    y = y[0:288] + y[288:576]
    for q in range(3):
        total = jnp.zeros((32, 128), F32)
        for k in range(min(4, 9 - 4 * q)):
            tap = y[32 * (4 * q + k) : 32 * (4 * q + k) + 32]
            total = jnp.where((lane >> 5) == k, pltpu.roll(tap, 32 * k, 1) if k else tap, total)
        taps[32 * q : 32 * q + 32, :] = total


LOCAL_SCRATCH = [
    pltpu.VMEM((16, 256), F32),
    pltpu.VMEM((272, 256), F32),
    pltpu.VMEM((96, 128), F32),
    pltpu.VMEM((512, 2304), BF16),
    pltpu.VMEM((10, 272, 768), BF16),
    pltpu.VMEM((9, 272, 256), F32),
    pltpu.VMEM((2304, 768), BF16),
    pltpu.VMEM((9, 272, 256), F32),
    pltpu.VMEM((256, 1536), BF16),
    pltpu.VMEM((544, 256), BF16),
    pltpu.VMEM((128, 1024), BF16),
    pltpu.VMEM((1024, 128), BF16),
    pltpu.VMEM((80, 128), BF16),
    pltpu.VMEM((12, 256, 128), F32),
    pltpu.VMEM((272, 256), F32),
    pltpu.VMEM((72, 256), F32),
    pltpu.VMEM((4, 16, 128), F32),
    pltpu.VMEM((2, 8, 128), F32),
    pltpu.VMEM((16, 128), F32),
    pltpu.VMEM((2, 8, 128), F32),
]


class Place:
    def __init__(self, nr, nc):
        r, c = lax.axis_index("row"), lax.axis_index("col")
        self.r, self.c, self.nr, self.nc = r, c, nr, nc
        self.per = nr // nc
        self.rb, self.rm = lax.div(r, self.per), lax.rem(r, self.per)
        _, self.quad = self.group(((r, 1, 0), (r, 2, 0)))
        _, self.line = self.group(((c, 1, 1), (c, 2, 1), (c, 4, 1)))
        self.plane = ((r, 1, 0), (r, 8, 0), (c, 2, 1), (r, 16, 0), (c, 4, 1))
        self.k1, self.group1 = self.group(self.plane)
        self.z_line = ((r, 2, 0), (r, 4, 0), (c, 1, 1))
        self.k2, self.group2 = self.group(self.z_line)
        self.has_up, self.has_down = r > 0, r < nr - 1
        self.has_left, self.has_right = c > 0, c < nc - 1
        self.ends_block = (self.rm == self.per - 1) & (self.rb < nc - 1)
        self.starts_block = (self.rm == 0) & (self.rb > 0)
        self.in_others = self.rb == c

    def group(self, bits):
        number, turns = 0, []
        for k, (x, weight, is_col) in enumerate(bits):
            bit = lax.rem(lax.div(x, weight), 2)
            number = number + bit * (1 << k)
            sign = 1 - 2 * bit
            turns.append((sign * weight, is_col, sign * (1 << k)))
        members = [(self.r, self.c, number)]
        for move, is_col, step in turns:
            members += [
                (a, b + move, n + step) if is_col else (a + move, b, n + step) for a, b, n in members
            ]
        return number, members[:0:-1]

    def member(self, bits, k):
        a, b = self.r, self.c
        for at, (x, weight, is_col) in enumerate(bits):
            move = weight * (k >> at & 1) - weight * lax.rem(lax.div(x, weight), 2)
            a, b = (a, b + move) if is_col else (a + move, b)
        return a, b

    def other(self, k):
        return self.per * self.c + k, self.rb

    def targets(self, col):
        return [(lax.rem(self.r + self.per * k, self.nr), col) for k in range(self.nr // self.per)]

    def greet(self):
        r, c, nc, per, rb, rm = self.r, self.c, self.nc, self.per, self.rb, self.rm
        barrier = pltpu.get_barrier_semaphore()

        def signal(a, b):
            pl.semaphore_signal(barrier, inc=1, device_id=(a, b), device_id_type=MESH)

        def signal_all(col):
            for k in range(per):
                signal(per * c + k, col)

        is_first, is_last = c == 0, c == nc - 1
        before_is_me = is_last & (rb == nc - 2)
        after_is_me = is_first & (rb == 1)
        for a, b, _ in self.quad + self.line:
            signal(a, b)
        pl.when(jnp.logical_not(self.in_others))(lambda: signal(per * c + rm, c))
        for _, b, _ in self.line:
            signal(per * c + rm, b)
        pl.when(self.has_up)(lambda: signal(r - 1, nc - 1))
        pl.when(self.has_down)(lambda: signal(r + 1, 0))
        pl.when(self.has_left & jnp.logical_not(before_is_me))(lambda: signal(per * (c - 1) + rm, nc - 1))
        pl.when(self.has_right & jnp.logical_not(after_is_me))(lambda: signal(per * (c + 1) + rm, 0))
        pl.when(jnp.logical_not(self.in_others))(lambda: signal(per * c + rm, rb))
        for a, _, _ in self.quad:
            signal(per * (c - rb) + a, rb)
        pl.when(self.has_up)(lambda: signal(r - 1, c))
        pl.when(self.has_down)(lambda: signal(r + 1, c))
        pl.when(self.ends_block)(lambda: signal_all(rb + 1))
        pl.when(self.starts_block)(lambda: signal_all(rb - 1))
        owner = self.k1 < PIECES

        @pl.when(owner)
        def _():
            for a, b, _ in self.group1 + self.group2:
                signal(a, b)

        @pl.when(jnp.logical_not(owner))
        def _():
            for k in range(PIECES):
                signal(*self.member(self.plane, k))

        n = len(self.quad + self.line) + nc + per
        n = n + jnp.where(owner, len(self.group1 + self.group2), PIECES)
        up, down = self.has_up, self.has_down
        for cond, m in (
            (self.in_others, -2), (is_last & down, nc), (is_first & up, nc),
            (is_last & (rb < nc - 1), nc), (before_is_me, -1), (is_first & (rb > 0), nc), (after_is_me, -1),
            (up, 1), (down, 1), (self.has_left, 1), (self.has_right, 1),
        ):
            n = n + jnp.where(cond, m, 0)
        return n

    def senders(self, send, recv):
        def put(src, dst_r, dst_c, dst, sem):
            pltpu.make_async_remote_copy(
                src, dst, send.at[sem], recv.at[sem], device_id=(dst_r, dst_c), device_id_type=MESH
            ).start()

        def put_other(src, k, dst, sem):
            a, b = self.other(k)
            mine = (a == self.r) & (b == self.c)
            pl.when(mine)(lambda: pltpu.make_async_copy(src, dst, recv.at[sem]).start())
            pl.when(jnp.logical_not(mine))(lambda: put(src, a, b, dst, sem))

        return put, put_other


def pair_kernel(
    nr, nc, e_hbm, lpt_hbm, rpt_hbm, w_hbm, cot_hbm,
    out_hbm, sums_hbm, eg_hbm,
    rowf, colf, taps, mall, mt, act, a3, z, tf, move, onto, pick, by_group, gram, cacc, rsum, cols, col_ends, row_main, row_ends,
    out_ref, eg_ref, feats, e_ref, w_ref, cot_ref, own, right, packed, quad, line, proj, es, eb, twice, blocks, row_feats, col_feats,
    cparts, cends, rends, turned, gparts, buf, r1, r2, mid, fin, recv, send, loads, stores,
):
    ins = ((e_hbm, e_ref), (w_hbm, w_ref), (lpt_hbm, proj.at[0:32]), (rpt_hbm, proj.at[32:64]), (cot_hbm, cot_ref))
    ins = [pltpu.make_async_copy(src, dst, loads.at[k]) for k, (src, dst) in enumerate(ins)]
    for copy in ins:
        copy.start()
    p = Place(nr, nc)
    r, c, per, rb, rm, k1, k2 = p.r, p.c, p.per, p.rb, p.rm, p.k1, p.k2
    greeted = p.greet()
    put, put_other = p.senders(send, recv)
    rows8, rows7 = gparts, gparts.at[0 : nc - 1]

    proj[64:128, :] = jnp.zeros((64, 512), BF16)
    ins[0].wait()
    e = e_ref[...].astype(F32)
    es[...] = jnp.concatenate([e[:, 0:256], e[:, 256:512]], axis=0).astype(BF16)
    ins[2].wait()
    ins[3].wait()
    own[...] = dot_nt(e_ref[...], proj[...]).astype(BF16).astype(F32)
    group = iota((8, 128), 1) >> 5
    right[...] = jnp.where(group == rm, pltpu.roll(own[...], lax.rem(32 * rm + 96, 128), 1), 0.0)
    ins[1].wait()
    build_taps(w_ref, tf)
    ins[4].wait()
    mask_cotangent(r, c, cot_ref, move, mall, mt)
    pl.semaphore_wait(pltpu.get_barrier_semaphore(), greeted)

    for a, b, _ in p.quad:
        put(right, a, b, quad.at[rm], 1)
    pltpu.make_async_copy(right, quad.at[rm], recv.at[1]).start()

    def put_line(row, dst, sem):
        for k in range(nc):
            put(own, row, k, dst, sem)

    is_first, is_last = c == 0, c == nc - 1
    row_after, row_before = is_last & p.has_down, is_first & p.has_up
    pl.when(row_after)(lambda: put_line(r + 1, row_feats.at[0], 2))
    pl.when(row_before)(lambda: put_line(r - 1, row_feats.at[1], 3))
    for a, b, _ in p.line:
        put(own, a, b, line.at[c], 16)
    pltpu.make_async_copy(own, line.at[c], recv.at[16]).start()

    def put_targets(src, col, dst, sem):
        first, *rest = p.targets(col)
        mine = c == col
        pl.when(mine)(lambda: pltpu.make_async_copy(src, dst, recv.at[sem]).start())
        pl.when(jnp.logical_not(mine))(lambda: put(src, *first, dst, sem))
        for a, b in rest:
            put(src, a, b, dst, sem)

    col_after, col_before = is_last & (rb < nc - 1), is_first & (rb > 0)
    input_gradient(mt, tf, z, (0, 1))
    wait_bytes(quad, recv.at[1])
    packed[...] = jnp.sum(quad[...], axis=0)
    put_targets(packed, rb, blocks.at[c], 15)
    pl.when(col_after)(lambda: put_targets(packed, rb + 1, col_feats.at[0], 4))
    pl.when(col_before)(lambda: put_targets(packed, rb - 1, col_feats.at[1], 5))
    input_gradient(mt, tf, z, (1, 3))
    build_constants(onto, pick, by_group)

    def arrive(cond, ref, sem):
        pl.when(cond)(lambda: wait_bytes(ref, sem))
        pl.when(jnp.logical_not(cond))(lambda: ref.__setitem__(..., jnp.full(ref.shape, OUTSIDE, F32)))

    arrive(p.has_up, row_feats.at[0], recv.at[2])
    arrive(p.has_down, row_feats.at[1], recv.at[3])
    arrive(p.has_left, col_feats.at[0], recv.at[4])
    arrive(p.has_right, col_feats.at[1], recv.at[5])
    wait_bytes(line, recv.at[16])
    wait_bytes(blocks, recv.at[15])
    feats[8:72, :] = line[...].reshape(8 * nc, 128)
    feats[0:8, :] = row_feats[0]
    feats[72:80, :] = row_feats[1]
    feats[80:136, :] = jnp.zeros((56, 128), F32)
    ends = [jnp.concatenate([col_feats[k], jnp.zeros((8, 128), F32)], axis=0).astype(BF16) for k in range(2)]
    features(feats[4:132, :].astype(BF16), blocks[...].reshape(8 * nc, 128).astype(BF16), *ends, onto, rowf, colf)
    for a, b, _ in p.line:
        put(es, a, b, eb.at[c], 0)
    pltpu.make_async_copy(es, eb.at[c], recv.at[0]).start()
    elementwise(rowf, colf, z, act, cacc, rsum)

    column_sums(cacc, pick, cols)
    for k in range(per):
        put_other(cols.at[k], k, cparts.at[rm], 6)
    column_end_sums(cacc, pick, col_ends)
    pl.when(p.has_left)(lambda: put(col_ends.at[0], per * c - 1, rb, cends.at[0, rm], 9))
    pl.when(p.has_right)(lambda: put(col_ends.at[1], per * c + per, rb, cends.at[1, rm], 10))
    row_sums(rsum, pick, by_group, row_main, row_ends)
    pl.when(p.has_up)(lambda: put(row_ends.at[0], r - 1, c, rends.at[0], 7))
    pl.when(p.has_down)(lambda: put(row_ends.at[1], r + 1, c, rends.at[1], 8))

    build_windows(act, a3)
    tap_gradient(mall, a3, pick, gram, taps)
    for k in range(PIECES - 16):
        buf[16 + k] = taps[16 * k : 16 * k + 16, :].astype(BF16)

    owner = k1 < PIECES

    def put_pieces(ks):
        def piece(k):
            put(buf.at[k], *p.member(p.plane, k), r1.at[k1], 11)

        @pl.when(owner)
        def _():
            for k in ks:
                pl.when(k1 != k)(lambda k=k: piece(k))

        @pl.when(jnp.logical_not(owner))
        def _():
            for k in ks:
                piece(k)

    put_pieces(range(16, PIECES))
    wait_bytes(eb, recv.at[0])
    e = eb[...].astype(F32)
    e = jnp.concatenate([e[:, 0:8].reshape(64, 256), e[:, 8:16].reshape(64, 256)], axis=1).astype(BF16)
    twice[...] = jnp.concatenate([e, e], axis=0)

    def gather_sum(cond, ref, sem):
        pl.when(cond)(lambda: wait_bytes(ref, sem))
        pl.when(jnp.logical_not(cond))(lambda: ref.__setitem__(..., jnp.zeros(ref.shape, F32)))

    gather_sum(p.has_down, rends.at[0], recv.at[7])
    gather_sum(p.has_up, rends.at[1], recv.at[8])
    gather_sum(p.ends_block, cends.at[0], recv.at[9])
    gather_sum(p.starts_block, cends.at[1], recv.at[10])
    wait_bytes(cparts, recv.at[6])
    grads = (
        row_main[...] + jnp.concatenate([rends[1], rends[0]], axis=0),
        jnp.sum(cparts[...], axis=0)
        + jnp.concatenate([jnp.sum(cends[1], axis=0), jnp.sum(cends[0], axis=0)], axis=0),
    )
    lane = iota((16, 128), 1)
    spread = []
    for g in range(4):
        parts = [x if turn % 128 == 0 else pltpu.roll(x, turn % 128, 1) for x, turn in zip(grads, (-32 * g, 32 - 32 * g))]
        spread.append(jnp.where(lane < 32, parts[0], jnp.where(lane < 64, parts[1], 0.0)))
    turned[...] = jnp.concatenate(spread, axis=0)

    part = dot_tn(jnp.concatenate(halves(turned[...]), axis=0), twice[...])
    for k in range(16):
        at = slice(16 * (k // 4), 16 * (k // 4) + 16), slice(128 * (k % 4), 128 * (k % 4) + 128)
        buf[k] = part[at].astype(BF16)

    put_pieces(range(16))
    pl.when(owner)(lambda: pltpu.make_async_copy(buf.at[k1], r1.at[k1], recv.at[11]).start())

    outs = [
        pltpu.make_async_copy(out_ref.at[:, 16 * q : 16 * q + 16, :], out_hbm.at[:, 16 * q : 16 * q + 16, :], stores.at[q])
        for q in range(4)
    ]
    convolve(r, c, 0, a3, tf, out_ref)
    outs[0].start()
    for a, b, _ in p.line:
        put(turned.at[pl.ds(pl.multiple_of(8 * b, 8), 8)], a, b, gparts.at[c], 14)
    pltpu.make_async_copy(turned.at[pl.ds(pl.multiple_of(8 * c, 8), 8)], gparts.at[c], recv.at[14]).start()
    convolve(r, c, 1, a3, tf, out_ref)
    outs[1].start()

    @pl.when(owner)
    def _():
        wait_bytes(r1, recv.at[11])
        mid[...] = jnp.sum(r1[...].astype(F32), axis=0).astype(BF16)
        for k in range(8):
            pl.when(k2 != k)(lambda k=k: put(mid, *p.member(p.z_line, k), r2.at[k2], 12))
        pltpu.make_async_copy(mid, r2.at[k2], recv.at[12]).start()

    convolve(r, c, 2, a3, tf, out_ref)
    outs[2].start()
    convolve(r, c, 3, a3, tf, out_ref)
    outs[3].start()

    @pl.when(owner)
    def _():
        wait_bytes(r2, recv.at[12])
        fin[...] = jnp.sum(r2[...].astype(F32), axis=0).astype(BF16)
        for a, b, _ in p.group1:
            put(fin, a, b, sums_hbm.at[k1], 13)
        pltpu.make_async_copy(fin, sums_hbm.at[k1], recv.at[13]).start()

    wait_bytes(gparts, recv.at[14])
    high, low = halves(jnp.sum(gparts[...], axis=0))
    eg_ref[...] = dot(high, proj[...]) + dot(low, proj[...])
    outs.append(pltpu.make_async_copy(eg_ref, eg_hbm, stores.at[4]))
    outs[4].start()

    for copy in outs:
        copy.wait()
    wait_bytes(eb.at[0 : nc - 1], send.at[0])
    wait_bytes(quad.at[0 : per - 1], send.at[1])
    pl.when(row_after)(lambda: wait_bytes(rows8, send.at[2]))
    pl.when(row_before)(lambda: wait_bytes(rows8, send.at[3]))

    def sent_targets(cond, mine, eight, seven, sem):
        pl.when(cond & mine)(lambda: wait_bytes(seven, send.at[sem]))
        pl.when(cond & jnp.logical_not(mine))(lambda: wait_bytes(eight, send.at[sem]))

    sent_targets(col_after, rb + 1 == c, rows8, rows7, 4)
    sent_targets(col_before, rb - 1 == c, rows8, rows7, 5)
    sent_targets(rb >= 0, p.in_others, blocks, blocks.at[0 : nc - 1], 15)
    pl.when(p.in_others)(lambda: wait_bytes(cparts.at[0 : per - 1], send.at[6]))
    pl.when(jnp.logical_not(p.in_others))(lambda: wait_bytes(cparts, send.at[6]))
    pl.when(p.has_up)(lambda: wait_bytes(row_ends.at[0], send.at[7]))
    pl.when(p.has_down)(lambda: wait_bytes(row_ends.at[1], send.at[8]))
    pl.when(p.has_left)(lambda: wait_bytes(col_ends.at[0], send.at[9]))
    pl.when(p.has_right)(lambda: wait_bytes(col_ends.at[1], send.at[10]))
    wait_bytes(line.at[0 : nc - 1], send.at[16])
    pl.when(owner)(lambda: wait_bytes(r1.at[0 : PIECES - 1], send.at[11]))
    pl.when(jnp.logical_not(owner))(lambda: wait_bytes(r1.at[0:PIECES], send.at[11]))
    pl.when(owner)(lambda: wait_bytes(r2.at[0 : r2.shape[0] - 1], send.at[12]))
    wait_bytes(gparts.at[0 : nc - 1], send.at[14])

    pl.when(owner)(lambda: wait_bytes(r1.at[0 : r1.shape[0] - 1], send.at[13]))
    wait_bytes(sums_hbm, recv.at[13])


def finish_kernel(
    scale, sums_in, eg_in, pair_in, conv_out, left_out, right_out, eg_out, pair_out,
    sums_ref, eg_ref, held, conv_ref, left_ref, right_ref, loads, stores,
):
    def piece(k):
        return slice(8 * k, 8 * k + 8)

    ins = [pltpu.make_async_copy(sums_in, sums_ref, loads.at[0]), pltpu.make_async_copy(eg_in, eg_ref, loads.at[1])]
    ins += [pltpu.make_async_copy(pair_in.at[piece(k)], held.at[piece(k)], loads.at[2 + k]) for k in range(4)]
    outs = [
        pltpu.make_async_copy(conv_ref, conv_out, stores.at[0]),
        pltpu.make_async_copy(left_ref, left_out, stores.at[1]),
        pltpu.make_async_copy(right_ref, right_out, stores.at[2]),
        pltpu.make_async_copy(eg_ref, eg_out, stores.at[3]),
    ]
    outs += [pltpu.make_async_copy(held.at[piece(k)], pair_out.at[piece(k)], stores.at[4 + k]) for k in range(4)]
    for copy in ins:
        copy.start()
    ins[0].wait()
    for ref, first, at in ((left_ref, 0, 1), (right_ref, 8, 2)):
        for k in range(8):
            x = sums_ref[first + k].astype(F32)
            ref[16 * (k // 4) : 16 * (k // 4) + 16, 128 * (k % 4) : 128 * (k % 4) + 128] = x * scale
        outs[at].start()
    ins[1].wait()
    outs[3].start()
    for k in range(4):
        ins[2 + k].wait()
        outs[4 + k].start()
    for k in range(9):
        q, at = divmod(k, 4)
        for part in range(2):
            x = sums_ref[16 + 2 * q + part].astype(F32)
            conv_ref[k, 16 * part : 16 * part + 16, :] = x[:, 32 * at : 32 * at + 32] * scale
    outs[0].start()
    for copy in outs:
        copy.wait()


def shards(nr, nc, embed, left_proj, right_proj, conv_w, cotangent):
    per = nr // nc
    pair_out, totals, embed_grad = pl.pallas_call(
        functools.partial(pair_kernel, nr, nc),
        out_shape=(
            jax.ShapeDtypeStruct((32, 64, 256), BF16),
            jax.ShapeDtypeStruct((PIECES, 16, 128), BF16),
            jax.ShapeDtypeStruct((8, 512), F32),
        ),
        in_specs=[HBM] * 5,
        out_specs=(HBM,) * 3,
        scratch_shapes=LOCAL_SCRATCH
        + [
            pltpu.VMEM((32, 64, 256), BF16),
            pltpu.VMEM((8, 512), F32),
            pltpu.VMEM((136, 128), F32),
            pltpu.VMEM((8, 512), BF16),
            pltpu.VMEM((9, 32, 32), BF16),
            pltpu.VMEM((32, 64, 256), BF16),
            pltpu.VMEM((8, 128), F32),
            pltpu.VMEM((8, 128), F32),
            pltpu.VMEM((8, 128), F32),
            pltpu.VMEM((per, 8, 128), F32),
            pltpu.VMEM((nc, 8, 128), F32),
            pltpu.VMEM((128, 512), BF16),
            pltpu.VMEM((16, 256), BF16),
            pltpu.VMEM((nc, 16, 256), BF16),
            pltpu.VMEM((128, 512), BF16),
            pltpu.VMEM((nc, 8, 128), F32),
            pltpu.VMEM((2, 8, 128), F32),
            pltpu.VMEM((2, 8, 128), F32),
            pltpu.VMEM((per, 16, 128), F32),
            pltpu.VMEM((2, per, 8, 128), F32),
            pltpu.VMEM((2, 8, 128), F32),
            pltpu.VMEM((64, 128), F32),
            pltpu.VMEM((nc, 8, 128), F32),
            pltpu.VMEM((PIECES, 16, 128), BF16),
            pltpu.VMEM((32, 16, 128), BF16),
            pltpu.VMEM((8, 16, 128), BF16),
            pltpu.VMEM((16, 128), BF16),
            pltpu.VMEM((16, 128), BF16),
            pltpu.SemaphoreType.DMA((17,)),
            pltpu.SemaphoreType.DMA((17,)),
            pltpu.SemaphoreType.DMA((5,)),
            pltpu.SemaphoreType.DMA((6,)),
        ],
        compiler_params=pltpu.CompilerParams(
            collective_id=0, has_side_effects=True, vmem_limit_bytes=60 * 1024 * 1024
        ),
        name="pair_kernel",
    )(embed, left_proj.T, right_proj.T, conv_w, cotangent)
    conv_grad, left_t, right_t, embed_grad, pair_out = pl.pallas_call(
        functools.partial(finish_kernel, 32.0 / (8 * nr * nc)),
        out_shape=(
            jax.ShapeDtypeStruct((9, 32, 32), F32),
            jax.ShapeDtypeStruct((32, 512), F32),
            jax.ShapeDtypeStruct((32, 512), F32),
            jax.ShapeDtypeStruct((8, 512), F32),
            jax.ShapeDtypeStruct((32, 64, 256), BF16),
        ),
        in_specs=[HBM] * 3,
        out_specs=(HBM,) * 5,
        scratch_shapes=[
            pltpu.VMEM((PIECES, 16, 128), BF16),
            pltpu.VMEM((8, 512), F32),
            pltpu.VMEM((32, 64, 256), BF16),
            pltpu.VMEM((9, 32, 32), F32),
            pltpu.VMEM((32, 512), F32),
            pltpu.VMEM((32, 512), F32),
            pltpu.SemaphoreType.DMA((6,)),
            pltpu.SemaphoreType.DMA((8,)),
        ],
        compiler_params=pltpu.CompilerParams(vmem_limit_bytes=60 * 1024 * 1024),
        name="finish",
    )(totals, embed_grad, pair_out)
    return pair_out, conv_grad, left_t.T, right_t.T, embed_grad


def solution(mesh):
    body = functools.partial(shards, mesh.shape["row"], mesh.shape["col"])
    in_specs = (P(("row", "col"), None), P(), P(), P(), P(None, "row", "col"))
    out_specs = (P(None, "row", "col"), P(), P(), P(), P(("row", "col"), None))
    return jax.shard_map(body, mesh=mesh, in_specs=in_specs, out_specs=out_specs, check_vma=False)
```
